32 devices in a mesh: comp: 2 (over core), gx: 2 (over y), gy: 8 (over z, x).
Axes of the slice: x: 2, y: 2, z: 4, core: 2. Of those that a mesh axis runs over, the one named last changes fastest.
Arguments:
- state_incr: float32 [2, 2, 128, 32, 1024], P('comp', None, None, 'gx', 'gy'), may hold values from -6 to 6
- winds: float32 [2, 2, 128, 32, 1024], P('comp', None, None, 'gx', 'gy'), may hold values from -0.4 to 0.4
- coupling: float32 [32, 1024], P('gx', 'gy'), may hold values from 0.1 to 0.6
- background: float32 [2, 2, 128], P('comp'), may hold values from 0.5 to 2
- obs_dest: int32 [16384, 1], P(('comp', 'gx', 'gy')), may hold values from 0 to 15; in each aligned block of 512 rows (0 to 511, 512 to 1023, ...) at most 64 rows name the same one
- obs_col: int32 [16384], P(('comp', 'gx', 'gy')), may hold values from 0 to 2047
- obs_op: float32 [16384, 256], P(('comp', 'gx', 'gy')), may hold values from -0.375 to 0.375
- obs_prec: float32 [16384], P(('comp', 'gx', 'gy')), may hold values from 0.5 to 4
Outputs:
- hess_vec: float32 [2, 2, 128, 32, 1024], P('comp', None, None, 'gx', 'gy')
The draws below stay inside these ranges and needn't reach their ends.
Inputs may be any that keep to these rules, and one draw needn't show every extreme that they name: `obs_dest`: among the rows of one device at most 64 name the same owner, a bound that some block reaches of them; owners are tiles of the record's own component. `obs_col`: column m of a tile is its cell (m // 128, m % 128).
All inputs are finite; a program needn't handle non-finite values.
Results may differ from the reference program's by a relative error of at most 0.000057.
Values sent between devices are 32-bit elements; how exact they have to be, the bound alone decides.
No kernel may reach another device: no remote copies, remote signals or barrier semaphores. Data moves between devices by JAX's collectives and lax.ppermute only.
A program may use at most 128 MiB of HBM per device.

```python
import math
import jax
import jax.numpy as jnp
import numpy as np
from jax import lax

CX = 16
CY = 128
L = 128
OBS_DEV = 512
NX = 32
NY = 1024
OBS_CAP = 64
OBS_ALL = 16384
N_GX = 2
N_GY = 8


def place_ends(values, key, low, high):
    extent = values.shape
    spot = [jax.random.randint(jax.random.fold_in(key, axis), (), 0, extent[axis]) for axis in range(len(extent))]
    values = values.at[tuple(spot)].set(low)
    longest = extent.index(max(extent))
    spot[longest] = (spot[longest] + 1) % extent[longest]
    return values.at[tuple(spot)].set(high)


def level_of(rng, shape, shards, low, high):
    def one(axis_at, shards_of):
        draws = jax.random.uniform(jax.random.fold_in(jax.random.fold_in(rng, 6), axis_at), (shards_of,), jnp.float32, low / len(shards), high / len(shards))
        return jnp.repeat(jnp.exp(draws), shape[axis_at] // shards_of).reshape((-1,) + (1,) * (len(shape) - axis_at - 1))

    gain = one(*shards[0])
    for cut in shards[1:]:
        gain = gain * one(*cut)
    return gain


def routed_block(own_key, own, number, rows, number_of, top, bound, slope):
    ranking = jax.random.permutation(own_key, number_of)
    heavy_load, ordinary = shares(number_of, rows * top, bound, slope, True), shares(number_of, rows * top, bound, slope, False)
    places = jnp.arange(number_of)

    def named(tallies, offset_by):
        used = int((tallies > 0).sum())
        fixed = max(1, used // 4)
        moved = fixed + (places - fixed + offset_by * (used - fixed)) % max(1, number_of - fixed)
        return jnp.zeros((number_of,), jnp.int32).at[ranking[jnp.where(places < fixed, places, moved)]].set(jnp.asarray(tallies, jnp.int32))

    tallies = jnp.where(number % 4 == 0, named(heavy_load, number // 4), named(ordinary, number - number // 4 - 1))
    mixed = jax.random.permutation(jax.random.fold_in(own, 3), number_of)
    giver, receiver = mixed[0:number_of // 2 * 2:2], mixed[1:number_of // 2 * 2:2]
    margin = jnp.minimum(tallies[giver] - 1, bound - tallies[receiver]) // 2
    margin = jnp.where((giver == ranking[0]) | (receiver == ranking[0]) | (tallies[receiver] == 0), 0, jnp.maximum(margin, 0))
    moved = jax.random.randint(jax.random.fold_in(own, 4), (number_of // 2,), 0, 1 << 20) % (margin + 1)
    tallies = tallies.at[giver].add(-moved).at[receiver].add(moved)
    labels = jnp.searchsorted(jnp.cumsum(tallies), jnp.arange(rows * top), side="right").astype(jnp.int32)
    listing = labels.reshape(top, rows).T
    listing = listing[jax.random.permutation(jax.random.fold_in(own, 1), rows)]
    offset_by = jax.random.randint(jax.random.fold_in(own, 2), (rows, 1), 0, top)
    return jnp.take_along_axis(listing, (jnp.arange(top)[None, :] + offset_by) % top, axis=1)


def shares(number_of, total, most, lean, full):
    loads = [(1 << 20) // math.isqrt(standing ** lean) + 1 for standing in range(1, number_of + 1)]
    largest = most if full else min(most, max(-(-total // number_of), total * loads[0] // sum(loads)))
    least = 1 if total - largest >= number_of - 1 else 0
    counts, surplus = [largest] + [least] * (number_of - 1), total - largest - least * (number_of - 1)
    while surplus > 0:
        movable = [i for i in range(1, number_of) if counts[i] < largest] or [i for i in range(1, number_of) if counts[i] < most]
        pool, left = sum([loads[i] for i in movable]), surplus
        for i in movable:
            more = min(most - counts[i], max(1, left * loads[i] // pool), surplus)
            counts[i] = counts[i] + more
            surplus = surplus - more
    return np.array(counts)


def centred(stream_key, dims, scale, most, shards=(), kind=jnp.bfloat16):
    array = jax.random.normal(stream_key, dims, jnp.float32) * scale
    if len(shards) > 0:
        array = level_of(stream_key, dims, shards, -0.22, 0.18) * array
    return jnp.clip(array, min=-most, max=most).astype(kind)


def setup_inputs(seed: int = 0) -> dict:
    keys = jax.random.split(jax.random.key(seed), 9)
    state_incr = centred(keys[0], (2, 2, L, NX, NY), 1.0, 6.0, ((0, 2), (3, 2), (4, 8)), jnp.float32)
    winds = jnp.clip(jax.random.uniform(keys[1], (2, 2, L, NX, NY), jnp.float32, -0.4, 0.4) * level_of(keys[1], (2, 2, L, NX, NY), ((0, 2), (3, 2), (4, 8)), -0.4, 0.0), -0.4, 0.4)
    coupling = jnp.clip(jnp.exp(math.log(0.6) - 1.7917595 * jax.random.uniform(keys[2], (NX, NY), jnp.float32) ** level_of(keys[2], (NX, NY), ((0, 2), (1, 8)), -0.2, 0.2)), 0.1, 0.6)
    background = jnp.clip(jnp.exp(math.log(2.0) - 1.3862944 * jax.random.uniform(keys[3], (2, 2, L), jnp.float32) ** level_of(keys[3], (2, 2, L), ((0, 2),), -0.2, 0.2)), 0.5, 2.0)
    obs_dest_keys = jax.random.split(jax.random.fold_in(keys[4], 1), OBS_ALL // OBS_DEV)
    obs_dest_turns = jax.random.permutation(jax.random.fold_in(keys[4], 3), OBS_ALL // OBS_DEV)
    obs_dest = jax.vmap(lambda own, number: routed_block(jax.random.fold_in(keys[4], 2), own, number, OBS_DEV, N_GX * N_GY, 1, OBS_CAP, 2))(obs_dest_keys, obs_dest_turns).reshape((OBS_ALL, 1))
    obs_col = place_ends(jax.random.randint(keys[5], (OBS_ALL,), 0, CX * CY), jax.random.fold_in(keys[5], 1), 0, (CX * CY) - 1).astype(jnp.int32)
    obs_op = centred(keys[6], (OBS_ALL, 2 * L), (2 * L) ** -0.5, 0.375, ((0, 32),), jnp.float32)
    obs_prec = jnp.clip(jnp.exp(math.log(4.0) - 2.0794415 * jax.random.uniform(keys[7], (OBS_ALL,), jnp.float32) ** level_of(keys[7], (OBS_ALL,), ((0, 32),), -0.2, 0.2)), 0.5, 4.0)
    return dict(state_incr=state_incr, winds=winds, coupling=coupling, background=background, obs_dest=obs_dest, obs_col=obs_col, obs_op=obs_op, obs_prec=obs_prec)


HORIZ_MIX = 0.1
VERT_MIX = 0.15

def vertical(field):
    upper = jnp.concatenate([field[:, :, 1:], field[:, :, -1:]], axis=2)
    lower = jnp.concatenate([field[:, :, :1], field[:, :, :-1]], axis=2)
    return VERT_MIX * (upper + lower - 2.0 * field)

def stencil(field, wind_x, wind_y):
    padded = jnp.pad(field, ((0, 0), (0, 0), (0, 0), (1, 1), (1, 1)))
    wind_x = wind_x[:, None]
    wind_y = wind_y[:, None]
    result = field * (1.0 - 4.0 * HORIZ_MIX) + vertical(field)
    result = result + (HORIZ_MIX - 0.5 * wind_x) * padded[:, :, :, 2:, 1:-1]
    result = result + (HORIZ_MIX + 0.5 * wind_x) * padded[:, :, :, :-2, 1:-1]
    result = result + (HORIZ_MIX - 0.5 * wind_y) * padded[:, :, :, 1:-1, 2:]
    result = result + (HORIZ_MIX + 0.5 * wind_y) * padded[:, :, :, 1:-1, :-2]
    return result

def couple(field, coupling):
    atmos = field[0, :, 0]
    ocean = field[1, :, 0]
    atmos_new = atmos - coupling * (atmos - ocean)
    ocean_new = ocean - 0.5 * coupling * (ocean - atmos)
    return field.at[0, :, 0].set(atmos_new).at[1, :, 0].set(ocean_new)

def reference(state_incr, winds, coupling, background, obs_dest, obs_col, obs_op, obs_prec):
    wind_x = winds[:, 0]
    wind_y = winds[:, 1]

    def tangent(field):
        for sweep in range(2):
            field = couple(stencil(field, wind_x, wind_y), coupling)
        return field
    second, pullback = jax.vjp(tangent, state_incr)
    record_ids = jnp.arange(OBS_ALL, dtype=jnp.int32)
    comp_ids = (record_ids // (N_GX * N_GY * OBS_DEV)).astype(jnp.int32)
    owners = obs_dest[:, 0]
    cell_x = owners // N_GY * CX + obs_col // CY
    cell_y = owners % N_GY * CY + obs_col % CY
    weighted = obs_op * jnp.sqrt(obs_prec)[:, None]
    sampled = second[comp_ids, :, :, cell_x, cell_y].reshape(OBS_ALL, 2 * L)
    innovation = lax.optimization_barrier(jnp.sum(sampled * weighted, axis=1))
    spread = (weighted * innovation[:, None]).reshape(OBS_ALL, 2, L)
    adjoint_obs = jnp.zeros_like(second).at[comp_ids, :, :, cell_x, cell_y].add(spread)
    adjoint_init = pullback(adjoint_obs)[0]
    return background[:, :, :, None, None] * state_incr + adjoint_init
```

```python
import functools

import jax
import jax.numpy as jnp
from jax import lax
from jax.experimental import pallas as pl
from jax.experimental.pallas import tpu as pltpu
from jax.sharding import PartitionSpec as P

HORIZ_MIX = 0.1
VERT_MIX = 0.15
LANES = 128
GROUP = 8
VMEM_LIMIT = 40 * 1024 * 1024


def call(body, out_shape, scratch=(), **kw):
    return pl.pallas_call(
        body,
        out_shape=out_shape,
        scratch_shapes=list(scratch),
        compiler_params=pltpu.CompilerParams(vmem_limit_bytes=VMEM_LIMIT),
        **kw,
    )


def f32(*shape):
    return jax.ShapeDtypeStruct(shape, jnp.float32)


def lane_iota():
    return lax.broadcasted_iota(jnp.int32, (GROUP, LANES), 1)


def sub_iota():
    return lax.broadcasted_iota(jnp.int32, (GROUP, LANES), 0)


def pair_swap(block, axis, start):
    count = lax.axis_size(axis)
    route = []
    for low in range(start, count - 1, 2):
        route += [(low, low + 1), (low + 1, low)]
    return lax.ppermute(block, axis, route)


def exchange(strips, packed):
    even = pair_swap(strips[0], "gx", 0)
    odd = pair_swap(strips[1], "gx", 1) if lax.axis_size("gx") > 2 else None
    y_even = pair_swap(packed, "gy", 0)
    y_odd = pair_swap(packed, "gy", 1)
    return even, odd, y_even, y_odd


def halo_args(halos):
    even, odd, y_even, y_odd = halos
    return [even, y_even, y_odd] + ([] if odd is None else [odd])


def read_sides(scal, refs):
    even = refs[0]
    odd = refs[3] if len(refs) > 3 else None
    at_even = scal[0] == 0

    def after(at):
        other = jnp.zeros_like(even[at]) if odd is None else odd[at]
        return jnp.where(at_even, even[at], other)

    def before(at):
        other = jnp.zeros_like(even[at]) if odd is None else odd[at]
        return jnp.where(at_even, other, even[at])

    return before, after


def merge_columns(scal, y_even, y_odd, sides):
    lane = lax.broadcasted_iota(jnp.int32, sides.shape, 1)
    take_even = (lane % 2) == (1 - scal[1])
    sides[...] = jnp.where(take_even, y_even[...], y_odd[...])


def slot_of(group):
    return group // 4, group % 4


def side_columns(sides, i, group):
    m, part = slot_of(group)
    shift = LANES - 1 - 2 * (4 * i + part)
    return pltpu.roll(sides[m * GROUP : (m + 1) * GROUP, :], shift, 1)


def pack_columns(packed, value, i, group):
    m, part = slot_of(group)
    slot = 4 * i + part
    rolled = pltpu.roll(value, 2 * slot + 1, 1)
    at = pl.ds(m * GROUP, GROUP)
    packed[at, :] = jnp.where(lane_iota() // 2 == slot, rolled, packed[at, :])


def levels_around(cells, i, base, group, groups):
    here = cells[i + 1, pl.ds(base + group * GROUP, GROUP), :]
    if group == groups - 1:
        upper = jnp.where(sub_iota() == GROUP - 1, here, pltpu.roll(here, GROUP - 1, 0))
    else:
        upper = cells[i + 1, pl.ds(base + group * GROUP + 1, GROUP), :]
    if group == 0:
        lower = jnp.where(sub_iota() == 0, here, pltpu.roll(here, 1, 0))
    else:
        lower = cells[i + 1, pl.ds(base + group * GROUP - 1, GROUP), :]
    return here, upper, lower


def forward_point(cells, winds, sides, i, f, group, levels, held, wind_levels):
    base = f * held
    here, upper, lower = levels_around(cells, i, base, group, levels // GROUP)
    at = pl.ds(base + group * GROUP, GROUP)
    after, before = cells[i + 2, at, :], cells[i, at, :]
    edge = side_columns(sides, i, f * (levels // GROUP) + group)
    lane = lane_iota()
    right = pltpu.roll(jnp.where(lane == 0, edge, here), LANES - 1, 1)
    left = pltpu.roll(jnp.where(lane == LANES - 1, edge, here), 1, 1)
    u = winds[i, pl.ds(group * GROUP, GROUP), :]
    w = winds[i, pl.ds(wind_levels + group * GROUP, GROUP), :]
    return (
        (1.0 - 4.0 * HORIZ_MIX - 2.0 * VERT_MIX) * here
        + VERT_MIX * (upper + lower)
        + HORIZ_MIX * ((after + before) + (right + left))
        - 0.5 * (u * (after - before) + w * (right - left))
    )


def products(x, wind):
    slope = 0.5 * (wind * x)
    return HORIZ_MIX * x - slope, HORIZ_MIX * x + slope


def adjoint_point(cells, winds, sides, i, f, group, levels, held, wind_levels, rows):
    base = f * held
    here, upper, lower = levels_around(cells, i, base, group, levels // GROUP)
    at = pl.ds(base + group * GROUP, GROUP)
    wind_at = pl.ds(group * GROUP, GROUP)
    after, before = cells[i + 2, at, :], cells[i, at, :]
    u_after = winds[jnp.minimum(i + 1, rows - 1), wind_at, :]
    u_before = winds[jnp.maximum(i - 1, 0), wind_at, :]
    w = winds[i, pl.ds(wind_levels + group * GROUP, GROUP), :]
    down, up = products(here, w)
    edge = side_columns(sides, i, f * (levels // GROUP) + group)
    lane = lane_iota()
    right = pltpu.roll(jnp.where(lane == 0, edge, up), LANES - 1, 1)
    left = pltpu.roll(jnp.where(lane == LANES - 1, edge, down), 1, 1)
    return (
        (1.0 - 4.0 * HORIZ_MIX - 2.0 * VERT_MIX) * here
        + VERT_MIX * (upper + lower)
        + HORIZ_MIX * (after + before)
        + 0.5 * (u_after * after - u_before * before)
        + (right + left)
    )


def couple_forward(value, other, shares, i):
    own = shares[0, pl.ds(i, 1), :]
    mixed = value - own * (value - other)
    return jnp.where(sub_iota() == 0, mixed, value)


def couple_adjoint(value, other, shares, i):
    own = shares[0, pl.ds(i, 1), :]
    peer = shares[1, pl.ds(i, 1), :]
    mixed = value - own * value + peer * other
    return jnp.where(sub_iota() == 0, mixed, value)


def put_strip(scal, strip_even, strip_odd, at, first, last):
    at_even = scal[0] == 0
    strip_even[at, :] = jnp.where(at_even, last, first)
    strip_odd[at, :] = jnp.where(at_even, first, last)


def to_rows_kernel(rows, levels, scal, state, winds, state_rows, wind_rows, s_even, s_odd, packed):
    packed[...] = jnp.zeros_like(packed)
    groups = levels // GROUP

    def row(i, _):
        for c in range(2 * groups):
            at = pl.ds(c * GROUP, GROUP)
            value = state[pl.ds(c * GROUP * rows + i, GROUP, stride=rows), :]
            state_rows[i, at, :] = value
            pack_columns(packed, value, i, c)
            wind_rows[i, at, :] = winds[pl.ds(c * GROUP * rows + i, GROUP, stride=rows), :]
        return 0

    lax.fori_loop(0, rows, row, 0)
    put_strip(scal, s_even, s_odd, slice(None), state_rows[0], state_rows[rows - 1])


def fill(cells, source, rows, before=None, after=None, fix=None):
    width = source.shape[1]

    def row(i, _):
        cells[i + 1] = source[i]
        if fix is not None:
            fix(i)
        return 0

    lax.fori_loop(0, rows, row, 0)
    everything = slice(None)
    cells[0] = jnp.zeros((width, LANES), jnp.float32) if before is None else before(everything)
    cells[rows + 1] = jnp.zeros((width, LANES), jnp.float32) if after is None else after(everything)


def forward_floor_kernel(rows, levels, held, scal, field, winds, *rest):
    *halos, floor, cells, sides = rest
    merge_columns(scal, halos[1], halos[2], sides)
    before, after = read_sides(scal, halos)

    def bottom(side):
        return lambda _: jnp.concatenate([side(pl.ds(f * levels, held)) for f in range(2)], axis=0)

    def copy(i, _):
        for f in range(2):
            cells[i + 1, pl.ds(f * held, held), :] = field[i, f]
        return 0

    lax.fori_loop(0, rows, copy, 0)
    cells[0] = bottom(before)(None)
    cells[rows + 1] = bottom(after)(None)

    def row(i, _):
        for f in range(2):
            value = forward_point(cells, winds, sides, i, f, 0, levels, held, GROUP)
            floor[pl.ds(f * rows + i, 1), :] = value[0:1]
        return 0

    lax.fori_loop(0, rows, row, 0)


def forward_kernel(rows, levels, strips, scal, shares, other, field, winds, *rest):
    if strips:
        *halos, out, s_even, s_odd, packed, cells, sides = rest
        packed[...] = jnp.zeros_like(packed)
    else:
        *halos, out, cells, sides = rest
    merge_columns(scal, halos[1], halos[2], sides)
    before, after = read_sides(scal, halos)
    fill(cells, field, rows, before, after)
    groups = levels // GROUP

    def row(i, _):
        for group in range(groups):
            for f in range(2):
                value = forward_point(cells, winds, sides, i, f, group, levels, levels, levels)
                if group == 0:
                    value = couple_forward(value, other[pl.ds(f * rows + i, 1), :], shares, i)
                out[i, pl.ds(f * levels + group * GROUP, GROUP), :] = value
                if strips:
                    pack_columns(packed, value, i, f * groups + group)
        return 0

    lax.fori_loop(0, rows, row, 0)
    if strips:
        put_strip(scal, s_even, s_odd, slice(None), out[0], out[rows - 1])


def put_products(scal, s_even, s_odd, cells_first, cells_last, winds, rows, levels):
    for f in range(2):
        at = pl.ds(f * levels, levels)
        _, first = products(cells_first(at), winds[0, pl.ds(0, levels), :])
        last, _ = products(cells_last(at), winds[rows - 1, pl.ds(0, levels), :])
        put_strip(scal, s_even, s_odd, at, first, last)


def pack_products(packed, value, winds, i, f, group, levels):
    w = winds[i, pl.ds(levels + group * GROUP, GROUP), :]
    down, up = products(value, w)
    both = jnp.where(lane_iota() == 0, up, down)
    pack_columns(packed, both, i, f * (levels // GROUP) + group)


def adjoint_pack_kernel(rows, levels, scal, shares, other, field, winds, s_even, s_odd, packed):
    packed[...] = jnp.zeros_like(packed)
    groups = levels // GROUP

    def value_at(i, f, group):
        value = field[i, pl.ds(f * levels + group * GROUP, GROUP), :]
        if group == 0:
            value = couple_adjoint(value, other[pl.ds(f * rows + i, 1), :], shares, i)
        return value

    def row(i, _):
        for group in range(groups):
            for f in range(2):
                pack_products(packed, value_at(i, f, group), winds, i, f, group, levels)
        return 0

    lax.fori_loop(0, rows, row, 0)
    for f in range(2):
        for group in range(groups):
            wind_at = pl.ds(group * GROUP, GROUP)
            _, first = products(value_at(0, f, group), winds[0, wind_at, :])
            last, _ = products(value_at(rows - 1, f, group), winds[rows - 1, wind_at, :])
            put_strip(scal, s_even, s_odd, pl.ds(f * levels + group * GROUP, GROUP), first, last)


def adjoint_floor_kernel(rows, levels, held, scal, shares, other, field, winds, *rest):
    *halos, floor, cells, sides = rest
    merge_columns(scal, halos[1], halos[2], sides)
    before, after = read_sides(scal, halos)

    def copy(i, _):
        for f in range(2):
            cells[i + 1, pl.ds(f * held, held), :] = field[i, f]
            at = pl.ds(f * held, GROUP)
            cells[i + 1, at, :] = couple_adjoint(
                field[i, f, pl.ds(0, GROUP), :], other[pl.ds(f * rows + i, 1), :], shares, i
            )
        return 0

    lax.fori_loop(0, rows, copy, 0)
    cells[0] = jnp.zeros_like(cells[0])
    cells[rows + 1] = jnp.zeros_like(cells[0])

    def row(i, _):
        for f in range(2):
            value = adjoint_point(cells, winds, sides, i, f, 0, levels, held, GROUP, rows)
            floor[pl.ds(f * rows + i, 1), :] = value[0:1]
        return 0

    lax.fori_loop(0, rows, row, 0)
    for f in range(2):
        at = pl.ds(f * levels, GROUP)
        floor[pl.ds(f * rows, 1), :] += before(at)[0:1]
        floor[pl.ds(f * rows + rows - 1, 1), :] += after(at)[0:1]


def adjoint_kernel(rows, levels, scal, shares, other, other_next, field, winds, *rest):
    *halos, out, s_even, s_odd, packed, cells, sides = rest
    packed[...] = jnp.zeros_like(packed)
    merge_columns(scal, halos[1], halos[2], sides)
    before, after = read_sides(scal, halos)
    groups = levels // GROUP

    def fix(i):
        for f in range(2):
            at = pl.ds(f * levels, GROUP)
            cells[i + 1, at, :] = couple_adjoint(
                field[i, at, :], other[pl.ds(f * rows + i, 1), :], shares, i
            )

    fill(cells, field, rows, fix=fix)

    def point(i, group, f, extra=None):
        at = pl.ds(f * levels + group * GROUP, GROUP)
        value = adjoint_point(cells, winds, sides, i, f, group, levels, levels, levels, rows)
        if extra is not None:
            value = value + extra(at)
        if group == 0:
            value = couple_adjoint(value, other_next[pl.ds(f * rows + i, 1), :], shares, i)
        out[i, at, :] = value
        pack_products(packed, value, winds, i, f, group, levels)

    def row(i, extra=None):
        for group in range(groups):
            for f in range(2):
                point(i, group, f, extra)
        return 0

    row(0, before)
    row(rows - 1, after)
    lax.fori_loop(1, rows - 1, lambda i, _: row(i), 0)
    put_products(scal, s_even, s_odd, lambda at: out[0, at, :], lambda at: out[rows - 1, at, :], winds, rows, levels)


def final_kernel(rows, levels, scal, scale, field, winds, state, *rest):
    *halos, out, cells, sides = rest
    merge_columns(scal, halos[1], halos[2], sides)
    before, after = read_sides(scal, halos)
    groups = levels // GROUP
    fill(cells, field, rows)

    def row(i, extra=None):
        for group in range(groups):
            for f in range(2):
                at = pl.ds(f * levels + group * GROUP, GROUP)
                value = adjoint_point(cells, winds, sides, i, f, group, levels, levels, levels, rows)
                if extra is not None:
                    value = value + extra(at)
                value = value + scale[at, :] * state[i, at, :]
                out[pl.ds((f * levels + group * GROUP) * rows + i, GROUP, stride=rows), :] = value
        return 0

    row(0, before)
    row(rows - 1, after)
    lax.fori_loop(1, rows - 1, lambda i, _: row(i), 0)


def split(value, terms):
    parts = []
    for _ in range(terms):
        part = value.astype(jnp.bfloat16)
        parts.append(part)
        value = value - part.astype(jnp.float32)
    return parts


def dot(a, b, contract):
    return lax.dot_general(a, b, ((contract[:1], contract[1:]), ((), ())), preferred_element_type=jnp.float32)


def route_kernel(tiles, cap, dest, col, prec, op, out):
    count = op.shape[0]
    width = op.shape[1]
    halves = width // LANES
    owner = lax.broadcasted_iota(jnp.int32, (tiles, count), 0)
    hits = owner == dest[...]
    ones = jnp.where(hits, 1.0, 0.0)
    earlier = lax.broadcasted_iota(jnp.int32, (count, count), 0) <= lax.broadcasted_iota(jnp.int32, (count, count), 1)
    running = dot(ones.astype(jnp.bfloat16), jnp.where(earlier, 1.0, 0.0).astype(jnp.bfloat16), (1, 0))
    slot = jnp.sum(running * ones, axis=0, keepdims=True) - 1.0
    slot = slot.astype(jnp.int32)
    place = dest[...] * cap + slot
    at_slot = lax.broadcasted_iota(jnp.int32, (LANES, count), 0) == slot
    at_slot = jnp.where(at_slot, 1.0, 0.0).astype(jnp.bfloat16)
    column = col[...].astype(jnp.float32)
    pieces = [ones * part.astype(jnp.float32) for part in split(column, 2) + split(prec[...], 3)]
    aux = dot(jnp.concatenate(pieces, axis=0).astype(jnp.bfloat16), at_slot, (1, 1))
    columns = aux[0:tiles] + aux[tiles : 2 * tiles]
    precs = (aux[2 * tiles : 3 * tiles] + aux[3 * tiles : 4 * tiles]) + aux[4 * tiles : 5 * tiles]
    sub = sub_iota()
    for owner_at in range(tiles):
        block = jnp.where(sub == 0, columns[owner_at : owner_at + 1], 0.0)
        block = jnp.where(sub == 1, precs[owner_at : owner_at + 1], block)
        out[owner_at, pl.ds(halves * cap, GROUP), :] = block
    rows_high, rows_low = split(op[...], 2)
    chunk = 256
    for first in range(0, tiles * cap, chunk):
        picks = lax.broadcasted_iota(jnp.int32, (chunk, count), 0) + first == place
        picks = jnp.where(picks, 1.0, 0.0).astype(jnp.bfloat16)
        moved = dot(picks, rows_high, (1, 0)) + dot(picks, rows_low, (1, 0))
        for part in range(chunk // cap):
            for half in range(halves):
                out[first // cap + part, pl.ds(half * cap, cap), :] = moved[
                    part * cap : (part + 1) * cap, half * LANES : (half + 1) * LANES
                ]


def observe_kernel(rows, width, tiles, cap, records, field, adjoint, floor, cols, sel, places, precs, spread):
    halves = width // LANES
    block = halves * cap + GROUP
    for i in range(rows):
        high, low = split(field[i], 2)
        cols[0:width, i * LANES : (i + 1) * LANES] = high
        cols[width:, i * LANES : (i + 1) * LANES] = low
    lane = lax.broadcasted_iota(jnp.int32, (cap, LANES), 1)
    own = lane == lax.broadcasted_iota(jnp.int32, (cap, LANES), 0)

    def source(s, _):
        aux = records[s, pl.ds(halves * cap, GROUP), :]
        at = pl.ds(pl.multiple_of(s * cap, cap), cap)
        for part, target in enumerate((places, precs)):
            value = jnp.sum(jnp.where(own, aux[part : part + 1], 0.0), axis=1, keepdims=True)
            target[at, :] = jnp.broadcast_to(value, (cap, LANES))
        return 0

    step = 64
    lane = lax.broadcasted_iota(jnp.int32, (step, LANES), 1).astype(jnp.float32)

    def select(block, _):
        at = pl.ds(pl.multiple_of(block * step, step), step)
        column = places[at, :] - lane
        for i in range(rows):
            sel[at, i * LANES : (i + 1) * LANES] = jnp.where(column == float(i * LANES), 1.0, 0.0).astype(jnp.bfloat16)
        return 0

    chunk = 256
    for first in range(0, tiles * cap, chunk):
        lax.fori_loop(first // cap, (first + chunk) // cap, source, 0)
        lax.fori_loop(first // step, (first + chunk) // step, select, 0)
        both = dot(sel[first : first + chunk, :], cols[...], (1, 1))
        sampled = both[:, :width] + both[:, width:]
        sources = range(first // cap, (first + chunk) // cap)
        ops = [
            jnp.concatenate([records[s, half * cap : (half + 1) * cap, :] for s in sources], axis=0)
            for half in range(halves)
        ]
        total = sum(sampled[:, half * LANES : (half + 1) * LANES] * ops[half] for half in range(halves))
        innovation = jnp.sum(total, axis=1, keepdims=True) * precs[first : first + chunk, :]
        for half in range(halves):
            high, low = split((ops[half] * innovation).T, 2)
            spread[half * LANES : (half + 1) * LANES, first : first + chunk] = high
            spread[width + half * LANES : width + (half + 1) * LANES, first : first + chunk] = low
    for i in range(0, rows, 2):
        both = dot(spread[...], sel[:, i * LANES : (i + 2) * LANES], (1, 0))
        sums = both[:width] + both[width:]
        adjoint[i] = sums[:, :LANES]
        adjoint[i + 1] = sums[:, LANES:]
    for f in range(2):
        for i in range(rows):
            floor[f * rows + i : f * rows + i + 1, :] = adjoint[i, f * (width // 2) : f * (width // 2) + 1, :]


def local(state_incr, winds, coupling, background, obs_dest, obs_col, obs_op, obs_prec):
    _, fields, levels, rows, lanes = state_incr.shape
    width = fields * levels
    groups = width // GROUP
    held = 2 * GROUP
    tiles = lax.axis_size("gx") * lax.axis_size("gy")
    count = obs_col.shape[0]
    cap = 2 * count // tiles
    halves = obs_op.shape[1] // LANES

    scal = jnp.stack([lax.axis_index("gx") % 2, lax.axis_index("gy") % 2]).astype(jnp.int32)
    own_share = jnp.where(lax.axis_index("comp") == 0, 1.0, 0.5)
    shares = jnp.stack([own_share * coupling, (1.5 - own_share) * coupling])

    smem = pl.BlockSpec(memory_space=pltpu.SMEM)
    vmem = pl.BlockSpec(memory_space=pltpu.VMEM)
    cells_shape = pltpu.VMEM((rows + 2, width, LANES), jnp.float32)
    packed_shape = f32(groups // 4 * GROUP, LANES)
    sides_shape = pltpu.VMEM(packed_shape.shape, jnp.float32)
    strip_shape = f32(width, LANES)
    field_shape = f32(rows, width, LANES)
    floor_shape = f32(fields * rows, LANES)

    def swap_floor(floor):
        return lax.ppermute(floor, "comp", [(0, 1), (1, 0)])

    send = call(functools.partial(route_kernel, tiles, cap), f32(tiles, halves * cap + GROUP, LANES))(
        obs_dest.reshape(1, count), obs_col.reshape(1, count), obs_prec.reshape(1, count), obs_op
    )
    records = lax.all_to_all(send, ("gx", "gy"), split_axis=0, concat_axis=0, tiled=True)

    field, wind_rows, s_even, s_odd, packed = call(
        functools.partial(to_rows_kernel, rows, levels),
        [field_shape, field_shape, strip_shape, strip_shape, packed_shape],
        in_specs=[smem, vmem, vmem],
    )(scal, state_incr.reshape(width * rows, lanes), winds.reshape(width * rows, lanes))
    state_rows = field

    floor_winds = wind_rows.reshape(rows, 2, levels, lanes)[:, :, :GROUP].reshape(rows, 2 * GROUP, lanes)

    for sweep in range(2):
        halos = halo_args(exchange((s_even, s_odd), packed))
        floor = call(
            functools.partial(forward_floor_kernel, rows, levels, held),
            floor_shape,
            [pltpu.VMEM((rows + 2, fields * held, LANES), jnp.float32), sides_shape],
            grid=(1,),
            in_specs=[smem, pl.BlockSpec((rows, fields, held, LANES), lambda _: (0, 0, 0, 0)), vmem]
            + [vmem] * len(halos),
        )(scal, field.reshape(rows, fields, levels, lanes), floor_winds, *halos)
        other = swap_floor(floor)
        more = sweep == 0
        result = call(
            functools.partial(forward_kernel, rows, levels, more),
            [field_shape] + ([strip_shape, strip_shape, packed_shape] if more else []),
            [cells_shape, sides_shape],
            in_specs=[smem] + [vmem] * (4 + len(halos)),
        )(scal, shares, other, field, wind_rows, *halos)
        if more:
            field, s_even, s_odd, packed = result
        else:
            (field,) = result

    adjoint, floor = call(
        functools.partial(observe_kernel, rows, width, tiles, cap),
        [field_shape, floor_shape],
        [
            pltpu.VMEM((2 * width, rows * LANES), jnp.bfloat16),
            pltpu.VMEM((tiles * cap, rows * LANES), jnp.bfloat16),
            pltpu.VMEM((tiles * cap, LANES), jnp.float32),
            pltpu.VMEM((tiles * cap, LANES), jnp.float32),
            pltpu.VMEM((2 * width, tiles * cap), jnp.bfloat16),
        ],
    )(records, field)

    other = swap_floor(floor)
    s_even, s_odd, packed = call(
        functools.partial(adjoint_pack_kernel, rows, levels),
        [strip_shape, strip_shape, packed_shape],
        in_specs=[smem] + [vmem] * 4,
    )(scal, shares, other, adjoint, wind_rows)
    halos = halo_args(exchange((s_even, s_odd), packed))
    floor = call(
        functools.partial(adjoint_floor_kernel, rows, levels, held),
        floor_shape,
        [pltpu.VMEM((rows + 2, fields * held, LANES), jnp.float32), sides_shape],
        grid=(1,),
        in_specs=[smem, vmem, vmem, pl.BlockSpec((rows, fields, held, LANES), lambda _: (0, 0, 0, 0)), vmem]
        + [vmem] * len(halos),
    )(scal, shares, other, adjoint.reshape(rows, fields, levels, lanes), floor_winds, *halos)
    other_next = swap_floor(floor)
    adjoint, s_even, s_odd, packed = call(
        functools.partial(adjoint_kernel, rows, levels),
        [field_shape, strip_shape, strip_shape, packed_shape],
        [cells_shape, sides_shape],
        in_specs=[smem] + [vmem] * (5 + len(halos)),
    )(scal, shares, other, other_next, adjoint, wind_rows, *halos)
    halos = halo_args(exchange((s_even, s_odd), packed))
    scale = jnp.broadcast_to(background.reshape(width, 1), (width, LANES))
    result = call(
        functools.partial(final_kernel, rows, levels),
        f32(width * rows, LANES),
        [cells_shape, sides_shape],
        in_specs=[smem] + [vmem] * (4 + len(halos)),
    )(scal, scale, adjoint, wind_rows, state_rows, *halos)
    return result.reshape(state_incr.shape)


def solution(mesh):
    placed = (
        P("comp", None, None, "gx", "gy"),
        P("comp", None, None, "gx", "gy"),
        P("gx", "gy"),
        P("comp", None, None),
        P(("comp", "gx", "gy"), None),
        P(("comp", "gx", "gy")),
        P(("comp", "gx", "gy"), None),
        P(("comp", "gx", "gy")),
    )
    return jax.shard_map(
        local,
        mesh=mesh,
        in_specs=placed,
        out_specs=P("comp", None, None, "gx", "gy"),
        check_vma=False,
    )
```

```python
import functools

import jax
import jax.numpy as jnp
from jax import lax
from jax.experimental import pallas as pl
from jax.experimental.pallas import tpu as pltpu
from jax.sharding import PartitionSpec as P

HORIZ_MIX = 0.1
VERT_MIX = 0.15
LANES = 128
GROUP = 8
MIB = 1024 * 1024
SWEEP_VMEM = 14 * MIB
OBSERVE_VMEM = 20 * MIB


def call(body, out_shape, scratch=(), limit=SWEEP_VMEM, **kw):
    return pl.pallas_call(
        body,
        out_shape=out_shape,
        scratch_shapes=list(scratch),
        compiler_params=pltpu.CompilerParams(vmem_limit_bytes=limit),
        **kw,
    )


def f32(*shape):
    return jax.ShapeDtypeStruct(shape, jnp.float32)


def lane_iota(rows=GROUP):
    return lax.broadcasted_iota(jnp.int32, (rows, LANES), 1)


def sub_iota(rows=GROUP):
    return lax.broadcasted_iota(jnp.int32, (rows, LANES), 0)


def pair_swap(block, axis, start):
    count = lax.axis_size(axis)
    route = []
    for low in range(start, count - 1, 2):
        route += [(low, low + 1), (low + 1, low)]
    return lax.ppermute(block, axis, route)


def exchange(strips, packed):
    y_even = pair_swap(packed, "gy", 0)
    y_odd = pair_swap(packed, "gy", 1)
    halos = [pair_swap(strips[0], "gx", 0), y_even, y_odd]
    if lax.axis_size("gx") > 2:
        halos.append(pair_swap(strips[1], "gx", 1))
    return halos


def read_sides(scal, refs):
    even = refs[0]
    odd = refs[3] if len(refs) > 3 else None
    at_even = scal[0] == 0

    def after(at):
        other = jnp.zeros_like(even[at]) if odd is None else odd[at]
        return jnp.where(at_even, even[at], other)

    def before(at):
        other = jnp.zeros_like(even[at]) if odd is None else odd[at]
        return jnp.where(at_even, other, even[at])

    return before, after


PARTS = 4


def merged(scal, y_even, y_odd, at):
    a, b = y_even[at, :], y_odd[at, :]
    lane = lax.broadcasted_iota(jnp.int32, a.shape, 1)
    return jnp.where((lane % 2) == (1 - scal[1]), a, b)


def merge_columns(scal, y_even, y_odd, sides):
    sides[...] = merged(scal, y_even, y_odd, slice(None))


def slot_of(i, part, rows):
    return PARTS * (rows - 1 - i) + part


def side_columns(sides, i, group):
    m, part = group // PARTS, group % PARTS
    rows = LANES // (2 * PARTS)
    return pltpu.roll(sides[m * GROUP : (m + 1) * GROUP, :], LANES - 1 - 2 * slot_of(i, part, rows), 1)


def pack_into(total, value, slot):
    return jnp.where(lane_iota() // 2 == slot, pltpu.roll(value, 2 * slot + 1, 1), total)


def pack_block(packed, values, i, m):
    at = pl.ds(m * GROUP, GROUP)
    total = packed[at, :]
    for part, value in enumerate(values):
        total = pack_into(total, value, slot_of(i, part, LANES // (2 * PARTS)))
    packed[at, :] = total


CENTRE = 1.0 - 4.0 * HORIZ_MIX - 2.0 * VERT_MIX


def levels_around(cells, i, base, group, groups):
    here = cells[i + 1, pl.ds(base + group * GROUP, GROUP), :]
    if group == groups - 1:
        upper = jnp.where(sub_iota() == GROUP - 1, here, pltpu.roll(here, GROUP - 1, 0))
    else:
        upper = cells[i + 1, pl.ds(base + group * GROUP + 1, GROUP), :]
    if group == 0:
        lower = jnp.where(sub_iota() == 0, here, pltpu.roll(here, 1, 0))
    else:
        lower = cells[i + 1, pl.ds(base + group * GROUP - 1, GROUP), :]
    return here, upper, lower


def shifted(first, last, edge, rows=GROUP):
    lane = lane_iota(rows)
    right = pltpu.roll(jnp.where(lane == 0, edge, first), LANES - 1, 1)
    left = pltpu.roll(jnp.where(lane == LANES - 1, edge, last), 1, 1)
    return right, left


def forward_sum(here, vertical, after, before, right, left, u, w):
    return (
        CENTRE * here
        + VERT_MIX * vertical
        + HORIZ_MIX * ((after + before) + (right + left))
        - 0.5 * (u * (after - before) + w * (right - left))
    )


def forward_point(cells, winds, sides, i, f, group, levels):
    groups = levels // GROUP
    here, upper, lower = levels_around(cells, i, f * levels, group, groups)
    at = pl.ds(f * levels + group * GROUP, GROUP)
    right, left = shifted(here, here, side_columns(sides, i, f * groups + group))
    u = winds[i + 1, pl.ds(group * GROUP, GROUP), :]
    w = winds[i + 1, pl.ds(levels + group * GROUP, GROUP), :]
    return forward_sum(here, upper + lower, cells[i + 2, at, :], cells[i, at, :], right, left, u, w)


def products(x, wind):
    slope = 0.5 * (wind * x)
    return HORIZ_MIX * x - slope, HORIZ_MIX * x + slope


def adjoint_point(cells, winds, sides, i, f, group, levels):
    groups = levels // GROUP
    here, upper, lower = levels_around(cells, i, f * levels, group, groups)
    at = pl.ds(f * levels + group * GROUP, GROUP)
    wind_at = pl.ds(group * GROUP, GROUP)
    after, before = cells[i + 2, at, :], cells[i, at, :]
    u_after, u_before = winds[i + 2, wind_at, :], winds[i, wind_at, :]
    w = winds[i + 1, pl.ds(levels + group * GROUP, GROUP), :]
    down, up = products(here, w)
    right, left = shifted(up, down, side_columns(sides, i, f * groups + group))
    return (
        CENTRE * here
        + VERT_MIX * (upper + lower)
        + HORIZ_MIX * (after + before)
        + 0.5 * (u_after * after - u_before * before)
        + (right + left)
    )


def couple_forward(value, other, shares):
    return value - shares[0] * (value - other)


def couple_adjoint(value, other, shares):
    return value - shares[0] * value + shares[1] * other


def coupled(rule, value, other, shares, i, f, rows):
    here = [shares[part, pl.ds(i, 1), :] for part in range(2)]
    return jnp.where(sub_iota() == 0, rule(value, other[pl.ds(f * rows + i, 1), :], here), value)


def put_strip(scal, strip_even, strip_odd, at, first, last):
    at_even = scal[0] == 0
    strip_even[at, :] = jnp.where(at_even, last, first)
    strip_odd[at, :] = jnp.where(at_even, first, last)


def edges_kernel(rows, levels, scal, state, s_even, s_odd, packed):
    width = state.shape[0] // rows

    def block(m, _):
        total = jnp.zeros((GROUP, LANES), jnp.float32)
        for part in range(PARTS):
            for i in range(rows):
                start = (m * PARTS + part) * GROUP * rows + i
                total = pack_into(total, state[pl.ds(start, GROUP, stride=rows), :], slot_of(i, part, rows))
        packed[pl.ds(pl.multiple_of(m * GROUP, GROUP), GROUP), :] = total
        return 0

    lax.fori_loop(0, width // (PARTS * GROUP), block, 0)
    first = state[pl.ds(0, width, stride=rows), :]
    last = state[pl.ds(rows - 1, width, stride=rows), :]
    put_strip(scal, s_even, s_odd, slice(None), first, last)


def to_rows_kernel(rows, state, winds, state_rows, wind_rows):
    width = state_rows.shape[1]

    def row(i, _):
        for c in range(width // GROUP):
            at = pl.ds(c * GROUP, GROUP)
            start = pl.ds(c * GROUP * rows + i, GROUP, stride=rows)
            state_rows[i, at, :] = state[start, :]
            wind_rows[i + 1, at, :] = winds[start, :]
        return 0

    lax.fori_loop(0, rows, row, 0)
    wind_rows[0] = jnp.zeros((width, LANES), jnp.float32)
    wind_rows[rows + 1] = jnp.zeros((width, LANES), jnp.float32)


def floor_inputs(scal, field, winds, halos, f, rows, levels):
    width = 2 * levels
    low = field[pl.ds(f * levels, rows, stride=width), :]
    next_up = field[pl.ds(f * levels + 1, rows, stride=width), :]
    u = winds[pl.ds(width, rows, stride=width), :]
    w = winds[pl.ds(width + levels, rows, stride=width), :]
    m = f * (levels // GROUP) // PARTS
    sides = jnp.broadcast_to(merged(scal, halos[1], halos[2], pl.ds(m * GROUP, 1)), (rows, LANES))
    edge = pltpu.roll(sides, 2 * PARTS - 1, 1, stride=2 * PARTS, stride_axis=0)
    return low, next_up, u, w, edge


def neighbours(value, first, last, rows):
    after = jnp.where(sub_iota(rows) == rows - 1, last, pltpu.roll(value, rows - 1, 0))
    before = jnp.where(sub_iota(rows) == 0, first, pltpu.roll(value, 1, 0))
    return after, before


def forward_floor_kernel(rows, levels, scal, field, winds, *rest):
    *halos, floor = rest
    side_before, side_after = read_sides(scal, halos)
    for f in range(2):
        low, up, u, w, edge = floor_inputs(scal, field, winds, halos, f, rows, levels)
        at = pl.ds(f * levels, 1)
        after, before = neighbours(low, side_before(at), side_after(at), rows)
        right, left = shifted(low, low, edge, rows)
        floor[f * rows : (f + 1) * rows, :] = forward_sum(low, up + low, after, before, right, left, u, w)


def adjoint_floor_kernel(rows, levels, scal, shares, other, field, winds, *rest):
    *halos, floor = rest
    side_before, side_after = read_sides(scal, halos)
    for f in range(2):
        low, up, u, w, edge = floor_inputs(scal, field, winds, halos, f, rows, levels)
        low = couple_adjoint(low, other[f * rows : (f + 1) * rows, :], shares)
        at = pl.ds(f * levels, 1)
        x_down, x_up = products(low, u)
        after, _ = neighbours(x_up, side_before(at), side_after(at), rows)
        _, before = neighbours(x_down, side_before(at), side_after(at), rows)
        down, up_wind = products(low, w)
        right, left = shifted(up_wind, down, edge, rows)
        floor[f * rows : (f + 1) * rows, :] = (
            CENTRE * low + VERT_MIX * (up + low) + (after + before) + (right + left)
        )


def fill(cells, source, rows, before, after, fix=None):
    def row(i, _):
        cells[i + 1] = source[i]
        if fix is not None:
            fix(i)
        return 0

    lax.fori_loop(0, rows, row, 0)
    cells[0] = before
    cells[rows + 1] = after


def forward_kernel(rows, levels, last, scal, shares, other, field, winds, *rest):
    if last:
        *halos, cols, cells, sides = rest
    else:
        *halos, out, s_even, s_odd, packed, cells, sides = rest
        packed[...] = jnp.zeros_like(packed)
    merge_columns(scal, halos[1], halos[2], sides)
    before, after = read_sides(scal, halos)
    fill(cells, field, rows, before(slice(None)), after(slice(None)))
    groups = levels // GROUP
    width = 2 * levels

    def row(i, _):
        for m in range(2 * groups // PARTS):
            f, first = m * PARTS // groups, m * PARTS % groups
            values = []
            for group in range(first, first + PARTS):
                value = forward_point(cells, winds, sides, i, f, group, levels)
                if group == 0:
                    value = coupled(couple_forward, value, other, shares, i, f, rows)
                values.append(value)
            base = m * PARTS * GROUP
            if last:
                lanes = pl.ds(pl.multiple_of(i * LANES, LANES), LANES)
                high, low = split(jnp.concatenate(values, axis=0), 2)
                cols[pl.ds(base, PARTS * GROUP), lanes] = high
                cols[pl.ds(width + base, PARTS * GROUP), lanes] = low
            else:
                for part, value in enumerate(values):
                    out[i, pl.ds(base + part * GROUP, GROUP), :] = value
                pack_block(packed, values, i, m)
        return 0

    lax.fori_loop(0, rows, row, 0)
    if not last:
        put_strip(scal, s_even, s_odd, slice(None), out[0], out[rows - 1])


def put_products(scal, s_even, s_odd, first_row, last_row, winds, rows, levels):
    for f in range(2):
        at = pl.ds(f * levels, levels)
        _, first = products(first_row(at), winds[1, pl.ds(0, levels), :])
        last, _ = products(last_row(at), winds[rows, pl.ds(0, levels), :])
        put_strip(scal, s_even, s_odd, at, first, last)


def with_products(value, winds, i, group, levels):
    down, up = products(value, winds[i + 1, pl.ds(levels + group * GROUP, GROUP), :])
    return jnp.where(lane_iota() == 0, up, down)


def adjoint_pack_kernel(rows, levels, scal, shares, other, field, winds, out, s_even, s_odd, packed):
    packed[...] = jnp.zeros_like(packed)
    groups = levels // GROUP

    def row(i, _):
        for m in range(2 * groups // PARTS):
            f, first = m * PARTS // groups, m * PARTS % groups
            values = []
            for group in range(first, first + PARTS):
                at = pl.ds(f * levels + group * GROUP, GROUP)
                value = field[i, at, :]
                if group == 0:
                    value = coupled(couple_adjoint, value, other, shares, i, f, rows)
                    out[i, pl.ds(f * GROUP, GROUP), :] = value
                values.append(with_products(value, winds, i, group, levels))
            pack_block(packed, values, i, m)
        return 0

    lax.fori_loop(0, rows, row, 0)

    def coupled_row(i):
        def read(at):
            f = at.start // levels
            bottom = out[i, pl.ds(f * GROUP, GROUP), :]
            return jnp.concatenate([bottom, field[i, pl.ds(f * levels + GROUP, levels - GROUP), :]], axis=0)

        return read

    put_products(scal, s_even, s_odd, coupled_row(0), coupled_row(rows - 1), winds, rows, levels)


def adjoint_kernel(rows, levels, scal, shares, bottom, other_next, field, winds, *rest):
    *halos, out, s_even, s_odd, packed, cells, sides = rest
    packed[...] = jnp.zeros_like(packed)
    merge_columns(scal, halos[1], halos[2], sides)
    before, after = read_sides(scal, halos)
    groups = levels // GROUP

    def fix(i):
        for f in range(2):
            cells[i + 1, pl.ds(f * levels, GROUP), :] = bottom[i, pl.ds(f * GROUP, GROUP), :]

    everything = slice(None)
    fill(cells, field, rows, before(everything) / HORIZ_MIX, after(everything) / HORIZ_MIX, fix)

    def row(i, _):
        for m in range(2 * groups // PARTS):
            f, first = m * PARTS // groups, m * PARTS % groups
            values = []
            for group in range(first, first + PARTS):
                value = adjoint_point(cells, winds, sides, i, f, group, levels)
                if group == 0:
                    value = coupled(couple_adjoint, value, other_next, shares, i, f, rows)
                out[i, pl.ds(f * levels + group * GROUP, GROUP), :] = value
                values.append(with_products(value, winds, i, group, levels))
            pack_block(packed, values, i, m)
        return 0

    lax.fori_loop(0, rows, row, 0)
    put_products(scal, s_even, s_odd, lambda at: out[0, at, :], lambda at: out[rows - 1, at, :], winds, rows, levels)


def final_kernel(rows, levels, scal, scale, field, winds, state, *rest):
    *halos, out, cells, sides = rest
    merge_columns(scal, halos[1], halos[2], sides)
    before, after = read_sides(scal, halos)
    groups = levels // GROUP
    everything = slice(None)
    fill(cells, field, rows, before(everything) / HORIZ_MIX, after(everything) / HORIZ_MIX)

    def row(i, _):
        for group in range(groups):
            for f in range(2):
                at = pl.ds(f * levels + group * GROUP, GROUP)
                value = adjoint_point(cells, winds, sides, i, f, group, levels)
                value = value + scale[at, :] * state[i, at, :]
                out[pl.ds((f * levels + group * GROUP) * rows + i, GROUP, stride=rows), :] = value
        return 0

    lax.fori_loop(0, rows, row, 0)


def split(value, terms):
    parts = []
    for _ in range(terms):
        part = value.astype(jnp.bfloat16)
        parts.append(part)
        value = value - part.astype(jnp.float32)
    return parts


def dot(a, b, contract):
    return lax.dot_general(a, b, ((contract[:1], contract[1:]), ((), ())), preferred_element_type=jnp.float32)


def route_kernel(tiles, cap, dest, col, prec, op, out):
    count = op.shape[0]
    width = op.shape[1]
    halves = width // LANES
    owner = lax.broadcasted_iota(jnp.int32, (tiles, count), 0)
    hits = owner == dest[...]
    ones = jnp.where(hits, 1.0, 0.0)
    earlier = lax.broadcasted_iota(jnp.int32, (count, count), 0) <= lax.broadcasted_iota(jnp.int32, (count, count), 1)
    running = dot(ones.astype(jnp.bfloat16), jnp.where(earlier, 1.0, 0.0).astype(jnp.bfloat16), (1, 0))
    slot = jnp.sum(running * ones, axis=0, keepdims=True) - 1.0
    slot = slot.astype(jnp.int32)
    place = dest[...] * cap + slot
    at_slot = lax.broadcasted_iota(jnp.int32, (LANES, count), 0) == slot
    at_slot = jnp.where(at_slot, 1.0, 0.0).astype(jnp.bfloat16)
    column = col[...].astype(jnp.float32)
    pieces = [ones * part.astype(jnp.float32) for part in split(column, 2) + split(prec[...], 3)]
    aux = dot(jnp.concatenate(pieces, axis=0).astype(jnp.bfloat16), at_slot, (1, 1))
    columns = aux[0:tiles] + aux[tiles : 2 * tiles]
    precs = (aux[2 * tiles : 3 * tiles] + aux[3 * tiles : 4 * tiles]) + aux[4 * tiles : 5 * tiles]
    sub = sub_iota()
    for owner_at in range(tiles):
        block = jnp.where(sub == 0, columns[owner_at : owner_at + 1], 0.0)
        block = jnp.where(sub == 1, precs[owner_at : owner_at + 1], block)
        out[owner_at, pl.ds(halves * cap, GROUP), :] = block
    rows_high, rows_low = split(op[...], 2)
    chunk = 256
    for first in range(0, tiles * cap, chunk):
        picks = lax.broadcasted_iota(jnp.int32, (chunk, count), 0) + first == place
        picks = jnp.where(picks, 1.0, 0.0).astype(jnp.bfloat16)
        moved = dot(picks, rows_high, (1, 0)) + dot(picks, rows_low, (1, 0))
        for part in range(chunk // cap):
            for half in range(halves):
                out[first // cap + part, pl.ds(half * cap, cap), :] = moved[
                    part * cap : (part + 1) * cap, half * LANES : (half + 1) * LANES
                ]


def observe_kernel(rows, width, tiles, cap, records, cols, adjoint, floor, sel, precs, both, spread):
    halves = width // LANES
    count = tiles * cap
    aux = halves * cap
    own = lax.broadcasted_iota(jnp.int32, (cap, LANES), 1) == lax.broadcasted_iota(jnp.int32, (cap, LANES), 0)
    ones = jnp.ones((LANES, LANES), jnp.bfloat16)
    step = 256
    lane = lax.broadcasted_iota(jnp.int32, (step, LANES), 1).astype(jnp.float32)

    def select(block, _):
        sources = step // cap

        def spread_out(part):
            rows_of = [
                jnp.where(own, records[block * sources + s, pl.ds(aux + part, 1), :], 0.0) for s in range(sources)
            ]
            terms = split(jnp.concatenate(rows_of, axis=0), 2 + part)
            return sum(dot(term, ones, (1, 0)) for term in terms)

        at = pl.ds(pl.multiple_of(block * step, step), step)
        column = spread_out(0) - lane
        precs[at, :] = spread_out(1)
        for i in range(rows):
            sel[at, i * LANES : (i + 1) * LANES] = jnp.where(column == float(i * LANES), 1.0, 0.0).astype(jnp.bfloat16)
        return 0

    lax.fori_loop(0, count // step, select, 0)
    both[...] = dot(sel[...], cols[...], (1, 1))

    def weigh(block, _):
        at = pl.ds(pl.multiple_of(block * LANES, LANES), LANES)
        sources = LANES // cap
        ops = [
            jnp.concatenate(
                [records[block * sources + s, half * cap : (half + 1) * cap, :] for s in range(sources)], axis=0
            )
            for half in range(halves)
        ]
        total = sum(
            (both[at, half * LANES : (half + 1) * LANES] + both[at, width + half * LANES : width + (half + 1) * LANES])
            * ops[half]
            for half in range(halves)
        )
        innovation = jnp.sum(total, axis=1, keepdims=True) * precs[at, :]
        for half in range(halves):
            high, low = split((ops[half] * innovation).T, 2)
            spread[half * LANES : (half + 1) * LANES, at] = high
            spread[width + half * LANES : width + (half + 1) * LANES, at] = low
        return 0

    lax.fori_loop(0, count // LANES, weigh, 0)
    sums = dot(spread[...], sel[...], (1, 0))
    for i in range(rows):
        lanes = slice(i * LANES, (i + 1) * LANES)
        adjoint[i] = sums[:width, lanes] + sums[width:, lanes]
        for f in range(2):
            floor[f * rows + i : f * rows + i + 1, :] = adjoint[i, f * (width // 2) : f * (width // 2) + 1, :]


def local(state_incr, winds, coupling, background, obs_dest, obs_col, obs_op, obs_prec):
    _, fields, levels, rows, lanes = state_incr.shape
    width = fields * levels
    groups = width // GROUP
    tiles = lax.axis_size("gx") * lax.axis_size("gy")
    count = obs_col.shape[0]
    cap = 2 * count // tiles
    halves = obs_op.shape[1] // LANES

    scal = jnp.stack([lax.axis_index("gx") % 2, lax.axis_index("gy") % 2]).astype(jnp.int32)
    own_share = jnp.where(lax.axis_index("comp") == 0, 1.0, 0.5)
    shares = jnp.stack([own_share * coupling, (1.5 - own_share) * coupling])
    scale = jnp.broadcast_to(background.reshape(width, 1), (width, LANES))

    smem = pl.BlockSpec(memory_space=pltpu.SMEM)
    vmem = pl.BlockSpec(memory_space=pltpu.VMEM)
    cells_shape = pltpu.VMEM((rows + 2, width, LANES), jnp.float32)
    packed_shape = f32(groups // PARTS * GROUP, LANES)
    sides_shape = pltpu.VMEM(packed_shape.shape, jnp.float32)
    strip_shapes = [f32(width, LANES), f32(width, LANES), packed_shape]
    field_shape = f32(rows, width, LANES)
    floor_shape = f32(fields * rows, LANES)

    def run(body, out_shape, scratch, *args, **kw):
        return call(functools.partial(body, rows, levels), out_shape, scratch, **kw, in_specs=[smem] + [vmem] * len(args))(
            scal, *args
        )

    def flat(field):
        return field.reshape(field.shape[0] * width, lanes)

    def swap_floor(floor):
        return lax.ppermute(floor, "comp", [(0, 1), (1, 0)])

    state_flat = state_incr.reshape(width * rows, lanes)
    s_even, s_odd, packed = run(edges_kernel, strip_shapes, [], state_flat)
    halos = exchange((s_even, s_odd), packed)

    send = call(functools.partial(route_kernel, tiles, cap), f32(tiles, halves * cap + GROUP, LANES))(
        obs_dest.reshape(1, count), obs_col.reshape(1, count), obs_prec.reshape(1, count), obs_op
    )
    send, halos[2] = lax.optimization_barrier((send, halos[2]))
    records = lax.all_to_all(send, ("gx", "gy"), split_axis=0, concat_axis=0, tiled=True)

    field, wind_rows = call(
        functools.partial(to_rows_kernel, rows), [field_shape, f32(rows + 2, width, LANES)], in_specs=[vmem, vmem]
    )(state_flat, winds.reshape(width * rows, lanes))
    state_rows = field

    for sweep in range(2):
        if sweep > 0:
            halos = exchange((s_even, s_odd), packed)
        floor = run(forward_floor_kernel, floor_shape, [], flat(field), flat(wind_rows), *halos)
        other = swap_floor(floor)
        args = (shares, other, field, wind_rows, *halos)
        scratch = [cells_shape, sides_shape]
        if sweep == 0:
            field, s_even, s_odd, packed = run(
                lambda r, v, *refs: forward_kernel(r, v, False, *refs), [field_shape] + strip_shapes, scratch, *args
            )
        else:
            cols = run(
                lambda r, v, *refs: forward_kernel(r, v, True, *refs),
                jax.ShapeDtypeStruct((2 * width, rows * LANES), jnp.bfloat16),
                scratch,
                *args,
            )

    slots = tiles * cap
    adjoint, floor = call(
        functools.partial(observe_kernel, rows, width, tiles, cap),
        [field_shape, floor_shape],
        [
            pltpu.VMEM((slots, rows * LANES), jnp.bfloat16),
            pltpu.VMEM((slots, LANES), jnp.float32),
            pltpu.VMEM((slots, 2 * width), jnp.float32),
            pltpu.VMEM((2 * width, slots), jnp.bfloat16),
        ],
        limit=OBSERVE_VMEM,
    )(records, cols)

    other = swap_floor(floor)
    bottom, s_even, s_odd, packed = run(
        adjoint_pack_kernel, [f32(rows, fields * GROUP, LANES)] + strip_shapes, [], shares, other, adjoint, wind_rows
    )
    halos = exchange((s_even, s_odd), packed)
    floor = run(adjoint_floor_kernel, floor_shape, [], shares, other, flat(adjoint), flat(wind_rows), *halos)
    other_next = swap_floor(floor)
    adjoint, s_even, s_odd, packed = run(
        adjoint_kernel,
        [field_shape] + strip_shapes,
        [cells_shape, sides_shape],
        shares, bottom, other_next, adjoint, wind_rows, *halos,
    )
    halos = exchange((s_even, s_odd), packed)
    result = run(
        final_kernel, f32(width * rows, LANES), [cells_shape, sides_shape], scale, adjoint, wind_rows, state_rows, *halos
    )
    return result.reshape(state_incr.shape)


def solution(mesh):
    placed = (
        P("comp", None, None, "gx", "gy"),
        P("comp", None, None, "gx", "gy"),
        P("gx", "gy"),
        P("comp", None, None),
        P(("comp", "gx", "gy"), None),
        P(("comp", "gx", "gy")),
        P(("comp", "gx", "gy"), None),
        P(("comp", "gx", "gy")),
    )
    return jax.shard_map(
        local,
        mesh=mesh,
        in_specs=placed,
        out_specs=P("comp", None, None, "gx", "gy"),
        check_vma=False,
    )
```

```python
import functools

import jax
import jax.numpy as jnp
from jax import lax
from jax.experimental import pallas as pl
from jax.experimental.pallas import tpu as pltpu
from jax.sharding import PartitionSpec as P

HORIZ_MIX = 0.1
VERT_MIX = 0.15
LANES = 128
GROUP = 8
MIB = 1024 * 1024
SWEEP_VMEM = 18 * MIB
OBSERVE_VMEM = 20 * MIB


def call(body, out_shape, scratch=(), limit=SWEEP_VMEM, **kw):
    return pl.pallas_call(
        body,
        out_shape=out_shape,
        scratch_shapes=list(scratch),
        compiler_params=pltpu.CompilerParams(vmem_limit_bytes=limit),
        **kw,
    )


def f32(*shape):
    return jax.ShapeDtypeStruct(shape, jnp.float32)


def lane_iota(rows=GROUP):
    return lax.broadcasted_iota(jnp.int32, (rows, LANES), 1)


def sub_iota(rows=GROUP):
    return lax.broadcasted_iota(jnp.int32, (rows, LANES), 0)


def pair_swap(block, axis, start):
    count = lax.axis_size(axis)
    route = []
    for low in range(start, count - 1, 2):
        route += [(low, low + 1), (low + 1, low)]
    return lax.ppermute(block, axis, route)


def exchange(strips, packed):
    y_even = pair_swap(packed, "gy", 0)
    y_odd = pair_swap(packed, "gy", 1)
    halos = [pair_swap(strips[0], "gx", 0), y_even, y_odd]
    if lax.axis_size("gx") > 2:
        halos.append(pair_swap(strips[1], "gx", 1))
    return halos


def is_odd(axis):
    return lax.rem(lax.axis_index(axis), 2) == 1


def read_sides(refs):
    even = refs[0]
    odd = refs[3] if len(refs) > 3 else None
    at_odd = is_odd("gx")

    def side(at, turned):
        other = jnp.zeros_like(even[at]) if odd is None else odd[at]
        return jnp.where(turned, other, even[at])

    return lambda at: side(at, jnp.logical_not(at_odd)), lambda at: side(at, at_odd)


PARTS = 4


def merged(y_even, y_odd, at):
    a, b = y_even[at, :], y_odd[at, :]
    lane = lax.broadcasted_iota(jnp.int32, a.shape, 1)
    return jnp.where((lane % 2 == 1) == jnp.logical_not(is_odd("gy")), a, b)


def merge_columns(y_even, y_odd, sides):
    sides[...] = merged(y_even, y_odd, slice(None))


def slot_of(i, part, rows):
    return PARTS * (rows - 1 - i) + part


def side_columns(sides, i, group):
    m, part = group // PARTS, group % PARTS
    rows = LANES // (2 * PARTS)
    return pltpu.roll(sides[m * GROUP : (m + 1) * GROUP, :], LANES - 1 - 2 * slot_of(i, part, rows), 1)


def pack_into(total, value, slot):
    return jnp.where(lane_iota() // 2 == slot, pltpu.roll(value, 2 * slot + 1, 1), total)


def pack_block(packed, values, i, m):
    at = pl.ds(m * GROUP, GROUP)
    total = packed[at, :]
    for part, value in enumerate(values):
        total = pack_into(total, value, slot_of(i, part, LANES // (2 * PARTS)))
    packed[at, :] = total


CENTRE = 1.0 - 4.0 * HORIZ_MIX - 2.0 * VERT_MIX


def levels_around(cells, i, base, group, groups):
    here = cells[i + 1, pl.ds(base + group * GROUP, GROUP), :]
    if group == groups - 1:
        upper = jnp.where(sub_iota() == GROUP - 1, here, pltpu.roll(here, GROUP - 1, 0))
    else:
        upper = cells[i + 1, pl.ds(base + group * GROUP + 1, GROUP), :]
    if group == 0:
        lower = jnp.where(sub_iota() == 0, here, pltpu.roll(here, 1, 0))
    else:
        lower = cells[i + 1, pl.ds(base + group * GROUP - 1, GROUP), :]
    return here, upper, lower


def shifted(first, last, edge, rows=GROUP):
    lane = lane_iota(rows)
    right = pltpu.roll(jnp.where(lane == 0, edge, first), LANES - 1, 1)
    left = pltpu.roll(jnp.where(lane == LANES - 1, edge, last), 1, 1)
    return right, left


def forward_sum(here, vertical, after, before, right, left, u, w):
    return (
        CENTRE * here
        + VERT_MIX * vertical
        + HORIZ_MIX * ((after + before) + (right + left))
        - 0.5 * (u * (after - before) + w * (right - left))
    )


def forward_point(cells, winds, sides, i, f, group, levels):
    groups = levels // GROUP
    here, upper, lower = levels_around(cells, i, f * levels, group, groups)
    at = pl.ds(f * levels + group * GROUP, GROUP)
    right, left = shifted(here, here, side_columns(sides, i, f * groups + group))
    u = winds[i, pl.ds(group * GROUP, GROUP), :]
    w = winds[i, pl.ds(levels + group * GROUP, GROUP), :]
    return forward_sum(here, upper + lower, cells[i + 2, at, :], cells[i, at, :], right, left, u, w)


def products(x, wind):
    slope = 0.5 * (wind * x)
    return HORIZ_MIX * x - slope, HORIZ_MIX * x + slope


def adjoint_point(cells, winds, sides, i, f, group, levels):
    groups = levels // GROUP
    here, upper, lower = levels_around(cells, i, f * levels, group, groups)
    at = pl.ds(f * levels + group * GROUP, GROUP)
    wind_at = pl.ds(group * GROUP, GROUP)
    after, before = cells[i + 2, at, :], cells[i, at, :]
    u_after, u_before = winds[i + 2, wind_at, :], winds[i, wind_at, :]
    w = winds[i + 1, pl.ds(levels + group * GROUP, GROUP), :]
    down, up = products(here, w)
    right, left = shifted(up, down, side_columns(sides, i, f * groups + group))
    return (
        CENTRE * here
        + VERT_MIX * (upper + lower)
        + HORIZ_MIX * (after + before)
        + 0.5 * (u_after * after - u_before * before)
        + (right + left)
    )


def shares_of(coupling):
    own = jnp.where(lax.axis_index("comp") == 0, 1.0, 0.5)
    return own * coupling, (1.5 - own) * coupling


def couple_forward(value, other, coupling):
    own, _ = shares_of(coupling)
    return value - own * (value - other)


def couple_adjoint(value, other, coupling):
    own, peer = shares_of(coupling)
    return value - own * value + peer * other


def coupled(rule, value, other, coupling, i, f, rows):
    mixed = rule(value, other[pl.ds(f * rows + i, 1), :], coupling[pl.ds(i, 1), :])
    return jnp.where(sub_iota() == 0, mixed, value)


def put_strip(strip_even, strip_odd, at, first, last):
    at_odd = is_odd("gx")
    strip_even[at, :] = jnp.where(at_odd, first, last)
    strip_odd[at, :] = jnp.where(at_odd, last, first)


def put_low(low, value, i, f, rows):
    for level in range(2):
        low[level][pl.ds(f * rows + i, 1), :] = value[level : level + 1]


class Rows:
    def __init__(self, source, target, sems, rows, as_it_comes, offset):
        self.source, self.target, self.sems = source, target, sems
        self.rows, self.as_it_comes, self.offset = rows, as_it_comes, offset

    def copy(self, i):
        row = self.source.at[:, i] if self.as_it_comes else self.source.at[i]
        return pltpu.make_async_copy(row, self.target.at[i + self.offset], self.sems.at[i])

    def wait(self, i):
        self.copy(i).wait()


def start_rows(rows, *groups):
    for i in range(rows):
        for group in groups:
            group.copy(i).start()


def edges_kernel(rows, levels, state, s_even, s_odd, packed, low0, low1, cells, sems):
    incoming = Rows(state, cells, sems, rows, True, 0)
    start_rows(rows, incoming)
    packed[...] = jnp.zeros_like(packed)
    groups = levels // GROUP

    def row(i, _):
        incoming.wait(i)
        for m in range(2 * groups // PARTS):
            values = [cells[i, pl.ds((m * PARTS + part) * GROUP, GROUP), :] for part in range(PARTS)]
            if m * PARTS % groups == 0:
                put_low((low0, low1), values[0], i, m * PARTS // groups, rows)
            pack_block(packed, values, i, m)
        return 0

    lax.fori_loop(0, rows, row, 0)
    put_strip(s_even, s_odd, slice(None), cells[0], cells[rows - 1])


def floor_edge(halos, f, rows, levels):
    m = f * (levels // GROUP) // PARTS
    sides = jnp.broadcast_to(merged(halos[1], halos[2], pl.ds(m * GROUP, 1)), (rows, LANES))
    return pltpu.roll(sides, 2 * PARTS - 1, 1, stride=2 * PARTS, stride_axis=0)


def row_after(value, last, rows):
    return jnp.where(sub_iota(rows) == rows - 1, last, pltpu.roll(value, rows - 1, 0))


def row_before(value, first, rows):
    return jnp.where(sub_iota(rows) == 0, first, pltpu.roll(value, 1, 0))


def forward_floor_kernel(rows, levels, low0, low1, winds, *rest):
    *halos, floor = rest
    side_before, side_after = read_sides(halos)
    for f in range(2):
        here = pl.ds(f * rows, rows)
        at = pl.ds(f * levels, 1)
        low, up = low0[here, :], low1[here, :]
        after, before = row_after(low, side_after(at), rows), row_before(low, side_before(at), rows)
        right, left = shifted(low, low, floor_edge(halos, f, rows, levels), rows)
        floor[here, :] = forward_sum(low, up + low, after, before, right, left, winds[0], winds[1])


def adjoint_floor_kernel(rows, levels, coupling, other, low0, low1, winds, *rest):
    *halos, floor = rest
    side_before, side_after = read_sides(halos)
    for f in range(2):
        here = pl.ds(f * rows, rows)
        at = pl.ds(f * levels, 1)
        low, up = couple_adjoint(low0[here, :], other[here, :], coupling[...]), low1[here, :]
        x_down, x_up = products(low, winds[0])
        after, before = row_after(x_up, side_after(at), rows), row_before(x_down, side_before(at), rows)
        y_down, y_up = products(low, winds[1])
        right, left = shifted(y_up, y_down, floor_edge(halos, f, rows, levels), rows)
        floor[here, :] = CENTRE * low + VERT_MIX * (up + low) + (after + before) + (right + left)


def forward_kernel(first, last, rows, levels, coupling, other, field, winds, *rest):
    if last:
        *halos, cols, cells, wind_cells, sides, sems, col_cells, col_sems = rest
    else:
        *halos, out, s_even, s_odd, packed, low0, low1, cells, wind_cells, sides, sems = rest
    incoming = Rows(field, cells, sems.at[0], rows, first, 1)
    wind_in = Rows(winds, wind_cells, sems.at[1], rows, True, 0)
    start_rows(rows, incoming, wind_in)
    if not last:
        packed[...] = jnp.zeros_like(packed)
    merge_columns(halos[1], halos[2], sides)
    before, after = read_sides(halos)
    cells[0] = before(slice(None))
    cells[rows + 1] = after(slice(None))
    groups = levels // GROUP
    width = 2 * levels
    incoming.wait(0)

    def col_copy(i):
        lanes = pl.ds(pl.multiple_of(i * LANES, LANES), LANES)
        return pltpu.make_async_copy(col_cells.at[:, lanes], cols.at[:, lanes], col_sems.at[i])

    def row(i, _):
        @pl.when(i < rows - 1)
        def _():
            incoming.wait(i + 1)

        wind_in.wait(i)
        for m in range(2 * groups // PARTS):
            f, start = m * PARTS // groups, m * PARTS % groups
            values = []
            for group in range(start, start + PARTS):
                value = forward_point(cells, wind_cells, sides, i, f, group, levels)
                if group == 0:
                    value = coupled(couple_forward, value, other, coupling, i, f, rows)
                    if not last:
                        put_low((low0, low1), value, i, f, rows)
                values.append(value)
            base = m * PARTS * GROUP
            if last:
                lanes = pl.ds(pl.multiple_of(i * LANES, LANES), LANES)
                high, low = split(jnp.concatenate(values, axis=0), 2)
                col_cells[pl.ds(base, PARTS * GROUP), lanes] = high
                col_cells[pl.ds(width + base, PARTS * GROUP), lanes] = low
            else:
                for part, value in enumerate(values):
                    out[i, pl.ds(base + part * GROUP, GROUP), :] = value
                pack_block(packed, values, i, m)
        if last:
            col_copy(i).start()
        return 0

    lax.fori_loop(0, rows, row, 0)
    if last:
        for i in range(rows):
            col_copy(i).wait()
    else:
        put_strip(s_even, s_odd, slice(None), out[0], out[rows - 1])


def with_products(value, w):
    down, up = products(value, w)
    return jnp.where(lane_iota() == 0, up, down)


def adjoint_pack_kernel(rows, levels, coupling, other, field, winds, bottom, s_even, s_odd, packed, w_cells, u_cells, sems):
    def w_copy(i):
        return pltpu.make_async_copy(winds.at[pl.ds(levels, levels), i], w_cells.at[i], sems.at[i])

    u_copies = [
        pltpu.make_async_copy(winds.at[pl.ds(0, levels), i], u_cells.at[k], sems.at[rows + k])
        for k, i in enumerate((0, rows - 1))
    ]
    for i in range(rows):
        w_copy(i).start()
    for copy in u_copies:
        copy.start()
    packed[...] = jnp.zeros_like(packed)
    groups = levels // GROUP

    def row(i, _):
        w_copy(i).wait()
        for m in range(2 * groups // PARTS):
            f, start = m * PARTS // groups, m * PARTS % groups
            values = []
            for group in range(start, start + PARTS):
                value = field[i, pl.ds(f * levels + group * GROUP, GROUP), :]
                if group == 0:
                    value = coupled(couple_adjoint, value, other, coupling, i, f, rows)
                    bottom[i, pl.ds(f * GROUP, GROUP), :] = value
                values.append(with_products(value, w_cells[i, pl.ds(group * GROUP, GROUP), :]))
            pack_block(packed, values, i, m)
        return 0

    lax.fori_loop(0, rows, row, 0)
    for copy in u_copies:
        copy.wait()
    for f in range(2):
        ends = []
        for i in (0, rows - 1):
            low = bottom[i, pl.ds(f * GROUP, GROUP), :]
            ends.append(jnp.concatenate([low, field[i, pl.ds(f * levels + GROUP, levels - GROUP), :]], axis=0))
        put_strip(
            s_even, s_odd, pl.ds(f * levels, levels), products(ends[0], u_cells[0])[1], products(ends[1], u_cells[1])[0]
        )


def adjoint_kernel(rows, levels, coupling, bottom, other_next, field, winds, *rest):
    *halos, out, s_even, s_odd, packed, cells, wind_cells, sides, sems = rest
    incoming = Rows(field, cells, sems.at[0], rows, False, 1)
    wind_in = Rows(winds, wind_cells, sems.at[1], rows, True, 1)
    start_rows(rows, incoming, wind_in)
    packed[...] = jnp.zeros_like(packed)
    groups = levels // GROUP
    adjoint_outside(halos, cells, wind_cells, sides, rows)

    def take(i):
        incoming.wait(i)
        wind_in.wait(i)
        for f in range(2):
            cells[i + 1, pl.ds(f * levels, GROUP), :] = bottom[i, pl.ds(f * GROUP, GROUP), :]

    take(0)

    def row(i, _):
        @pl.when(i < rows - 1)
        def _():
            take(i + 1)

        for m in range(2 * groups // PARTS):
            f, start = m * PARTS // groups, m * PARTS % groups
            values = []
            for group in range(start, start + PARTS):
                value = adjoint_point(cells, wind_cells, sides, i, f, group, levels)
                if group == 0:
                    value = coupled(couple_adjoint, value, other_next, coupling, i, f, rows)
                out[i, pl.ds(f * levels + group * GROUP, GROUP), :] = value
                values.append(with_products(value, wind_cells[i + 1, pl.ds(levels + group * GROUP, GROUP), :]))
            pack_block(packed, values, i, m)
        return 0

    lax.fori_loop(0, rows, row, 0)
    for f in range(2):
        at = pl.ds(f * levels, levels)
        first = products(out[0, at, :], wind_cells[1, pl.ds(0, levels), :])[1]
        last = products(out[rows - 1, at, :], wind_cells[rows, pl.ds(0, levels), :])[0]
        put_strip(s_even, s_odd, at, first, last)


def adjoint_outside(halos, cells, wind_cells, sides, rows):
    merge_columns(halos[1], halos[2], sides)
    before, after = read_sides(halos)
    cells[0] = before(slice(None)) / HORIZ_MIX
    cells[rows + 1] = after(slice(None)) / HORIZ_MIX
    wind_cells[0] = jnp.zeros_like(wind_cells[0])
    wind_cells[rows + 1] = jnp.zeros_like(wind_cells[0])


def final_kernel(rows, levels, scale, field, winds, state, *rest):
    *halos, out, cells, wind_cells, state_cells, out_cells, sides, sems = rest
    incoming = Rows(field, cells, sems.at[0], rows, False, 1)
    wind_in = Rows(winds, wind_cells, sems.at[1], rows, True, 1)
    state_in = Rows(state, state_cells, sems.at[2], rows, True, 0)
    start_rows(rows, incoming, wind_in, state_in)
    groups = levels // GROUP
    adjoint_outside(halos, cells, wind_cells, sides, rows)
    incoming.wait(0)
    wind_in.wait(0)

    def out_copy(i):
        return pltpu.make_async_copy(out_cells.at[i], out.at[:, i], sems.at[3, i])

    def row(i, _):
        @pl.when(i < rows - 1)
        def _():
            incoming.wait(i + 1)
            wind_in.wait(i + 1)

        state_in.wait(i)
        for group in range(groups):
            for f in range(2):
                at = pl.ds(f * levels + group * GROUP, GROUP)
                value = adjoint_point(cells, wind_cells, sides, i, f, group, levels)
                out_cells[i, at, :] = value + scale[at, :] * state_cells[i, at, :]
        out_copy(i).start()
        return 0

    lax.fori_loop(0, rows, row, 0)
    for i in range(rows):
        out_copy(i).wait()


def split(value, terms):
    parts = []
    for _ in range(terms):
        part = value.astype(jnp.bfloat16)
        parts.append(part)
        value = value - part.astype(jnp.float32)
    return parts


def dot(a, b, contract):
    return lax.dot_general(a, b, ((contract[:1], contract[1:]), ((), ())), preferred_element_type=jnp.float32)


def route_kernel(tiles, cap, dest, col, prec, op, out):
    count = op.shape[0]
    width = op.shape[1]
    halves = width // LANES
    owner = lax.broadcasted_iota(jnp.int32, (tiles, count), 0)
    hits = owner == dest[...]
    ones = jnp.where(hits, 1.0, 0.0)
    earlier = lax.broadcasted_iota(jnp.int32, (count, count), 0) <= lax.broadcasted_iota(jnp.int32, (count, count), 1)
    running = dot(ones.astype(jnp.bfloat16), jnp.where(earlier, 1.0, 0.0).astype(jnp.bfloat16), (1, 0))
    slot = jnp.sum(running * ones, axis=0, keepdims=True) - 1.0
    slot = slot.astype(jnp.int32)
    place = dest[...] * cap + slot
    at_slot = lax.broadcasted_iota(jnp.int32, (LANES, count), 0) == slot
    at_slot = jnp.where(at_slot, 1.0, 0.0).astype(jnp.bfloat16)
    column = col[...].astype(jnp.float32)
    pieces = [ones * part.astype(jnp.float32) for part in split(column, 2) + split(prec[...], 3)]
    aux = dot(jnp.concatenate(pieces, axis=0).astype(jnp.bfloat16), at_slot, (1, 1))
    columns = aux[0:tiles] + aux[tiles : 2 * tiles]
    precs = (aux[2 * tiles : 3 * tiles] + aux[3 * tiles : 4 * tiles]) + aux[4 * tiles : 5 * tiles]
    sub = sub_iota()
    for owner_at in range(tiles):
        block = jnp.where(sub == 0, columns[owner_at : owner_at + 1], 0.0)
        block = jnp.where(sub == 1, precs[owner_at : owner_at + 1], block)
        out[owner_at, pl.ds(halves * cap, GROUP), :] = block
    rows_high, rows_low = split(op[...], 2)
    chunk = 256
    for first in range(0, tiles * cap, chunk):
        picks = lax.broadcasted_iota(jnp.int32, (chunk, count), 0) + first == place
        picks = jnp.where(picks, 1.0, 0.0).astype(jnp.bfloat16)
        moved = dot(picks, rows_high, (1, 0)) + dot(picks, rows_low, (1, 0))
        for part in range(chunk // cap):
            for half in range(halves):
                out[first // cap + part, pl.ds(half * cap, cap), :] = moved[
                    part * cap : (part + 1) * cap, half * LANES : (half + 1) * LANES
                ]


def observe_kernel(rows, width, tiles, cap, records, cols, adjoint, low0, low1, col_cells, sel, precs, both, spread, sems):
    part_rows = 2 * width // sems.shape[0]
    copies = []
    for part in range(sems.shape[0]):
        at = pl.ds(part * part_rows, part_rows)
        copies.append(pltpu.make_async_copy(cols.at[at], col_cells.at[at], sems.at[part]))
        copies[-1].start()
    halves = width // LANES
    count = tiles * cap
    aux = halves * cap
    own = lax.broadcasted_iota(jnp.int32, (cap, LANES), 1) == lax.broadcasted_iota(jnp.int32, (cap, LANES), 0)
    ones = jnp.ones((LANES, LANES), jnp.bfloat16)
    step = 256
    lane = lax.broadcasted_iota(jnp.int32, (step, LANES), 1).astype(jnp.float32)

    def select(block, _):
        sources = step // cap

        def spread_out(part):
            rows_of = [
                jnp.where(own, records[block * sources + s, pl.ds(aux + part, 1), :], 0.0) for s in range(sources)
            ]
            terms = split(jnp.concatenate(rows_of, axis=0), 2 + part)
            return sum(dot(term, ones, (1, 0)) for term in terms)

        at = pl.ds(pl.multiple_of(block * step, step), step)
        column = spread_out(0) - lane
        precs[at, :] = spread_out(1)
        for i in range(rows):
            sel[at, i * LANES : (i + 1) * LANES] = jnp.where(column == float(i * LANES), 1.0, 0.0).astype(jnp.bfloat16)
        return 0

    lax.fori_loop(0, count // step, select, 0)
    for copy in copies:
        copy.wait()
    both[...] = dot(sel[...], col_cells[...], (1, 1))

    def weigh(block, _):
        at = pl.ds(pl.multiple_of(block * LANES, LANES), LANES)
        sources = LANES // cap
        ops = [
            jnp.concatenate(
                [records[block * sources + s, half * cap : (half + 1) * cap, :] for s in range(sources)], axis=0
            )
            for half in range(halves)
        ]
        total = sum(
            (both[at, half * LANES : (half + 1) * LANES] + both[at, width + half * LANES : width + (half + 1) * LANES])
            * ops[half]
            for half in range(halves)
        )
        innovation = jnp.sum(total, axis=1, keepdims=True) * precs[at, :]
        for half in range(halves):
            high, low = split((ops[half] * innovation).T, 2)
            spread[half * LANES : (half + 1) * LANES, at] = high
            spread[width + half * LANES : width + (half + 1) * LANES, at] = low
        return 0

    lax.fori_loop(0, count // LANES, weigh, 0)
    sums = dot(spread[...], sel[...], (1, 0))
    for i in range(rows):
        lanes = slice(i * LANES, (i + 1) * LANES)
        adjoint[i] = sums[:width, lanes] + sums[width:, lanes]
        for f in range(2):
            put_low((low0, low1), adjoint[i, f * (width // 2) : f * (width // 2) + GROUP, :], i, f, rows)


def local(state_incr, winds, coupling, background, obs_dest, obs_col, obs_op, obs_prec):
    _, fields, levels, rows, lanes = state_incr.shape
    width = fields * levels
    groups = width // GROUP
    tiles = lax.axis_size("gx") * lax.axis_size("gy")
    count = obs_col.shape[0]
    cap = 2 * count // tiles
    halves = obs_op.shape[1] // LANES

    scale = jnp.broadcast_to(background.reshape(width, 1), (width, LANES))

    vmem = pl.BlockSpec(memory_space=pltpu.VMEM)
    anywhere = pl.BlockSpec(memory_space=pl.ANY)
    hbm = pl.BlockSpec(memory_space=pltpu.HBM)
    own = pltpu.VMEM((rows, width, LANES), jnp.float32)
    framed = pltpu.VMEM((rows + 2, width, LANES), jnp.float32)
    packed_shape = f32(groups // PARTS * GROUP, LANES)
    sides = pltpu.VMEM(packed_shape.shape, jnp.float32)
    strip_shapes = [f32(width, LANES), f32(width, LANES), packed_shape]
    field_shape = f32(rows, width, LANES)
    low_shape = f32(fields * rows, LANES)
    cols_shape = ((2 * width, rows * LANES), jnp.bfloat16)

    def sems(*shape):
        return pltpu.SemaphoreType.DMA(shape)

    def run(body, out_shape, scratch, args, far=(), **kw):
        specs = [anywhere if k in far else vmem for k in range(len(args))]
        return call(functools.partial(body, rows, levels), out_shape, scratch, in_specs=specs, **kw)(*args)

    def swap_floor(floor):
        return lax.ppermute(floor, "comp", [(0, 1), (1, 0)])

    state = state_incr.reshape(width, rows, lanes)
    wind = winds.reshape(width, rows, lanes)
    floor_winds = winds[0, :, 0]

    s_even, s_odd, packed, low0, low1 = run(
        edges_kernel, strip_shapes + [low_shape] * 2, [own, sems(rows)], (state,), far=(0,)
    )
    halos = exchange((s_even, s_odd), packed)

    send = call(functools.partial(route_kernel, tiles, cap), f32(tiles, halves * cap + GROUP, LANES))(
        obs_dest.reshape(1, count), obs_col.reshape(1, count), obs_prec.reshape(1, count), obs_op
    )
    send, halos = lax.optimization_barrier((send, halos))
    records = lax.all_to_all(send, ("gx", "gy"), split_axis=0, concat_axis=0, tiled=True)

    floor = run(forward_floor_kernel, low_shape, [], (low0, low1, floor_winds, *halos))
    field, s_even, s_odd, packed, low0, low1 = run(
        functools.partial(forward_kernel, True, False),
        [field_shape] + strip_shapes + [low_shape] * 2,
        [framed, own, sides, sems(2, rows)],
        (coupling, swap_floor(floor), state, wind, *halos),
        far=(2, 3),
    )
    halos = exchange((s_even, s_odd), packed)
    floor = run(forward_floor_kernel, low_shape, [], (low0, low1, floor_winds, *halos))
    cols = run(
        functools.partial(forward_kernel, False, True),
        jax.ShapeDtypeStruct(*cols_shape),
        [framed, own, sides, sems(2, rows), pltpu.VMEM(*cols_shape), sems(rows)],
        (coupling, swap_floor(floor), field, wind, *halos),
        far=(2, 3),
        out_specs=hbm,
    )

    slots = tiles * cap
    adjoint, low0, low1 = call(
        functools.partial(observe_kernel, rows, width, tiles, cap),
        [field_shape, low_shape, low_shape],
        [
            pltpu.VMEM(*cols_shape),
            pltpu.VMEM((slots, rows * LANES), jnp.bfloat16),
            pltpu.VMEM((slots, LANES), jnp.float32),
            pltpu.VMEM((slots, 2 * width), jnp.float32),
            pltpu.VMEM((2 * width, slots), jnp.bfloat16),
            sems(8),
        ],
        limit=OBSERVE_VMEM,
        in_specs=[vmem, hbm],
    )(records, cols)

    other = swap_floor(low0)
    bottom, s_even, s_odd, packed = run(
        adjoint_pack_kernel,
        [f32(rows, fields * GROUP, LANES)] + strip_shapes,
        [pltpu.VMEM((rows, levels, LANES), jnp.float32), pltpu.VMEM((2, levels, LANES), jnp.float32), sems(rows + 2)],
        (coupling, other, adjoint, wind),
        far=(3,),
    )
    halos = exchange((s_even, s_odd), packed)
    floor = run(adjoint_floor_kernel, low_shape, [], (coupling, other, low0, low1, floor_winds, *halos))
    adjoint, s_even, s_odd, packed = run(
        adjoint_kernel,
        [field_shape] + strip_shapes,
        [framed, framed, sides, sems(2, rows)],
        (coupling, bottom, swap_floor(floor), adjoint, wind, *halos),
        far=(3, 4),
    )
    halos = exchange((s_even, s_odd), packed)
    result = run(
        final_kernel,
        f32(width, rows, LANES),
        [framed, framed, own, own, sides, sems(4, rows)],
        (scale, adjoint, wind, state, *halos),
        far=(1, 2, 3),
        out_specs=hbm,
    )
    return result.reshape(state_incr.shape)


def solution(mesh):
    placed = (
        P("comp", None, None, "gx", "gy"),
        P("comp", None, None, "gx", "gy"),
        P("gx", "gy"),
        P("comp", None, None),
        P(("comp", "gx", "gy"), None),
        P(("comp", "gx", "gy")),
        P(("comp", "gx", "gy"), None),
        P(("comp", "gx", "gy")),
    )
    return jax.shard_map(
        local,
        mesh=mesh,
        in_specs=placed,
        out_specs=P("comp", None, None, "gx", "gy"),
        check_vma=False,
    )
```

```python
import functools

import jax
import jax.numpy as jnp
from jax import lax
from jax.experimental import pallas as pl
from jax.experimental.pallas import tpu as pltpu
from jax.sharding import PartitionSpec as P

HORIZ_MIX = 0.1
VERT_MIX = 0.15
LANES = 128
GROUP = 8
MIB = 1024 * 1024
VMEM_GRANT = 59 * MIB


def call(body, out_shape, scratch=(), limit=VMEM_GRANT, **kw):
    return pl.pallas_call(
        body,
        out_shape=out_shape,
        scratch_shapes=list(scratch),
        compiler_params=pltpu.CompilerParams(vmem_limit_bytes=limit),
        **kw,
    )


def f32(*shape):
    return jax.ShapeDtypeStruct(shape, jnp.float32)


def lane_iota(rows=GROUP):
    return lax.broadcasted_iota(jnp.int32, (rows, LANES), 1)


def sub_iota(rows=GROUP):
    return lax.broadcasted_iota(jnp.int32, (rows, LANES), 0)


def pair_swap(block, axis, start):
    count = lax.axis_size(axis)
    route = []
    for low in range(start, count - 1, 2):
        route += [(low, low + 1), (low + 1, low)]
    return lax.ppermute(block, axis, route)


def exchange(strips, packed):
    y_even = pair_swap(packed, "gy", 0)
    y_odd = pair_swap(packed, "gy", 1)
    halos = [pair_swap(strips[0], "gx", 0), y_even, y_odd]
    if lax.axis_size("gx") > 2:
        halos.append(pair_swap(strips[1], "gx", 1))
    return halos


def is_odd(axis):
    return lax.rem(lax.axis_index(axis), 2) == 1


def read_sides(refs):
    even = refs[0]
    odd = refs[3] if len(refs) > 3 else None
    at_odd = is_odd("gx")

    def side(at, turned):
        other = jnp.zeros_like(even[at]) if odd is None else odd[at]
        return jnp.where(turned, other, even[at])

    return lambda at: side(at, jnp.logical_not(at_odd)), lambda at: side(at, at_odd)


PARTS = 4


def merged(y_even, y_odd, at):
    a, b = y_even[at, :], y_odd[at, :]
    lane = lax.broadcasted_iota(jnp.int32, a.shape, 1)
    return jnp.where((lane % 2 == 1) == jnp.logical_not(is_odd("gy")), a, b)


def merge_columns(y_even, y_odd, sides):
    sides[...] = merged(y_even, y_odd, slice(None))


def slot_of(i, part, rows):
    return PARTS * (rows - 1 - i) + part


def side_columns(sides, i, group):
    m, part = group // PARTS, group % PARTS
    rows = LANES // (2 * PARTS)
    return pltpu.roll(sides[m * GROUP : (m + 1) * GROUP, :], LANES - 1 - 2 * slot_of(i, part, rows), 1)


def pack_into(total, value, slot):
    return jnp.where(lane_iota() // 2 == slot, pltpu.roll(value, 2 * slot + 1, 1), total)


def pack_block(packed, values, i, m):
    at = pl.ds(m * GROUP, GROUP)
    total = packed[at, :]
    for part, value in enumerate(values):
        total = pack_into(total, value, slot_of(i, part, LANES // (2 * PARTS)))
    packed[at, :] = total


CENTRE = 1.0 - 4.0 * HORIZ_MIX - 2.0 * VERT_MIX


def levels_around(cells, i, base, group, groups):
    here = cells[i + 1, pl.ds(base + group * GROUP, GROUP), :]
    if group == groups - 1:
        upper = jnp.where(sub_iota() == GROUP - 1, here, pltpu.roll(here, GROUP - 1, 0))
    else:
        upper = cells[i + 1, pl.ds(base + group * GROUP + 1, GROUP), :]
    if group == 0:
        lower = jnp.where(sub_iota() == 0, here, pltpu.roll(here, 1, 0))
    else:
        lower = cells[i + 1, pl.ds(base + group * GROUP - 1, GROUP), :]
    return here, upper, lower


def shifted(first, last, edge, rows=GROUP):
    lane = lane_iota(rows)
    right = pltpu.roll(jnp.where(lane == 0, edge, first), LANES - 1, 1)
    left = pltpu.roll(jnp.where(lane == LANES - 1, edge, last), 1, 1)
    return right, left


def forward_sum(here, vertical, after, before, right, left, u, w):
    return (
        CENTRE * here
        + VERT_MIX * vertical
        + HORIZ_MIX * ((after + before) + (right + left))
        - 0.5 * (u * (after - before) + w * (right - left))
    )


def forward_point(cells, winds, sides, i, f, group, levels):
    groups = levels // GROUP
    here, upper, lower = levels_around(cells, i, f * levels, group, groups)
    at = pl.ds(f * levels + group * GROUP, GROUP)
    right, left = shifted(here, here, side_columns(sides, i, f * groups + group))
    u = winds[i, pl.ds(group * GROUP, GROUP), :]
    w = winds[i, pl.ds(levels + group * GROUP, GROUP), :]
    return forward_sum(here, upper + lower, cells[i + 2, at, :], cells[i, at, :], right, left, u, w)


def products(x, wind):
    slope = 0.5 * (wind * x)
    return HORIZ_MIX * x - slope, HORIZ_MIX * x + slope


def adjoint_point(cells, winds, i, f, group, levels):
    here, upper, lower = levels_around(cells, i, f * levels, group, levels // GROUP)
    at = pl.ds(f * levels + group * GROUP, GROUP)
    wind_at = pl.ds(group * GROUP, GROUP)
    after, before = cells[i + 2, at, :], cells[i, at, :]
    u_after, u_before = winds[i + 2, wind_at, :], winds[i, wind_at, :]
    down, up = products(here, winds[i + 1, pl.ds(levels + group * GROUP, GROUP), :])
    right, left = shifted(up, down, 0.0)
    return (
        CENTRE * here
        + VERT_MIX * (upper + lower)
        + HORIZ_MIX * (after + before)
        + 0.5 * (u_after * after - u_before * before)
        + (right + left)
    )


def shares_of(coupling):
    own = jnp.where(lax.axis_index("comp") == 0, 1.0, 0.5)
    return own * coupling, (1.5 - own) * coupling


def couple_forward(value, other, coupling):
    own, _ = shares_of(coupling)
    return value - own * (value - other)


def couple_adjoint(value, other, coupling):
    own, peer = shares_of(coupling)
    return value - own * value + peer * other


def coupled(rule, value, other, coupling, i, f, rows):
    mixed = rule(value, other[pl.ds(f * rows + i, 1), :], coupling[pl.ds(i, 1), :])
    return jnp.where(sub_iota() == 0, mixed, value)


def put_strip(strip_even, strip_odd, at, first, last):
    at_odd = is_odd("gx")
    strip_even[at, :] = jnp.where(at_odd, first, last)
    strip_odd[at, :] = jnp.where(at_odd, last, first)


def put_low(low, value, i, f, rows):
    for level in range(2):
        low[level][pl.ds(f * rows + i, 1), :] = value[level : level + 1]


class Rows:
    def __init__(self, source, target, sems, rows, as_it_comes, offset):
        self.source, self.target, self.sems = source, target, sems
        self.rows, self.as_it_comes, self.offset = rows, as_it_comes, offset

    def copy(self, i):
        row = self.source.at[:, i] if self.as_it_comes else self.source.at[i]
        return pltpu.make_async_copy(row, self.target.at[i + self.offset], self.sems.at[i])

    def wait(self, i):
        self.copy(i).wait()


def start_rows(rows, *groups):
    for i in range(rows):
        for group in groups:
            group.copy(i).start()


def edges_kernel(rows, levels, state, s_even, s_odd, packed, low0, low1, cells, sems):
    incoming = Rows(state, cells, sems, rows, True, 0)
    start_rows(rows, incoming)
    packed[...] = jnp.zeros_like(packed)
    groups = levels // GROUP

    def row(i, _):
        incoming.wait(i)
        for m in range(2 * groups // PARTS):
            values = [cells[i, pl.ds((m * PARTS + part) * GROUP, GROUP), :] for part in range(PARTS)]
            if m * PARTS % groups == 0:
                put_low((low0, low1), values[0], i, m * PARTS // groups, rows)
            pack_block(packed, values, i, m)
        return 0

    lax.fori_loop(0, rows, row, 0)
    put_strip(s_even, s_odd, slice(None), cells[0], cells[rows - 1])


def floor_edge(halos, f, rows, levels):
    m = f * (levels // GROUP) // PARTS
    sides = jnp.broadcast_to(merged(halos[1], halos[2], pl.ds(m * GROUP, 1)), (rows, LANES))
    return pltpu.roll(sides, 2 * PARTS - 1, 1, stride=2 * PARTS, stride_axis=0)


def row_after(value, last, rows):
    return jnp.where(sub_iota(rows) == rows - 1, last, pltpu.roll(value, rows - 1, 0))


def row_before(value, first, rows):
    return jnp.where(sub_iota(rows) == 0, first, pltpu.roll(value, 1, 0))


def forward_floor_kernel(rows, levels, low0, low1, winds, *rest):
    *halos, floor = rest
    side_before, side_after = read_sides(halos)
    for f in range(2):
        here = pl.ds(f * rows, rows)
        at = pl.ds(f * levels, 1)
        low, up = low0[here, :], low1[here, :]
        after, before = row_after(low, side_after(at), rows), row_before(low, side_before(at), rows)
        right, left = shifted(low, low, floor_edge(halos, f, rows, levels), rows)
        floor[here, :] = forward_sum(low, up + low, after, before, right, left, winds[0], winds[1])


class Out:
    def __init__(self, source, target, sems, rows, as_it_goes):
        self.source, self.target, self.sems, self.rows, self.as_it_goes = source, target, sems, rows, as_it_goes

    def copy(self, i):
        row = self.target.at[:, i] if self.as_it_goes else self.target.at[i]
        return pltpu.make_async_copy(self.source.at[i], row, self.sems.at[i])

    def start(self, i):
        self.copy(i).start()

    def finish(self):
        for i in range(self.rows):
            self.copy(i).wait()


def dense_row(field, first, rows):
    total = jnp.zeros((1, LANES), jnp.float32)
    lane = lax.broadcasted_iota(jnp.int32, (1, LANES), 1)
    for i in range(rows):
        slot = slot_of(i, 0, rows)
        total = jnp.where(lane // 2 == slot, pltpu.roll(field[first + i : first + i + 1, :], 2 * slot + 1, 1), total)
    return total


def forward_kernel(first, last, rows, levels, coupling, other, field, winds, *rest):
    halo_count = len(rest) - (7 if last else 14)
    halos, rest = rest[:halo_count], rest[halo_count:]
    if last:
        cols, cells, wind_cells, sides, sems, col_cells, col_sems = rest
    else:
        out, s_even, s_odd, packed, low0, low1, wind_ends, wind_dense, dense_g, cells, wind_cells, out_cells, sides, sems = rest
        leaving = Out(out_cells, out, sems.at[2], rows, False)
        packed[...] = jnp.zeros_like(packed)
        wind_dense[...] = jnp.zeros_like(wind_dense)
    incoming = Rows(field, cells, sems.at[0], rows, first, 1)
    wind_in = Rows(winds, wind_cells, sems.at[1], rows, True, 0)
    start_rows(rows, incoming, wind_in)
    merge_columns(halos[1], halos[2], sides)
    before, after = read_sides(halos)
    cells[0] = before(slice(None))
    cells[rows + 1] = after(slice(None))
    groups = levels // GROUP
    width = 2 * levels
    incoming.wait(0)

    def col_copy(i):
        lanes = pl.ds(pl.multiple_of(i * LANES, LANES), LANES)
        return pltpu.make_async_copy(col_cells.at[:, lanes], cols.at[:, lanes], col_sems.at[i])

    def row(i, _):
        @pl.when(i < rows - 1)
        def _():
            incoming.wait(i + 1)

        wind_in.wait(i)
        for m in range(2 * groups // PARTS):
            f, start = m * PARTS // groups, m * PARTS % groups
            values = []
            for group in range(start, start + PARTS):
                value = forward_point(cells, wind_cells, sides, i, f, group, levels)
                if group == 0:
                    value = coupled(couple_forward, value, other, coupling, i, f, rows)
                    if not last:
                        put_low((low0, low1), value, i, f, rows)
                values.append(value)
            base = m * PARTS * GROUP
            if last:
                lanes = pl.ds(pl.multiple_of(i * LANES, LANES), LANES)
                high, low = split(jnp.concatenate(values, axis=0), 2)
                col_cells[pl.ds(base, PARTS * GROUP), lanes] = high
                col_cells[pl.ds(width + base, PARTS * GROUP), lanes] = low
            else:
                for part, value in enumerate(values):
                    out_cells[i, pl.ds(base + part * GROUP, GROUP), :] = value
                pack_block(packed, values, i, m)
                if f == 0:
                    w = [wind_cells[i, pl.ds(levels + base + part * GROUP, GROUP), :] for part in range(PARTS)]
                    pack_block(wind_dense, w, i, m)
        if last:
            col_copy(i).start()
        else:
            leaving.start(i)
        return 0

    lax.fori_loop(0, rows, row, 0)
    if last:
        for i in range(rows):
            col_copy(i).wait()
        return
    put_strip(s_even, s_odd, slice(None), out_cells[0], out_cells[rows - 1])
    wind_ends[0] = wind_cells[0, pl.ds(0, levels), :]
    wind_ends[1] = wind_cells[rows - 1, pl.ds(0, levels), :]
    dense_g[...] = jnp.broadcast_to(dense_row(coupling, 0, rows), dense_g.shape)
    leaving.finish()


def dense_products(packed, value, wind_dense):
    half = wind_dense.shape[0]
    for f in range(2):
        at = slice(f * half, (f + 1) * half)
        down, up = products(value[at], wind_dense[...])
        lane = lax.broadcasted_iota(jnp.int32, down.shape, 1)
        packed[at, :] = jnp.where(lane % 2 == 1, up, down)


def level0_row(value, new, f):
    half = value.shape[0] // 2
    sub = lax.broadcasted_iota(jnp.int32, value.shape, 0)
    lane = lax.broadcasted_iota(jnp.int32, value.shape, 1)
    return jnp.where((sub == f * half) & (lane % (2 * PARTS) < 2), new, value)


def end_rows(ends, s_even, s_odd, wind_ends, levels):
    for f in range(2):
        at = slice(f * levels, (f + 1) * levels)
        put_strip(
            s_even, s_odd, at, products(ends[0][at], wind_ends[0])[1], products(ends[1][at], wind_ends[1])[0]
        )


def with_first(value, new):
    return jnp.where(lax.broadcasted_iota(jnp.int32, value.shape, 0) == 0, new, value)


def border_kernel(rows, levels, coupling, other, ends, columns, wind_ends, wind_dense, dense_g, s_even, s_odd, packed):
    half = columns.shape[0] // 2
    dense = columns[...]
    full = [ends[0], ends[1]]
    for f in range(2):
        mixed = couple_adjoint(columns[f * half : f * half + 1, :], other[4 + f : 5 + f, :], dense_g[0:1, :])
        dense = level0_row(dense, mixed, f)
    for k, i in enumerate((0, rows - 1)):
        parts = []
        for f in range(2):
            value = ends[k, f * levels : (f + 1) * levels, :]
            at = 2 * k + f
            parts.append(with_first(value, couple_adjoint(value[0:1], other[at : at + 1, :], coupling[i : i + 1, :])))
        full[k] = jnp.concatenate(parts, axis=0)
    dense_products(packed, dense, wind_dense)
    end_rows(full, s_even, s_odd, wind_ends, levels)


def outside_floor(halos, low, f, rows, levels):
    before, after = read_sides(halos)
    at = pl.ds(f * levels, 1)
    sub, lane = sub_iota(rows), lane_iota(rows)
    low = low + jnp.where(sub == 0, before(at), 0.0) + jnp.where(sub == rows - 1, after(at), 0.0)
    edge = floor_edge(halos, f, rows, levels)
    edge = jnp.where(lane == 0, pltpu.roll(edge, 1, 1), pltpu.roll(edge, LANES - 1, 1))
    return low + jnp.where((lane == 0) | (lane == LANES - 1), edge, 0.0)


def floor_kernel(rows, levels, low0, *rest):
    *halos, floor = rest
    for f in range(2):
        here = pl.ds(f * rows, rows)
        floor[here, :] = outside_floor(halos, low0[here, :], f, rows, levels)


def swap_pairs(value):
    lane = lax.broadcasted_iota(jnp.int32, value.shape, 1)
    return jnp.where(lane % 2 == 1, pltpu.roll(value, 1, 1), pltpu.roll(value, LANES - 1, 1))


def edge_lanes(sides, i, group):
    m, part = group // PARTS, group % PARTS
    rows = LANES // (2 * PARTS)
    moved = pltpu.roll(sides[m * GROUP : (m + 1) * GROUP, :], LANES - 1 - 2 * slot_of(i, part, rows), 1)
    lane = lane_iota()
    return jnp.where((lane == 0) | (lane == LANES - 1), moved, 0.0)


def border_again_kernel(rows, levels, coupling, floor, other, ends, columns, wind_ends, wind_dense, dense_g, *rest):
    *halos, s_even, s_odd, packed, sides = rest
    before, after = read_sides(halos)
    sides[...] = swap_pairs(merged(halos[1], halos[2], slice(None)))
    half = columns.shape[0] // 2
    groups = levels // GROUP
    outer = [before(slice(None)), after(slice(None))]
    full = []
    for k, i in enumerate((0, rows - 1)):
        edges = jnp.concatenate([edge_lanes(sides, i, group) for group in range(2 * groups)], axis=0)
        value = ends[k] + outer[k] + edges
        parts = []
        for f in range(2):
            part = value[f * levels : (f + 1) * levels]
            at = f * rows + i
            parts.append(with_first(part, couple_adjoint(part[0:1], other[at : at + 1, :], coupling[i : i + 1, :])))
        full.append(jnp.concatenate(parts, axis=0))
    end_rows(full, s_even, s_odd, wind_ends, levels)
    dense = columns[...] + sides[...]
    corners = []
    for m in range(2 * groups // PARTS):
        total = jnp.zeros((GROUP, LANES), jnp.float32)
        for part in range(PARTS):
            at = slice((m * PARTS + part) * GROUP, (m * PARTS + part + 1) * GROUP)
            for k, i in enumerate((0, rows - 1)):
                total = pack_into(total, outer[k][at], slot_of(i, part, rows))
        corners.append(total)
    dense = dense + jnp.concatenate(corners, axis=0)
    for f in range(2):
        mine = dense_row(floor, f * rows, rows)
        mixed = couple_adjoint(mine, dense_row(other, f * rows, rows), dense_g[0:1, :])
        dense = level0_row(dense, mixed, f)
    dense_products(packed, dense, wind_dense)


def adjoint_rows(rows, levels, cells, wind_cells, out_cells, leaving, take, each):
    groups = levels // GROUP
    cells[0] = jnp.zeros_like(cells[0])
    cells[rows + 1] = jnp.zeros_like(cells[0])
    wind_cells[0] = jnp.zeros_like(wind_cells[0])
    wind_cells[rows + 1] = jnp.zeros_like(wind_cells[0])
    take(0)

    def row(i, _):
        @pl.when(i < rows - 1)
        def _():
            take(i + 1)

        for m in range(2 * groups // PARTS):
            f, start = m * PARTS // groups, m * PARTS % groups
            values = []
            for group in range(start, start + PARTS):
                value = adjoint_point(cells, wind_cells, i, f, group, levels)
                out_cells[i, pl.ds(f * levels + group * GROUP, GROUP), :] = value
                values.append(value)
            each(i, m, f, start, values)
        leaving.start(i)
        return 0

    lax.fori_loop(0, rows, row, 0)


def first_adjoint_kernel(
    rows, levels, coupling, other, field, winds, out, ends, columns, low0, cells, wind_cells, out_cells, sems
):
    incoming = Rows(field, cells, sems.at[0], rows, False, 1)
    wind_in = Rows(winds, wind_cells, sems.at[1], rows, True, 1)
    start_rows(rows, incoming, wind_in)
    leaving = Out(out_cells, out, sems.at[2], rows, False)
    columns[...] = jnp.zeros_like(columns)

    def take(i):
        incoming.wait(i)
        wind_in.wait(i)
        for f in range(2):
            at = pl.ds(f * levels, GROUP)
            cells[i + 1, at, :] = coupled(couple_adjoint, cells[i + 1, at, :], other, coupling, i, f, rows)

    def each(i, m, f, start, values):
        if start == 0:
            low0[pl.ds(f * rows + i, 1), :] = values[0][0:1]
        pack_block(columns, values, i, m)

    adjoint_rows(rows, levels, cells, wind_cells, out_cells, leaving, take, each)
    ends[0] = out_cells[0]
    ends[1] = out_cells[rows - 1]
    leaving.finish()


def second_adjoint_kernel(rows, levels, coupling, other, field, winds, *rest):
    *halos, out, cells, wind_cells, out_cells, sides, sems = rest
    incoming = Rows(field, cells, sems.at[0], rows, False, 1)
    wind_in = Rows(winds, wind_cells, sems.at[1], rows, True, 1)
    start_rows(rows, incoming, wind_in)
    leaving = Out(out_cells, out, sems.at[2], rows, False)
    sides[...] = swap_pairs(merged(halos[1], halos[2], slice(None)))
    before, after = read_sides(halos)
    groups = levels // GROUP

    def take(i):
        incoming.wait(i)
        wind_in.wait(i)
        for group in range(2 * groups):
            at = pl.ds(group * GROUP, GROUP)
            value = cells[i + 1, at, :] + edge_lanes(sides, i, group)
            if group % groups == 0:
                f = group // groups
                value = value + jnp.where(i == 0, before(at), 0.0) + jnp.where(i == rows - 1, after(at), 0.0)
                value = coupled(couple_adjoint, value, other, coupling, i, f, rows)
            cells[i + 1, at, :] = value

    def add_outer(i, side):
        for f in range(2):
            at = pl.ds(f * levels + GROUP, levels - GROUP)
            cells[i + 1, at, :] = cells[i + 1, at, :] + side(at)

    def take_all(i):
        take(i)

        @pl.when(i == 0)
        def _():
            add_outer(0, before)

        @pl.when(i == rows - 1)
        def _():
            add_outer(rows - 1, after)

    adjoint_rows(rows, levels, cells, wind_cells, out_cells, leaving, take_all, lambda *_: None)
    leaving.finish()


def final_kernel(rows, levels, scale, field, state, *rest):
    *halos, out, cells, state_cells, sides, sems = rest
    incoming = Rows(field, cells, sems.at[0], rows, False, 0)
    state_in = Rows(state, state_cells, sems.at[1], rows, True, 0)
    start_rows(rows, incoming, state_in)
    leaving = Out(cells, out, sems.at[2], rows, True)
    sides[...] = swap_pairs(merged(halos[1], halos[2], slice(None)))
    before, after = read_sides(halos)
    groups = levels // GROUP

    def add(i, outer):
        incoming.wait(i)
        state_in.wait(i)
        for group in range(2 * groups):
            at = pl.ds(group * GROUP, GROUP)
            value = cells[i, at, :] + scale[at, :] * state_cells[i, at, :] + edge_lanes(sides, i, group)
            cells[i, at, :] = value if outer is None else value + outer(at)
        leaving.start(i)
        return 0

    add(0, before)
    lax.fori_loop(1, rows - 1, lambda i, _: add(i, None), 0)
    add(rows - 1, after)
    leaving.finish()


def split(value, terms):
    parts = []
    for _ in range(terms):
        part = value.astype(jnp.bfloat16)
        parts.append(part)
        value = value - part.astype(jnp.float32)
    return parts


def dot(a, b, contract):
    return lax.dot_general(a, b, ((contract[:1], contract[1:]), ((), ())), preferred_element_type=jnp.float32)


def route_kernel(tiles, cap, dest, col, prec, op, out):
    count = op.shape[0]
    width = op.shape[1]
    halves = width // LANES
    owner = lax.broadcasted_iota(jnp.int32, (tiles, count), 0)
    hits = owner == dest[...]
    ones = jnp.where(hits, 1.0, 0.0)
    earlier = lax.broadcasted_iota(jnp.int32, (count, count), 0) <= lax.broadcasted_iota(jnp.int32, (count, count), 1)
    running = dot(ones.astype(jnp.bfloat16), jnp.where(earlier, 1.0, 0.0).astype(jnp.bfloat16), (1, 0))
    slot = jnp.sum(running * ones, axis=0, keepdims=True) - 1.0
    slot = slot.astype(jnp.int32)
    place = dest[...] * cap + slot
    at_slot = lax.broadcasted_iota(jnp.int32, (LANES, count), 0) == slot
    at_slot = jnp.where(at_slot, 1.0, 0.0).astype(jnp.bfloat16)
    column = col[...].astype(jnp.float32)
    pieces = [ones * part.astype(jnp.float32) for part in split(column, 2) + split(prec[...], 3)]
    aux = dot(jnp.concatenate(pieces, axis=0).astype(jnp.bfloat16), at_slot, (1, 1))
    columns = aux[0:tiles] + aux[tiles : 2 * tiles]
    precs = (aux[2 * tiles : 3 * tiles] + aux[3 * tiles : 4 * tiles]) + aux[4 * tiles : 5 * tiles]
    sub = sub_iota()
    for owner_at in range(tiles):
        block = jnp.where(sub == 0, columns[owner_at : owner_at + 1], 0.0)
        block = jnp.where(sub == 1, precs[owner_at : owner_at + 1], block)
        out[owner_at, pl.ds(halves * cap, GROUP), :] = block
    rows_high, rows_low = split(op[...], 2)
    chunk = 256
    for first in range(0, tiles * cap, chunk):
        picks = lax.broadcasted_iota(jnp.int32, (chunk, count), 0) + first == place
        picks = jnp.where(picks, 1.0, 0.0).astype(jnp.bfloat16)
        moved = dot(picks, rows_high, (1, 0)) + dot(picks, rows_low, (1, 0))
        for part in range(chunk // cap):
            for half in range(halves):
                out[first // cap + part, pl.ds(half * cap, cap), :] = moved[
                    part * cap : (part + 1) * cap, half * LANES : (half + 1) * LANES
                ]


def innovate_kernel(rows, width, tiles, cap, records, cols, spread, sel, ends, columns, floor, *scratch):
    col_cells, sel_cells, border_sel, places, precs, both, spread_cells, sems = scratch
    chunks = 8
    copies = []
    for part in range(chunks):
        at = pl.ds(part * (2 * width // chunks), 2 * width // chunks)
        copies.append(pltpu.make_async_copy(cols.at[at], col_cells.at[at], sems.at[part]))
        copies[-1].start()
    halves = width // LANES
    count = tiles * cap
    aux = halves * cap
    own = lax.broadcasted_iota(jnp.int32, (cap, LANES), 1) == lax.broadcasted_iota(jnp.int32, (cap, LANES), 0)
    ones = jnp.ones((LANES, LANES), jnp.bfloat16)
    step = 256
    lane = lax.broadcasted_iota(jnp.int32, (step, LANES), 1)
    border = (rows - 1 - lane // (2 * PARTS)) * LANES + jnp.where(lane % 2 == 1, 0, LANES - 1)
    border = jnp.where(lane % (2 * PARTS) < 2, border, -1).astype(jnp.float32)
    lane = lane.astype(jnp.float32)

    def sel_copy(block):
        at = pl.ds(pl.multiple_of(block * step, step), step)
        return pltpu.make_async_copy(sel_cells.at[at], sel.at[at], sems.at[chunks + block])

    def select(block, _):
        sources = step // cap

        def spread_out(part):
            rows_of = [
                jnp.where(own, records[block * sources + s, pl.ds(aux + part, 1), :], 0.0) for s in range(sources)
            ]
            terms = split(jnp.concatenate(rows_of, axis=0), 2 + part)
            return sum(dot(term, ones, (1, 0)) for term in terms)

        at = pl.ds(pl.multiple_of(block * step, step), step)
        place = spread_out(0)
        column = place - lane
        precs[at, :] = spread_out(1)
        for i in range(rows):
            sel_cells[at, i * LANES : (i + 1) * LANES] = jnp.where(column == float(i * LANES), 1.0, 0.0).astype(
                jnp.bfloat16
            )
        border_sel[at, :] = jnp.where(place == border, 1.0, 0.0).astype(jnp.bfloat16)
        sel_copy(block).start()
        return 0

    lax.fori_loop(0, count // step, select, 0)
    for copy in copies:
        copy.wait()
    both[...] = dot(sel_cells[...], col_cells[...], (1, 1))

    def weigh(block, _):
        at = pl.ds(pl.multiple_of(block * LANES, LANES), LANES)
        sources = LANES // cap
        ops = [
            jnp.concatenate(
                [records[block * sources + s, half * cap : (half + 1) * cap, :] for s in range(sources)], axis=0
            )
            for half in range(halves)
        ]
        total = sum(
            (both[at, half * LANES : (half + 1) * LANES] + both[at, width + half * LANES : width + (half + 1) * LANES])
            * ops[half]
            for half in range(halves)
        )
        innovation = jnp.sum(total, axis=1, keepdims=True) * precs[at, :]
        for half in range(halves):
            high, low = split((ops[half] * innovation).T, 2)
            spread_cells[half * LANES : (half + 1) * LANES, at] = high
            spread_cells[width + half * LANES : width + (half + 1) * LANES, at] = low
        return 0

    lax.fori_loop(0, count // LANES, weigh, 0)
    spread_copy = pltpu.make_async_copy(spread_cells, spread, sems.at[chunks + count // step])
    spread_copy.start()

    def cells_of(ones_at):
        terms = dot(spread_cells[...], ones_at, (1, 0))
        return terms[:width] + terms[width:]

    ends[0] = cells_of(sel_cells[:, 0:LANES])
    ends[1] = cells_of(sel_cells[:, (rows - 1) * LANES : rows * LANES])
    thin = cells_of(border_sel[...])
    for m in range(width // (GROUP * PARTS)):
        total = thin[m * PARTS * GROUP : (m * PARTS + 1) * GROUP]
        for part in range(1, PARTS):
            at = (m * PARTS + part) * GROUP
            total = total + pltpu.roll(thin[at : at + GROUP], 2 * part, 1)
        columns[m * GROUP : (m + 1) * GROUP, :] = total
    half = columns.shape[0] // 2
    floor[...] = jnp.zeros_like(floor)
    for f in range(2):
        for k in range(2):
            floor[2 * k + f : 2 * k + f + 1, :] = ends[k, f * (width // 2) : f * (width // 2) + 1, :]
        floor[4 + f : 5 + f, :] = columns[f * half : f * half + 1, :]
    for block in range(count // step):
        sel_copy(block).wait()
    spread_copy.wait()


def scatter_kernel(rows, width, spread, sel, adjoint, low0, low1, spread_cells, sel_cells, out_cells, sems):
    count = sel.shape[0]
    chunks = 4
    copies = [pltpu.make_async_copy(spread, spread_cells, sems.at[2 * rows])]
    for part in range(chunks):
        at = pl.ds(part * (count // chunks), count // chunks)
        copies.append(pltpu.make_async_copy(sel.at[at], sel_cells.at[at], sems.at[rows + part]))
    for copy in copies:
        copy.start()
    for copy in copies:
        copy.wait()
    leaving = Out(out_cells, adjoint, sems, rows, False)
    sums = dot(spread_cells[...], sel_cells[...], (1, 0))
    for i in range(rows):
        lanes = slice(i * LANES, (i + 1) * LANES)
        out_cells[i] = sums[:width, lanes] + sums[width:, lanes]
        leaving.start(i)
        for f in range(2):
            put_low((low0, low1), out_cells[i, f * (width // 2) : f * (width // 2) + GROUP, :], i, f, rows)
    leaving.finish()


def local(state_incr, winds, coupling, background, obs_dest, obs_col, obs_op, obs_prec):
    _, fields, levels, rows, lanes = state_incr.shape
    width = fields * levels
    groups = width // GROUP
    tiles = lax.axis_size("gx") * lax.axis_size("gy")
    count = obs_col.shape[0]
    cap = 2 * count // tiles
    halves = obs_op.shape[1] // LANES

    scale = jnp.broadcast_to(background.reshape(width, 1), (width, LANES))

    vmem = pl.BlockSpec(memory_space=pltpu.VMEM)
    anywhere = pl.BlockSpec(memory_space=pl.ANY)
    own = pltpu.VMEM((rows, width, LANES), jnp.float32)
    framed = pltpu.VMEM((rows + 2, width, LANES), jnp.float32)
    packed_shape = f32(groups // PARTS * GROUP, LANES)
    sides = pltpu.VMEM(packed_shape.shape, jnp.float32)
    strip_shapes = [f32(width, LANES), f32(width, LANES), packed_shape]
    field_shape = f32(rows, width, LANES)
    low_shape = f32(fields * rows, LANES)
    cols_shape = ((2 * width, rows * LANES), jnp.bfloat16)

    def sems(*shape):
        return pltpu.SemaphoreType.DMA(shape)

    def run(body, out_shape, scratch, args, far=(), out_far=()):
        specs = [anywhere if k in far else vmem for k in range(len(args))]
        outs = [anywhere if k in out_far else vmem for k in range(len(out_shape))]
        return call(body, out_shape, scratch, in_specs=specs, out_specs=outs)(*args)

    def on_rows(body):
        return functools.partial(body, rows, levels)

    def swap_floor(floor):
        return lax.ppermute(floor, "comp", [(0, 1), (1, 0)])

    state = state_incr.reshape(width, rows, lanes)
    wind = winds.reshape(width, rows, lanes)
    floor_winds = winds[0, :, 0]
    slots = tiles * cap
    thin_shape = f32(GROUP, LANES)

    s_even, s_odd, packed, low0, low1 = run(
        on_rows(edges_kernel), strip_shapes + [low_shape] * 2, [own, sems(rows)], (state,), far=(0,)
    )
    halos = exchange((s_even, s_odd), packed)

    send = call(functools.partial(route_kernel, tiles, cap), f32(tiles, halves * cap + GROUP, LANES))(
        obs_dest.reshape(1, count), obs_col.reshape(1, count), obs_prec.reshape(1, count), obs_op
    )
    send, halos = lax.optimization_barrier((send, halos))
    records = lax.all_to_all(send, ("gx", "gy"), split_axis=0, concat_axis=0, tiled=True)

    (floor,) = run(on_rows(forward_floor_kernel), [low_shape], [], (low0, low1, floor_winds, *halos))
    field, s_even, s_odd, packed, low0, low1, wind_ends, wind_dense, dense_g = run(
        on_rows(functools.partial(forward_kernel, True, False)),
        [field_shape] + strip_shapes + [low_shape] * 2 + [f32(2, levels, LANES), f32(groups // PARTS * GROUP // 2, LANES), thin_shape],
        [framed, own, own, sides, sems(3, rows)],
        (coupling, swap_floor(floor), state, wind, *halos),
        far=(2, 3),
        out_far=(0,),
    )
    halos = exchange((s_even, s_odd), packed)
    (floor,) = run(on_rows(forward_floor_kernel), [low_shape], [], (low0, low1, floor_winds, *halos))
    (cols,) = run(
        on_rows(functools.partial(forward_kernel, False, True)),
        [jax.ShapeDtypeStruct(*cols_shape)],
        [framed, own, sides, sems(2, rows), pltpu.VMEM(*cols_shape), sems(rows)],
        (coupling, swap_floor(floor), field, wind, *halos),
        far=(2, 3),
        out_far=(0,),
    )

    spread_shape = ((2 * width, slots), jnp.bfloat16)
    sel_shape = ((slots, rows * LANES), jnp.bfloat16)
    spread, sel, ends, columns, border_floor = run(
        functools.partial(innovate_kernel, rows, width, tiles, cap),
        [jax.ShapeDtypeStruct(*spread_shape), jax.ShapeDtypeStruct(*sel_shape), f32(2, width, LANES), packed_shape, thin_shape],
        [
            pltpu.VMEM(*cols_shape),
            pltpu.VMEM(*sel_shape),
            pltpu.VMEM((slots, LANES), jnp.bfloat16),
            pltpu.VMEM((slots, LANES), jnp.float32),
            pltpu.VMEM((slots, LANES), jnp.float32),
            pltpu.VMEM((slots, 2 * width), jnp.float32),
            pltpu.VMEM(*spread_shape),
            sems(8 + slots // 256 + 1),
        ],
        (records, cols),
        far=(1,),
        out_far=(0, 1),
    )
    strips = run(
        on_rows(border_kernel),
        strip_shapes,
        [],
        (coupling, swap_floor(border_floor), ends, columns, wind_ends, wind_dense, dense_g),
    )
    halos = exchange(strips[:2], strips[2])
    adjoint, low0, _ = run(
        functools.partial(scatter_kernel, rows, width),
        [field_shape, low_shape, low_shape],
        [pltpu.VMEM(*spread_shape), pltpu.VMEM(*sel_shape), own, sems(2 * rows + 1)],
        (spread, sel),
        far=(0, 1),
        out_far=(0,),
    )
    adjoint, ends, columns, low0 = run(
        on_rows(first_adjoint_kernel),
        [field_shape, f32(2, width, LANES), packed_shape, low_shape],
        [framed, framed, own, sems(3, rows)],
        (coupling, swap_floor(low0), adjoint, wind),
        far=(2, 3),
        out_far=(0,),
    )
    (floor,) = run(on_rows(floor_kernel), [low_shape], [], (low0, *halos))
    other = swap_floor(floor)
    strips = run(
        on_rows(border_again_kernel),
        strip_shapes,
        [sides],
        (coupling, floor, other, ends, columns, wind_ends, wind_dense, dense_g, *halos),
    )
    last_halos = exchange(strips[:2], strips[2])
    (adjoint,) = run(
        on_rows(second_adjoint_kernel),
        [field_shape],
        [framed, framed, own, sides, sems(3, rows)],
        (coupling, other, adjoint, wind, *halos),
        far=(2, 3),
        out_far=(0,),
    )
    (result,) = run(
        on_rows(final_kernel),
        [f32(width, rows, LANES)],
        [own, own, sides, sems(3, rows)],
        (scale, adjoint, state, *last_halos),
        far=(1, 2),
        out_far=(0,),
    )
    return result.reshape(state_incr.shape)


def solution(mesh):
    placed = (
        P("comp", None, None, "gx", "gy"),
        P("comp", None, None, "gx", "gy"),
        P("gx", "gy"),
        P("comp", None, None),
        P(("comp", "gx", "gy"), None),
        P(("comp", "gx", "gy")),
        P(("comp", "gx", "gy"), None),
        P(("comp", "gx", "gy")),
    )
    return jax.shard_map(
        local,
        mesh=mesh,
        in_specs=placed,
        out_specs=P("comp", None, None, "gx", "gy"),
        check_vma=False,
    )
```

```python
import functools

import jax
import jax.numpy as jnp
from jax import lax
from jax.experimental import pallas as pl
from jax.experimental.pallas import tpu as pltpu
from jax.sharding import PartitionSpec as P

HORIZ_MIX = 0.1
VERT_MIX = 0.15
LANES = 128
GROUP = 8
MIB = 1024 * 1024
SWEEP_VMEM = 16 * MIB
OBSERVE_VMEM = 22 * MIB


def call(body, out_shape, scratch=(), limit=SWEEP_VMEM, traffic=0, **kw):
    cost = pl.CostEstimate(flops=0, bytes_accessed=traffic, transcendentals=0) if traffic else None
    return pl.pallas_call(
        body,
        out_shape=out_shape,
        scratch_shapes=list(scratch),
        cost_estimate=cost,
        compiler_params=pltpu.CompilerParams(vmem_limit_bytes=limit),
        **kw,
    )


def f32(*shape):
    return jax.ShapeDtypeStruct(shape, jnp.float32)


def lane_iota(rows=GROUP):
    return lax.broadcasted_iota(jnp.int32, (rows, LANES), 1)


def sub_iota(rows=GROUP):
    return lax.broadcasted_iota(jnp.int32, (rows, LANES), 0)


def pair_swap(block, axis, start):
    count = lax.axis_size(axis)
    route = []
    for low in range(start, count - 1, 2):
        route += [(low, low + 1), (low + 1, low)]
    return lax.ppermute(block, axis, route)


def exchange(strips, packed):
    y_even = pair_swap(packed, "gy", 0)
    y_odd = pair_swap(packed, "gy", 1)
    halos = [pair_swap(strips[0], "gx", 0), y_even, y_odd]
    if lax.axis_size("gx") > 2:
        halos.append(pair_swap(strips[1], "gx", 1))
    return halos


def is_odd(axis):
    return lax.rem(lax.axis_index(axis), 2) == 1


def read_sides(refs):
    even = refs[0]
    odd = refs[3] if len(refs) > 3 else None
    at_odd = is_odd("gx")

    def side(at, turned):
        other = jnp.zeros_like(even[at]) if odd is None else odd[at]
        return jnp.where(turned, other, even[at])

    return lambda at: side(at, jnp.logical_not(at_odd)), lambda at: side(at, at_odd)


PARTS = 4


def merged(y_even, y_odd, at):
    a, b = y_even[at, :], y_odd[at, :]
    lane = lax.broadcasted_iota(jnp.int32, a.shape, 1)
    return jnp.where((lane % 2 == 1) == jnp.logical_not(is_odd("gy")), a, b)


def merge_columns(y_even, y_odd, sides):
    sides[...] = merged(y_even, y_odd, slice(None))


def slot_of(i, part, rows):
    return PARTS * (rows - 1 - i) + part


def side_columns(sides, i, group):
    m, part = group // PARTS, group % PARTS
    rows = LANES // (2 * PARTS)
    return pltpu.roll(sides[m * GROUP : (m + 1) * GROUP, :], LANES - 1 - 2 * slot_of(i, part, rows), 1)


def pack_into(total, value, slot):
    return jnp.where(lane_iota() // 2 == slot, pltpu.roll(value, 2 * slot + 1, 1), total)


def pack_block(packed, values, i, m):
    at = pl.ds(m * GROUP, GROUP)
    total = packed[at, :]
    for part, value in enumerate(values):
        total = pack_into(total, value, slot_of(i, part, LANES // (2 * PARTS)))
    packed[at, :] = total


CENTRE = 1.0 - 4.0 * HORIZ_MIX - 2.0 * VERT_MIX


def levels_around(cells, i, base, group, groups):
    here = cells[i + 1, pl.ds(base + group * GROUP, GROUP), :]
    if group == groups - 1:
        upper = jnp.where(sub_iota() == GROUP - 1, here, pltpu.roll(here, GROUP - 1, 0))
    else:
        upper = cells[i + 1, pl.ds(base + group * GROUP + 1, GROUP), :]
    if group == 0:
        lower = jnp.where(sub_iota() == 0, here, pltpu.roll(here, 1, 0))
    else:
        lower = cells[i + 1, pl.ds(base + group * GROUP - 1, GROUP), :]
    return here, upper, lower


def shifted(first, last, edge, rows=GROUP):
    lane = lane_iota(rows)
    right = pltpu.roll(jnp.where(lane == 0, edge, first), LANES - 1, 1)
    left = pltpu.roll(jnp.where(lane == LANES - 1, edge, last), 1, 1)
    return right, left


def forward_sum(here, vertical, after, before, right, left, u, w):
    return (
        CENTRE * here
        + VERT_MIX * vertical
        + HORIZ_MIX * ((after + before) + (right + left))
        - 0.5 * (u * (after - before) + w * (right - left))
    )


def forward_point(cells, winds, sides, i, f, group, levels):
    groups = levels // GROUP
    here, upper, lower = levels_around(cells, i, f * levels, group, groups)
    at = pl.ds(f * levels + group * GROUP, GROUP)
    right, left = shifted(here, here, 0.0 if sides is None else side_columns(sides, i, f * groups + group))
    u = winds[i, pl.ds(group * GROUP, GROUP), :]
    w = winds[i, pl.ds(levels + group * GROUP, GROUP), :]
    return forward_sum(here, upper + lower, cells[i + 2, at, :], cells[i, at, :], right, left, u, w)


def products(x, wind):
    slope = 0.5 * (wind * x)
    return HORIZ_MIX * x - slope, HORIZ_MIX * x + slope


def adjoint_point(cells, winds, i, f, group, levels):
    here, upper, lower = levels_around(cells, i, f * levels, group, levels // GROUP)
    at = pl.ds(f * levels + group * GROUP, GROUP)
    wind_at = pl.ds(group * GROUP, GROUP)
    after, before = cells[i + 2, at, :], cells[i, at, :]
    u_after, u_before = winds[i + 2, wind_at, :], winds[i, wind_at, :]
    down, up = products(here, winds[i + 1, pl.ds(levels + group * GROUP, GROUP), :])
    right, left = shifted(up, down, 0.0)
    return (
        CENTRE * here
        + VERT_MIX * (upper + lower)
        + HORIZ_MIX * (after + before)
        + 0.5 * (u_after * after - u_before * before)
        + (right + left)
    )


def shares_of(coupling):
    own = jnp.where(lax.axis_index("comp") == 0, 1.0, 0.5)
    return own * coupling, (1.5 - own) * coupling


def couple_forward(value, other, coupling):
    own, _ = shares_of(coupling)
    return value - own * (value - other)


def couple_adjoint(value, other, coupling):
    own, peer = shares_of(coupling)
    return value - own * value + peer * other


def coupled(rule, value, other, coupling, i, f, rows):
    mixed = rule(value, other[pl.ds(f * rows + i, 1), :], coupling[pl.ds(i, 1), :])
    return jnp.where(sub_iota() == 0, mixed, value)


def put_strip(strip_even, strip_odd, at, first, last):
    at_odd = is_odd("gx")
    strip_even[at, :] = jnp.where(at_odd, first, last)
    strip_odd[at, :] = jnp.where(at_odd, last, first)


def put_low(low, value, i, f, rows):
    for level in range(2):
        low[level][pl.ds(f * rows + i, 1), :] = value[level : level + 1]


class Rows:
    def __init__(self, source, target, sems, rows, as_it_comes, offset):
        self.source, self.target, self.sems = source, target, sems
        self.rows, self.as_it_comes, self.offset = rows, as_it_comes, offset

    def copy(self, i):
        row = self.source.at[:, i] if self.as_it_comes else self.source.at[i]
        return pltpu.make_async_copy(row, self.target.at[i + self.offset], self.sems.at[i])

    def wait(self, i):
        self.copy(i).wait()


def start_rows(rows, *groups):
    for i in range(rows):
        for group in groups:
            group.copy(i).start()


def edges_kernel(rows, levels, state, s_even, s_odd, packed, low0, low1, cells, sems):
    part_levels = PARTS * GROUP
    blocks = 2 * levels // part_levels

    def copy(m):
        return pltpu.make_async_copy(
            state.at[pl.ds(m * part_levels * rows, part_levels * rows)],
            cells.at[pl.ds(m * part_levels * rows, part_levels * rows)],
            sems.at[m],
        )

    for m in range(blocks):
        copy(m).start()

    def block(m, _):
        copy(m).wait()
        total = jnp.zeros((GROUP, LANES), jnp.float32)
        for part in range(PARTS):
            for i in range(rows):
                start = (m * PARTS + part) * GROUP * rows + i
                total = pack_into(total, cells[pl.ds(start, GROUP, stride=rows), :], slot_of(i, part, rows))
        packed[pl.ds(pl.multiple_of(m * GROUP, GROUP), GROUP), :] = total
        start = m * part_levels * rows
        first = cells[pl.ds(start, part_levels, stride=rows), :]
        last = cells[pl.ds(start + rows - 1, part_levels, stride=rows), :]
        put_strip(s_even, s_odd, pl.ds(pl.multiple_of(m * part_levels, part_levels), part_levels), first, last)
        return 0

    lax.fori_loop(0, blocks, block, 0)
    for f in range(2):
        for level, low in enumerate((low0, low1)):
            low[f * rows : (f + 1) * rows, :] = cells[pl.ds((f * levels + level) * rows, rows), :]


def floor_edge(halos, f, rows, levels):
    m = f * (levels // GROUP) // PARTS
    sides = jnp.broadcast_to(merged(halos[1], halos[2], pl.ds(m * GROUP, 1)), (rows, LANES))
    return pltpu.roll(sides, 2 * PARTS - 1, 1, stride=2 * PARTS, stride_axis=0)


def row_after(value, last, rows):
    return jnp.where(sub_iota(rows) == rows - 1, last, pltpu.roll(value, rows - 1, 0))


def row_before(value, first, rows):
    return jnp.where(sub_iota(rows) == 0, first, pltpu.roll(value, 1, 0))


def forward_floor_kernel(rows, levels, low0, low1, winds, *rest):
    *halos, floor = rest
    side_before, side_after = read_sides(halos)
    for f in range(2):
        here = pl.ds(f * rows, rows)
        at = pl.ds(f * levels, 1)
        low, up = low0[here, :], low1[here, :]
        after, before = row_after(low, side_after(at), rows), row_before(low, side_before(at), rows)
        right, left = shifted(low, low, floor_edge(halos, f, rows, levels), rows)
        floor[here, :] = forward_sum(low, up + low, after, before, right, left, winds[0], winds[1])


class Out:
    def __init__(self, source, target, sems, rows, as_it_goes):
        self.source, self.target, self.sems, self.rows, self.as_it_goes = source, target, sems, rows, as_it_goes

    def copy(self, i):
        row = self.target.at[:, i] if self.as_it_goes else self.target.at[i]
        return pltpu.make_async_copy(self.source.at[i], row, self.sems.at[i])

    def start(self, i):
        self.copy(i).start()

    def finish(self):
        for i in range(self.rows):
            self.copy(i).wait()


def dense_row(field, first, rows):
    total = jnp.zeros((1, LANES), jnp.float32)
    lane = lax.broadcasted_iota(jnp.int32, (1, LANES), 1)
    for i in range(rows):
        slot = slot_of(i, 0, rows)
        total = jnp.where(lane // 2 == slot, pltpu.roll(field[first + i : first + i + 1, :], 2 * slot + 1, 1), total)
    return total


def forward_kernel(rows, levels, coupling, other, field, winds, *rest):
    *halos, out, s_even, s_odd, packed, low0, low1, wind_ends, wind_dense, dense_g = rest[:-5]
    cells, wind_cells, out_cells, sides, sems = rest[-5:]
    leaving = Out(out_cells, out, sems.at[2], rows, False)
    incoming = Rows(field, cells, sems.at[0], rows, True, 1)
    wind_in = Rows(winds, wind_cells, sems.at[1], rows, True, 0)
    start_rows(rows, incoming, wind_in)
    packed[...] = jnp.zeros_like(packed)
    wind_dense[...] = jnp.zeros_like(wind_dense)
    merge_columns(halos[1], halos[2], sides)
    before, after = read_sides(halos)
    cells[0] = before(slice(None))
    cells[rows + 1] = after(slice(None))
    groups = levels // GROUP
    incoming.wait(0)

    def row(i, _):
        @pl.when(i < rows - 1)
        def _():
            incoming.wait(i + 1)

        wind_in.wait(i)
        for m in range(2 * groups // PARTS):
            f, start = m * PARTS // groups, m * PARTS % groups
            values = []
            for group in range(start, start + PARTS):
                value = forward_point(cells, wind_cells, sides, i, f, group, levels)
                if group == 0:
                    value = coupled(couple_forward, value, other, coupling, i, f, rows)
                    put_low((low0, low1), value, i, f, rows)
                values.append(value)
            base = m * PARTS * GROUP
            for part, value in enumerate(values):
                out_cells[i, pl.ds(base + part * GROUP, GROUP), :] = value
            pack_block(packed, values, i, m)
            if f == 0:
                w = [wind_cells[i, pl.ds(levels + base + part * GROUP, GROUP), :] for part in range(PARTS)]
                pack_block(wind_dense, w, i, m)
        leaving.start(i)
        return 0

    lax.fori_loop(0, rows, row, 0)
    put_strip(s_even, s_odd, slice(None), out_cells[0], out_cells[rows - 1])
    wind_ends[0] = wind_cells[0, pl.ds(0, levels), :]
    wind_ends[1] = wind_cells[rows - 1, pl.ds(0, levels), :]
    dense_g[...] = jnp.broadcast_to(dense_row(coupling, 0, rows), dense_g.shape)
    leaving.finish()


def forward_again_kernel(rows, levels, field, winds, cols, cells, wind_cells, sems, col_cells, col_sems):
    incoming = Rows(field, cells, sems.at[0], rows, False, 1)
    wind_in = Rows(winds, wind_cells, sems.at[1], rows, True, 0)
    start_rows(rows, incoming, wind_in)
    cells[0] = jnp.zeros_like(cells[0])
    cells[rows + 1] = jnp.zeros_like(cells[0])
    groups = levels // GROUP
    width = 2 * levels
    incoming.wait(0)

    def col_copy(i):
        lanes = pl.ds(pl.multiple_of(i * LANES, LANES), LANES)
        return pltpu.make_async_copy(col_cells.at[:, lanes], cols.at[:, lanes], col_sems.at[i])

    def row(i, _):
        @pl.when(i < rows - 1)
        def _():
            incoming.wait(i + 1)

        wind_in.wait(i)
        lanes = pl.ds(pl.multiple_of(i * LANES, LANES), LANES)
        for m in range(2 * groups // PARTS):
            f, start = m * PARTS // groups, m * PARTS % groups
            values = [
                forward_point(cells, wind_cells, None, i, f, group, levels) for group in range(start, start + PARTS)
            ]
            high, low = split(jnp.concatenate(values, axis=0), 2)
            col_cells[pl.ds(m * PARTS * GROUP, PARTS * GROUP), lanes] = high
            col_cells[pl.ds(width + m * PARTS * GROUP, PARTS * GROUP), lanes] = low
        col_copy(i).start()
        return 0

    lax.fori_loop(0, rows, row, 0)
    for i in range(rows):
        col_copy(i).wait()


def outside_kernel(rows, levels, coupling, floor, other, wind_ends, wind_dense, *rest):
    *halos, extra, bottom, dense = rest
    width = 2 * levels
    for f in range(2):
        here = pl.ds(f * rows, rows)
        bottom[here, :] = couple_forward(floor[here, :], other[here, :], coupling[...])
    dense_products(dense, swap_pairs(merged(halos[1], halos[2], slice(None))), wind_dense)
    before, after = read_sides(halos)
    sub = lax.broadcasted_iota(jnp.int32, (levels, LANES), 0)

    def put(value, f, lanes):
        high, low = split(jnp.where(sub == 0, 0.0, value), 2)
        extra[f * levels : (f + 1) * levels, lanes] = high
        extra[width + f * levels : width + (f + 1) * levels, lanes] = low

    lane = lane_iota()
    for f in range(2):
        at = pl.ds(f * levels, levels)
        put(products(before(at), wind_ends[0])[1], f, slice(0, LANES))
        put(products(after(at), wind_ends[1])[0], f, slice(LANES, 2 * LANES))
        thin = []
        for group in range(f * levels // GROUP, (f + 1) * levels // GROUP):
            m, part = group // PARTS, group % PARTS
            moved = pltpu.roll(dense[m * GROUP : (m + 1) * GROUP, :], (LANES - 2 * part) % LANES, 1)
            thin.append(jnp.where(lane % (2 * PARTS) < 2, moved, 0.0))
        put(jnp.concatenate(thin, axis=0), f, slice(2 * LANES, 3 * LANES))


def dense_products(packed, value, wind_dense):
    half = wind_dense.shape[0]
    for f in range(2):
        at = slice(f * half, (f + 1) * half)
        down, up = products(value[at], wind_dense[...])
        lane = lax.broadcasted_iota(jnp.int32, down.shape, 1)
        packed[at, :] = jnp.where(lane % 2 == 1, up, down)


def level0_row(value, new, f):
    half = value.shape[0] // 2
    sub = lax.broadcasted_iota(jnp.int32, value.shape, 0)
    lane = lax.broadcasted_iota(jnp.int32, value.shape, 1)
    return jnp.where((sub == f * half) & (lane % (2 * PARTS) < 2), new, value)


def end_rows(ends, s_even, s_odd, wind_ends, levels):
    for f in range(2):
        at = slice(f * levels, (f + 1) * levels)
        put_strip(
            s_even, s_odd, at, products(ends[0][at], wind_ends[0])[1], products(ends[1][at], wind_ends[1])[0]
        )


def with_first(value, new):
    return jnp.where(lax.broadcasted_iota(jnp.int32, value.shape, 0) == 0, new, value)


def border_kernel(rows, levels, coupling, other, ends, columns, wind_ends, wind_dense, dense_g, s_even, s_odd, packed):
    half = columns.shape[0] // 2
    dense = columns[...]
    full = [ends[0], ends[1]]
    for f in range(2):
        mixed = couple_adjoint(columns[f * half : f * half + 1, :], other[4 + f : 5 + f, :], dense_g[0:1, :])
        dense = level0_row(dense, mixed, f)
    for k, i in enumerate((0, rows - 1)):
        parts = []
        for f in range(2):
            value = ends[k, f * levels : (f + 1) * levels, :]
            at = 2 * k + f
            parts.append(with_first(value, couple_adjoint(value[0:1], other[at : at + 1, :], coupling[i : i + 1, :])))
        full[k] = jnp.concatenate(parts, axis=0)
    dense_products(packed, dense, wind_dense)
    end_rows(full, s_even, s_odd, wind_ends, levels)


def outside_floor(halos, low, f, rows, levels):
    before, after = read_sides(halos)
    at = pl.ds(f * levels, 1)
    sub, lane = sub_iota(rows), lane_iota(rows)
    low = low + jnp.where(sub == 0, before(at), 0.0) + jnp.where(sub == rows - 1, after(at), 0.0)
    edge = floor_edge(halos, f, rows, levels)
    edge = jnp.where(lane == 0, pltpu.roll(edge, 1, 1), pltpu.roll(edge, LANES - 1, 1))
    return low + jnp.where((lane == 0) | (lane == LANES - 1), edge, 0.0)


def floor_kernel(rows, levels, low0, *rest):
    *halos, floor = rest
    for f in range(2):
        here = pl.ds(f * rows, rows)
        floor[here, :] = outside_floor(halos, low0[here, :], f, rows, levels)


def swap_pairs(value):
    lane = lax.broadcasted_iota(jnp.int32, value.shape, 1)
    return jnp.where(lane % 2 == 1, pltpu.roll(value, 1, 1), pltpu.roll(value, LANES - 1, 1))


def edge_lanes(sides, i, group):
    m, part = group // PARTS, group % PARTS
    rows = LANES // (2 * PARTS)
    moved = pltpu.roll(sides[m * GROUP : (m + 1) * GROUP, :], LANES - 1 - 2 * slot_of(i, part, rows), 1)
    lane = lane_iota()
    return jnp.where((lane == 0) | (lane == LANES - 1), moved, 0.0)


def border_again_kernel(rows, levels, coupling, floor, other, ends, columns, wind_ends, wind_dense, dense_g, *rest):
    *halos, s_even, s_odd, packed, sides = rest
    before, after = read_sides(halos)
    sides[...] = swap_pairs(merged(halos[1], halos[2], slice(None)))
    half = columns.shape[0] // 2
    groups = levels // GROUP
    outer = [before(slice(None)), after(slice(None))]
    full = []
    for k, i in enumerate((0, rows - 1)):
        edges = jnp.concatenate([edge_lanes(sides, i, group) for group in range(2 * groups)], axis=0)
        value = ends[k] + outer[k] + edges
        parts = []
        for f in range(2):
            part = value[f * levels : (f + 1) * levels]
            at = f * rows + i
            parts.append(with_first(part, couple_adjoint(part[0:1], other[at : at + 1, :], coupling[i : i + 1, :])))
        full.append(jnp.concatenate(parts, axis=0))
    end_rows(full, s_even, s_odd, wind_ends, levels)
    dense = columns[...] + sides[...]
    corners = []
    for m in range(2 * groups // PARTS):
        total = jnp.zeros((GROUP, LANES), jnp.float32)
        for part in range(PARTS):
            at = slice((m * PARTS + part) * GROUP, (m * PARTS + part + 1) * GROUP)
            for k, i in enumerate((0, rows - 1)):
                total = pack_into(total, outer[k][at], slot_of(i, part, rows))
        corners.append(total)
    dense = dense + jnp.concatenate(corners, axis=0)
    for f in range(2):
        mine = dense_row(floor, f * rows, rows)
        mixed = couple_adjoint(mine, dense_row(other, f * rows, rows), dense_g[0:1, :])
        dense = level0_row(dense, mixed, f)
    dense_products(packed, dense, wind_dense)


def adjoint_rows(rows, levels, cells, wind_cells, take, each):
    groups = levels // GROUP
    cells[0] = jnp.zeros_like(cells[0])
    cells[rows + 1] = jnp.zeros_like(cells[0])
    wind_cells[0] = jnp.zeros_like(wind_cells[0])
    wind_cells[rows + 1] = jnp.zeros_like(wind_cells[0])
    take(0)

    def row(i, _):
        @pl.when(i < rows - 1)
        def _():
            take(i + 1)

        for m in range(2 * groups // PARTS):
            f, start = m * PARTS // groups, m * PARTS % groups
            each(i, m, f, start, [
                adjoint_point(cells, wind_cells, i, f, group, levels) for group in range(start, start + PARTS)
            ])
        return 0

    lax.fori_loop(0, rows, row, 0)


def first_adjoint_kernel(
    rows, levels, coupling, other, field, winds, out, ends, columns, low0, cells, wind_cells, sems
):
    wind_in = Rows(winds, wind_cells, sems, rows, True, 1)
    start_rows(rows, wind_in)
    columns[...] = jnp.zeros_like(columns)

    def take(i):
        wind_in.wait(i)
        cells[i + 1] = field[i]
        for f in range(2):
            at = pl.ds(f * levels, GROUP)
            cells[i + 1, at, :] = coupled(couple_adjoint, field[i, at, :], other, coupling, i, f, rows)

    def each(i, m, f, start, values):
        for part, value in enumerate(values):
            out[i, pl.ds((m * PARTS + part) * GROUP, GROUP), :] = value
        if start == 0:
            low0[pl.ds(f * rows + i, 1), :] = values[0][0:1]
        pack_block(columns, values, i, m)

    adjoint_rows(rows, levels, cells, wind_cells, take, each)
    ends[0] = out[0]
    ends[1] = out[rows - 1]


def second_adjoint_kernel(rows, levels, coupling, other, field, winds, scale, state, *rest):
    *halos, out, cells, wind_cells, state_cells, sides, sems = rest
    wind_in = Rows(winds, wind_cells, sems.at[0], rows, True, 1)
    state_in = Rows(state, state_cells, sems.at[1], rows, True, 0)
    start_rows(rows, wind_in, state_in)
    sides[...] = swap_pairs(merged(halos[1], halos[2], slice(None)))
    before, after = read_sides(halos)
    groups = levels // GROUP

    def take(i):
        wind_in.wait(i)
        for group in range(2 * groups):
            at = pl.ds(group * GROUP, GROUP)
            value = field[i, at, :] + edge_lanes(sides, i, group)
            if group % groups == 0:
                f = group // groups
                value = value + jnp.where(i == 0, before(at), 0.0) + jnp.where(i == rows - 1, after(at), 0.0)
                value = coupled(couple_adjoint, value, other, coupling, i, f, rows)
            cells[i + 1, at, :] = value

    def add_outer(i, side):
        for f in range(2):
            at = pl.ds(f * levels + GROUP, levels - GROUP)
            cells[i + 1, at, :] = cells[i + 1, at, :] + side(at)

    def take_all(i):
        take(i)

        @pl.when(i == 0)
        def _():
            add_outer(0, before)

        @pl.when(i == rows - 1)
        def _():
            add_outer(rows - 1, after)

    def each(i, m, f, start, values):
        if m == 0:
            state_in.wait(i)
        for part, value in enumerate(values):
            at = pl.ds((m * PARTS + part) * GROUP, GROUP)
            out[i, at, :] = value + scale[at, :] * state_cells[i, at, :]

    adjoint_rows(rows, levels, cells, wind_cells, take_all, each)


def final_kernel(rows, levels, field, *rest):
    *halos, out, cells, sides, sems = rest
    leaving = Out(cells, out, sems, rows, True)
    sides[...] = swap_pairs(merged(halos[1], halos[2], slice(None)))
    before, after = read_sides(halos)
    groups = levels // GROUP

    def add(i, outer):
        for group in range(2 * groups):
            at = pl.ds(group * GROUP, GROUP)
            value = field[i, at, :] + edge_lanes(sides, i, group)
            cells[i, at, :] = value if outer is None else value + outer(at)
        leaving.start(i)
        return 0

    lax.fori_loop(1, rows - 1, lambda i, _: add(i, None), 0)
    add(0, before)
    add(rows - 1, after)
    leaving.finish()


def split(value, terms):
    parts = []
    for _ in range(terms):
        part = value.astype(jnp.bfloat16)
        parts.append(part)
        value = value - part.astype(jnp.float32)
    return parts


def dot(a, b, contract):
    return lax.dot_general(a, b, ((contract[:1], contract[1:]), ((), ())), preferred_element_type=jnp.float32)


def route_kernel(tiles, cap, dest, col, prec, op, out):
    count = op.shape[0]
    width = op.shape[1]
    halves = width // LANES
    owner = lax.broadcasted_iota(jnp.int32, (tiles, count), 0)
    hits = owner == dest[...]
    ones = jnp.where(hits, 1.0, 0.0)
    earlier = lax.broadcasted_iota(jnp.int32, (count, count), 0) <= lax.broadcasted_iota(jnp.int32, (count, count), 1)
    running = dot(ones.astype(jnp.bfloat16), jnp.where(earlier, 1.0, 0.0).astype(jnp.bfloat16), (1, 0))
    slot = jnp.sum(running * ones, axis=0, keepdims=True) - 1.0
    slot = slot.astype(jnp.int32)
    place = dest[...] * cap + slot
    at_slot = lax.broadcasted_iota(jnp.int32, (LANES, count), 0) == slot
    at_slot = jnp.where(at_slot, 1.0, 0.0).astype(jnp.bfloat16)
    column = col[...].astype(jnp.float32)
    pieces = [ones * part.astype(jnp.float32) for part in split(column, 2) + split(prec[...], 3)]
    aux = dot(jnp.concatenate(pieces, axis=0).astype(jnp.bfloat16), at_slot, (1, 1))
    columns = aux[0:tiles] + aux[tiles : 2 * tiles]
    precs = (aux[2 * tiles : 3 * tiles] + aux[3 * tiles : 4 * tiles]) + aux[4 * tiles : 5 * tiles]
    sub = sub_iota()
    for owner_at in range(tiles):
        block = jnp.where(sub == 0, columns[owner_at : owner_at + 1], 0.0)
        block = jnp.where(sub == 1, precs[owner_at : owner_at + 1], block)
        out[owner_at, pl.ds(halves * cap, GROUP), :] = block
    rows_high, rows_low = split(op[...], 2)
    chunk = 256
    for first in range(0, tiles * cap, chunk):
        picks = lax.broadcasted_iota(jnp.int32, (chunk, count), 0) + first == place
        picks = jnp.where(picks, 1.0, 0.0).astype(jnp.bfloat16)
        moved = dot(picks, rows_high, (1, 0)) + dot(picks, rows_low, (1, 0))
        for part in range(chunk // cap):
            for half in range(halves):
                out[first // cap + part, pl.ds(half * cap, cap), :] = moved[
                    part * cap : (part + 1) * cap, half * LANES : (half + 1) * LANES
                ]


def innovate_kernel(rows, width, tiles, cap, records, cols, extra, bottom, spread, sel, ends, columns, floor, *scratch):
    col_cells, border_sel, precs, both, sems = scratch
    chunks = 8
    copies = []
    for part in range(chunks):
        at = pl.ds(part * (2 * width // chunks), 2 * width // chunks)
        copies.append(pltpu.make_async_copy(cols.at[at], col_cells.at[at], sems.at[part]))
        copies[-1].start()
    halves = width // LANES
    count = tiles * cap
    aux = halves * cap
    own = lax.broadcasted_iota(jnp.int32, (cap, LANES), 1) == lax.broadcasted_iota(jnp.int32, (cap, LANES), 0)
    ones = jnp.ones((LANES, LANES), jnp.bfloat16)
    step = 256
    lane = lax.broadcasted_iota(jnp.int32, (step, LANES), 1)
    border = (rows - 1 - lane // (2 * PARTS)) * LANES + jnp.where(lane % 2 == 1, 0, LANES - 1)
    border = jnp.where(lane % (2 * PARTS) < 2, border, -1).astype(jnp.float32)
    lane = lane.astype(jnp.float32)

    def select(block, _):
        sources = step // cap

        def spread_out(part):
            rows_of = [
                jnp.where(own, records[block * sources + s, pl.ds(aux + part, 1), :], 0.0) for s in range(sources)
            ]
            terms = split(jnp.concatenate(rows_of, axis=0), 2 + part)
            return sum(dot(term, ones, (1, 0)) for term in terms)

        at = pl.ds(pl.multiple_of(block * step, step), step)
        place = spread_out(0)
        column = place - lane
        precs[at, :] = spread_out(1)
        for i in range(rows):
            sel[at, i * LANES : (i + 1) * LANES] = jnp.where(column == float(i * LANES), 1.0, 0.0).astype(
                jnp.bfloat16
            )
        border_sel[at, :] = jnp.where(place == border, 1.0, 0.0).astype(jnp.bfloat16)
        return 0

    lax.fori_loop(0, count // step, select, 0)
    for copy in copies:
        copy.wait()
    pair = 2 * GROUP
    first = lax.broadcasted_iota(jnp.int32, (pair, LANES), 0) == 0
    for f in range(2):
        for i in range(rows):
            lanes = slice(i * LANES, (i + 1) * LANES)
            for term, value in enumerate(split(bottom[f * rows + i : f * rows + i + 1, :], 2)):
                at = pl.ds(term * width + f * (width // 2), pair)
                old = col_cells[at, lanes].astype(jnp.float32)
                new = jnp.where(first, value.astype(jnp.float32), old)
                col_cells[at, lanes] = new.astype(jnp.bfloat16)
    both[...] = dot(sel[...], col_cells[...], (1, 1))
    border_cells = jnp.concatenate([sel[:, 0:LANES], sel[:, (rows - 1) * LANES : rows * LANES], border_sel[...]], axis=1)
    both[...] += dot(border_cells, extra[...], (1, 1))

    def weigh(block, _):
        at = pl.ds(pl.multiple_of(block * LANES, LANES), LANES)
        sources = LANES // cap
        ops = [
            jnp.concatenate(
                [records[block * sources + s, half * cap : (half + 1) * cap, :] for s in range(sources)], axis=0
            )
            for half in range(halves)
        ]
        total = sum(
            (both[at, half * LANES : (half + 1) * LANES] + both[at, width + half * LANES : width + (half + 1) * LANES])
            * ops[half]
            for half in range(halves)
        )
        innovation = jnp.sum(total, axis=1, keepdims=True) * precs[at, :]
        for half in range(halves):
            high, low = split((ops[half] * innovation).T, 2)
            spread[half * LANES : (half + 1) * LANES, at] = high
            spread[width + half * LANES : width + (half + 1) * LANES, at] = low
        return 0

    lax.fori_loop(0, count // LANES, weigh, 0, unroll=4)

    terms = dot(spread[...], border_cells, (1, 0))
    border_sums = terms[:width] + terms[width:]
    ends[0] = border_sums[:, 0:LANES]
    ends[1] = border_sums[:, LANES : 2 * LANES]
    thin = border_sums[:, 2 * LANES :]
    for m in range(width // (GROUP * PARTS)):
        total = thin[m * PARTS * GROUP : (m * PARTS + 1) * GROUP]
        for part in range(1, PARTS):
            at = (m * PARTS + part) * GROUP
            total = total + pltpu.roll(thin[at : at + GROUP], 2 * part, 1)
        columns[m * GROUP : (m + 1) * GROUP, :] = total
    half = columns.shape[0] // 2
    floor[...] = jnp.zeros_like(floor)
    for f in range(2):
        for k in range(2):
            floor[2 * k + f : 2 * k + f + 1, :] = ends[k, f * (width // 2) : f * (width // 2) + 1, :]
        floor[4 + f : 5 + f, :] = columns[f * half : f * half + 1, :]


def scatter_kernel(rows, width, spread, sel, adjoint, low0):
    sums = dot(spread[...], sel[...], (1, 0))
    for i in range(rows):
        lanes = slice(i * LANES, (i + 1) * LANES)
        adjoint[i] = sums[:width, lanes] + sums[width:, lanes]
        for f in range(2):
            low0[f * rows + i : f * rows + i + 1, :] = adjoint[i, f * (width // 2) : f * (width // 2) + 1, :]


def local(state_incr, winds, coupling, background, obs_dest, obs_col, obs_op, obs_prec):
    _, fields, levels, rows, lanes = state_incr.shape
    width = fields * levels
    groups = width // GROUP
    tiles = lax.axis_size("gx") * lax.axis_size("gy")
    count = obs_col.shape[0]
    cap = 2 * count // tiles
    halves = obs_op.shape[1] // LANES

    scale = jnp.broadcast_to(background.reshape(width, 1), (width, LANES))

    vmem = pl.BlockSpec(memory_space=pltpu.VMEM)
    anywhere = pl.BlockSpec(memory_space=pl.ANY)
    own = pltpu.VMEM((rows, width, LANES), jnp.float32)
    framed = pltpu.VMEM((rows + 2, width, LANES), jnp.float32)
    packed_shape = f32(groups // PARTS * GROUP, LANES)
    sides = pltpu.VMEM(packed_shape.shape, jnp.float32)
    strip_shapes = [f32(width, LANES), f32(width, LANES), packed_shape]
    field_shape = f32(rows, width, LANES)
    low_shape = f32(fields * rows, LANES)
    cols_shape = ((2 * width, rows * LANES), jnp.bfloat16)

    def sems(*shape):
        return pltpu.SemaphoreType.DMA(shape)

    def run(body, out_shape, scratch, args, far=(), out_far=(), **kw):
        args = [pltpu.with_memory_space_constraint(x, pltpu.HBM) if k in far else x for k, x in enumerate(args)]
        specs = [anywhere if k in far else vmem for k in range(len(args))]
        outs = [anywhere if k in out_far else vmem for k in range(len(out_shape))]
        out_shape = [pltpu.HBM(x.shape, x.dtype) if k in out_far else x for k, x in enumerate(out_shape)]
        return call(body, out_shape, scratch, in_specs=specs, out_specs=outs, **kw)(*args)

    def on_rows(body):
        return functools.partial(body, rows, levels)

    def swap_floor(floor):
        return lax.ppermute(floor, "comp", [(0, 1), (1, 0)])

    state = state_incr.reshape(width, rows, lanes)
    wind = winds.reshape(width, rows, lanes)
    floor_winds = winds[0, :, 0]
    slots = tiles * cap
    thin_shape = f32(GROUP, LANES)

    s_even, s_odd, packed, low0, low1 = run(
        on_rows(edges_kernel),
        strip_shapes + [low_shape] * 2,
        [pltpu.VMEM((width * rows, LANES), jnp.float32), sems(groups // PARTS)],
        (state_incr.reshape(width * rows, lanes),),
        far=(0,),
    )
    halos = exchange((s_even, s_odd), packed)

    send = call(functools.partial(route_kernel, tiles, cap), f32(tiles, halves * cap + GROUP, LANES))(
        obs_dest.reshape(1, count), obs_col.reshape(1, count), obs_prec.reshape(1, count), obs_op
    )
    send, halos[0], halos[2] = lax.optimization_barrier((send, halos[0], halos[2]))
    records = lax.all_to_all(send, ("gx", "gy"), split_axis=0, concat_axis=0, tiled=True)

    (floor,) = run(on_rows(forward_floor_kernel), [low_shape], [], (low0, low1, floor_winds, *halos))
    field, s_even, s_odd, packed, low0, low1, wind_ends, wind_dense, dense_g = run(
        on_rows(forward_kernel),
        [field_shape]
        + strip_shapes
        + [low_shape] * 2
        + [f32(2, levels, LANES), f32(groups // PARTS * GROUP // 2, LANES), thin_shape],
        [framed, own, own, sides, sems(3, rows)],
        (coupling, swap_floor(floor), state, wind, *halos),
        far=(2, 3),
        out_far=(0,),
    )
    halos = exchange((s_even, s_odd), packed)
    (cols,) = run(
        on_rows(forward_again_kernel),
        [jax.ShapeDtypeStruct(*cols_shape)],
        [framed, own, sems(2, rows), pltpu.VMEM(*cols_shape), sems(rows)],
        (field, wind),
        far=(0, 1),
        out_far=(0,),
        traffic=20 * MIB,
    )
    cols, halos = lax.optimization_barrier((cols, halos))
    (floor,) = run(on_rows(forward_floor_kernel), [low_shape], [], (low0, low1, floor_winds, *halos))
    extra, bottom = run(
        on_rows(outside_kernel),
        [jax.ShapeDtypeStruct((2 * width, 3 * LANES), jnp.bfloat16), low_shape],
        [sides],
        (coupling, floor, swap_floor(floor), wind_ends, wind_dense, *halos),
    )

    spread_shape = ((2 * width, slots), jnp.bfloat16)
    sel_shape = ((slots, rows * LANES), jnp.bfloat16)
    spread, sel, ends, columns, border_floor = run(
        functools.partial(innovate_kernel, rows, width, tiles, cap),
        [jax.ShapeDtypeStruct(*spread_shape), jax.ShapeDtypeStruct(*sel_shape), f32(2, width, LANES), packed_shape, thin_shape],
        [
            pltpu.VMEM(*cols_shape),
            pltpu.VMEM((slots, LANES), jnp.bfloat16),
            pltpu.VMEM((slots, LANES), jnp.float32),
            pltpu.VMEM((slots, 2 * width), jnp.float32),
            sems(8),
        ],
        (records, cols, extra, bottom),
        far=(1,),
        limit=OBSERVE_VMEM,
    )
    strips = run(
        on_rows(border_kernel),
        strip_shapes,
        [],
        (coupling, swap_floor(border_floor), ends, columns, wind_ends, wind_dense, dense_g),
    )
    halos = exchange(strips[:2], strips[2])
    adjoint, low0 = run(
        functools.partial(scatter_kernel, rows, width), [field_shape, low_shape], [], (spread, sel), limit=OBSERVE_VMEM
    )
    adjoint, ends, columns, low0 = run(
        on_rows(first_adjoint_kernel),
        [field_shape, f32(2, width, LANES), packed_shape, low_shape],
        [framed, framed, sems(rows)],
        (coupling, swap_floor(low0), adjoint, wind),
        far=(3,),
    )
    (floor,) = run(on_rows(floor_kernel), [low_shape], [], (low0, *halos))
    other = swap_floor(floor)
    strips = run(
        on_rows(border_again_kernel),
        strip_shapes,
        [sides],
        (coupling, floor, other, ends, columns, wind_ends, wind_dense, dense_g, *halos),
    )
    last_halos = exchange(strips[:2], strips[2])
    (adjoint,) = run(
        on_rows(second_adjoint_kernel),
        [field_shape],
        [framed, framed, own, sides, sems(2, rows)],
        (coupling, other, adjoint, wind, scale, state, *halos),
        far=(3, 5),
    )
    (result,) = run(
        on_rows(final_kernel),
        [f32(width, rows, LANES)],
        [own, sides, sems(rows)],
        (adjoint, *last_halos),
        out_far=(0,),
    )
    return result.reshape(state_incr.shape)


def solution(mesh):
    placed = (
        P("comp", None, None, "gx", "gy"),
        P("comp", None, None, "gx", "gy"),
        P("gx", "gy"),
        P("comp", None, None),
        P(("comp", "gx", "gy"), None),
        P(("comp", "gx", "gy")),
        P(("comp", "gx", "gy"), None),
        P(("comp", "gx", "gy")),
    )
    return jax.shard_map(
        local,
        mesh=mesh,
        in_specs=placed,
        out_specs=P("comp", None, None, "gx", "gy"),
        check_vma=False,
    )
```

```python
import functools

import jax
import jax.numpy as jnp
from jax import lax
from jax.experimental import pallas as pl
from jax.experimental.pallas import tpu as pltpu
from jax.sharding import PartitionSpec as P

HORIZ_MIX = 0.1
VERT_MIX = 0.15
LANES = 128
GROUP = 8
MIB = 1024 * 1024
SWEEP_VMEM = 16 * MIB
OBSERVE_VMEM = 22 * MIB


def call(body, out_shape, scratch=(), limit=SWEEP_VMEM, traffic=0, **kw):
    cost = pl.CostEstimate(flops=0, bytes_accessed=traffic, transcendentals=0) if traffic else None
    return pl.pallas_call(
        body,
        out_shape=out_shape,
        scratch_shapes=list(scratch),
        cost_estimate=cost,
        compiler_params=pltpu.CompilerParams(vmem_limit_bytes=limit),
        **kw,
    )


def f32(*shape):
    return jax.ShapeDtypeStruct(shape, jnp.float32)


def lane_iota(rows=GROUP):
    return lax.broadcasted_iota(jnp.int32, (rows, LANES), 1)


def sub_iota(rows=GROUP):
    return lax.broadcasted_iota(jnp.int32, (rows, LANES), 0)


def pair_swap(block, axis, start):
    count = lax.axis_size(axis)
    route = []
    for low in range(start, count - 1, 2):
        route += [(low, low + 1), (low + 1, low)]
    return lax.ppermute(block, axis, route)


def exchange(strips, packed):
    y_even = pair_swap(packed, "gy", 0)
    y_odd = pair_swap(packed, "gy", 1)
    halos = [pair_swap(strips[0], "gx", 0), y_even, y_odd]
    if lax.axis_size("gx") > 2:
        halos.append(pair_swap(strips[1], "gx", 1))
    return halos


def is_odd(axis):
    return lax.rem(lax.axis_index(axis), 2) == 1


def read_sides(refs):
    even = refs[0]
    odd = refs[3] if len(refs) > 3 else None
    at_odd = is_odd("gx")

    def side(at, turned):
        other = jnp.zeros_like(even[at]) if odd is None else odd[at]
        return jnp.where(turned, other, even[at])

    return lambda at: side(at, jnp.logical_not(at_odd)), lambda at: side(at, at_odd)


PARTS = 4


def merged(y_even, y_odd, at):
    a, b = y_even[at, :], y_odd[at, :]
    lane = lax.broadcasted_iota(jnp.int32, a.shape, 1)
    return jnp.where((lane % 2 == 1) == jnp.logical_not(is_odd("gy")), a, b)


def merge_columns(y_even, y_odd, sides):
    sides[...] = merged(y_even, y_odd, slice(None))


def slot_of(i, part, rows):
    return PARTS * (rows - 1 - i) + part


def side_columns(sides, i, group):
    m, part = group // PARTS, group % PARTS
    rows = LANES // (2 * PARTS)
    return pltpu.roll(sides[m * GROUP : (m + 1) * GROUP, :], LANES - 1 - 2 * slot_of(i, part, rows), 1)


def pack_into(total, value, slot):
    return jnp.where(lane_iota() // 2 == slot, pltpu.roll(value, 2 * slot + 1, 1), total)


def pack_block(packed, values, i, m):
    at = pl.ds(m * GROUP, GROUP)
    total = packed[at, :]
    for part, value in enumerate(values):
        total = pack_into(total, value, slot_of(i, part, LANES // (2 * PARTS)))
    packed[at, :] = total


CENTRE = 1.0 - 4.0 * HORIZ_MIX - 2.0 * VERT_MIX


def levels_around(cells, i, base, group, groups):
    here = cells[i + 1, pl.ds(base + group * GROUP, GROUP), :]
    if group == groups - 1:
        upper = jnp.where(sub_iota() == GROUP - 1, here, pltpu.roll(here, GROUP - 1, 0))
    else:
        upper = cells[i + 1, pl.ds(base + group * GROUP + 1, GROUP), :]
    if group == 0:
        lower = jnp.where(sub_iota() == 0, here, pltpu.roll(here, 1, 0))
    else:
        lower = cells[i + 1, pl.ds(base + group * GROUP - 1, GROUP), :]
    return here, upper, lower


def shifted(first, last, edge, rows=GROUP):
    lane = lane_iota(rows)
    right = pltpu.roll(jnp.where(lane == 0, edge, first), LANES - 1, 1)
    left = pltpu.roll(jnp.where(lane == LANES - 1, edge, last), 1, 1)
    return right, left


def forward_sum(here, vertical, after, before, right, left, u, w):
    return (
        CENTRE * here
        + VERT_MIX * vertical
        + HORIZ_MIX * ((after + before) + (right + left))
        - 0.5 * (u * (after - before) + w * (right - left))
    )


def forward_point(cells, winds, sides, i, f, group, levels):
    groups = levels // GROUP
    here, upper, lower = levels_around(cells, i, f * levels, group, groups)
    at = pl.ds(f * levels + group * GROUP, GROUP)
    right, left = shifted(here, here, 0.0 if sides is None else side_columns(sides, i, f * groups + group))
    u = winds[i, pl.ds(group * GROUP, GROUP), :]
    w = winds[i, pl.ds(levels + group * GROUP, GROUP), :]
    return forward_sum(here, upper + lower, cells[i + 2, at, :], cells[i, at, :], right, left, u, w)


def products(x, wind):
    slope = 0.5 * (wind * x)
    return HORIZ_MIX * x - slope, HORIZ_MIX * x + slope


def adjoint_point(cells, winds, i, f, group, levels):
    here, upper, lower = levels_around(cells, i, f * levels, group, levels // GROUP)
    at = pl.ds(f * levels + group * GROUP, GROUP)
    wind_at = pl.ds(group * GROUP, GROUP)
    after, before = cells[i + 2, at, :], cells[i, at, :]
    u_after, u_before = winds[i + 2, wind_at, :], winds[i, wind_at, :]
    down, up = products(here, winds[i + 1, pl.ds(levels + group * GROUP, GROUP), :])
    right, left = shifted(up, down, 0.0)
    return (
        CENTRE * here
        + VERT_MIX * (upper + lower)
        + HORIZ_MIX * (after + before)
        + 0.5 * (u_after * after - u_before * before)
        + (right + left)
    )


def shares_of(coupling):
    own = jnp.where(lax.axis_index("comp") == 0, 1.0, 0.5)
    return own * coupling, (1.5 - own) * coupling


def couple_forward(value, other, coupling):
    own, _ = shares_of(coupling)
    return value - own * (value - other)


def couple_adjoint(value, other, coupling):
    own, peer = shares_of(coupling)
    return value - own * value + peer * other


def coupled(rule, value, other, coupling, i, f, rows):
    mixed = rule(value, other[pl.ds(f * rows + i, 1), :], coupling[pl.ds(i, 1), :])
    return jnp.where(sub_iota() == 0, mixed, value)


def put_strip(strip_even, strip_odd, at, first, last):
    at_odd = is_odd("gx")
    strip_even[at, :] = jnp.where(at_odd, first, last)
    strip_odd[at, :] = jnp.where(at_odd, last, first)


def put_low(low, value, i, f, rows):
    for level in range(2):
        low[level][pl.ds(f * rows + i, 1), :] = value[level : level + 1]


class Rows:
    def __init__(self, source, target, sems, rows, as_it_comes, offset):
        self.source, self.target, self.sems = source, target, sems
        self.rows, self.as_it_comes, self.offset = rows, as_it_comes, offset

    def copy(self, i):
        row = self.source.at[:, i] if self.as_it_comes else self.source.at[i]
        return pltpu.make_async_copy(row, self.target.at[i + self.offset], self.sems.at[i])

    def wait(self, i):
        self.copy(i).wait()


def start_rows(rows, *groups):
    for i in range(rows):
        for group in groups:
            group.copy(i).start()


def edges_kernel(rows, levels, state, s_even, s_odd, packed, low0, low1, cells, sems):
    part_levels = PARTS * GROUP
    blocks = 2 * levels // part_levels

    def copy(m):
        return pltpu.make_async_copy(
            state.at[pl.ds(m * part_levels * rows, part_levels * rows)],
            cells.at[pl.ds(m * part_levels * rows, part_levels * rows)],
            sems.at[m],
        )

    for m in range(blocks):
        copy(m).start()

    def block(m, _):
        copy(m).wait()
        total = jnp.zeros((GROUP, LANES), jnp.float32)
        for part in range(PARTS):
            for i in range(rows):
                start = (m * PARTS + part) * GROUP * rows + i
                total = pack_into(total, cells[pl.ds(start, GROUP, stride=rows), :], slot_of(i, part, rows))
        packed[pl.ds(pl.multiple_of(m * GROUP, GROUP), GROUP), :] = total
        start = m * part_levels * rows
        first = cells[pl.ds(start, part_levels, stride=rows), :]
        last = cells[pl.ds(start + rows - 1, part_levels, stride=rows), :]
        put_strip(s_even, s_odd, pl.ds(pl.multiple_of(m * part_levels, part_levels), part_levels), first, last)
        return 0

    lax.fori_loop(0, blocks, block, 0)
    for f in range(2):
        for level, low in enumerate((low0, low1)):
            low[f * rows : (f + 1) * rows, :] = cells[pl.ds((f * levels + level) * rows, rows), :]


def floor_edge(halos, f, rows, levels):
    m = f * (levels // GROUP) // PARTS
    sides = jnp.broadcast_to(merged(halos[1], halos[2], pl.ds(m * GROUP, 1)), (rows, LANES))
    return pltpu.roll(sides, 2 * PARTS - 1, 1, stride=2 * PARTS, stride_axis=0)


def row_after(value, last, rows):
    return jnp.where(sub_iota(rows) == rows - 1, last, pltpu.roll(value, rows - 1, 0))


def row_before(value, first, rows):
    return jnp.where(sub_iota(rows) == 0, first, pltpu.roll(value, 1, 0))


def forward_floor_kernel(rows, levels, low0, low1, winds, *rest):
    *halos, floor = rest
    side_before, side_after = read_sides(halos)
    for f in range(2):
        here = pl.ds(f * rows, rows)
        at = pl.ds(f * levels, 1)
        low, up = low0[here, :], low1[here, :]
        after, before = row_after(low, side_after(at), rows), row_before(low, side_before(at), rows)
        right, left = shifted(low, low, floor_edge(halos, f, rows, levels), rows)
        floor[here, :] = forward_sum(low, up + low, after, before, right, left, winds[0], winds[1])


class Out:
    def __init__(self, source, target, sems, rows, as_it_goes):
        self.source, self.target, self.sems, self.rows, self.as_it_goes = source, target, sems, rows, as_it_goes

    def copy(self, i):
        row = self.target.at[:, i] if self.as_it_goes else self.target.at[i]
        return pltpu.make_async_copy(self.source.at[i], row, self.sems.at[i])

    def start(self, i):
        self.copy(i).start()

    def finish(self):
        for i in range(self.rows):
            self.copy(i).wait()


def dense_row(field, first, rows):
    total = jnp.zeros((1, LANES), jnp.float32)
    lane = lax.broadcasted_iota(jnp.int32, (1, LANES), 1)
    for i in range(rows):
        slot = slot_of(i, 0, rows)
        total = jnp.where(lane // 2 == slot, pltpu.roll(field[first + i : first + i + 1, :], 2 * slot + 1, 1), total)
    return total


def load_kernel(rows, state, winds, state_rows, wind_rows, sems):
    state_in = Rows(state, state_rows, sems.at[0], rows, True, 0)
    wind_in = Rows(winds, wind_rows, sems.at[1], rows, True, 0)
    start_rows(rows, state_in, wind_in)
    for i in range(rows):
        state_in.wait(i)
        wind_in.wait(i)


def forward_kernel(rows, levels, coupling, other, field, winds, *rest):
    *halos, out, s_even, s_odd, packed, low0, low1, wind_ends, wind_dense, dense_g, cells, sides = rest
    packed[...] = jnp.zeros_like(packed)
    wind_dense[...] = jnp.zeros_like(wind_dense)
    merge_columns(halos[1], halos[2], sides)
    before, after = read_sides(halos)
    cells[0] = before(slice(None))
    cells[1] = field[0]
    cells[rows + 1] = after(slice(None))
    out[0] = jnp.zeros_like(out[0])
    out[rows + 1] = jnp.zeros_like(out[0])
    groups = levels // GROUP

    def row(i, _):
        @pl.when(i < rows - 1)
        def _():
            cells[i + 2] = field[i + 1]

        for m in range(2 * groups // PARTS):
            f, start = m * PARTS // groups, m * PARTS % groups
            values = []
            for group in range(start, start + PARTS):
                value = forward_point(cells, winds, sides, i, f, group, levels)
                if group == 0:
                    value = coupled(couple_forward, value, other, coupling, i, f, rows)
                    put_low((low0, low1), value, i, f, rows)
                values.append(value)
            base = m * PARTS * GROUP
            for part, value in enumerate(values):
                out[i + 1, pl.ds(base + part * GROUP, GROUP), :] = value
            pack_block(packed, values, i, m)
            if f == 0:
                w = [winds[i, pl.ds(levels + base + part * GROUP, GROUP), :] for part in range(PARTS)]
                pack_block(wind_dense, w, i, m)
        return 0

    lax.fori_loop(0, rows, row, 0)
    put_strip(s_even, s_odd, slice(None), out[1], out[rows])
    wind_ends[0] = winds[0, pl.ds(0, levels), :]
    wind_ends[1] = winds[rows - 1, pl.ds(0, levels), :]
    dense_g[...] = jnp.broadcast_to(dense_row(coupling, 0, rows), dense_g.shape)


def forward_again_kernel(rows, levels, cells, winds, cols, col_cells, col_sems):
    groups = levels // GROUP
    width = 2 * levels

    def col_copy(i):
        lanes = pl.ds(pl.multiple_of(i * LANES, LANES), LANES)
        return pltpu.make_async_copy(col_cells.at[:, lanes], cols.at[:, lanes], col_sems.at[i])

    def row(i, _):
        lanes = pl.ds(pl.multiple_of(i * LANES, LANES), LANES)
        for m in range(2 * groups // PARTS):
            f, start = m * PARTS // groups, m * PARTS % groups
            values = [forward_point(cells, winds, None, i, f, group, levels) for group in range(start, start + PARTS)]
            high, low = split(jnp.concatenate(values, axis=0), 2)
            col_cells[pl.ds(m * PARTS * GROUP, PARTS * GROUP), lanes] = high
            col_cells[pl.ds(width + m * PARTS * GROUP, PARTS * GROUP), lanes] = low
        col_copy(i).start()
        return 0

    lax.fori_loop(0, rows, row, 0)
    for i in range(rows):
        col_copy(i).wait()


def outside_kernel(rows, levels, coupling, floor, other, wind_ends, wind_dense, *rest):
    *halos, extra, bottom, dense = rest
    width = 2 * levels
    for f in range(2):
        here = pl.ds(f * rows, rows)
        bottom[here, :] = couple_forward(floor[here, :], other[here, :], coupling[...])
    dense_products(dense, swap_pairs(merged(halos[1], halos[2], slice(None))), wind_dense)
    before, after = read_sides(halos)
    sub = lax.broadcasted_iota(jnp.int32, (levels, LANES), 0)

    def put(value, f, lanes):
        high, low = split(jnp.where(sub == 0, 0.0, value), 2)
        extra[f * levels : (f + 1) * levels, lanes] = high
        extra[width + f * levels : width + (f + 1) * levels, lanes] = low

    lane = lane_iota()
    for f in range(2):
        at = pl.ds(f * levels, levels)
        put(products(before(at), wind_ends[0])[1], f, slice(0, LANES))
        put(products(after(at), wind_ends[1])[0], f, slice(LANES, 2 * LANES))
        thin = []
        for group in range(f * levels // GROUP, (f + 1) * levels // GROUP):
            m, part = group // PARTS, group % PARTS
            moved = pltpu.roll(dense[m * GROUP : (m + 1) * GROUP, :], (LANES - 2 * part) % LANES, 1)
            thin.append(jnp.where(lane % (2 * PARTS) < 2, moved, 0.0))
        put(jnp.concatenate(thin, axis=0), f, slice(2 * LANES, 3 * LANES))


def dense_products(packed, value, wind_dense):
    half = wind_dense.shape[0]
    for f in range(2):
        at = slice(f * half, (f + 1) * half)
        down, up = products(value[at], wind_dense[...])
        lane = lax.broadcasted_iota(jnp.int32, down.shape, 1)
        packed[at, :] = jnp.where(lane % 2 == 1, up, down)


def level0_row(value, new, f):
    half = value.shape[0] // 2
    sub = lax.broadcasted_iota(jnp.int32, value.shape, 0)
    lane = lax.broadcasted_iota(jnp.int32, value.shape, 1)
    return jnp.where((sub == f * half) & (lane % (2 * PARTS) < 2), new, value)


def end_rows(ends, s_even, s_odd, wind_ends, levels):
    for f in range(2):
        at = slice(f * levels, (f + 1) * levels)
        put_strip(
            s_even, s_odd, at, products(ends[0][at], wind_ends[0])[1], products(ends[1][at], wind_ends[1])[0]
        )


def with_first(value, new):
    return jnp.where(lax.broadcasted_iota(jnp.int32, value.shape, 0) == 0, new, value)


def border_kernel(rows, levels, coupling, other, ends, columns, wind_ends, wind_dense, dense_g, s_even, s_odd, packed):
    half = columns.shape[0] // 2
    dense = columns[...]
    full = [ends[0], ends[1]]
    for f in range(2):
        mixed = couple_adjoint(columns[f * half : f * half + 1, :], other[4 + f : 5 + f, :], dense_g[0:1, :])
        dense = level0_row(dense, mixed, f)
    for k, i in enumerate((0, rows - 1)):
        parts = []
        for f in range(2):
            value = ends[k, f * levels : (f + 1) * levels, :]
            at = 2 * k + f
            parts.append(with_first(value, couple_adjoint(value[0:1], other[at : at + 1, :], coupling[i : i + 1, :])))
        full[k] = jnp.concatenate(parts, axis=0)
    dense_products(packed, dense, wind_dense)
    end_rows(full, s_even, s_odd, wind_ends, levels)


def outside_floor(halos, low, f, rows, levels):
    before, after = read_sides(halos)
    at = pl.ds(f * levels, 1)
    sub, lane = sub_iota(rows), lane_iota(rows)
    low = low + jnp.where(sub == 0, before(at), 0.0) + jnp.where(sub == rows - 1, after(at), 0.0)
    edge = floor_edge(halos, f, rows, levels)
    edge = jnp.where(lane == 0, pltpu.roll(edge, 1, 1), pltpu.roll(edge, LANES - 1, 1))
    return low + jnp.where((lane == 0) | (lane == LANES - 1), edge, 0.0)


def floor_kernel(rows, levels, coupling, other, low0, winds, *rest):
    *halos, floor, missing = rest
    for f in range(2):
        here = pl.ds(f * rows, rows)
        _, peer = shares_of(coupling[...])
        share = peer * other[here, :]
        x_down, x_up = products(share, winds[0])
        y_down, y_up = products(share, winds[1])
        right, left = shifted(y_up, y_down, 0.0, rows)
        spread = (row_after(x_up, 0.0, rows) + row_before(x_down, 0.0, rows)) + (right + left)
        spread = spread + (CENTRE + VERT_MIX) * share
        floor[here, :] = outside_floor(halos, low0[here, :] + spread, f, rows, levels)
        missing[here, :] = VERT_MIX * share


def swap_pairs(value):
    lane = lax.broadcasted_iota(jnp.int32, value.shape, 1)
    return jnp.where(lane % 2 == 1, pltpu.roll(value, 1, 1), pltpu.roll(value, LANES - 1, 1))


def edge_lanes(sides, i, group):
    m, part = group // PARTS, group % PARTS
    rows = LANES // (2 * PARTS)
    moved = pltpu.roll(sides[m * GROUP : (m + 1) * GROUP, :], LANES - 1 - 2 * slot_of(i, part, rows), 1)
    lane = lane_iota()
    return jnp.where((lane == 0) | (lane == LANES - 1), moved, 0.0)


def with_level(value, level, new):
    return jnp.where(lax.broadcasted_iota(jnp.int32, value.shape, 0) == level, new, value)


def border_again_kernel(
    rows, levels, coupling, floor, other, missing, ends, columns, wind_ends, wind_dense, dense_g, *rest
):
    *halos, s_even, s_odd, packed, sides = rest
    before, after = read_sides(halos)
    sides[...] = swap_pairs(merged(halos[1], halos[2], slice(None)))
    half = columns.shape[0] // 2
    groups = levels // GROUP
    outer = [before(slice(None)), after(slice(None))]
    full = []
    for k, i in enumerate((0, rows - 1)):
        edges = jnp.concatenate([edge_lanes(sides, i, group) for group in range(2 * groups)], axis=0)
        value = ends[k] + outer[k] + edges
        parts = []
        for f in range(2):
            part = value[f * levels : (f + 1) * levels]
            at = slice(f * rows + i, f * rows + i + 1)
            part = part + with_level(jnp.zeros_like(part), 1, missing[at, :])
            parts.append(with_first(part, couple_adjoint(floor[at, :], other[at, :], coupling[i : i + 1, :])))
        full.append(jnp.concatenate(parts, axis=0))
    end_rows(full, s_even, s_odd, wind_ends, levels)
    dense = columns[...] + sides[...]
    corners = []
    for m in range(2 * groups // PARTS):
        total = jnp.zeros((GROUP, LANES), jnp.float32)
        for part in range(PARTS):
            at = slice((m * PARTS + part) * GROUP, (m * PARTS + part + 1) * GROUP)
            for k, i in enumerate((0, rows - 1)):
                total = pack_into(total, outer[k][at], slot_of(i, part, rows))
        corners.append(total)
    dense = dense + jnp.concatenate(corners, axis=0)
    for f in range(2):
        sub = lax.broadcasted_iota(jnp.int32, dense.shape, 0)
        dense = dense + jnp.where(sub == f * half + 1, dense_row(missing, f * rows, rows), 0.0)
        mine = dense_row(floor, f * rows, rows)
        mixed = couple_adjoint(mine, dense_row(other, f * rows, rows), dense_g[0:1, :])
        dense = level0_row(dense, mixed, f)
    dense_products(packed, dense, wind_dense)


def adjoint_rows(rows, levels, cells, winds, take, each):
    groups = levels // GROUP
    cells[0] = jnp.zeros_like(cells[0])
    cells[rows + 1] = jnp.zeros_like(cells[0])
    take(0)

    def row(i, _):
        @pl.when(i < rows - 1)
        def _():
            take(i + 1)

        for m in range(2 * groups // PARTS):
            f, start = m * PARTS // groups, m * PARTS % groups
            each(i, m, f, start, [
                adjoint_point(cells, winds, i, f, group, levels) for group in range(start, start + PARTS)
            ])
        return 0

    lax.fori_loop(0, rows, row, 0)


def first_adjoint_kernel(rows, levels, coupling, field, winds, state, out, ends, columns, low0, state_rows, cells, sems):
    state_in = Rows(state, state_rows, sems, rows, True, 0)
    start_rows(rows, state_in)
    columns[...] = jnp.zeros_like(columns)

    def take(i):
        cells[i + 1] = field[i]
        for f in range(2):
            at = pl.ds(f * levels, GROUP)
            own, _ = shares_of(coupling[pl.ds(i, 1), :])
            value = field[i, at, :]
            cells[i + 1, at, :] = jnp.where(sub_iota() == 0, value - own * value, value)

    def each(i, m, f, start, values):
        for part, value in enumerate(values):
            out[i, pl.ds((m * PARTS + part) * GROUP, GROUP), :] = value
        if start == 0:
            low0[pl.ds(f * rows + i, 1), :] = values[0][0:1]
        pack_block(columns, values, i, m)

    adjoint_rows(rows, levels, cells, winds, take, each)
    ends[0] = out[0]
    ends[1] = out[rows - 1]
    for i in range(rows):
        state_in.wait(i)


def second_adjoint_kernel(rows, levels, coupling, floor, other, missing, field, winds, scale, state, *rest):
    *halos, out, cells, sides = rest
    sides[...] = swap_pairs(merged(halos[1], halos[2], slice(None)))
    before, after = read_sides(halos)
    groups = levels // GROUP

    def take(i):
        for group in range(2 * groups):
            at = pl.ds(group * GROUP, GROUP)
            value = field[i, at, :] + edge_lanes(sides, i, group)
            if group % groups == 0:
                value = value + jnp.where(i == 0, before(at), 0.0) + jnp.where(i == rows - 1, after(at), 0.0)
                here = pl.ds(group // groups * rows + i, 1)
                value = value + jnp.where(sub_iota() == 1, missing[here, :], 0.0)
                bottom = couple_adjoint(floor[here, :], other[here, :], coupling[pl.ds(i, 1), :])
                value = jnp.where(sub_iota() == 0, bottom, value)
            cells[i + 1, at, :] = value

    def add_outer(i, side):
        for f in range(2):
            at = pl.ds(f * levels + GROUP, levels - GROUP)
            cells[i + 1, at, :] = cells[i + 1, at, :] + side(at)

    def take_all(i):
        take(i)

        @pl.when(i == 0)
        def _():
            add_outer(0, before)

        @pl.when(i == rows - 1)
        def _():
            add_outer(rows - 1, after)

    def each(i, m, f, start, values):
        for part, value in enumerate(values):
            at = pl.ds((m * PARTS + part) * GROUP, GROUP)
            out[i, at, :] = value + scale[at, :] * state[i, at, :]

    adjoint_rows(rows, levels, cells, winds, take_all, each)


def final_kernel(rows, levels, field, *rest):
    *halos, out, cells, sides, sems = rest
    leaving = Out(cells, out, sems, rows, True)
    sides[...] = swap_pairs(merged(halos[1], halos[2], slice(None)))
    before, after = read_sides(halos)
    groups = levels // GROUP

    def add(i, outer):
        for group in range(2 * groups):
            at = pl.ds(group * GROUP, GROUP)
            value = field[i, at, :] + edge_lanes(sides, i, group)
            cells[i, at, :] = value if outer is None else value + outer(at)
        leaving.start(i)
        return 0

    lax.fori_loop(1, rows - 1, lambda i, _: add(i, None), 0)
    add(0, before)
    add(rows - 1, after)
    leaving.finish()


def split(value, terms):
    parts = []
    for _ in range(terms):
        part = value.astype(jnp.bfloat16)
        parts.append(part)
        value = value - part.astype(jnp.float32)
    return parts


def dot(a, b, contract):
    return lax.dot_general(a, b, ((contract[:1], contract[1:]), ((), ())), preferred_element_type=jnp.float32)


def route_kernel(tiles, cap, dest, col, prec, op, out):
    count = op.shape[0]
    width = op.shape[1]
    halves = width // LANES
    owner = lax.broadcasted_iota(jnp.int32, (tiles, count), 0)
    hits = owner == dest[...]
    ones = jnp.where(hits, 1.0, 0.0)
    earlier = lax.broadcasted_iota(jnp.int32, (count, count), 0) <= lax.broadcasted_iota(jnp.int32, (count, count), 1)
    running = dot(ones.astype(jnp.bfloat16), jnp.where(earlier, 1.0, 0.0).astype(jnp.bfloat16), (1, 0))
    slot = jnp.sum(running * ones, axis=0, keepdims=True) - 1.0
    slot = slot.astype(jnp.int32)
    place = dest[...] * cap + slot
    at_slot = lax.broadcasted_iota(jnp.int32, (LANES, count), 0) == slot
    at_slot = jnp.where(at_slot, 1.0, 0.0).astype(jnp.bfloat16)
    column = col[...].astype(jnp.float32)
    pieces = [ones * part.astype(jnp.float32) for part in split(column, 2) + split(prec[...], 3)]
    aux = dot(jnp.concatenate(pieces, axis=0).astype(jnp.bfloat16), at_slot, (1, 1))
    columns = aux[0:tiles] + aux[tiles : 2 * tiles]
    precs = (aux[2 * tiles : 3 * tiles] + aux[3 * tiles : 4 * tiles]) + aux[4 * tiles : 5 * tiles]
    sub = sub_iota()
    for owner_at in range(tiles):
        block = jnp.where(sub == 0, columns[owner_at : owner_at + 1], 0.0)
        block = jnp.where(sub == 1, precs[owner_at : owner_at + 1], block)
        out[owner_at, pl.ds(halves * cap, GROUP), :] = block
    rows_high, rows_low = split(op[...], 2)
    chunk = 256
    for first in range(0, tiles * cap, chunk):
        picks = lax.broadcasted_iota(jnp.int32, (chunk, count), 0) + first == place
        picks = jnp.where(picks, 1.0, 0.0).astype(jnp.bfloat16)
        moved = dot(picks, rows_high, (1, 0)) + dot(picks, rows_low, (1, 0))
        for part in range(chunk // cap):
            for half in range(halves):
                out[first // cap + part, pl.ds(half * cap, cap), :] = moved[
                    part * cap : (part + 1) * cap, half * LANES : (half + 1) * LANES
                ]


def innovate_kernel(rows, width, tiles, cap, records, cols, extra, bottom, *rest):
    spread, sel, ends, columns, floor, col_cells, border_sel, precs, both, sems = rest
    chunks = 8
    copies = []
    for part in range(chunks):
        at = pl.ds(part * (2 * width // chunks), 2 * width // chunks)
        copies.append(pltpu.make_async_copy(cols.at[at], col_cells.at[at], sems.at[part]))
        copies[-1].start()
    halves = width // LANES
    count = tiles * cap
    aux = halves * cap
    own = lax.broadcasted_iota(jnp.int32, (cap, LANES), 1) == lax.broadcasted_iota(jnp.int32, (cap, LANES), 0)
    ones = jnp.ones((LANES, LANES), jnp.bfloat16)
    step = 256
    lane = lax.broadcasted_iota(jnp.int32, (step, LANES), 1)
    border = (rows - 1 - lane // (2 * PARTS)) * LANES + jnp.where(lane % 2 == 1, 0, LANES - 1)
    border = jnp.where(lane % (2 * PARTS) < 2, border, -1).astype(jnp.float32)
    lane = lane.astype(jnp.float32)

    def select(block, _):
        sources = step // cap

        def spread_out(part):
            rows_of = [
                jnp.where(own, records[block * sources + s, pl.ds(aux + part, 1), :], 0.0) for s in range(sources)
            ]
            terms = split(jnp.concatenate(rows_of, axis=0), 2 + part)
            return sum(dot(term, ones, (1, 0)) for term in terms)

        at = pl.ds(pl.multiple_of(block * step, step), step)
        place = spread_out(0)
        column = place - lane
        precs[at, :] = spread_out(1)
        for i in range(rows):
            sel[at, i * LANES : (i + 1) * LANES] = jnp.where(column == float(i * LANES), 1.0, 0.0).astype(
                jnp.bfloat16
            )
        border_sel[at, :] = jnp.where(place == border, 1.0, 0.0).astype(jnp.bfloat16)
        return 0

    lax.fori_loop(0, count // step, select, 0)
    for copy in copies:
        copy.wait()
    pair = 2 * GROUP
    first = lax.broadcasted_iota(jnp.int32, (pair, LANES), 0) == 0
    for f in range(2):
        for i in range(rows):
            lanes = slice(i * LANES, (i + 1) * LANES)
            for term, value in enumerate(split(bottom[f * rows + i : f * rows + i + 1, :], 2)):
                at = pl.ds(term * width + f * (width // 2), pair)
                old = col_cells[at, lanes].astype(jnp.float32)
                new = jnp.where(first, value.astype(jnp.float32), old)
                col_cells[at, lanes] = new.astype(jnp.bfloat16)
    both[...] = dot(sel[...], col_cells[...], (1, 1))
    border_cells = jnp.concatenate([sel[:, 0:LANES], sel[:, (rows - 1) * LANES : rows * LANES], border_sel[...]], axis=1)
    both[...] += dot(border_cells, extra[...], (1, 1))

    def weigh(block, _):
        at = pl.ds(pl.multiple_of(block * LANES, LANES), LANES)
        sources = LANES // cap
        ops = [
            jnp.concatenate(
                [records[block * sources + s, half * cap : (half + 1) * cap, :] for s in range(sources)], axis=0
            )
            for half in range(halves)
        ]
        total = sum(
            (both[at, half * LANES : (half + 1) * LANES] + both[at, width + half * LANES : width + (half + 1) * LANES])
            * ops[half]
            for half in range(halves)
        )
        innovation = jnp.sum(total, axis=1, keepdims=True) * precs[at, :]
        for half in range(halves):
            high, low = split((ops[half] * innovation).T, 2)
            spread[half * LANES : (half + 1) * LANES, at] = high
            spread[width + half * LANES : width + (half + 1) * LANES, at] = low
        return 0

    lax.fori_loop(0, count // LANES, weigh, 0, unroll=4)

    terms = dot(spread[...], border_cells, (1, 0))
    border_sums = terms[:width] + terms[width:]
    ends[0] = border_sums[:, 0:LANES]
    ends[1] = border_sums[:, LANES : 2 * LANES]
    thin = border_sums[:, 2 * LANES :]
    for m in range(width // (GROUP * PARTS)):
        total = thin[m * PARTS * GROUP : (m * PARTS + 1) * GROUP]
        for part in range(1, PARTS):
            at = (m * PARTS + part) * GROUP
            total = total + pltpu.roll(thin[at : at + GROUP], 2 * part, 1)
        columns[m * GROUP : (m + 1) * GROUP, :] = total
    half = columns.shape[0] // 2
    floor[...] = jnp.zeros_like(floor)
    for f in range(2):
        for k in range(2):
            floor[2 * k + f : 2 * k + f + 1, :] = ends[k, f * (width // 2) : f * (width // 2) + 1, :]
        floor[4 + f : 5 + f, :] = columns[f * half : f * half + 1, :]


def scatter_kernel(rows, width, spread, sel, winds, adjoint, low0, wind_rows, sems):
    wind_in = Rows(winds, wind_rows, sems, rows, True, 1)
    start_rows(rows, wind_in)
    wind_rows[0] = jnp.zeros_like(wind_rows[0])
    wind_rows[rows + 1] = jnp.zeros_like(wind_rows[0])
    sums = dot(spread[...], sel[...], (1, 0))
    for i in range(rows):
        lanes = slice(i * LANES, (i + 1) * LANES)
        adjoint[i] = sums[:width, lanes] + sums[width:, lanes]
        for f in range(2):
            low0[f * rows + i : f * rows + i + 1, :] = adjoint[i, f * (width // 2) : f * (width // 2) + 1, :]
    for i in range(rows):
        wind_in.wait(i)


def local(state_incr, winds, coupling, background, obs_dest, obs_col, obs_op, obs_prec):
    _, fields, levels, rows, lanes = state_incr.shape
    width = fields * levels
    groups = width // GROUP
    tiles = lax.axis_size("gx") * lax.axis_size("gy")
    count = obs_col.shape[0]
    cap = 2 * count // tiles
    halves = obs_op.shape[1] // LANES

    scale = jnp.broadcast_to(background.reshape(width, 1), (width, LANES))

    vmem = pl.BlockSpec(memory_space=pltpu.VMEM)
    anywhere = pl.BlockSpec(memory_space=pl.ANY)
    own = pltpu.VMEM((rows, width, LANES), jnp.float32)
    framed = pltpu.VMEM((rows + 2, width, LANES), jnp.float32)
    packed_shape = f32(groups // PARTS * GROUP, LANES)
    sides = pltpu.VMEM(packed_shape.shape, jnp.float32)
    strip_shapes = [f32(width, LANES), f32(width, LANES), packed_shape]
    field_shape = f32(rows, width, LANES)
    framed_shape = f32(rows + 2, width, LANES)
    low_shape = f32(fields * rows, LANES)
    cols_shape = ((2 * width, rows * LANES), jnp.bfloat16)

    def sems(*shape):
        return pltpu.SemaphoreType.DMA(shape)

    def run(body, out_shape, scratch, args, far=(), out_far=(), **kw):
        args = [pltpu.with_memory_space_constraint(x, pltpu.HBM) if k in far else x for k, x in enumerate(args)]
        specs = [anywhere if k in far else vmem for k in range(len(args))]
        outs = [anywhere if k in out_far else vmem for k in range(len(out_shape))]
        out_shape = [pltpu.HBM(x.shape, x.dtype) if k in out_far else x for k, x in enumerate(out_shape)]
        return call(body, out_shape, scratch, in_specs=specs, out_specs=outs, **kw)(*args)

    def on_rows(body):
        return functools.partial(body, rows, levels)

    def swap_floor(floor):
        return lax.ppermute(floor, "comp", [(0, 1), (1, 0)])

    state = state_incr.reshape(width, rows, lanes)
    wind = winds.reshape(width, rows, lanes)
    floor_winds = winds[0, :, 0]
    slots = tiles * cap
    thin_shape = f32(GROUP, LANES)

    s_even, s_odd, packed, low0, low1 = run(
        on_rows(edges_kernel),
        strip_shapes + [low_shape] * 2,
        [pltpu.VMEM((width * rows, LANES), jnp.float32), sems(groups // PARTS)],
        (state_incr.reshape(width * rows, lanes),),
        far=(0,),
    )
    halos = exchange((s_even, s_odd), packed)

    send = call(functools.partial(route_kernel, tiles, cap), f32(tiles, halves * cap + GROUP, LANES))(
        obs_dest.reshape(1, count), obs_col.reshape(1, count), obs_prec.reshape(1, count), obs_op
    )
    send, halos[0], halos[2], state_far, wind_far = lax.optimization_barrier((send, halos[0], halos[2], state, wind))
    records = lax.all_to_all(send, ("gx", "gy"), split_axis=0, concat_axis=0, tiled=True)

    state_rows, wind_rows = run(
        functools.partial(load_kernel, rows),
        [field_shape, field_shape],
        [sems(2, rows)],
        (state_far, wind_far),
        far=(0, 1),
        traffic=10 * MIB,
    )
    halos[1], state_rows, wind_rows = lax.optimization_barrier((halos[1], state_rows, wind_rows))
    (floor,) = run(on_rows(forward_floor_kernel), [low_shape], [], (low0, low1, floor_winds, *halos))
    field, s_even, s_odd, packed, low0, low1, wind_ends, wind_dense, dense_g = run(
        on_rows(forward_kernel),
        [framed_shape]
        + strip_shapes
        + [low_shape] * 2
        + [f32(2, levels, LANES), f32(groups // PARTS * GROUP // 2, LANES), thin_shape],
        [framed, sides],
        (coupling, swap_floor(floor), state_rows, wind_rows, *halos),
    )
    halos = exchange((s_even, s_odd), packed)
    (cols,) = run(
        on_rows(forward_again_kernel),
        [jax.ShapeDtypeStruct(*cols_shape)],
        [pltpu.VMEM(*cols_shape), sems(rows)],
        (field, wind_rows),
        out_far=(0,),
        traffic=20 * MIB,
    )
    cols, halos = lax.optimization_barrier((cols, halos))
    (floor,) = run(on_rows(forward_floor_kernel), [low_shape], [], (low0, low1, floor_winds, *halos))
    extra, bottom = run(
        on_rows(outside_kernel),
        [jax.ShapeDtypeStruct((2 * width, 3 * LANES), jnp.bfloat16), low_shape],
        [sides],
        (coupling, floor, swap_floor(floor), wind_ends, wind_dense, *halos),
    )

    spread_shape = ((2 * width, slots), jnp.bfloat16)
    sel_shape = ((slots, rows * LANES), jnp.bfloat16)
    spread, sel, ends, columns, border_floor = run(
        functools.partial(innovate_kernel, rows, width, tiles, cap),
        [
            jax.ShapeDtypeStruct(*spread_shape),
            jax.ShapeDtypeStruct(*sel_shape),
            f32(2, width, LANES),
            packed_shape,
            thin_shape,
        ],
        [
            pltpu.VMEM(*cols_shape),
            pltpu.VMEM((slots, LANES), jnp.bfloat16),
            pltpu.VMEM((slots, LANES), jnp.float32),
            pltpu.VMEM((slots, 2 * width), jnp.float32),
            sems(8),
        ],
        (records, cols, extra, bottom),
        far=(1,),
        limit=OBSERVE_VMEM,
    )
    strips = run(
        on_rows(border_kernel),
        strip_shapes,
        [],
        (coupling, swap_floor(border_floor), ends, columns, wind_ends, wind_dense, dense_g),
    )
    halos = exchange(strips[:2], strips[2])
    adjoint, low0, wind_rows = run(
        functools.partial(scatter_kernel, rows, width),
        [field_shape, low_shape, framed_shape],
        [sems(rows)],
        (spread, sel, wind),
        far=(2,),
        limit=OBSERVE_VMEM,
        traffic=8 * MIB,
    )
    partner = swap_floor(low0)
    adjoint, ends, columns, low0, state_rows = run(
        on_rows(first_adjoint_kernel),
        [field_shape, f32(2, width, LANES), packed_shape, low_shape, field_shape],
        [framed, sems(rows)],
        (coupling, adjoint, wind_rows, state),
        far=(3,),
        traffic=16 * MIB,
    )
    low0, partner, halos = lax.optimization_barrier((low0, partner, halos))
    floor, missing = run(
        on_rows(floor_kernel), [low_shape, low_shape], [], (coupling, partner, low0, floor_winds, *halos)
    )
    other = swap_floor(floor)
    strips = run(
        on_rows(border_again_kernel),
        strip_shapes,
        [sides],
        (coupling, floor, other, missing, ends, columns, wind_ends, wind_dense, dense_g, *halos),
    )
    last_halos = exchange(strips[:2], strips[2])
    (adjoint,) = run(
        on_rows(second_adjoint_kernel),
        [field_shape],
        [framed, sides],
        (coupling, floor, other, missing, adjoint, wind_rows, scale, state_rows, *halos),
        traffic=20 * MIB,
    )
    (result,) = run(
        on_rows(final_kernel),
        [f32(width, rows, LANES)],
        [own, sides, sems(rows)],
        (adjoint, *last_halos),
        out_far=(0,),
    )
    return result.reshape(state_incr.shape)


def solution(mesh):
    placed = (
        P("comp", None, None, "gx", "gy"),
        P("comp", None, None, "gx", "gy"),
        P("gx", "gy"),
        P("comp", None, None),
        P(("comp", "gx", "gy"), None),
        P(("comp", "gx", "gy")),
        P(("comp", "gx", "gy"), None),
        P(("comp", "gx", "gy")),
    )
    return jax.shard_map(
        local,
        mesh=mesh,
        in_specs=placed,
        out_specs=P("comp", None, None, "gx", "gy"),
        check_vma=False,
    )
```

```python
import functools

import jax
import jax.numpy as jnp
from jax import lax
from jax.experimental import pallas as pl
from jax.experimental.pallas import tpu as pltpu
from jax.sharding import PartitionSpec as P

HORIZ_MIX = 0.1
VERT_MIX = 0.15
LANES = 128
GROUP = 8
MIB = 1024 * 1024
SWEEP_VMEM = 16 * MIB
OBSERVE_VMEM = 22 * MIB


def call(body, out_shape, scratch=(), limit=SWEEP_VMEM, traffic=0, **kw):
    cost = pl.CostEstimate(flops=0, bytes_accessed=traffic, transcendentals=0) if traffic else None
    return pl.pallas_call(
        body,
        out_shape=out_shape,
        scratch_shapes=list(scratch),
        cost_estimate=cost,
        compiler_params=pltpu.CompilerParams(vmem_limit_bytes=limit),
        **kw,
    )


def f32(*shape):
    return jax.ShapeDtypeStruct(shape, jnp.float32)


def lane_iota(rows=GROUP):
    return lax.broadcasted_iota(jnp.int32, (rows, LANES), 1)


def sub_iota(rows=GROUP):
    return lax.broadcasted_iota(jnp.int32, (rows, LANES), 0)


def pair_swap(block, axis, start):
    count = lax.axis_size(axis)
    route = []
    for low in range(start, count - 1, 2):
        route += [(low, low + 1), (low + 1, low)]
    return lax.ppermute(block, axis, route)


def pair_sets():
    return 2 if lax.axis_size("gx") > 2 else 1


def exchange(strips, packed):
    y_even = pair_swap(packed, "gy", 0)
    y_odd = pair_swap(packed, "gy", 1)
    even, *odd = [pair_swap(strips[start], "gx", start) for start in range(pair_sets())]
    return [even, y_even, y_odd, *odd]


def is_odd(axis):
    return lax.rem(lax.axis_index(axis), 2) == 1


def read_sides(refs):
    even = refs[0]
    odd = refs[3] if len(refs) > 3 else None
    at_odd = is_odd("gx")

    def side(at, turned):
        other = jnp.zeros_like(even[at]) if odd is None else odd[at]
        return jnp.where(turned, other, even[at])

    return lambda at: side(at, jnp.logical_not(at_odd)), lambda at: side(at, at_odd)


PARTS = 4


def merged(y_even, y_odd, at):
    a, b = y_even[at, :], y_odd[at, :]
    lane = lax.broadcasted_iota(jnp.int32, a.shape, 1)
    return jnp.where((lane % 2 == 1) == jnp.logical_not(is_odd("gy")), a, b)


def merge_columns(y_even, y_odd, sides):
    sides[...] = merged(y_even, y_odd, slice(0, sides.shape[0]))


def slot_of(i, part, rows):
    return PARTS * (rows - 1 - i) + part


def side_columns(sides, i, group):
    m, part = group // PARTS, group % PARTS
    rows = LANES // (2 * PARTS)
    return pltpu.roll(sides[m * GROUP : (m + 1) * GROUP, :], LANES - 1 - 2 * slot_of(i, part, rows), 1)


def pack_into(total, value, slot):
    return jnp.where(lane_iota() // 2 == slot, pltpu.roll(value, 2 * slot + 1, 1), total)


def pack_block(packed, values, i, m):
    at = pl.ds(m * GROUP, GROUP)
    total = packed[at, :]
    for part, value in enumerate(values):
        total = pack_into(total, value, slot_of(i, part, LANES // (2 * PARTS)))
    packed[at, :] = total


CENTRE = 1.0 - 4.0 * HORIZ_MIX - 2.0 * VERT_MIX


def levels_around(cells, i, base, group, groups):
    here = cells[i + 1, pl.ds(base + group * GROUP, GROUP), :]
    if group == groups - 1:
        upper = jnp.where(sub_iota() == GROUP - 1, here, pltpu.roll(here, GROUP - 1, 0))
    else:
        upper = cells[i + 1, pl.ds(base + group * GROUP + 1, GROUP), :]
    if group == 0:
        lower = jnp.where(sub_iota() == 0, here, pltpu.roll(here, 1, 0))
    else:
        lower = cells[i + 1, pl.ds(base + group * GROUP - 1, GROUP), :]
    return here, upper, lower


def shifted(first, last, edge, rows=GROUP):
    lane = lane_iota(rows)
    right = pltpu.roll(jnp.where(lane == 0, edge, first), LANES - 1, 1)
    left = pltpu.roll(jnp.where(lane == LANES - 1, edge, last), 1, 1)
    return right, left


def forward_sum(here, vertical, after, before, right, left, u, w):
    return (
        CENTRE * here
        + VERT_MIX * vertical
        + HORIZ_MIX * ((after + before) + (right + left))
        - 0.5 * (u * (after - before) + w * (right - left))
    )


def forward_point(cells, winds, sides, i, f, group, levels):
    groups = levels // GROUP
    here, upper, lower = levels_around(cells, i, f * levels, group, groups)
    at = pl.ds(f * levels + group * GROUP, GROUP)
    right, left = shifted(here, here, 0.0 if sides is None else side_columns(sides, i, f * groups + group))
    u = winds[i, pl.ds(group * GROUP, GROUP), :]
    w = winds[i, pl.ds(levels + group * GROUP, GROUP), :]
    return forward_sum(here, upper + lower, cells[i + 2, at, :], cells[i, at, :], right, left, u, w)


def products(x, wind):
    slope = 0.5 * (wind * x)
    return HORIZ_MIX * x - slope, HORIZ_MIX * x + slope


def adjoint_point(cells, winds, i, f, group, levels):
    here, upper, lower = levels_around(cells, i, f * levels, group, levels // GROUP)
    at = pl.ds(f * levels + group * GROUP, GROUP)
    wind_at = pl.ds(group * GROUP, GROUP)
    after, before = cells[i + 2, at, :], cells[i, at, :]
    u_after, u_before = winds[i + 2, wind_at, :], winds[i, wind_at, :]
    down, up = products(here, winds[i + 1, pl.ds(levels + group * GROUP, GROUP), :])
    right, left = shifted(up, down, 0.0)
    return (
        CENTRE * here
        + VERT_MIX * (upper + lower)
        + HORIZ_MIX * (after + before)
        + 0.5 * (u_after * after - u_before * before)
        + (right + left)
    )


def shares_of(coupling):
    own = jnp.where(lax.axis_index("comp") == 0, 1.0, 0.5)
    return own * coupling, (1.5 - own) * coupling


def couple_forward(value, other, coupling):
    own, _ = shares_of(coupling)
    return value - own * (value - other)


def couple_adjoint(value, other, coupling):
    own, peer = shares_of(coupling)
    return value - own * value + peer * other


def coupled(rule, value, other, coupling, i, f, rows):
    mixed = rule(value, other[pl.ds(f * rows + i, 1), :], coupling[pl.ds(i, 1), :])
    return jnp.where(sub_iota() == 0, mixed, value)


def put_strip(strips, at, first, last):
    at_odd = is_odd("gx")
    strips[0, at, :] = jnp.where(at_odd, first, last)
    if strips.shape[0] > 1:
        strips[1, at, :] = jnp.where(at_odd, last, first)


def put_low(low, value, i, f, rows):
    for level in range(2):
        low[level][pl.ds(f * rows + i, 1), :] = value[level : level + 1]


class Rows:
    def __init__(self, source, target, sems, rows, as_it_comes, offset):
        self.source, self.target, self.sems = source, target, sems
        self.rows, self.as_it_comes, self.offset = rows, as_it_comes, offset

    def copy(self, i):
        row = self.source.at[:, i] if self.as_it_comes else self.source.at[i]
        return pltpu.make_async_copy(row, self.target.at[i + self.offset], self.sems.at[i])

    def wait(self, i):
        self.copy(i).wait()


def start_rows(rows, *groups):
    for i in range(rows):
        for group in groups:
            group.copy(i).start()


def edges_kernel(rows, levels, state, strips, packed, low0, low1, cells, sems):
    part_levels = PARTS * GROUP
    blocks = 2 * levels // part_levels

    def copy(m):
        return pltpu.make_async_copy(
            state.at[pl.ds(m * part_levels * rows, part_levels * rows)],
            cells.at[pl.ds(m * part_levels * rows, part_levels * rows)],
            sems.at[m],
        )

    for m in range(blocks):
        copy(m).start()

    def block(m, _):
        copy(m).wait()
        total = jnp.zeros((GROUP, LANES), jnp.float32)
        for part in range(PARTS):
            for i in range(rows):
                start = (m * PARTS + part) * GROUP * rows + i
                total = pack_into(total, cells[pl.ds(start, GROUP, stride=rows), :], slot_of(i, part, rows))
        packed[pl.ds(pl.multiple_of(m * GROUP, GROUP), GROUP), :] = total
        start = m * part_levels * rows
        first = cells[pl.ds(start, part_levels, stride=rows), :]
        last = cells[pl.ds(start + rows - 1, part_levels, stride=rows), :]
        put_strip(strips, pl.ds(pl.multiple_of(m * part_levels, part_levels), part_levels), first, last)
        return 0

    lax.fori_loop(0, blocks, block, 0)
    for f in range(2):
        for level, low in enumerate((low0, low1)):
            low[f * rows : (f + 1) * rows, :] = cells[pl.ds((f * levels + level) * rows, rows), :]


def floor_edge(halos, f, rows, levels, more=0.0):
    m = f * (levels // GROUP) // PARTS
    sides = jnp.broadcast_to(merged(halos[1], halos[2], pl.ds(m * GROUP, 1)) + more, (rows, LANES))
    return pltpu.roll(sides, 2 * PARTS - 1, 1, stride=2 * PARTS, stride_axis=0)


def row_after(value, last, rows):
    return jnp.where(sub_iota(rows) == rows - 1, last, pltpu.roll(value, rows - 1, 0))


def row_before(value, first, rows):
    return jnp.where(sub_iota(rows) == 0, first, pltpu.roll(value, 1, 0))


def forward_floor_kernel(rows, levels, low0, low1, winds, *rest):
    *halos, floor = rest
    side_before, side_after = read_sides(halos)
    for f in range(2):
        here = pl.ds(f * rows, rows)
        at = pl.ds(f * levels, 1)
        low, up = low0[here, :], low1[here, :]
        after, before = row_after(low, side_after(at), rows), row_before(low, side_before(at), rows)
        right, left = shifted(low, low, floor_edge(halos, f, rows, levels), rows)
        floor[here, :] = forward_sum(low, up + low, after, before, right, left, winds[0], winds[1])


class Out:
    def __init__(self, source, target, sems, rows, as_it_goes):
        self.source, self.target, self.sems, self.rows, self.as_it_goes = source, target, sems, rows, as_it_goes

    def copy(self, i):
        row = self.target.at[:, i] if self.as_it_goes else self.target.at[i]
        return pltpu.make_async_copy(self.source.at[i], row, self.sems.at[i])

    def start(self, i):
        self.copy(i).start()

    def finish(self):
        for i in range(self.rows):
            self.copy(i).wait()


def dense_row(field, first, rows):
    total = jnp.zeros((1, LANES), jnp.float32)
    lane = lax.broadcasted_iota(jnp.int32, (1, LANES), 1)
    for i in range(rows):
        slot = slot_of(i, 0, rows)
        total = jnp.where(lane // 2 == slot, pltpu.roll(field[first + i : first + i + 1, :], 2 * slot + 1, 1), total)
    return total


def load_kernel(rows, state, winds, state_rows, wind_rows, sems):
    state_in = Rows(state, state_rows, sems.at[0], rows, True, 0)
    wind_in = Rows(winds, wind_rows, sems.at[1], rows, True, 0)
    start_rows(rows, state_in, wind_in)
    for i in range(rows):
        state_in.wait(i)
        wind_in.wait(i)


def forward_kernel(rows, levels, coupling, other, field, winds, *rest):
    *halos, out, strips, packed, low0, low1, wind_ends, wind_dense, dense_g, cells, sides = rest
    packed[...] = jnp.zeros_like(packed)
    wind_dense[...] = jnp.zeros_like(wind_dense)
    merge_columns(halos[1], halos[2], sides)
    before, after = read_sides(halos)
    cells[0] = before(pl.ds(0, 2 * levels))
    cells[1] = field[0]
    cells[rows + 1] = after(pl.ds(0, 2 * levels))
    out[0] = jnp.zeros_like(out[0])
    out[rows + 1] = jnp.zeros_like(out[0])
    groups = levels // GROUP

    def row(i, _):
        @pl.when(i < rows - 1)
        def _():
            cells[i + 2] = field[i + 1]

        for m in range(2 * groups // PARTS):
            f, start = m * PARTS // groups, m * PARTS % groups
            values = []
            for group in range(start, start + PARTS):
                value = forward_point(cells, winds, sides, i, f, group, levels)
                if group == 0:
                    value = coupled(couple_forward, value, other, coupling, i, f, rows)
                    put_low((low0, low1), value, i, f, rows)
                values.append(value)
            base = m * PARTS * GROUP
            for part, value in enumerate(values):
                out[i + 1, pl.ds(base + part * GROUP, GROUP), :] = value
            pack_block(packed, values, i, m)
            if f == 0:
                w = [winds[i, pl.ds(levels + base + part * GROUP, GROUP), :] for part in range(PARTS)]
                pack_block(wind_dense, w, i, m)
        return 0

    lax.fori_loop(0, rows, row, 0)
    put_strip(strips, pl.ds(0, 2 * levels), out[1], out[rows])
    wind_ends[0] = winds[0, pl.ds(0, levels), :]
    wind_ends[1] = winds[rows - 1, pl.ds(0, levels), :]
    dense_g[...] = jnp.broadcast_to(dense_row(coupling, 0, rows), dense_g.shape)
    _, peer = shares_of(coupling[...])
    first = products(peer[0:1], winds[0, 0:1, :])[1]
    last = products(peer[rows - 1 : rows], winds[rows - 1, 0:1, :])[0]
    whole = (GROUP, LANES)
    put_strip(strips, slice(2 * levels, 2 * levels + GROUP), jnp.broadcast_to(first, whole), jnp.broadcast_to(last, whole))
    _, peer = shares_of(dense_g[...])
    packed[packed.shape[0] - GROUP :, :] = first_and_last(peer, wind_dense[0:1, :])


def forward_again_kernel(rows, levels, cells, winds, cols, col_cells, col_sems):
    groups = levels // GROUP
    width = 2 * levels

    def col_copy(i):
        lanes = pl.ds(pl.multiple_of(i * LANES, LANES), LANES)
        return pltpu.make_async_copy(col_cells.at[:, lanes], cols.at[:, lanes], col_sems.at[i])

    def row(i, _):
        lanes = pl.ds(pl.multiple_of(i * LANES, LANES), LANES)
        for m in range(2 * groups // PARTS):
            f, start = m * PARTS // groups, m * PARTS % groups
            values = [forward_point(cells, winds, None, i, f, group, levels) for group in range(start, start + PARTS)]
            high, low = split(jnp.concatenate(values, axis=0), 2)
            col_cells[pl.ds(m * PARTS * GROUP, PARTS * GROUP), lanes] = high
            col_cells[pl.ds(width + m * PARTS * GROUP, PARTS * GROUP), lanes] = low
        col_copy(i).start()
        return 0

    lax.fori_loop(0, rows, row, 0)
    for i in range(rows):
        col_copy(i).wait()


def outside_kernel(rows, levels, coupling, floor, other, wind_ends, wind_dense, *rest):
    *halos, extra, bottom, dense = rest
    width = 2 * levels
    for f in range(2):
        here = pl.ds(f * rows, rows)
        bottom[here, :] = couple_forward(floor[here, :], other[here, :], coupling[...])
    dense_products(dense, swap_pairs(merged(halos[1], halos[2], slice(0, dense.shape[0]))), wind_dense)
    before, after = read_sides(halos)
    sub = lax.broadcasted_iota(jnp.int32, (levels, LANES), 0)

    def put(value, f, lanes):
        high, low = split(jnp.where(sub == 0, 0.0, value), 2)
        extra[f * levels : (f + 1) * levels, lanes] = high
        extra[width + f * levels : width + (f + 1) * levels, lanes] = low

    lane = lane_iota()
    for f in range(2):
        at = pl.ds(f * levels, levels)
        put(products(before(at), wind_ends[0])[1], f, slice(0, LANES))
        put(products(after(at), wind_ends[1])[0], f, slice(LANES, 2 * LANES))
        thin = []
        for group in range(f * levels // GROUP, (f + 1) * levels // GROUP):
            m, part = group // PARTS, group % PARTS
            moved = pltpu.roll(dense[m * GROUP : (m + 1) * GROUP, :], (LANES - 2 * part) % LANES, 1)
            thin.append(jnp.where(lane % (2 * PARTS) < 2, moved, 0.0))
        put(jnp.concatenate(thin, axis=0), f, slice(2 * LANES, 3 * LANES))


def first_and_last(value, wind):
    down, up = products(value, wind)
    lane = lax.broadcasted_iota(jnp.int32, down.shape, 1)
    return jnp.where(lane % 2 == 1, up, down)


def dense_products(packed, value, wind_dense):
    half = wind_dense.shape[0]
    for f in range(2):
        at = slice(f * half, (f + 1) * half)
        packed[at, :] = first_and_last(value[at], wind_dense[...])


def level0_row(value, new, f):
    half = value.shape[0] // 2
    sub = lax.broadcasted_iota(jnp.int32, value.shape, 0)
    lane = lax.broadcasted_iota(jnp.int32, value.shape, 1)
    return jnp.where((sub == f * half) & (lane % (2 * PARTS) < 2), new, value)


def end_rows(ends, strips, wind_ends, levels):
    for f in range(2):
        at = slice(f * levels, (f + 1) * levels)
        put_strip(
            strips, at, products(ends[0][at], wind_ends[0])[1], products(ends[1][at], wind_ends[1])[0]
        )


def with_first(value, new):
    return jnp.where(lax.broadcasted_iota(jnp.int32, value.shape, 0) == 0, new, value)


def border_strips(rows, levels, coupling, ends, dense, wind_ends, wind_dense, dense_g, strips, packed):
    half = dense.shape[0] // 2
    width = 2 * levels
    own, _ = shares_of(dense_g[0:1, :])
    new = dense
    for f in range(2):
        bottom = dense[f * half : f * half + 1]
        new = level0_row(new, bottom - own * bottom, f)
        packed[2 * half + f : 2 * half + f + 1, :] = bottom
    dense_products(packed, new, wind_dense)
    full = []
    for k, i in enumerate((0, rows - 1)):
        own, _ = shares_of(coupling[i : i + 1, :])
        parts = []
        for f in range(2):
            value = ends[k][f * levels : (f + 1) * levels]
            parts.append(with_first(value, value[0:1] - own * value[0:1]))
        full.append(jnp.concatenate(parts, axis=0))
    end_rows(full, strips, wind_ends, levels)
    for f in range(2):
        at = f * levels
        put_strip(strips, slice(width + f, width + f + 1), ends[0][at : at + 1], ends[1][at : at + 1])


def beside_kernel(rows, levels, *rest):
    *halos, raw = rest
    before, after = read_sides(halos)
    at = pl.ds(2 * levels, 2)
    half = halos[1].shape[0] - GROUP
    raw[...] = jnp.zeros_like(raw)
    raw[0:2, :] = before(at)
    raw[2:4, :] = after(at)
    raw[4:6, :] = merged(halos[1], halos[2], pl.ds(half, 2))


def outside_floor(halos, factors, raw, low, f, rows, levels):
    before, after = read_sides(halos)
    factor_before, factor_after = read_sides(factors)
    at, tail = pl.ds(f * levels, 1), pl.ds(2 * levels, 1)
    sub, lane = sub_iota(rows), lane_iota(rows)
    from_before = before(at) + factor_before(tail) * raw[f : f + 1, :]
    from_after = after(at) + factor_after(tail) * raw[2 + f : 3 + f, :]
    low = low + jnp.where(sub == 0, from_before, 0.0) + jnp.where(sub == rows - 1, from_after, 0.0)
    factor = merged(factors[1], factors[2], pl.ds(factors[1].shape[0] - GROUP, 1))
    edge = floor_edge(halos, f, rows, levels, factor * raw[4 + f : 5 + f, :])
    edge = jnp.where(lane == 0, pltpu.roll(edge, 1, 1), pltpu.roll(edge, LANES - 1, 1))
    return low + jnp.where((lane == 0) | (lane == LANES - 1), edge, 0.0)


def floor_kernel(rows, levels, coupling, other, low0, raw, winds, *rest):
    *both, floor, missing = rest
    halos, factors = both[: len(both) // 2], both[len(both) // 2 :]
    for f in range(2):
        here = pl.ds(f * rows, rows)
        _, peer = shares_of(coupling[...])
        share = peer * other[here, :]
        x_down, x_up = products(share, winds[0])
        y_down, y_up = products(share, winds[1])
        right, left = shifted(y_up, y_down, 0.0, rows)
        spread = (row_after(x_up, 0.0, rows) + row_before(x_down, 0.0, rows)) + (right + left)
        spread = spread + (CENTRE + VERT_MIX) * share
        floor[here, :] = outside_floor(halos, factors, raw, low0[here, :] + spread, f, rows, levels)
        missing[here, :] = VERT_MIX * share


def swap_pairs(value):
    lane = lax.broadcasted_iota(jnp.int32, value.shape, 1)
    return jnp.where(lane % 2 == 1, pltpu.roll(value, 1, 1), pltpu.roll(value, LANES - 1, 1))


def edge_lanes(sides, i, group):
    m, part = group // PARTS, group % PARTS
    rows = LANES // (2 * PARTS)
    moved = pltpu.roll(sides[m * GROUP : (m + 1) * GROUP, :], LANES - 1 - 2 * slot_of(i, part, rows), 1)
    lane = lane_iota()
    return jnp.where((lane == 0) | (lane == LANES - 1), moved, 0.0)


def with_level(value, level, new):
    return jnp.where(lax.broadcasted_iota(jnp.int32, value.shape, 0) == level, new, value)


def border_again_kernel(
    rows, levels, coupling, floor, other, missing, ends, columns, wind_ends, wind_dense, dense_g, *rest
):
    *halos, strips, packed, sides = rest
    before, after = read_sides(halos)
    sides[...] = swap_pairs(merged(halos[1], halos[2], slice(0, sides.shape[0])))
    half = columns.shape[0] // 2
    groups = levels // GROUP
    outer = [before(pl.ds(0, 2 * levels)), after(pl.ds(0, 2 * levels))]
    full = []
    for k, i in enumerate((0, rows - 1)):
        edges = jnp.concatenate([edge_lanes(sides, i, group) for group in range(2 * groups)], axis=0)
        value = ends[k] + outer[k] + edges
        parts = []
        for f in range(2):
            part = value[f * levels : (f + 1) * levels]
            at = slice(f * rows + i, f * rows + i + 1)
            part = part + with_level(jnp.zeros_like(part), 1, missing[at, :])
            parts.append(with_first(part, couple_adjoint(floor[at, :], other[at, :], coupling[i : i + 1, :])))
        full.append(jnp.concatenate(parts, axis=0))
    end_rows(full, strips, wind_ends, levels)
    dense = columns[...] + sides[...]
    corners = []
    for m in range(2 * groups // PARTS):
        total = jnp.zeros((GROUP, LANES), jnp.float32)
        for part in range(PARTS):
            at = slice((m * PARTS + part) * GROUP, (m * PARTS + part + 1) * GROUP)
            for k, i in enumerate((0, rows - 1)):
                total = pack_into(total, outer[k][at], slot_of(i, part, rows))
        corners.append(total)
    dense = dense + jnp.concatenate(corners, axis=0)
    for f in range(2):
        sub = lax.broadcasted_iota(jnp.int32, dense.shape, 0)
        dense = dense + jnp.where(sub == f * half + 1, dense_row(missing, f * rows, rows), 0.0)
        mine = dense_row(floor, f * rows, rows)
        mixed = couple_adjoint(mine, dense_row(other, f * rows, rows), dense_g[0:1, :])
        dense = level0_row(dense, mixed, f)
    dense_products(packed, dense, wind_dense)


def adjoint_rows(rows, levels, cells, winds, take, each):
    groups = levels // GROUP
    cells[0] = jnp.zeros_like(cells[0])
    cells[rows + 1] = jnp.zeros_like(cells[0])
    take(0)

    def row(i, _):
        @pl.when(i < rows - 1)
        def _():
            take(i + 1)

        for m in range(2 * groups // PARTS):
            f, start = m * PARTS // groups, m * PARTS % groups
            each(i, m, f, start, [
                adjoint_point(cells, winds, i, f, group, levels) for group in range(start, start + PARTS)
            ])
        return 0

    lax.fori_loop(0, rows, row, 0)


def first_adjoint_kernel(rows, levels, coupling, field, winds, state, out, ends, columns, low0, state_rows, cells, sems):
    state_in = Rows(state, state_rows, sems, rows, True, 0)
    start_rows(rows, state_in)
    columns[...] = jnp.zeros_like(columns)

    def take(i):
        cells[i + 1] = field[i]
        for f in range(2):
            at = pl.ds(f * levels, GROUP)
            own, _ = shares_of(coupling[pl.ds(i, 1), :])
            value = field[i, at, :]
            cells[i + 1, at, :] = jnp.where(sub_iota() == 0, value - own * value, value)

    def each(i, m, f, start, values):
        for part, value in enumerate(values):
            out[i, pl.ds((m * PARTS + part) * GROUP, GROUP), :] = value
        if start == 0:
            low0[pl.ds(f * rows + i, 1), :] = values[0][0:1]
        pack_block(columns, values, i, m)

    adjoint_rows(rows, levels, cells, winds, take, each)
    ends[0] = out[0]
    ends[1] = out[rows - 1]
    for i in range(rows):
        state_in.wait(i)


def second_adjoint_kernel(rows, levels, coupling, floor, other, missing, field, winds, scale, state, *rest):
    *halos, out, cells, sides = rest
    sides[...] = swap_pairs(merged(halos[1], halos[2], slice(0, sides.shape[0])))
    before, after = read_sides(halos)
    groups = levels // GROUP

    def take(i):
        for group in range(2 * groups):
            at = pl.ds(group * GROUP, GROUP)
            value = field[i, at, :] + edge_lanes(sides, i, group)
            if group % groups == 0:
                value = value + jnp.where(i == 0, before(at), 0.0) + jnp.where(i == rows - 1, after(at), 0.0)
                here = pl.ds(group // groups * rows + i, 1)
                value = value + jnp.where(sub_iota() == 1, missing[here, :], 0.0)
                bottom = couple_adjoint(floor[here, :], other[here, :], coupling[pl.ds(i, 1), :])
                value = jnp.where(sub_iota() == 0, bottom, value)
            cells[i + 1, at, :] = value

    def add_outer(i, side):
        for f in range(2):
            at = pl.ds(f * levels + GROUP, levels - GROUP)
            cells[i + 1, at, :] = cells[i + 1, at, :] + side(at)

    def take_all(i):
        take(i)

        @pl.when(i == 0)
        def _():
            add_outer(0, before)

        @pl.when(i == rows - 1)
        def _():
            add_outer(rows - 1, after)

    def each(i, m, f, start, values):
        for part, value in enumerate(values):
            at = pl.ds((m * PARTS + part) * GROUP, GROUP)
            out[i, at, :] = value + scale[at, :] * state[i, at, :]

    adjoint_rows(rows, levels, cells, winds, take_all, each)


def final_kernel(rows, levels, field, *rest):
    *halos, out, cells, sides, sems = rest
    leaving = Out(cells, out, sems, rows, True)
    sides[...] = swap_pairs(merged(halos[1], halos[2], slice(0, sides.shape[0])))
    before, after = read_sides(halos)
    groups = levels // GROUP

    def add(i, outer):
        for group in range(2 * groups):
            at = pl.ds(group * GROUP, GROUP)
            value = field[i, at, :] + edge_lanes(sides, i, group)
            cells[i, at, :] = value if outer is None else value + outer(at)
        leaving.start(i)
        return 0

    lax.fori_loop(1, rows - 1, lambda i, _: add(i, None), 0, unroll=2)
    add(0, before)
    add(rows - 1, after)
    leaving.finish()


def split(value, terms):
    parts = []
    for _ in range(terms):
        part = value.astype(jnp.bfloat16)
        parts.append(part)
        value = value - part.astype(jnp.float32)
    return parts


def dot(a, b, contract):
    return lax.dot_general(a, b, ((contract[:1], contract[1:]), ((), ())), preferred_element_type=jnp.float32)


def route_kernel(tiles, cap, dest, col, prec, op, out):
    count = op.shape[0]
    width = op.shape[1]
    halves = width // LANES
    owner = lax.broadcasted_iota(jnp.int32, (tiles, count), 0)
    hits = owner == dest[...]
    ones = jnp.where(hits, 1.0, 0.0)
    earlier = lax.broadcasted_iota(jnp.int32, (count, count), 0) <= lax.broadcasted_iota(jnp.int32, (count, count), 1)
    running = dot(ones.astype(jnp.bfloat16), jnp.where(earlier, 1.0, 0.0).astype(jnp.bfloat16), (1, 0))
    slot = jnp.sum(running * ones, axis=0, keepdims=True) - 1.0
    slot = slot.astype(jnp.int32)
    place = dest[...] * cap + slot
    at_slot = lax.broadcasted_iota(jnp.int32, (LANES, count), 0) == slot
    at_slot = jnp.where(at_slot, 1.0, 0.0).astype(jnp.bfloat16)
    column = col[...].astype(jnp.float32)
    pieces = [ones * part.astype(jnp.float32) for part in split(column, 2) + split(prec[...], 3)]
    aux = dot(jnp.concatenate(pieces, axis=0).astype(jnp.bfloat16), at_slot, (1, 1))
    columns = aux[0:tiles] + aux[tiles : 2 * tiles]
    precs = (aux[2 * tiles : 3 * tiles] + aux[3 * tiles : 4 * tiles]) + aux[4 * tiles : 5 * tiles]
    sub = sub_iota()
    for owner_at in range(tiles):
        block = jnp.where(sub == 0, columns[owner_at : owner_at + 1], 0.0)
        block = jnp.where(sub == 1, precs[owner_at : owner_at + 1], block)
        out[owner_at, pl.ds(halves * cap, GROUP), :] = block
    rows_high, rows_low = split(op[...], 2)
    chunk = 256
    for first in range(0, tiles * cap, chunk):
        picks = lax.broadcasted_iota(jnp.int32, (chunk, count), 0) + first == place
        picks = jnp.where(picks, 1.0, 0.0).astype(jnp.bfloat16)
        moved = dot(picks, rows_high, (1, 0)) + dot(picks, rows_low, (1, 0))
        for part in range(chunk // cap):
            for half in range(halves):
                out[first // cap + part, pl.ds(half * cap, cap), :] = moved[
                    part * cap : (part + 1) * cap, half * LANES : (half + 1) * LANES
                ]


def innovate_kernel(rows, width, tiles, cap, records, cols, extra, bottom, *rest):
    coupling, wind_ends, wind_dense, dense_g, spread, sel, strips, packed = rest[:8]
    col_cells, border_sel, precs, both, sems = rest[8:]
    chunks = 8
    copies = []
    for part in range(chunks):
        at = pl.ds(part * (2 * width // chunks), 2 * width // chunks)
        copies.append(pltpu.make_async_copy(cols.at[at], col_cells.at[at], sems.at[part]))
        copies[-1].start()
    halves = width // LANES
    count = tiles * cap
    aux = halves * cap
    own = lax.broadcasted_iota(jnp.int32, (cap, LANES), 1) == lax.broadcasted_iota(jnp.int32, (cap, LANES), 0)
    ones = jnp.ones((LANES, LANES), jnp.bfloat16)
    step = 256
    lane = lax.broadcasted_iota(jnp.int32, (step, LANES), 1)
    border = (rows - 1 - lane // (2 * PARTS)) * LANES + jnp.where(lane % 2 == 1, 0, LANES - 1)
    border = jnp.where(lane % (2 * PARTS) < 2, border, -1).astype(jnp.float32)
    lane = lane.astype(jnp.float32)

    def select(block, _):
        sources = step // cap

        def spread_out(part):
            rows_of = [
                jnp.where(own, records[block * sources + s, pl.ds(aux + part, 1), :], 0.0) for s in range(sources)
            ]
            terms = split(jnp.concatenate(rows_of, axis=0), 2 + part)
            return sum(dot(term, ones, (1, 0)) for term in terms)

        at = pl.ds(pl.multiple_of(block * step, step), step)
        place = spread_out(0)
        column = place - lane
        precs[at, :] = spread_out(1)
        for i in range(rows):
            sel[at, i * LANES : (i + 1) * LANES] = jnp.where(column == float(i * LANES), 1.0, 0.0).astype(
                jnp.bfloat16
            )
        border_sel[at, :] = jnp.where(place == border, 1.0, 0.0).astype(jnp.bfloat16)
        return 0

    lax.fori_loop(0, count // step, select, 0)
    for copy in copies:
        copy.wait()
    pair = 2 * GROUP
    first = lax.broadcasted_iota(jnp.int32, (pair, LANES), 0) == 0
    for f in range(2):
        for i in range(rows):
            lanes = slice(i * LANES, (i + 1) * LANES)
            for term, value in enumerate(split(bottom[f * rows + i : f * rows + i + 1, :], 2)):
                at = pl.ds(term * width + f * (width // 2), pair)
                old = col_cells[at, lanes].astype(jnp.float32)
                new = jnp.where(first, value.astype(jnp.float32), old)
                col_cells[at, lanes] = new.astype(jnp.bfloat16)
    both[...] = dot(sel[...], col_cells[...], (1, 1))
    border_cells = jnp.concatenate([sel[:, 0:LANES], sel[:, (rows - 1) * LANES : rows * LANES], border_sel[...]], axis=1)
    both[...] += dot(border_cells, extra[...], (1, 1))

    def weigh(block, _):
        at = pl.ds(pl.multiple_of(block * LANES, LANES), LANES)
        sources = LANES // cap
        ops = [
            jnp.concatenate(
                [records[block * sources + s, half * cap : (half + 1) * cap, :] for s in range(sources)], axis=0
            )
            for half in range(halves)
        ]
        total = sum(
            (both[at, half * LANES : (half + 1) * LANES] + both[at, width + half * LANES : width + (half + 1) * LANES])
            * ops[half]
            for half in range(halves)
        )
        innovation = jnp.sum(total, axis=1, keepdims=True) * precs[at, :]
        for half in range(halves):
            high, low = split((ops[half] * innovation).T, 2)
            spread[half * LANES : (half + 1) * LANES, at] = high
            spread[width + half * LANES : width + (half + 1) * LANES, at] = low
        return 0

    lax.fori_loop(0, count // LANES, weigh, 0, unroll=4)

    terms = dot(spread[...], border_cells, (1, 0))
    border_sums = terms[:width] + terms[width:]
    thin = border_sums[:, 2 * LANES :]
    dense = []
    for m in range(width // (GROUP * PARTS)):
        total = thin[m * PARTS * GROUP : (m * PARTS + 1) * GROUP]
        for part in range(1, PARTS):
            at = (m * PARTS + part) * GROUP
            total = total + pltpu.roll(thin[at : at + GROUP], 2 * part, 1)
        dense.append(total)
    ends = (border_sums[:, 0:LANES], border_sums[:, LANES : 2 * LANES])
    packed[packed.shape[0] - GROUP :, :] = jnp.zeros((GROUP, LANES), jnp.float32)
    put_strip(strips, slice(width, width + GROUP), *[jnp.zeros((GROUP, LANES), jnp.float32)] * 2)
    border_strips(
        rows, width // 2, coupling, ends, jnp.concatenate(dense, axis=0), wind_ends, wind_dense, dense_g, strips, packed
    )


def scatter_kernel(rows, width, spread, sel, winds, adjoint, low0, wind_rows, sems):
    wind_in = Rows(winds, wind_rows, sems, rows, True, 1)
    start_rows(rows, wind_in)
    wind_rows[0] = jnp.zeros_like(wind_rows[0])
    wind_rows[rows + 1] = jnp.zeros_like(wind_rows[0])
    sums = dot(spread[...], sel[...], (1, 0))
    for i in range(rows):
        lanes = slice(i * LANES, (i + 1) * LANES)
        adjoint[i] = sums[:width, lanes] + sums[width:, lanes]
        for f in range(2):
            low0[f * rows + i : f * rows + i + 1, :] = adjoint[i, f * (width // 2) : f * (width // 2) + 1, :]
    for i in range(rows):
        wind_in.wait(i)


def local(state_incr, winds, coupling, background, obs_dest, obs_col, obs_op, obs_prec):
    _, fields, levels, rows, lanes = state_incr.shape
    width = fields * levels
    groups = width // GROUP
    tiles = lax.axis_size("gx") * lax.axis_size("gy")
    count = obs_col.shape[0]
    cap = 2 * count // tiles
    halves = obs_op.shape[1] // LANES

    scale = jnp.broadcast_to(background.reshape(width, 1), (width, LANES))

    vmem = pl.BlockSpec(memory_space=pltpu.VMEM)
    anywhere = pl.BlockSpec(memory_space=pl.ANY)
    own = pltpu.VMEM((rows, width, LANES), jnp.float32)
    framed = pltpu.VMEM((rows + 2, width, LANES), jnp.float32)
    packed_shape = f32(groups // PARTS * GROUP, LANES)
    sides = pltpu.VMEM(packed_shape.shape, jnp.float32)
    strip_shapes = [f32(pair_sets(), width, LANES), packed_shape]
    long_shapes = [f32(pair_sets(), width + GROUP, LANES), f32(packed_shape.shape[0] + GROUP, LANES)]
    field_shape = f32(rows, width, LANES)
    framed_shape = f32(rows + 2, width, LANES)
    low_shape = f32(fields * rows, LANES)
    cols_shape = ((2 * width, rows * LANES), jnp.bfloat16)

    def sems(*shape):
        return pltpu.SemaphoreType.DMA(shape)

    def run(body, out_shape, scratch, args, far=(), out_far=(), **kw):
        args = [pltpu.with_memory_space_constraint(x, pltpu.HBM) if k in far else x for k, x in enumerate(args)]
        specs = [anywhere if k in far else vmem for k in range(len(args))]
        outs = [anywhere if k in out_far else vmem for k in range(len(out_shape))]
        out_shape = [pltpu.HBM(x.shape, x.dtype) if k in out_far else x for k, x in enumerate(out_shape)]
        return call(body, out_shape, scratch, in_specs=specs, out_specs=outs, **kw)(*args)

    def on_rows(body):
        return functools.partial(body, rows, levels)

    def swap_floor(floor):
        return lax.ppermute(floor, "comp", [(0, 1), (1, 0)])

    state = state_incr.reshape(width, rows, lanes)
    wind = winds.reshape(width, rows, lanes)
    floor_winds = winds[0, :, 0]
    slots = tiles * cap
    thin_shape = f32(GROUP, LANES)

    strips, packed, low0, low1 = run(
        on_rows(edges_kernel),
        strip_shapes + [low_shape] * 2,
        [pltpu.VMEM((width * rows, LANES), jnp.float32), sems(groups // PARTS)],
        (state_incr.reshape(width * rows, lanes),),
        far=(0,),
    )
    halos = exchange(strips, packed)

    send = call(functools.partial(route_kernel, tiles, cap), f32(tiles, halves * cap + GROUP, LANES))(
        obs_dest.reshape(1, count), obs_col.reshape(1, count), obs_prec.reshape(1, count), obs_op
    )
    send, halos[0], halos[2], state_far, wind_far = lax.optimization_barrier((send, halos[0], halos[2], state, wind))
    records = lax.all_to_all(send, ("gx", "gy"), split_axis=0, concat_axis=0, tiled=True)

    state_rows, wind_rows = run(
        functools.partial(load_kernel, rows),
        [field_shape, field_shape],
        [sems(2, rows)],
        (state_far, wind_far),
        far=(0, 1),
        traffic=10 * MIB,
    )
    halos[1], state_rows, wind_rows = lax.optimization_barrier((halos[1], state_rows, wind_rows))
    (floor,) = run(on_rows(forward_floor_kernel), [low_shape], [], (low0, low1, floor_winds, *halos))
    field, strips, packed, low0, low1, wind_ends, wind_dense, dense_g = run(
        on_rows(forward_kernel),
        [framed_shape]
        + long_shapes
        + [low_shape] * 2
        + [f32(2, levels, LANES), f32(groups // PARTS * GROUP // 2, LANES), thin_shape],
        [framed, sides],
        (coupling, swap_floor(floor), state_rows, wind_rows, *halos),
    )
    halos = exchange(strips, packed)
    (cols,) = run(
        on_rows(forward_again_kernel),
        [jax.ShapeDtypeStruct(*cols_shape)],
        [pltpu.VMEM(*cols_shape), sems(rows)],
        (field, wind_rows),
        out_far=(0,),
        traffic=20 * MIB,
    )
    cols, halos = lax.optimization_barrier((cols, halos))
    (floor,) = run(on_rows(forward_floor_kernel), [low_shape], [], (low0, low1, floor_winds, *halos))
    extra, bottom = run(
        on_rows(outside_kernel),
        [jax.ShapeDtypeStruct((2 * width, 3 * LANES), jnp.bfloat16), low_shape],
        [sides],
        (coupling, floor, swap_floor(floor), wind_ends, wind_dense, *halos),
    )

    spread_shape = ((2 * width, slots), jnp.bfloat16)
    sel_shape = ((slots, rows * LANES), jnp.bfloat16)
    spread, sel, strips, packed = run(
        functools.partial(innovate_kernel, rows, width, tiles, cap),
        [jax.ShapeDtypeStruct(*spread_shape), jax.ShapeDtypeStruct(*sel_shape)] + long_shapes,
        [
            pltpu.VMEM(*cols_shape),
            pltpu.VMEM((slots, LANES), jnp.bfloat16),
            pltpu.VMEM((slots, LANES), jnp.float32),
            pltpu.VMEM((slots, 2 * width), jnp.float32),
            sems(8),
        ],
        (records, cols, extra, bottom, coupling, wind_ends, wind_dense, dense_g),
        far=(1,),
        limit=OBSERVE_VMEM,
    )
    factors = halos
    halos = exchange(strips, packed)
    adjoint, low0, wind_rows = run(
        functools.partial(scatter_kernel, rows, width),
        [field_shape, low_shape, framed_shape],
        [sems(rows)],
        (spread, sel, wind),
        far=(2,),
        limit=OBSERVE_VMEM,
        traffic=8 * MIB,
    )
    low0, halos = lax.optimization_barrier((low0, halos))
    (raw,) = run(on_rows(beside_kernel), [thin_shape], [], halos)
    partner, raw = swap_floor(low0), swap_floor(raw)
    adjoint, ends, columns, low0, state_rows = run(
        on_rows(first_adjoint_kernel),
        [field_shape, f32(2, width, LANES), packed_shape, low_shape, field_shape],
        [framed, sems(rows)],
        (coupling, adjoint, wind_rows, state),
        far=(3,),
        traffic=16 * MIB,
    )
    low0, partner, raw = lax.optimization_barrier((low0, partner, raw))
    floor, missing = run(
        on_rows(floor_kernel),
        [low_shape, low_shape],
        [],
        (coupling, partner, low0, raw, floor_winds, *halos, *factors),
    )
    other = swap_floor(floor)
    strips, packed = run(
        on_rows(border_again_kernel),
        strip_shapes,
        [sides],
        (coupling, floor, other, missing, ends, columns, wind_ends, wind_dense, dense_g, *halos),
    )
    last_halos = exchange(strips, packed)
    (adjoint,) = run(
        on_rows(second_adjoint_kernel),
        [field_shape],
        [framed, sides],
        (coupling, floor, other, missing, adjoint, wind_rows, scale, state_rows, *halos),
        traffic=20 * MIB,
    )
    (result,) = run(
        on_rows(final_kernel),
        [f32(width, rows, LANES)],
        [own, sides, sems(rows)],
        (adjoint, *last_halos),
        out_far=(0,),
    )
    return result.reshape(state_incr.shape)


def solution(mesh):
    placed = (
        P("comp", None, None, "gx", "gy"),
        P("comp", None, None, "gx", "gy"),
        P("gx", "gy"),
        P("comp", None, None),
        P(("comp", "gx", "gy"), None),
        P(("comp", "gx", "gy")),
        P(("comp", "gx", "gy"), None),
        P(("comp", "gx", "gy")),
    )
    return jax.shard_map(
        local,
        mesh=mesh,
        in_specs=placed,
        out_specs=P("comp", None, None, "gx", "gy"),
        check_vma=False,
    )
```

```python
import functools

import jax
import jax.numpy as jnp
from jax import lax
from jax.experimental import pallas as pl
from jax.experimental.pallas import tpu as pltpu
from jax.sharding import PartitionSpec as P

HORIZ_MIX = 0.1
VERT_MIX = 0.15
LANES = 128
GROUP = 8
MIB = 1024 * 1024
SWEEP_VMEM = 16 * MIB
OBSERVE_VMEM = 22 * MIB


def call(body, out_shape, scratch=(), limit=SWEEP_VMEM, traffic=0, **kw):
    cost = pl.CostEstimate(flops=0, bytes_accessed=traffic, transcendentals=0) if traffic else None
    return pl.pallas_call(
        body,
        out_shape=out_shape,
        scratch_shapes=list(scratch),
        cost_estimate=cost,
        compiler_params=pltpu.CompilerParams(vmem_limit_bytes=limit),
        **kw,
    )


def f32(*shape):
    return jax.ShapeDtypeStruct(shape, jnp.float32)


def lane_iota(rows=GROUP):
    return lax.broadcasted_iota(jnp.int32, (rows, LANES), 1)


def sub_iota(rows=GROUP):
    return lax.broadcasted_iota(jnp.int32, (rows, LANES), 0)


def pair_swap(block, axis, start):
    count = lax.axis_size(axis)
    route = []
    for low in range(start, count - 1, 2):
        route += [(low, low + 1), (low + 1, low)]
    return lax.ppermute(block, axis, route)


def pair_sets():
    return 2 if lax.axis_size("gx") > 2 else 1


def exchange(strips, packed):
    y_even = pair_swap(packed, "gy", 0)
    y_odd = pair_swap(packed, "gy", 1)
    even, *odd = [pair_swap(strips[start], "gx", start) for start in range(pair_sets())]
    return [even, y_even, y_odd, *odd]


def is_odd(axis):
    return lax.rem(lax.axis_index(axis), 2) == 1


def read_sides(refs):
    even = refs[0]
    odd = refs[3] if len(refs) > 3 else None
    at_odd = is_odd("gx")

    def side(at, turned):
        other = jnp.zeros_like(even[at]) if odd is None else odd[at]
        return jnp.where(turned, other, even[at])

    return lambda at: side(at, jnp.logical_not(at_odd)), lambda at: side(at, at_odd)


PARTS = 4


def merged(y_even, y_odd, at):
    a, b = y_even[at, :], y_odd[at, :]
    lane = lax.broadcasted_iota(jnp.int32, a.shape, 1)
    return jnp.where((lane % 2 == 1) == jnp.logical_not(is_odd("gy")), a, b)


def merge_columns(y_even, y_odd, sides):
    sides[...] = merged(y_even, y_odd, slice(0, sides.shape[0]))


def slot_of(i, part, rows):
    return PARTS * (rows - 1 - i) + part


def side_columns(sides, i, group):
    m, part = group // PARTS, group % PARTS
    rows = LANES // (2 * PARTS)
    return pltpu.roll(sides[m * GROUP : (m + 1) * GROUP, :], LANES - 1 - 2 * slot_of(i, part, rows), 1)


def pack_into(total, value, slot):
    return jnp.where(lane_iota() // 2 == slot, pltpu.roll(value, 2 * slot + 1, 1), total)


def pack_block(packed, values, i, m):
    at = pl.ds(m * GROUP, GROUP)
    total = packed[at, :]
    for part, value in enumerate(values):
        total = pack_into(total, value, slot_of(i, part, LANES // (2 * PARTS)))
    packed[at, :] = total


CENTRE = 1.0 - 4.0 * HORIZ_MIX - 2.0 * VERT_MIX


def levels_around(cells, i, base, group, groups):
    here = cells[i + 1, pl.ds(base + group * GROUP, GROUP), :]
    if group == groups - 1:
        upper = jnp.where(sub_iota() == GROUP - 1, here, pltpu.roll(here, GROUP - 1, 0))
    else:
        upper = cells[i + 1, pl.ds(base + group * GROUP + 1, GROUP), :]
    if group == 0:
        lower = jnp.where(sub_iota() == 0, here, pltpu.roll(here, 1, 0))
    else:
        lower = cells[i + 1, pl.ds(base + group * GROUP - 1, GROUP), :]
    return here, upper, lower


def shifted(first, last, edge, rows=GROUP):
    lane = lane_iota(rows)
    right = pltpu.roll(jnp.where(lane == 0, edge, first), LANES - 1, 1)
    left = pltpu.roll(jnp.where(lane == LANES - 1, edge, last), 1, 1)
    return right, left


def forward_sum(here, vertical, after, before, right, left, u, w):
    return (
        CENTRE * here
        + VERT_MIX * vertical
        + HORIZ_MIX * ((after + before) + (right + left))
        - 0.5 * (u * (after - before) + w * (right - left))
    )


def forward_point(cells, winds, sides, i, f, group, levels):
    groups = levels // GROUP
    here, upper, lower = levels_around(cells, i, f * levels, group, groups)
    at = pl.ds(f * levels + group * GROUP, GROUP)
    right, left = shifted(here, here, 0.0 if sides is None else side_columns(sides, i, f * groups + group))
    u = winds[i, pl.ds(group * GROUP, GROUP), :]
    w = winds[i, pl.ds(levels + group * GROUP, GROUP), :]
    return forward_sum(here, upper + lower, cells[i + 2, at, :], cells[i, at, :], right, left, u, w)


def products(x, wind):
    slope = 0.5 * (wind * x)
    return HORIZ_MIX * x - slope, HORIZ_MIX * x + slope


def adjoint_point(cells, winds, i, f, group, levels):
    here, upper, lower = levels_around(cells, i, f * levels, group, levels // GROUP)
    at = pl.ds(f * levels + group * GROUP, GROUP)
    wind_at = pl.ds(group * GROUP, GROUP)
    after, before = cells[i + 2, at, :], cells[i, at, :]
    u_after, u_before = winds[i + 2, wind_at, :], winds[i, wind_at, :]
    down, up = products(here, winds[i + 1, pl.ds(levels + group * GROUP, GROUP), :])
    right, left = shifted(up, down, 0.0)
    return (
        CENTRE * here
        + VERT_MIX * (upper + lower)
        + HORIZ_MIX * (after + before)
        + 0.5 * (u_after * after - u_before * before)
        + (right + left)
    )


def shares_of(coupling):
    own = jnp.where(lax.axis_index("comp") == 0, 1.0, 0.5)
    return own * coupling, (1.5 - own) * coupling


def couple_forward(value, other, coupling):
    own, _ = shares_of(coupling)
    return value - own * (value - other)


def couple_adjoint(value, other, coupling):
    own, peer = shares_of(coupling)
    return value - own * value + peer * other


def coupled(rule, value, other, coupling, i, f, rows):
    mixed = rule(value, other[pl.ds(f * rows + i, 1), :], coupling[pl.ds(i, 1), :])
    return jnp.where(sub_iota() == 0, mixed, value)


def put_strip(strips, at, first, last):
    at_odd = is_odd("gx")
    strips[0, at, :] = jnp.where(at_odd, first, last)
    if strips.shape[0] > 1:
        strips[1, at, :] = jnp.where(at_odd, last, first)


def put_low(low, value, i, f, rows):
    for level in range(2):
        low[level][pl.ds(f * rows + i, 1), :] = value[level : level + 1]


class Rows:
    def __init__(self, source, target, sems, rows, as_it_comes, offset):
        self.source, self.target, self.sems = source, target, sems
        self.rows, self.as_it_comes, self.offset = rows, as_it_comes, offset

    def copy(self, i):
        row = self.source.at[:, i] if self.as_it_comes else self.source.at[i]
        return pltpu.make_async_copy(row, self.target.at[i + self.offset], self.sems.at[i])

    def wait(self, i):
        self.copy(i).wait()


def start_rows(rows, *groups):
    for i in range(rows):
        for group in groups:
            group.copy(i).start()


def edges_kernel(rows, levels, state, strips, packed, low0, low1, cells, sems):
    part_levels = PARTS * GROUP
    blocks = 2 * levels // part_levels

    def copy(m):
        return pltpu.make_async_copy(
            state.at[pl.ds(m * part_levels * rows, part_levels * rows)],
            cells.at[pl.ds(m * part_levels * rows, part_levels * rows)],
            sems.at[m],
        )

    for m in range(blocks):
        copy(m).start()

    def block(m, _):
        copy(m).wait()
        total = jnp.zeros((GROUP, LANES), jnp.float32)
        for part in range(PARTS):
            for i in range(rows):
                start = (m * PARTS + part) * GROUP * rows + i
                total = pack_into(total, cells[pl.ds(start, GROUP, stride=rows), :], slot_of(i, part, rows))
        packed[pl.ds(pl.multiple_of(m * GROUP, GROUP), GROUP), :] = total
        start = m * part_levels * rows
        first = cells[pl.ds(start, part_levels, stride=rows), :]
        last = cells[pl.ds(start + rows - 1, part_levels, stride=rows), :]
        put_strip(strips, pl.ds(pl.multiple_of(m * part_levels, part_levels), part_levels), first, last)
        return 0

    lax.fori_loop(0, blocks, block, 0)
    for f in range(2):
        for level, low in enumerate((low0, low1)):
            low[f * rows : (f + 1) * rows, :] = cells[pl.ds((f * levels + level) * rows, rows), :]


def floor_edge(halos, f, rows, levels):
    m = f * (levels // GROUP) // PARTS
    sides = jnp.broadcast_to(merged(halos[1], halos[2], pl.ds(m * GROUP, 1)), (rows, LANES))
    return pltpu.roll(sides, 2 * PARTS - 1, 1, stride=2 * PARTS, stride_axis=0)


def row_after(value, last, rows):
    return jnp.where(sub_iota(rows) == rows - 1, last, pltpu.roll(value, rows - 1, 0))


def row_before(value, first, rows):
    return jnp.where(sub_iota(rows) == 0, first, pltpu.roll(value, 1, 0))


def forward_floor_kernel(rows, levels, low0, low1, winds, *rest):
    *halos, floor = rest
    side_before, side_after = read_sides(halos)
    for f in range(2):
        here = pl.ds(f * rows, rows)
        at = pl.ds(f * levels, 1)
        low, up = low0[here, :], low1[here, :]
        after, before = row_after(low, side_after(at), rows), row_before(low, side_before(at), rows)
        right, left = shifted(low, low, floor_edge(halos, f, rows, levels), rows)
        floor[here, :] = forward_sum(low, up + low, after, before, right, left, winds[0], winds[1])


class Out:
    def __init__(self, source, target, sems, rows, as_it_goes):
        self.source, self.target, self.sems, self.rows, self.as_it_goes = source, target, sems, rows, as_it_goes

    def copy(self, i):
        row = self.target.at[:, i] if self.as_it_goes else self.target.at[i]
        return pltpu.make_async_copy(self.source.at[i], row, self.sems.at[i])

    def start(self, i):
        self.copy(i).start()

    def finish(self):
        for i in range(self.rows):
            self.copy(i).wait()


def dense_row(field, first, rows):
    total = jnp.zeros((1, LANES), jnp.float32)
    lane = lax.broadcasted_iota(jnp.int32, (1, LANES), 1)
    for i in range(rows):
        slot = slot_of(i, 0, rows)
        total = jnp.where(lane // 2 == slot, pltpu.roll(field[first + i : first + i + 1, :], 2 * slot + 1, 1), total)
    return total


def load_kernel(rows, state, winds, state_rows, wind_rows, state_later, wind_later, sems):
    state_in = Rows(state, state_rows, sems.at[0], rows, True, 0)
    wind_in = Rows(winds, wind_rows, sems.at[1], rows, True, 0)
    state_out = Out(state_rows, state_later, sems.at[2], rows, False)
    wind_out = Out(wind_rows, wind_later, sems.at[3], rows, False)
    start_rows(rows, state_in, wind_in)
    for i in range(rows):
        state_in.wait(i)
        wind_in.wait(i)
        state_out.start(i)
        wind_out.start(i)
    state_out.finish()
    wind_out.finish()


def forward_kernel(rows, levels, coupling, other, field, winds, *rest):
    *halos, out, strips, packed, low0, low1, wind_ends, wind_dense, dense_g, cells, sides = rest
    packed[...] = jnp.zeros_like(packed)
    wind_dense[...] = jnp.zeros_like(wind_dense)
    merge_columns(halos[1], halos[2], sides)
    before, after = read_sides(halos)
    cells[0] = before(pl.ds(0, 2 * levels))
    cells[1] = field[0]
    cells[rows + 1] = after(pl.ds(0, 2 * levels))
    out[0] = jnp.zeros_like(out[0])
    out[rows + 1] = jnp.zeros_like(out[0])
    groups = levels // GROUP

    def row(i, _):
        @pl.when(i < rows - 1)
        def _():
            cells[i + 2] = field[i + 1]

        for m in range(2 * groups // PARTS):
            f, start = m * PARTS // groups, m * PARTS % groups
            values = []
            for group in range(start, start + PARTS):
                value = forward_point(cells, winds, sides, i, f, group, levels)
                if group == 0:
                    value = coupled(couple_forward, value, other, coupling, i, f, rows)
                    put_low((low0, low1), value, i, f, rows)
                values.append(value)
            base = m * PARTS * GROUP
            for part, value in enumerate(values):
                out[i + 1, pl.ds(base + part * GROUP, GROUP), :] = value
            pack_block(packed, values, i, m)
            if f == 0:
                w = [winds[i, pl.ds(levels + base + part * GROUP, GROUP), :] for part in range(PARTS)]
                pack_block(wind_dense, w, i, m)
        return 0

    lax.fori_loop(0, rows, row, 0)
    put_strip(strips, pl.ds(0, 2 * levels), out[1], out[rows])
    wind_ends[0] = winds[0, pl.ds(0, levels), :]
    wind_ends[1] = winds[rows - 1, pl.ds(0, levels), :]
    dense_g[...] = jnp.broadcast_to(dense_row(coupling, 0, rows), dense_g.shape)
    _, peer = shares_of(coupling[...])
    first = products(peer[0:1], winds[0, 0:1, :])[1]
    last = products(peer[rows - 1 : rows], winds[rows - 1, 0:1, :])[0]
    whole = (GROUP, LANES)
    put_strip(strips, slice(2 * levels, 2 * levels + GROUP), jnp.broadcast_to(first, whole), jnp.broadcast_to(last, whole))
    _, peer = shares_of(dense_g[...])
    packed[packed.shape[0] - GROUP :, :] = first_and_last(peer, wind_dense[0:1, :])


def forward_again_kernel(rows, levels, cells, winds, cols, col_cells, col_sems):
    groups = levels // GROUP
    width = 2 * levels

    def col_copy(i):
        lanes = pl.ds(pl.multiple_of(i * LANES, LANES), LANES)
        return pltpu.make_async_copy(col_cells.at[:, lanes], cols.at[:, lanes], col_sems.at[i])

    def row(i, _):
        lanes = pl.ds(pl.multiple_of(i * LANES, LANES), LANES)
        for m in range(2 * groups // PARTS):
            f, start = m * PARTS // groups, m * PARTS % groups
            values = [forward_point(cells, winds, None, i, f, group, levels) for group in range(start, start + PARTS)]
            high, low = split(jnp.concatenate(values, axis=0), 2)
            col_cells[pl.ds(m * PARTS * GROUP, PARTS * GROUP), lanes] = high
            col_cells[pl.ds(width + m * PARTS * GROUP, PARTS * GROUP), lanes] = low
        col_copy(i).start()
        return 0

    lax.fori_loop(0, rows, row, 0)
    for i in range(rows):
        col_copy(i).wait()


def outside_kernel(rows, levels, coupling, floor, other, wind_ends, wind_dense, *rest):
    *halos, extra, bottom, factors, dense = rest
    width = 2 * levels
    tail = pl.ds(width, 1)
    factors[...] = jnp.zeros_like(factors)
    for k, side in enumerate(read_sides(halos)):
        factors[k : k + 1, :] = side(tail)
    factors[2:3, :] = merged(halos[1], halos[2], pl.ds(dense.shape[0], 1))
    for f in range(2):
        here = pl.ds(f * rows, rows)
        bottom[here, :] = couple_forward(floor[here, :], other[here, :], coupling[...])
    dense_products(dense, swap_pairs(merged(halos[1], halos[2], slice(0, dense.shape[0]))), wind_dense)
    before, after = read_sides(halos)
    sub = lax.broadcasted_iota(jnp.int32, (levels, LANES), 0)

    def put(value, f, lanes):
        high, low = split(jnp.where(sub == 0, 0.0, value), 2)
        extra[f * levels : (f + 1) * levels, lanes] = high
        extra[width + f * levels : width + (f + 1) * levels, lanes] = low

    lane = lane_iota()
    for f in range(2):
        at = pl.ds(f * levels, levels)
        put(products(before(at), wind_ends[0])[1], f, slice(0, LANES))
        put(products(after(at), wind_ends[1])[0], f, slice(LANES, 2 * LANES))
        thin = []
        for group in range(f * levels // GROUP, (f + 1) * levels // GROUP):
            m, part = group // PARTS, group % PARTS
            moved = pltpu.roll(dense[m * GROUP : (m + 1) * GROUP, :], (LANES - 2 * part) % LANES, 1)
            thin.append(jnp.where(lane % (2 * PARTS) < 2, moved, 0.0))
        put(jnp.concatenate(thin, axis=0), f, slice(2 * LANES, 3 * LANES))


def first_and_last(value, wind):
    down, up = products(value, wind)
    lane = lax.broadcasted_iota(jnp.int32, down.shape, 1)
    return jnp.where(lane % 2 == 1, up, down)


def dense_products(packed, value, wind_dense):
    half = wind_dense.shape[0]
    for f in range(2):
        at = slice(f * half, (f + 1) * half)
        packed[at, :] = first_and_last(value[at], wind_dense[...])


def level0_row(value, new, f):
    half = value.shape[0] // 2
    sub = lax.broadcasted_iota(jnp.int32, value.shape, 0)
    lane = lax.broadcasted_iota(jnp.int32, value.shape, 1)
    return jnp.where((sub == f * half) & (lane % (2 * PARTS) < 2), new, value)


def end_rows(ends, strips, wind_ends, levels):
    for f in range(2):
        at = slice(f * levels, (f + 1) * levels)
        put_strip(
            strips, at, products(ends[0][at], wind_ends[0])[1], products(ends[1][at], wind_ends[1])[0]
        )


def with_first(value, new):
    return jnp.where(lax.broadcasted_iota(jnp.int32, value.shape, 0) == 0, new, value)


def border_strips(rows, levels, coupling, ends, dense, wind_ends, wind_dense, dense_g, strips, packed):
    half = dense.shape[0] // 2
    width = 2 * levels
    own, _ = shares_of(dense_g[0:1, :])
    new = dense
    for f in range(2):
        bottom = dense[f * half : f * half + 1]
        new = level0_row(new, bottom - own * bottom, f)
        packed[2 * half + f : 2 * half + f + 1, :] = bottom
    dense_products(packed, new, wind_dense)
    full = []
    for k, i in enumerate((0, rows - 1)):
        own, _ = shares_of(coupling[i : i + 1, :])
        parts = []
        for f in range(2):
            value = ends[k][f * levels : (f + 1) * levels]
            parts.append(with_first(value, value[0:1] - own * value[0:1]))
        full.append(jnp.concatenate(parts, axis=0))
    end_rows(full, strips, wind_ends, levels)
    for f in range(2):
        at = f * levels
        put_strip(strips, slice(width + f, width + f + 1), ends[0][at : at + 1], ends[1][at : at + 1])


def to_border(low, before, after, sides, rows):
    sub, lane = sub_iota(rows), lane_iota(rows)
    low = low + jnp.where(sub == 0, before, 0.0) + jnp.where(sub == rows - 1, after, 0.0)
    edge = pltpu.roll(jnp.broadcast_to(sides, (rows, LANES)), 2 * PARTS - 1, 1, stride=2 * PARTS, stride_axis=0)
    edge = jnp.where(lane == 0, pltpu.roll(edge, 1, 1), pltpu.roll(edge, LANES - 1, 1))
    return low + jnp.where((lane == 0) | (lane == LANES - 1), edge, 0.0)


def floor_kernel(rows, levels, coupling, other, low0, winds, *rest):
    *halos, floor, missing = rest
    before, after = read_sides(halos)
    half = halos[1].shape[0] - GROUP
    for f in range(2):
        here = pl.ds(f * rows, rows)
        _, peer = shares_of(coupling[...])
        share = peer * other[here, :]
        x_down, x_up = products(share, winds[0])
        y_down, y_up = products(share, winds[1])
        right, left = shifted(y_up, y_down, 0.0, rows)
        spread = (row_after(x_up, 0.0, rows) + row_before(x_down, 0.0, rows)) + (right + left)
        spread = spread + (CENTRE + VERT_MIX) * share
        at = pl.ds(f * levels, 1)
        sides = merged(halos[1], halos[2], pl.ds(f * half // 2, 1))
        floor[here, :] = to_border(low0[here, :] + spread, before(at), after(at), sides, rows)
        missing[here, :] = VERT_MIX * share
    raw = 2 * rows
    floor[raw : raw + 2, :] = before(pl.ds(2 * levels, 2))
    floor[raw + 2 : raw + 4, :] = after(pl.ds(2 * levels, 2))
    floor[raw + 4 : raw + 6, :] = merged(halos[1], halos[2], pl.ds(half, 2))
    floor[raw + 6 : raw + GROUP, :] = jnp.zeros((2, LANES), jnp.float32)


def level0_kernel(rows, levels, floor, other, factors, partner, floor_out, other_out):
    raw = 2 * rows
    for mine, theirs, factor, at, out in ((floor, other, factors, 0, floor_out), (other, floor, partner, raw, other_out)):
        for f in range(2):
            here = pl.ds(f * rows, rows)
            parts = [factor[at + k : at + k + 1, :] * theirs[raw + 2 * k + f : raw + 2 * k + f + 1, :] for k in range(3)]
            out[here, :] = to_border(mine[here, :], *parts, rows)


def swap_pairs(value):
    lane = lax.broadcasted_iota(jnp.int32, value.shape, 1)
    return jnp.where(lane % 2 == 1, pltpu.roll(value, 1, 1), pltpu.roll(value, LANES - 1, 1))


def edge_lanes(sides, i, group):
    m, part = group // PARTS, group % PARTS
    rows = LANES // (2 * PARTS)
    moved = pltpu.roll(sides[m * GROUP : (m + 1) * GROUP, :], LANES - 1 - 2 * slot_of(i, part, rows), 1)
    lane = lane_iota()
    return jnp.where((lane == 0) | (lane == LANES - 1), moved, 0.0)


def with_level(value, level, new):
    return jnp.where(lax.broadcasted_iota(jnp.int32, value.shape, 0) == level, new, value)


def border_again_kernel(
    rows, levels, coupling, floor, other, missing, ends, columns, wind_ends, wind_dense, dense_g, *rest
):
    *halos, strips, packed, sides = rest
    before, after = read_sides(halos)
    sides[...] = swap_pairs(merged(halos[1], halos[2], slice(0, sides.shape[0])))
    half = columns.shape[0] // 2
    groups = levels // GROUP
    outer = [before(pl.ds(0, 2 * levels)), after(pl.ds(0, 2 * levels))]
    full = []
    for k, i in enumerate((0, rows - 1)):
        edges = jnp.concatenate([edge_lanes(sides, i, group) for group in range(2 * groups)], axis=0)
        value = ends[k] + outer[k] + edges
        parts = []
        for f in range(2):
            part = value[f * levels : (f + 1) * levels]
            at = slice(f * rows + i, f * rows + i + 1)
            part = part + with_level(jnp.zeros_like(part), 1, missing[at, :])
            parts.append(with_first(part, couple_adjoint(floor[at, :], other[at, :], coupling[i : i + 1, :])))
        full.append(jnp.concatenate(parts, axis=0))
    end_rows(full, strips, wind_ends, levels)
    dense = columns[...] + sides[...]
    corners = []
    for m in range(2 * groups // PARTS):
        total = jnp.zeros((GROUP, LANES), jnp.float32)
        for part in range(PARTS):
            at = slice((m * PARTS + part) * GROUP, (m * PARTS + part + 1) * GROUP)
            for k, i in enumerate((0, rows - 1)):
                total = pack_into(total, outer[k][at], slot_of(i, part, rows))
        corners.append(total)
    dense = dense + jnp.concatenate(corners, axis=0)
    for f in range(2):
        sub = lax.broadcasted_iota(jnp.int32, dense.shape, 0)
        dense = dense + jnp.where(sub == f * half + 1, dense_row(missing, f * rows, rows), 0.0)
        mine = dense_row(floor, f * rows, rows)
        mixed = couple_adjoint(mine, dense_row(other, f * rows, rows), dense_g[0:1, :])
        dense = level0_row(dense, mixed, f)
    dense_products(packed, dense, wind_dense)


def adjoint_rows(rows, levels, cells, winds, take, each):
    groups = levels // GROUP
    cells[0] = jnp.zeros_like(cells[0])
    cells[rows + 1] = jnp.zeros_like(cells[0])
    take(0)

    def row(i, _):
        @pl.when(i < rows - 1)
        def _():
            take(i + 1)

        for m in range(2 * groups // PARTS):
            f, start = m * PARTS // groups, m * PARTS % groups
            each(i, m, f, start, [
                adjoint_point(cells, winds, i, f, group, levels) for group in range(start, start + PARTS)
            ])
        return 0

    lax.fori_loop(0, rows, row, 0)


def first_adjoint_kernel(rows, levels, coupling, field, winds, state, out, ends, columns, low0, state_rows, cells, sems):
    state_in = pltpu.make_async_copy(state, state_rows, sems.at[0])
    state_in.start()
    columns[...] = jnp.zeros_like(columns)

    def take(i):
        cells[i + 1] = field[i]
        for f in range(2):
            at = pl.ds(f * levels, GROUP)
            own, _ = shares_of(coupling[pl.ds(i, 1), :])
            value = field[i, at, :]
            cells[i + 1, at, :] = jnp.where(sub_iota() == 0, value - own * value, value)

    def each(i, m, f, start, values):
        for part, value in enumerate(values):
            out[i, pl.ds((m * PARTS + part) * GROUP, GROUP), :] = value
        if start == 0:
            low0[pl.ds(f * rows + i, 1), :] = values[0][0:1]
        pack_block(columns, values, i, m)

    adjoint_rows(rows, levels, cells, winds, take, each)
    ends[0] = out[0]
    ends[1] = out[rows - 1]
    state_in.wait()


def second_adjoint_kernel(rows, levels, coupling, floor, other, missing, field, winds, scale, state, *rest):
    *halos, out, cells, sides = rest
    sides[...] = swap_pairs(merged(halos[1], halos[2], slice(0, sides.shape[0])))
    before, after = read_sides(halos)
    groups = levels // GROUP

    def take(i):
        for group in range(2 * groups):
            at = pl.ds(group * GROUP, GROUP)
            value = field[i, at, :] + edge_lanes(sides, i, group)
            if group % groups == 0:
                value = value + jnp.where(i == 0, before(at), 0.0) + jnp.where(i == rows - 1, after(at), 0.0)
                here = pl.ds(group // groups * rows + i, 1)
                value = value + jnp.where(sub_iota() == 1, missing[here, :], 0.0)
                bottom = couple_adjoint(floor[here, :], other[here, :], coupling[pl.ds(i, 1), :])
                value = jnp.where(sub_iota() == 0, bottom, value)
            cells[i + 1, at, :] = value

    def add_outer(i, side):
        for f in range(2):
            at = pl.ds(f * levels + GROUP, levels - GROUP)
            cells[i + 1, at, :] = cells[i + 1, at, :] + side(at)

    def take_all(i):
        take(i)

        @pl.when(i == 0)
        def _():
            add_outer(0, before)

        @pl.when(i == rows - 1)
        def _():
            add_outer(rows - 1, after)

    def each(i, m, f, start, values):
        for part, value in enumerate(values):
            at = pl.ds((m * PARTS + part) * GROUP, GROUP)
            out[i, at, :] = value + scale[at, :] * state[i, at, :]

    adjoint_rows(rows, levels, cells, winds, take_all, each)


def final_kernel(rows, levels, field, *rest):
    *halos, out, cells, sides, sems = rest
    leaving = Out(cells, out, sems, rows, True)
    sides[...] = swap_pairs(merged(halos[1], halos[2], slice(0, sides.shape[0])))
    before, after = read_sides(halos)
    groups = levels // GROUP

    def add(i, outer):
        for group in range(2 * groups):
            at = pl.ds(group * GROUP, GROUP)
            value = field[i, at, :] + edge_lanes(sides, i, group)
            cells[i, at, :] = value if outer is None else value + outer(at)
        leaving.start(i)
        return 0

    lax.fori_loop(1, rows - 1, lambda i, _: add(i, None), 0, unroll=2)
    add(0, before)
    add(rows - 1, after)
    leaving.finish()


def split(value, terms):
    parts = []
    for _ in range(terms):
        part = value.astype(jnp.bfloat16)
        parts.append(part)
        value = value - part.astype(jnp.float32)
    return parts


def dot(a, b, contract):
    return lax.dot_general(a, b, ((contract[:1], contract[1:]), ((), ())), preferred_element_type=jnp.float32)


def route_kernel(tiles, cap, dest, col, prec, op, out):
    count = op.shape[0]
    width = op.shape[1]
    halves = width // LANES
    owner = lax.broadcasted_iota(jnp.int32, (tiles, count), 0)
    hits = owner == dest[...]
    ones = jnp.where(hits, 1.0, 0.0)
    earlier = lax.broadcasted_iota(jnp.int32, (count, count), 0) <= lax.broadcasted_iota(jnp.int32, (count, count), 1)
    running = dot(ones.astype(jnp.bfloat16), jnp.where(earlier, 1.0, 0.0).astype(jnp.bfloat16), (1, 0))
    slot = jnp.sum(running * ones, axis=0, keepdims=True) - 1.0
    slot = slot.astype(jnp.int32)
    place = dest[...] * cap + slot
    at_slot = lax.broadcasted_iota(jnp.int32, (LANES, count), 0) == slot
    at_slot = jnp.where(at_slot, 1.0, 0.0).astype(jnp.bfloat16)
    column = col[...].astype(jnp.float32)
    pieces = [ones * part.astype(jnp.float32) for part in split(column, 2) + split(prec[...], 3)]
    aux = dot(jnp.concatenate(pieces, axis=0).astype(jnp.bfloat16), at_slot, (1, 1))
    columns = aux[0:tiles] + aux[tiles : 2 * tiles]
    precs = (aux[2 * tiles : 3 * tiles] + aux[3 * tiles : 4 * tiles]) + aux[4 * tiles : 5 * tiles]
    sub = sub_iota()
    for owner_at in range(tiles):
        block = jnp.where(sub == 0, columns[owner_at : owner_at + 1], 0.0)
        block = jnp.where(sub == 1, precs[owner_at : owner_at + 1], block)
        out[owner_at, pl.ds(halves * cap, GROUP), :] = block
    rows_high, rows_low = split(op[...], 2)
    chunk = 256
    for first in range(0, tiles * cap, chunk):
        picks = lax.broadcasted_iota(jnp.int32, (chunk, count), 0) + first == place
        picks = jnp.where(picks, 1.0, 0.0).astype(jnp.bfloat16)
        moved = dot(picks, rows_high, (1, 0)) + dot(picks, rows_low, (1, 0))
        for part in range(chunk // cap):
            for half in range(halves):
                out[first // cap + part, pl.ds(half * cap, cap), :] = moved[
                    part * cap : (part + 1) * cap, half * LANES : (half + 1) * LANES
                ]


def innovate_kernel(rows, width, tiles, cap, records, cols, extra, bottom, *rest):
    coupling, wind_ends, wind_dense, dense_g, spread, sel, strips, packed = rest[:8]
    col_cells, precs, both, sems = rest[8:]
    inside = rows * LANES
    chunks = 8
    copies = []
    for part in range(chunks):
        at = pl.ds(part * (2 * width // chunks), 2 * width // chunks)
        copies.append(pltpu.make_async_copy(cols.at[at], col_cells.at[at, pl.ds(0, inside)], sems.at[part]))
        copies[-1].start()
    halves = width // LANES
    count = tiles * cap
    aux = halves * cap
    own = lax.broadcasted_iota(jnp.int32, (cap, LANES), 1) == lax.broadcasted_iota(jnp.int32, (cap, LANES), 0)
    ones = jnp.ones((LANES, LANES), jnp.bfloat16)
    step = 256
    lane = lax.broadcasted_iota(jnp.int32, (step, LANES), 1)
    border = (rows - 1 - lane // (2 * PARTS)) * LANES + jnp.where(lane % 2 == 1, 0, LANES - 1)
    border = jnp.where(lane % (2 * PARTS) < 2, border, -1).astype(jnp.float32)
    lane = lane.astype(jnp.float32)

    def select(block, _):
        sources = step // cap

        def spread_out(part):
            rows_of = [
                jnp.where(own, records[block * sources + s, pl.ds(aux + part, 1), :], 0.0) for s in range(sources)
            ]
            terms = split(jnp.concatenate(rows_of, axis=0), 2 + part)
            return sum(dot(term, ones, (1, 0)) for term in terms)

        at = pl.ds(pl.multiple_of(block * step, step), step)
        place = spread_out(0)
        column = place - lane
        precs[at, :] = spread_out(1)
        for i in range(rows):
            sel[at, i * LANES : (i + 1) * LANES] = jnp.where(column == float(i * LANES), 1.0, 0.0).astype(
                jnp.bfloat16
            )
        sel[at, inside:] = jnp.where(place == border, 1.0, 0.0).astype(jnp.bfloat16)
        return 0

    lax.fori_loop(0, count // step, select, 0)
    for copy in copies:
        copy.wait()
    pair = 2 * GROUP
    first = lax.broadcasted_iota(jnp.int32, (pair, LANES), 0) == 0
    for f in range(2):
        for i in range(rows):
            lanes = slice(i * LANES, (i + 1) * LANES)
            for term, value in enumerate(split(bottom[f * rows + i : f * rows + i + 1, :], 2)):
                at = pl.ds(term * width + f * (width // 2), pair)
                old = col_cells[at, lanes].astype(jnp.float32)
                new = jnp.where(first, value.astype(jnp.float32), old)
                col_cells[at, lanes] = new.astype(jnp.bfloat16)
    for k, i in enumerate((0, rows - 1)):
        lanes = slice(i * LANES, (i + 1) * LANES)
        old = col_cells[:width, lanes].astype(jnp.float32) + col_cells[width:, lanes].astype(jnp.float32)
        more = extra[:, k * LANES : (k + 1) * LANES].astype(jnp.float32)
        high, low = split(old + (more[:width] + more[width:]), 2)
        col_cells[:width, lanes] = high
        col_cells[width:, lanes] = low
    col_cells[:, inside:] = extra[:, 2 * LANES :]
    both[...] = dot(sel[...], col_cells[...], (1, 1))

    def weigh(block, _):
        at = pl.ds(pl.multiple_of(block * LANES, LANES), LANES)
        sources = LANES // cap
        ops = [
            jnp.concatenate(
                [records[block * sources + s, half * cap : (half + 1) * cap, :] for s in range(sources)], axis=0
            )
            for half in range(halves)
        ]
        total = sum(
            (both[at, half * LANES : (half + 1) * LANES] + both[at, width + half * LANES : width + (half + 1) * LANES])
            * ops[half]
            for half in range(halves)
        )
        innovation = jnp.sum(total, axis=1, keepdims=True) * precs[at, :]
        for half in range(halves):
            high, low = split((ops[half] * innovation).T, 2)
            spread[half * LANES : (half + 1) * LANES, at] = high
            spread[width + half * LANES : width + (half + 1) * LANES, at] = low
        return 0

    lax.fori_loop(0, count // LANES, weigh, 0, unroll=4)

    border_cells = jnp.concatenate([sel[:, 0:LANES], sel[:, (rows - 1) * LANES :]], axis=1)
    terms = dot(spread[...], border_cells, (1, 0))
    border_sums = terms[:width] + terms[width:]
    thin = border_sums[:, 2 * LANES :]
    dense = []
    for m in range(width // (GROUP * PARTS)):
        total = thin[m * PARTS * GROUP : (m * PARTS + 1) * GROUP]
        for part in range(1, PARTS):
            at = (m * PARTS + part) * GROUP
            total = total + pltpu.roll(thin[at : at + GROUP], 2 * part, 1)
        dense.append(total)
    ends = (border_sums[:, 0:LANES], border_sums[:, LANES : 2 * LANES])
    packed[packed.shape[0] - GROUP :, :] = jnp.zeros((GROUP, LANES), jnp.float32)
    put_strip(strips, slice(width, width + GROUP), *[jnp.zeros((GROUP, LANES), jnp.float32)] * 2)
    border_strips(
        rows, width // 2, coupling, ends, jnp.concatenate(dense, axis=0), wind_ends, wind_dense, dense_g, strips, packed
    )


def scatter_kernel(rows, width, spread, sel, winds, factors, adjoint, low0, wind_rows, sems):
    low0[2 * rows :, :] = factors[...]
    wind_in = pltpu.make_async_copy(winds, wind_rows.at[pl.ds(1, rows)], sems.at[0])
    wind_in.start()
    wind_rows[0] = jnp.zeros_like(wind_rows[0])
    wind_rows[rows + 1] = jnp.zeros_like(wind_rows[0])
    sums = dot(spread[...], sel[:, : rows * LANES], (1, 0))
    for i in range(rows):
        lanes = slice(i * LANES, (i + 1) * LANES)
        adjoint[i] = sums[:width, lanes] + sums[width:, lanes]
        for f in range(2):
            low0[f * rows + i : f * rows + i + 1, :] = adjoint[i, f * (width // 2) : f * (width // 2) + 1, :]
    wind_in.wait()


def local(state_incr, winds, coupling, background, obs_dest, obs_col, obs_op, obs_prec):
    _, fields, levels, rows, lanes = state_incr.shape
    width = fields * levels
    groups = width // GROUP
    tiles = lax.axis_size("gx") * lax.axis_size("gy")
    count = obs_col.shape[0]
    cap = 2 * count // tiles
    halves = obs_op.shape[1] // LANES

    scale = jnp.broadcast_to(background.reshape(width, 1), (width, LANES))

    vmem = pl.BlockSpec(memory_space=pltpu.VMEM)
    anywhere = pl.BlockSpec(memory_space=pl.ANY)
    own = pltpu.VMEM((rows, width, LANES), jnp.float32)
    framed = pltpu.VMEM((rows + 2, width, LANES), jnp.float32)
    packed_shape = f32(groups // PARTS * GROUP, LANES)
    sides = pltpu.VMEM(packed_shape.shape, jnp.float32)
    strip_shapes = [f32(pair_sets(), width, LANES), packed_shape]
    long_shapes = [f32(pair_sets(), width + GROUP, LANES), f32(packed_shape.shape[0] + GROUP, LANES)]
    field_shape = f32(rows, width, LANES)
    framed_shape = f32(rows + 2, width, LANES)
    low_shape = f32(fields * rows, LANES)
    cols_shape = ((2 * width, rows * LANES), jnp.bfloat16)

    def sems(*shape):
        return pltpu.SemaphoreType.DMA(shape)

    def run(body, out_shape, scratch, args, far=(), out_far=(), **kw):
        args = [pltpu.with_memory_space_constraint(x, pltpu.HBM) if k in far else x for k, x in enumerate(args)]
        specs = [anywhere if k in far else vmem for k in range(len(args))]
        outs = [anywhere if k in out_far else vmem for k in range(len(out_shape))]
        out_shape = [pltpu.HBM(x.shape, x.dtype) if k in out_far else x for k, x in enumerate(out_shape)]
        return call(body, out_shape, scratch, in_specs=specs, out_specs=outs, **kw)(*args)

    def on_rows(body):
        return functools.partial(body, rows, levels)

    def swap_floor(floor):
        return lax.ppermute(floor, "comp", [(0, 1), (1, 0)])

    state = state_incr.reshape(width, rows, lanes)
    wind = winds.reshape(width, rows, lanes)
    floor_winds = winds[0, :, 0]
    slots = tiles * cap
    thin_shape = f32(GROUP, LANES)

    strips, packed, low0, low1 = run(
        on_rows(edges_kernel),
        strip_shapes + [low_shape] * 2,
        [pltpu.VMEM((width * rows, LANES), jnp.float32), sems(groups // PARTS)],
        (state_incr.reshape(width * rows, lanes),),
        far=(0,),
    )
    halos = exchange(strips, packed)

    send = call(functools.partial(route_kernel, tiles, cap), f32(tiles, halves * cap + GROUP, LANES))(
        obs_dest.reshape(1, count), obs_col.reshape(1, count), obs_prec.reshape(1, count), obs_op
    )
    send, halos[0], halos[2], state_far, wind_far = lax.optimization_barrier((send, halos[0], halos[2], state, wind))
    records = lax.all_to_all(send, ("gx", "gy"), split_axis=0, concat_axis=0, tiled=True)

    state_rows, wind_rows, state_later, wind_later = run(
        functools.partial(load_kernel, rows),
        [field_shape] * 4,
        [sems(4, rows)],
        (state_far, wind_far),
        far=(0, 1),
        out_far=(2, 3),
        traffic=10 * MIB,
    )
    halos[1], state_rows, wind_rows = lax.optimization_barrier((halos[1], state_rows, wind_rows))
    (floor,) = run(on_rows(forward_floor_kernel), [low_shape], [], (low0, low1, floor_winds, *halos))
    field, strips, packed, low0, low1, wind_ends, wind_dense, dense_g = run(
        on_rows(forward_kernel),
        [framed_shape]
        + long_shapes
        + [low_shape] * 2
        + [f32(2, levels, LANES), f32(groups // PARTS * GROUP // 2, LANES), thin_shape],
        [framed, sides],
        (coupling, swap_floor(floor), state_rows, wind_rows, *halos),
    )
    halos = exchange(strips, packed)
    (cols,) = run(
        on_rows(forward_again_kernel),
        [jax.ShapeDtypeStruct(*cols_shape)],
        [pltpu.VMEM(*cols_shape), sems(rows)],
        (field, wind_rows),
        out_far=(0,),
        traffic=20 * MIB,
    )
    cols, halos = lax.optimization_barrier((cols, halos))
    (floor,) = run(on_rows(forward_floor_kernel), [low_shape], [], (low0, low1, floor_winds, *halos))
    extra, bottom, factors = run(
        on_rows(outside_kernel),
        [jax.ShapeDtypeStruct((2 * width, 3 * LANES), jnp.bfloat16), low_shape, thin_shape],
        [sides],
        (coupling, floor, swap_floor(floor), wind_ends, wind_dense, *halos),
    )

    spread_shape = ((2 * width, slots), jnp.bfloat16)
    sel_shape = ((slots, (rows + 1) * LANES), jnp.bfloat16)
    spread, sel, strips, packed = run(
        functools.partial(innovate_kernel, rows, width, tiles, cap),
        [jax.ShapeDtypeStruct(*spread_shape), jax.ShapeDtypeStruct(*sel_shape)] + long_shapes,
        [
            pltpu.VMEM((2 * width, (rows + 1) * LANES), jnp.bfloat16),
            pltpu.VMEM((slots, LANES), jnp.float32),
            pltpu.VMEM((slots, 2 * width), jnp.float32),
            sems(8),
        ],
        (records, cols, extra, bottom, coupling, wind_ends, wind_dense, dense_g),
        far=(1,),
        limit=OBSERVE_VMEM,
    )
    halos = exchange(strips, packed)
    adjoint, low0, wind_rows = run(
        functools.partial(scatter_kernel, rows, width),
        [field_shape, f32(fields * rows + GROUP, LANES), framed_shape],
        [sems(1)],
        (spread, sel, wind_later, factors),
        far=(2,),
        limit=OBSERVE_VMEM,
        traffic=8 * MIB,
    )
    partner = swap_floor(low0)
    adjoint, ends, columns, low0, state_rows = run(
        on_rows(first_adjoint_kernel),
        [field_shape, f32(2, width, LANES), packed_shape, low_shape, field_shape],
        [framed, sems(1)],
        (coupling, adjoint, wind_rows, state_later),
        far=(3,),
        traffic=16 * MIB,
    )
    low0, partner, halos = lax.optimization_barrier((low0, partner, halos))
    floor, missing = run(
        on_rows(floor_kernel),
        [f32(fields * rows + GROUP, LANES), low_shape],
        [],
        (coupling, partner, low0, floor_winds, *halos),
    )
    floor, other = run(
        on_rows(level0_kernel),
        [low_shape, low_shape],
        [],
        (floor, swap_floor(floor), factors, partner),
    )
    strips, packed = run(
        on_rows(border_again_kernel),
        strip_shapes,
        [sides],
        (coupling, floor, other, missing, ends, columns, wind_ends, wind_dense, dense_g, *halos),
    )
    last_halos = exchange(strips, packed)
    (adjoint,) = run(
        on_rows(second_adjoint_kernel),
        [field_shape],
        [framed, sides],
        (coupling, floor, other, missing, adjoint, wind_rows, scale, state_rows, *halos),
        traffic=20 * MIB,
    )
    (result,) = run(
        on_rows(final_kernel),
        [f32(width, rows, LANES)],
        [own, sides, sems(rows)],
        (adjoint, *last_halos),
        out_far=(0,),
    )
    return result.reshape(state_incr.shape)


def solution(mesh):
    placed = (
        P("comp", None, None, "gx", "gy"),
        P("comp", None, None, "gx", "gy"),
        P("gx", "gy"),
        P("comp", None, None),
        P(("comp", "gx", "gy"), None),
        P(("comp", "gx", "gy")),
        P(("comp", "gx", "gy"), None),
        P(("comp", "gx", "gy")),
    )
    return jax.shard_map(
        local,
        mesh=mesh,
        in_specs=placed,
        out_specs=P("comp", None, None, "gx", "gy"),
        check_vma=False,
    )
```

```python
import functools

import jax
import jax.numpy as jnp
from jax import lax
from jax.experimental import pallas as pl
from jax.experimental.pallas import tpu as pltpu
from jax.sharding import PartitionSpec as P

HORIZ_MIX = 0.1
VERT_MIX = 0.15
LANES = 128
GROUP = 8
MIB = 1024 * 1024
SWEEP_VMEM = 16 * MIB
OBSERVE_VMEM = 22 * MIB


def call(body, out_shape, scratch=(), limit=SWEEP_VMEM, traffic=0, **kw):
    cost = pl.CostEstimate(flops=0, bytes_accessed=traffic, transcendentals=0) if traffic else None
    return pl.pallas_call(
        body,
        out_shape=out_shape,
        scratch_shapes=list(scratch),
        cost_estimate=cost,
        compiler_params=pltpu.CompilerParams(vmem_limit_bytes=limit),
        **kw,
    )


def f32(*shape):
    return jax.ShapeDtypeStruct(shape, jnp.float32)


def lane_iota(rows=GROUP):
    return lax.broadcasted_iota(jnp.int32, (rows, LANES), 1)


def sub_iota(rows=GROUP):
    return lax.broadcasted_iota(jnp.int32, (rows, LANES), 0)


def pair_swap(block, axis, start):
    count = lax.axis_size(axis)
    route = []
    for low in range(start, count - 1, 2):
        route += [(low, low + 1), (low + 1, low)]
    return lax.ppermute(block, axis, route)


def pair_sets():
    return 2 if lax.axis_size("gx") > 2 else 1


def exchange(strips, packed):
    y_even = pair_swap(packed, "gy", 0)
    y_odd = pair_swap(packed, "gy", 1)
    even, *odd = [pair_swap(strips[start], "gx", start) for start in range(pair_sets())]
    return [even, y_even, y_odd, *odd]


def is_odd(axis):
    return lax.rem(lax.axis_index(axis), 2) == 1


def read_sides(refs):
    even = refs[0]
    odd = refs[3] if len(refs) > 3 else None
    at_odd = is_odd("gx")

    def side(at, turned):
        other = jnp.zeros_like(even[at]) if odd is None else odd[at]
        return jnp.where(turned, other, even[at])

    return lambda at: side(at, jnp.logical_not(at_odd)), lambda at: side(at, at_odd)


PARTS = 4


def merged(y_even, y_odd, at):
    a, b = y_even[at, :], y_odd[at, :]
    lane = lax.broadcasted_iota(jnp.int32, a.shape, 1)
    return jnp.where((lane % 2 == 1) == jnp.logical_not(is_odd("gy")), a, b)


def merge_columns(y_even, y_odd, sides):
    sides[...] = merged(y_even, y_odd, slice(0, sides.shape[0]))


def slot_of(i, part, rows):
    return PARTS * (rows - 1 - i) + part


def side_columns(sides, i, group):
    m, part = group // PARTS, group % PARTS
    rows = LANES // (2 * PARTS)
    return pltpu.roll(sides[m * GROUP : (m + 1) * GROUP, :], LANES - 1 - 2 * slot_of(i, part, rows), 1)


def pack_into(total, value, slot):
    return jnp.where(lane_iota() // 2 == slot, pltpu.roll(value, 2 * slot + 1, 1), total)


def pack_block(packed, values, i, m):
    at = pl.ds(m * GROUP, GROUP)
    total = packed[at, :]
    for part, value in enumerate(values):
        total = pack_into(total, value, slot_of(i, part, LANES // (2 * PARTS)))
    packed[at, :] = total


CENTRE = 1.0 - 4.0 * HORIZ_MIX - 2.0 * VERT_MIX


def levels_around(cells, i, base, group, groups):
    here = cells[i + 1, pl.ds(base + group * GROUP, GROUP), :]
    if group == groups - 1:
        upper = jnp.where(sub_iota() == GROUP - 1, here, pltpu.roll(here, GROUP - 1, 0))
    else:
        upper = cells[i + 1, pl.ds(base + group * GROUP + 1, GROUP), :]
    if group == 0:
        lower = jnp.where(sub_iota() == 0, here, pltpu.roll(here, 1, 0))
    else:
        lower = cells[i + 1, pl.ds(base + group * GROUP - 1, GROUP), :]
    return here, upper, lower


def shifted(first, last, edge, rows=GROUP):
    lane = lane_iota(rows)
    right = pltpu.roll(jnp.where(lane == 0, edge, first), LANES - 1, 1)
    left = pltpu.roll(jnp.where(lane == LANES - 1, edge, last), 1, 1)
    return right, left


def forward_sum(here, vertical, after, before, right, left, u, w):
    return (
        CENTRE * here
        + VERT_MIX * vertical
        + HORIZ_MIX * ((after + before) + (right + left))
        - 0.5 * (u * (after - before) + w * (right - left))
    )


def forward_point(cells, winds, sides, i, f, group, levels):
    groups = levels // GROUP
    here, upper, lower = levels_around(cells, i, f * levels, group, groups)
    at = pl.ds(f * levels + group * GROUP, GROUP)
    right, left = shifted(here, here, 0.0 if sides is None else side_columns(sides, i, f * groups + group))
    u = winds[i, pl.ds(group * GROUP, GROUP), :]
    w = winds[i, pl.ds(levels + group * GROUP, GROUP), :]
    return forward_sum(here, upper + lower, cells[i + 2, at, :], cells[i, at, :], right, left, u, w)


def products(x, wind):
    slope = 0.5 * (wind * x)
    return HORIZ_MIX * x - slope, HORIZ_MIX * x + slope


def adjoint_point(cells, winds, i, f, group, levels):
    here, upper, lower = levels_around(cells, i, f * levels, group, levels // GROUP)
    at = pl.ds(f * levels + group * GROUP, GROUP)
    wind_at = pl.ds(group * GROUP, GROUP)
    after, before = cells[i + 2, at, :], cells[i, at, :]
    u_after, u_before = winds[i + 2, wind_at, :], winds[i, wind_at, :]
    down, up = products(here, winds[i + 1, pl.ds(levels + group * GROUP, GROUP), :])
    right, left = shifted(up, down, 0.0)
    return (
        CENTRE * here
        + VERT_MIX * (upper + lower)
        + HORIZ_MIX * (after + before)
        + 0.5 * (u_after * after - u_before * before)
        + (right + left)
    )


def shares_of(coupling):
    own = jnp.where(lax.axis_index("comp") == 0, 1.0, 0.5)
    return own * coupling, (1.5 - own) * coupling


def couple_forward(value, other, coupling):
    own, _ = shares_of(coupling)
    return value - own * (value - other)


def couple_adjoint(value, other, coupling):
    own, peer = shares_of(coupling)
    return value - own * value + peer * other


def coupled(rule, value, other, coupling, i, f, rows):
    mixed = rule(value, other[pl.ds(f * rows + i, 1), :], coupling[pl.ds(i, 1), :])
    return jnp.where(sub_iota() == 0, mixed, value)


def put_strip(strips, at, first, last):
    at_odd = is_odd("gx")
    strips[0, at, :] = jnp.where(at_odd, first, last)
    if strips.shape[0] > 1:
        strips[1, at, :] = jnp.where(at_odd, last, first)


def put_low(low, value, i, f, rows):
    for level in range(2):
        low[level][pl.ds(f * rows + i, 1), :] = value[level : level + 1]


class Rows:
    def __init__(self, source, target, sems, rows, as_it_comes, offset):
        self.source, self.target, self.sems = source, target, sems
        self.rows, self.as_it_comes, self.offset = rows, as_it_comes, offset

    def copy(self, i):
        row = self.source.at[:, i] if self.as_it_comes else self.source.at[i]
        return pltpu.make_async_copy(row, self.target.at[i + self.offset], self.sems.at[i])

    def wait(self, i):
        self.copy(i).wait()


def start_rows(rows, *groups):
    for i in range(rows):
        for group in groups:
            group.copy(i).start()


def edges_kernel(rows, levels, state, strips, packed, low0, low1, cells, sems):
    part_levels = PARTS * GROUP
    blocks = 2 * levels // part_levels

    def copy(m):
        return pltpu.make_async_copy(
            state.at[pl.ds(m * part_levels * rows, part_levels * rows)],
            cells.at[pl.ds(m * part_levels * rows, part_levels * rows)],
            sems.at[m],
        )

    for m in range(blocks):
        copy(m).start()

    def block(m, _):
        copy(m).wait()
        total = jnp.zeros((GROUP, LANES), jnp.float32)
        for part in range(PARTS):
            for i in range(rows):
                start = (m * PARTS + part) * GROUP * rows + i
                total = pack_into(total, cells[pl.ds(start, GROUP, stride=rows), :], slot_of(i, part, rows))
        packed[pl.ds(pl.multiple_of(m * GROUP, GROUP), GROUP), :] = total
        start = m * part_levels * rows
        first = cells[pl.ds(start, part_levels, stride=rows), :]
        last = cells[pl.ds(start + rows - 1, part_levels, stride=rows), :]
        put_strip(strips, pl.ds(pl.multiple_of(m * part_levels, part_levels), part_levels), first, last)
        return 0

    lax.fori_loop(0, blocks, block, 0)
    for f in range(2):
        for level, low in enumerate((low0, low1)):
            low[f * rows : (f + 1) * rows, :] = cells[pl.ds((f * levels + level) * rows, rows), :]


def floor_edge(halos, f, rows, levels):
    m = f * (levels // GROUP) // PARTS
    sides = jnp.broadcast_to(merged(halos[1], halos[2], pl.ds(m * GROUP, 1)), (rows, LANES))
    return pltpu.roll(sides, 2 * PARTS - 1, 1, stride=2 * PARTS, stride_axis=0)


def row_after(value, last, rows):
    return jnp.where(sub_iota(rows) == rows - 1, last, pltpu.roll(value, rows - 1, 0))


def row_before(value, first, rows):
    return jnp.where(sub_iota(rows) == 0, first, pltpu.roll(value, 1, 0))


def forward_floor_kernel(rows, levels, low0, low1, winds, *rest):
    *halos, floor = rest
    side_before, side_after = read_sides(halos)
    for f in range(2):
        here = pl.ds(f * rows, rows)
        at = pl.ds(f * levels, 1)
        low, up = low0[here, :], low1[here, :]
        after, before = row_after(low, side_after(at), rows), row_before(low, side_before(at), rows)
        right, left = shifted(low, low, floor_edge(halos, f, rows, levels), rows)
        floor[here, :] = forward_sum(low, up + low, after, before, right, left, winds[0], winds[1])


class Out:
    def __init__(self, source, target, sems, rows, as_it_goes):
        self.source, self.target, self.sems, self.rows, self.as_it_goes = source, target, sems, rows, as_it_goes

    def copy(self, i):
        row = self.target.at[:, i] if self.as_it_goes else self.target.at[i]
        return pltpu.make_async_copy(self.source.at[i], row, self.sems.at[i])

    def start(self, i):
        self.copy(i).start()

    def finish(self):
        for i in range(self.rows):
            self.copy(i).wait()


def dense_row(field, first, rows):
    total = jnp.zeros((1, LANES), jnp.float32)
    lane = lax.broadcasted_iota(jnp.int32, (1, LANES), 1)
    for i in range(rows):
        slot = slot_of(i, 0, rows)
        total = jnp.where(lane // 2 == slot, pltpu.roll(field[first + i : first + i + 1, :], 2 * slot + 1, 1), total)
    return total


def load_kernel(rows, state, winds, state_rows, wind_rows, state_later, wind_later, sems):
    state_in = Rows(state, state_rows, sems.at[0], rows, True, 0)
    wind_in = Rows(winds, wind_rows, sems.at[1], rows, True, 0)
    state_out = Out(state_rows, state_later, sems.at[2], rows, False)
    wind_out = Out(wind_rows, wind_later, sems.at[3], rows, False)
    start_rows(rows, state_in, wind_in)
    for i in range(rows):
        state_in.wait(i)
        wind_in.wait(i)
        state_out.start(i)
        wind_out.start(i)
    state_out.finish()
    wind_out.finish()


def forward_kernel(rows, levels, coupling, other, field, winds, *rest):
    *halos, out, strips, packed, low0, low1, wind_ends, wind_dense, dense_g, cells, sides = rest
    packed[...] = jnp.zeros_like(packed)
    wind_dense[...] = jnp.zeros_like(wind_dense)
    merge_columns(halos[1], halos[2], sides)
    before, after = read_sides(halos)
    cells[0] = before(pl.ds(0, 2 * levels))
    cells[1] = field[0]
    cells[rows + 1] = after(pl.ds(0, 2 * levels))
    out[0] = jnp.zeros_like(out[0])
    out[rows + 1] = jnp.zeros_like(out[0])
    groups = levels // GROUP

    def row(i, _):
        @pl.when(i < rows - 1)
        def _():
            cells[i + 2] = field[i + 1]

        for m in range(2 * groups // PARTS):
            f, start = m * PARTS // groups, m * PARTS % groups
            values = []
            for group in range(start, start + PARTS):
                value = forward_point(cells, winds, sides, i, f, group, levels)
                if group == 0:
                    value = coupled(couple_forward, value, other, coupling, i, f, rows)
                    put_low((low0, low1), value, i, f, rows)
                values.append(value)
            base = m * PARTS * GROUP
            for part, value in enumerate(values):
                out[i + 1, pl.ds(base + part * GROUP, GROUP), :] = value
            pack_block(packed, values, i, m)
            if f == 0:
                w = [winds[i, pl.ds(levels + base + part * GROUP, GROUP), :] for part in range(PARTS)]
                pack_block(wind_dense, w, i, m)
        return 0

    lax.fori_loop(0, rows, row, 0)
    put_strip(strips, pl.ds(0, 2 * levels), out[1], out[rows])
    wind_ends[0] = winds[0, pl.ds(0, levels), :]
    wind_ends[1] = winds[rows - 1, pl.ds(0, levels), :]
    dense_g[...] = jnp.broadcast_to(dense_row(coupling, 0, rows), dense_g.shape)
    _, peer = shares_of(coupling[...])
    first = products(peer[0:1], winds[0, 0:1, :])[1]
    last = products(peer[rows - 1 : rows], winds[rows - 1, 0:1, :])[0]
    whole = (GROUP, LANES)
    put_strip(strips, slice(2 * levels, 2 * levels + GROUP), jnp.broadcast_to(first, whole), jnp.broadcast_to(last, whole))
    _, peer = shares_of(dense_g[...])
    packed[packed.shape[0] - GROUP :, :] = first_and_last(peer, wind_dense[0:1, :])


def forward_again_kernel(rows, levels, cells, winds, cols, col_cells, col_sems):
    groups = levels // GROUP
    width = 2 * levels

    def col_copy(i):
        lanes = pl.ds(pl.multiple_of(i * LANES, LANES), LANES)
        return pltpu.make_async_copy(col_cells.at[:, lanes], cols.at[:, lanes], col_sems.at[i])

    def row(i, _):
        lanes = pl.ds(pl.multiple_of(i * LANES, LANES), LANES)
        for m in range(2 * groups // PARTS):
            f, start = m * PARTS // groups, m * PARTS % groups
            values = [forward_point(cells, winds, None, i, f, group, levels) for group in range(start, start + PARTS)]
            high, low = split(jnp.concatenate(values, axis=0), 2)
            col_cells[pl.ds(m * PARTS * GROUP, PARTS * GROUP), lanes] = high
            col_cells[pl.ds(width + m * PARTS * GROUP, PARTS * GROUP), lanes] = low
        col_copy(i).start()
        return 0

    lax.fori_loop(0, rows, row, 0)
    for i in range(rows):
        col_copy(i).wait()


def outside_kernel(rows, levels, coupling, floor, other, wind_ends, wind_dense, *rest):
    *halos, extra, bottom, factors, dense = rest
    width = 2 * levels
    tail = pl.ds(width, 1)
    factors[...] = jnp.zeros_like(factors)
    for k, side in enumerate(read_sides(halos)):
        factors[k : k + 1, :] = side(tail)
    factors[2:3, :] = merged(halos[1], halos[2], pl.ds(dense.shape[0], 1))
    for f in range(2):
        here = pl.ds(f * rows, rows)
        bottom[here, :] = couple_forward(floor[here, :], other[here, :], coupling[...])
    dense_products(dense, swap_pairs(merged(halos[1], halos[2], slice(0, dense.shape[0]))), wind_dense)
    before, after = read_sides(halos)
    sub = lax.broadcasted_iota(jnp.int32, (levels, LANES), 0)

    def put(value, f, lanes):
        high, low = split(jnp.where(sub == 0, 0.0, value), 2)
        extra[f * levels : (f + 1) * levels, lanes] = high
        extra[width + f * levels : width + (f + 1) * levels, lanes] = low

    lane = lane_iota()
    for f in range(2):
        at = pl.ds(f * levels, levels)
        put(products(before(at), wind_ends[0])[1], f, slice(0, LANES))
        put(products(after(at), wind_ends[1])[0], f, slice(LANES, 2 * LANES))
        thin = []
        for group in range(f * levels // GROUP, (f + 1) * levels // GROUP):
            m, part = group // PARTS, group % PARTS
            moved = pltpu.roll(dense[m * GROUP : (m + 1) * GROUP, :], (LANES - 2 * part) % LANES, 1)
            thin.append(jnp.where(lane % (2 * PARTS) < 2, moved, 0.0))
        put(jnp.concatenate(thin, axis=0), f, slice(2 * LANES, 3 * LANES))


def first_and_last(value, wind):
    down, up = products(value, wind)
    lane = lax.broadcasted_iota(jnp.int32, down.shape, 1)
    return jnp.where(lane % 2 == 1, up, down)


def dense_products(packed, value, wind_dense):
    half = wind_dense.shape[0]
    for f in range(2):
        at = slice(f * half, (f + 1) * half)
        packed[at, :] = first_and_last(value[at], wind_dense[...])


def level0_row(value, new, f):
    half = value.shape[0] // 2
    sub = lax.broadcasted_iota(jnp.int32, value.shape, 0)
    lane = lax.broadcasted_iota(jnp.int32, value.shape, 1)
    return jnp.where((sub == f * half) & (lane % (2 * PARTS) < 2), new, value)


def end_rows(ends, strips, wind_ends, levels):
    for f in range(2):
        at = slice(f * levels, (f + 1) * levels)
        put_strip(
            strips, at, products(ends[0][at], wind_ends[0])[1], products(ends[1][at], wind_ends[1])[0]
        )


def with_first(value, new):
    return jnp.where(lax.broadcasted_iota(jnp.int32, value.shape, 0) == 0, new, value)


def border_strips(rows, levels, coupling, ends, dense, wind_ends, wind_dense, dense_g, strips, packed):
    half = dense.shape[0] // 2
    width = 2 * levels
    own, _ = shares_of(dense_g[0:1, :])
    new = dense
    for f in range(2):
        bottom = dense[f * half : f * half + 1]
        new = level0_row(new, bottom - own * bottom, f)
        packed[2 * half + f : 2 * half + f + 1, :] = bottom
    dense_products(packed, new, wind_dense)
    full = []
    for k, i in enumerate((0, rows - 1)):
        own, _ = shares_of(coupling[i : i + 1, :])
        parts = []
        for f in range(2):
            value = ends[k][f * levels : (f + 1) * levels]
            parts.append(with_first(value, value[0:1] - own * value[0:1]))
        full.append(jnp.concatenate(parts, axis=0))
    end_rows(full, strips, wind_ends, levels)
    for f in range(2):
        at = f * levels
        put_strip(strips, slice(width + f, width + f + 1), ends[0][at : at + 1], ends[1][at : at + 1])


def to_border(low, before, after, sides, rows):
    sub, lane = sub_iota(rows), lane_iota(rows)
    low = low + jnp.where(sub == 0, before, 0.0) + jnp.where(sub == rows - 1, after, 0.0)
    edge = pltpu.roll(jnp.broadcast_to(sides, (rows, LANES)), 2 * PARTS - 1, 1, stride=2 * PARTS, stride_axis=0)
    edge = jnp.where(lane == 0, pltpu.roll(edge, 1, 1), pltpu.roll(edge, LANES - 1, 1))
    return low + jnp.where((lane == 0) | (lane == LANES - 1), edge, 0.0)


def floor_kernel(rows, levels, coupling, other, low0, winds, *rest):
    *halos, floor, missing = rest
    before, after = read_sides(halos)
    half = halos[1].shape[0] - GROUP
    for f in range(2):
        here = pl.ds(f * rows, rows)
        _, peer = shares_of(coupling[...])
        share = peer * other[here, :]
        x_down, x_up = products(share, winds[0])
        y_down, y_up = products(share, winds[1])
        right, left = shifted(y_up, y_down, 0.0, rows)
        spread = (row_after(x_up, 0.0, rows) + row_before(x_down, 0.0, rows)) + (right + left)
        spread = spread + (CENTRE + VERT_MIX) * share
        at = pl.ds(f * levels, 1)
        sides = merged(halos[1], halos[2], pl.ds(f * half // 2, 1))
        floor[here, :] = to_border(low0[here, :] + spread, before(at), after(at), sides, rows)
        missing[here, :] = VERT_MIX * share
    raw = 2 * rows
    floor[raw : raw + 2, :] = before(pl.ds(2 * levels, 2))
    floor[raw + 2 : raw + 4, :] = after(pl.ds(2 * levels, 2))
    floor[raw + 4 : raw + 6, :] = merged(halos[1], halos[2], pl.ds(half, 2))
    floor[raw + 6 : raw + GROUP, :] = jnp.zeros((2, LANES), jnp.float32)


def level0_kernel(rows, levels, floor, other, factors, partner, floor_out, other_out):
    raw = 2 * rows
    for mine, theirs, factor, at, out in ((floor, other, factors, 0, floor_out), (other, floor, partner, raw, other_out)):
        for f in range(2):
            here = pl.ds(f * rows, rows)
            parts = [factor[at + k : at + k + 1, :] * theirs[raw + 2 * k + f : raw + 2 * k + f + 1, :] for k in range(3)]
            out[here, :] = to_border(mine[here, :], *parts, rows)


def swap_pairs(value):
    lane = lax.broadcasted_iota(jnp.int32, value.shape, 1)
    return jnp.where(lane % 2 == 1, pltpu.roll(value, 1, 1), pltpu.roll(value, LANES - 1, 1))


def edge_lanes(sides, i, group):
    m, part = group // PARTS, group % PARTS
    rows = LANES // (2 * PARTS)
    moved = pltpu.roll(sides[m * GROUP : (m + 1) * GROUP, :], LANES - 1 - 2 * slot_of(i, part, rows), 1)
    lane = lane_iota()
    return jnp.where((lane == 0) | (lane == LANES - 1), moved, 0.0)


def with_level(value, level, new):
    return jnp.where(lax.broadcasted_iota(jnp.int32, value.shape, 0) == level, new, value)


def border_again_kernel(
    rows, levels, coupling, floor, other, missing, ends, columns, wind_ends, wind_dense, dense_g, *rest
):
    *halos, strips, packed, sides = rest
    before, after = read_sides(halos)
    sides[...] = swap_pairs(merged(halos[1], halos[2], slice(0, sides.shape[0])))
    half = columns.shape[0] // 2
    groups = levels // GROUP
    outer = [before(pl.ds(0, 2 * levels)), after(pl.ds(0, 2 * levels))]
    full = []
    for k, i in enumerate((0, rows - 1)):
        edges = jnp.concatenate([edge_lanes(sides, i, group) for group in range(2 * groups)], axis=0)
        value = ends[k] + outer[k] + edges
        parts = []
        for f in range(2):
            part = value[f * levels : (f + 1) * levels]
            at = slice(f * rows + i, f * rows + i + 1)
            part = part + with_level(jnp.zeros_like(part), 1, missing[at, :])
            parts.append(with_first(part, couple_adjoint(floor[at, :], other[at, :], coupling[i : i + 1, :])))
        full.append(jnp.concatenate(parts, axis=0))
    end_rows(full, strips, wind_ends, levels)
    dense = columns[...] + sides[...]
    corners = []
    for m in range(2 * groups // PARTS):
        total = jnp.zeros((GROUP, LANES), jnp.float32)
        for part in range(PARTS):
            at = slice((m * PARTS + part) * GROUP, (m * PARTS + part + 1) * GROUP)
            for k, i in enumerate((0, rows - 1)):
                total = pack_into(total, outer[k][at], slot_of(i, part, rows))
        corners.append(total)
    dense = dense + jnp.concatenate(corners, axis=0)
    for f in range(2):
        sub = lax.broadcasted_iota(jnp.int32, dense.shape, 0)
        dense = dense + jnp.where(sub == f * half + 1, dense_row(missing, f * rows, rows), 0.0)
        mine = dense_row(floor, f * rows, rows)
        mixed = couple_adjoint(mine, dense_row(other, f * rows, rows), dense_g[0:1, :])
        dense = level0_row(dense, mixed, f)
    dense_products(packed, dense, wind_dense)


def adjoint_rows(rows, levels, cells, winds, take, each, behind=None):
    groups = levels // GROUP
    cells[0] = jnp.zeros_like(cells[0])
    cells[rows + 1] = jnp.zeros_like(cells[0])
    take(0)
    take(1)

    def row(i, _):
        if behind is not None:
            behind(jnp.maximum(i - 1, 0))
        for m in range(2 * groups // PARTS):
            f, start = m * PARTS // groups, m * PARTS % groups
            each(i, m, f, start, [
                adjoint_point(cells, winds, i, f, group, levels) for group in range(start, start + PARTS)
            ])
        take(jnp.minimum(i + 2, rows - 2))
        return 0

    lax.fori_loop(0, rows, row, 0)
    if behind is not None:
        behind(rows - 1)


def first_adjoint_kernel(rows, levels, coupling, field, winds, state, out, ends, columns, low0, state_rows, cells, sems):
    state_in = pltpu.make_async_copy(state, state_rows, sems.at[0])
    state_in.start()
    columns[...] = jnp.zeros_like(columns)

    def take(i):
        cells[i + 1] = field[i]
        for f in range(2):
            at = pl.ds(f * levels, GROUP)
            own, _ = shares_of(coupling[pl.ds(i, 1), :])
            value = field[i, at, :]
            cells[i + 1, at, :] = jnp.where(sub_iota() == 0, value - own * value, value)

    def each(i, m, f, start, values):
        for part, value in enumerate(values):
            out[i, pl.ds((m * PARTS + part) * GROUP, GROUP), :] = value
        if start == 0:
            low0[pl.ds(f * rows + i, 1), :] = values[0][0:1]

    def pack(i):
        for m in range(columns.shape[0] // GROUP):
            values = [out[i, pl.ds((m * PARTS + part) * GROUP, GROUP), :] for part in range(PARTS)]
            pack_block(columns, values, i, m)

    out[0] = jnp.zeros_like(out[0])
    take(rows - 1)
    adjoint_rows(rows, levels, cells, winds, take, each, pack)
    ends[0] = out[0]
    ends[1] = out[rows - 1]
    state_in.wait()


def second_adjoint_kernel(rows, levels, coupling, floor, other, missing, field, winds, scale, state, *rest):
    *halos, out, cells, sides = rest
    sides[...] = swap_pairs(merged(halos[1], halos[2], slice(0, sides.shape[0])))
    before, after = read_sides(halos)
    groups = levels // GROUP

    def take(i, outer=None):
        for group in range(2 * groups):
            at = pl.ds(group * GROUP, GROUP)
            value = field[i, at, :] + edge_lanes(sides, i, group)
            if outer is not None:
                value = value + outer(at)
            if group % groups == 0:
                here = pl.ds(group // groups * rows + i, 1)
                value = value + jnp.where(sub_iota() == 1, missing[here, :], 0.0)
                bottom = couple_adjoint(floor[here, :], other[here, :], coupling[pl.ds(i, 1), :])
                value = jnp.where(sub_iota() == 0, bottom, value)
            cells[i + 1, at, :] = value

    def take_inner(i):
        take(i, before if isinstance(i, int) and i == 0 else None)

    def each(i, m, f, start, values):
        for part, value in enumerate(values):
            at = pl.ds((m * PARTS + part) * GROUP, GROUP)
            out[i, at, :] = value + scale[at, :] * state[i, at, :]

    take(rows - 1, after)
    adjoint_rows(rows, levels, cells, winds, take_inner, each)


def final_kernel(rows, levels, field, *rest):
    *halos, out, cells, sides, sems = rest
    leaving = Out(cells, out, sems, rows, True)
    sides[...] = swap_pairs(merged(halos[1], halos[2], slice(0, sides.shape[0])))
    before, after = read_sides(halos)
    groups = levels // GROUP

    def add(i, outer):
        for group in range(2 * groups):
            at = pl.ds(group * GROUP, GROUP)
            value = field[i, at, :] + edge_lanes(sides, i, group)
            cells[i, at, :] = value if outer is None else value + outer(at)
        leaving.start(i)
        return 0

    lax.fori_loop(1, rows - 1, lambda i, _: add(i, None), 0, unroll=7)
    add(0, before)
    add(rows - 1, after)
    leaving.finish()


def split(value, terms):
    parts = []
    for _ in range(terms):
        part = value.astype(jnp.bfloat16)
        parts.append(part)
        value = value - part.astype(jnp.float32)
    return parts


def dot(a, b, contract):
    return lax.dot_general(a, b, ((contract[:1], contract[1:]), ((), ())), preferred_element_type=jnp.float32)


def route_kernel(tiles, cap, dest, col, prec, op, out):
    count = op.shape[0]
    width = op.shape[1]
    halves = width // LANES
    owner = lax.broadcasted_iota(jnp.int32, (tiles, count), 0)
    hits = owner == dest[...]
    ones = jnp.where(hits, 1.0, 0.0)
    earlier = lax.broadcasted_iota(jnp.int32, (count, count), 0) <= lax.broadcasted_iota(jnp.int32, (count, count), 1)
    running = dot(ones.astype(jnp.bfloat16), jnp.where(earlier, 1.0, 0.0).astype(jnp.bfloat16), (1, 0))
    slot = jnp.sum(running * ones, axis=0, keepdims=True) - 1.0
    slot = slot.astype(jnp.int32)
    place = dest[...] * cap + slot
    at_slot = lax.broadcasted_iota(jnp.int32, (LANES, count), 0) == slot
    at_slot = jnp.where(at_slot, 1.0, 0.0).astype(jnp.bfloat16)
    column = col[...].astype(jnp.float32)
    pieces = [ones * part.astype(jnp.float32) for part in split(column, 2) + split(prec[...], 3)]
    aux = dot(jnp.concatenate(pieces, axis=0).astype(jnp.bfloat16), at_slot, (1, 1))
    columns = aux[0:tiles] + aux[tiles : 2 * tiles]
    precs = (aux[2 * tiles : 3 * tiles] + aux[3 * tiles : 4 * tiles]) + aux[4 * tiles : 5 * tiles]
    sub = sub_iota()
    for owner_at in range(tiles):
        block = jnp.where(sub == 0, columns[owner_at : owner_at + 1], 0.0)
        block = jnp.where(sub == 1, precs[owner_at : owner_at + 1], block)
        out[owner_at, pl.ds(halves * cap, GROUP), :] = block
    rows_high, rows_low = split(op[...], 2)
    chunk = 256
    for first in range(0, tiles * cap, chunk):
        picks = lax.broadcasted_iota(jnp.int32, (chunk, count), 0) + first == place
        picks = jnp.where(picks, 1.0, 0.0).astype(jnp.bfloat16)
        moved = dot(picks, rows_high, (1, 0)) + dot(picks, rows_low, (1, 0))
        for part in range(chunk // cap):
            for half in range(halves):
                out[first // cap + part, pl.ds(half * cap, cap), :] = moved[
                    part * cap : (part + 1) * cap, half * LANES : (half + 1) * LANES
                ]


def innovate_kernel(rows, width, tiles, cap, records, cols, extra, bottom, *rest):
    coupling, wind_ends, wind_dense, dense_g, spread, sel, strips, packed = rest[:8]
    col_cells, precs, both, sems = rest[8:]
    inside = rows * LANES
    chunks = 8
    copies = []
    for part in range(chunks):
        at = pl.ds(part * (2 * width // chunks), 2 * width // chunks)
        copies.append(pltpu.make_async_copy(cols.at[at], col_cells.at[at, pl.ds(0, inside)], sems.at[part]))
        copies[-1].start()
    halves = width // LANES
    count = tiles * cap
    aux = halves * cap
    own = lax.broadcasted_iota(jnp.int32, (cap, LANES), 1) == lax.broadcasted_iota(jnp.int32, (cap, LANES), 0)
    ones = jnp.ones((LANES, LANES), jnp.bfloat16)
    step = 256
    lane = lax.broadcasted_iota(jnp.int32, (step, LANES), 1)
    border = (rows - 1 - lane // (2 * PARTS)) * LANES + jnp.where(lane % 2 == 1, 0, LANES - 1)
    border = jnp.where(lane % (2 * PARTS) < 2, border, -1).astype(jnp.float32)
    lane = lane.astype(jnp.float32)

    def select(block, _):
        sources = step // cap

        def spread_out(part):
            rows_of = [
                jnp.where(own, records[block * sources + s, pl.ds(aux + part, 1), :], 0.0) for s in range(sources)
            ]
            terms = split(jnp.concatenate(rows_of, axis=0), 2 + part)
            return sum(dot(term, ones, (1, 0)) for term in terms)

        at = pl.ds(pl.multiple_of(block * step, step), step)
        place = spread_out(0)
        column = place - lane
        precs[at, :] = spread_out(1)
        for i in range(rows):
            sel[at, i * LANES : (i + 1) * LANES] = jnp.where(column == float(i * LANES), 1.0, 0.0).astype(
                jnp.bfloat16
            )
        sel[at, inside:] = jnp.where(place == border, 1.0, 0.0).astype(jnp.bfloat16)
        return 0

    lax.fori_loop(0, count // step, select, 0)
    for copy in copies:
        copy.wait()
    pair = 2 * GROUP
    first = lax.broadcasted_iota(jnp.int32, (pair, LANES), 0) == 0
    for f in range(2):
        for i in range(rows):
            lanes = slice(i * LANES, (i + 1) * LANES)
            for term, value in enumerate(split(bottom[f * rows + i : f * rows + i + 1, :], 2)):
                at = pl.ds(term * width + f * (width // 2), pair)
                old = col_cells[at, lanes].astype(jnp.float32)
                new = jnp.where(first, value.astype(jnp.float32), old)
                col_cells[at, lanes] = new.astype(jnp.bfloat16)
    for k, i in enumerate((0, rows - 1)):
        lanes = slice(i * LANES, (i + 1) * LANES)
        old = col_cells[:width, lanes].astype(jnp.float32) + col_cells[width:, lanes].astype(jnp.float32)
        more = extra[:, k * LANES : (k + 1) * LANES].astype(jnp.float32)
        high, low = split(old + (more[:width] + more[width:]), 2)
        col_cells[:width, lanes] = high
        col_cells[width:, lanes] = low
    col_cells[:, inside:] = extra[:, 2 * LANES :]
    both[...] = dot(sel[...], col_cells[...], (1, 1))

    def weigh(block, _):
        at = pl.ds(pl.multiple_of(block * LANES, LANES), LANES)
        sources = LANES // cap
        ops = [
            jnp.concatenate(
                [records[block * sources + s, half * cap : (half + 1) * cap, :] for s in range(sources)], axis=0
            )
            for half in range(halves)
        ]
        total = sum(
            (both[at, half * LANES : (half + 1) * LANES] + both[at, width + half * LANES : width + (half + 1) * LANES])
            * ops[half]
            for half in range(halves)
        )
        innovation = jnp.sum(total, axis=1, keepdims=True) * precs[at, :]
        for half in range(halves):
            high, low = split((ops[half] * innovation).T, 2)
            spread[half * LANES : (half + 1) * LANES, at] = high
            spread[width + half * LANES : width + (half + 1) * LANES, at] = low
        return 0

    lax.fori_loop(0, count // LANES, weigh, 0, unroll=4)

    border_cells = jnp.concatenate([sel[:, 0:LANES], sel[:, (rows - 1) * LANES :]], axis=1)
    terms = dot(spread[...], border_cells, (1, 0))
    border_sums = terms[:width] + terms[width:]
    thin = border_sums[:, 2 * LANES :]
    dense = []
    for m in range(width // (GROUP * PARTS)):
        total = thin[m * PARTS * GROUP : (m * PARTS + 1) * GROUP]
        for part in range(1, PARTS):
            at = (m * PARTS + part) * GROUP
            total = total + pltpu.roll(thin[at : at + GROUP], 2 * part, 1)
        dense.append(total)
    ends = (border_sums[:, 0:LANES], border_sums[:, LANES : 2 * LANES])
    packed[packed.shape[0] - GROUP :, :] = jnp.zeros((GROUP, LANES), jnp.float32)
    put_strip(strips, slice(width, width + GROUP), *[jnp.zeros((GROUP, LANES), jnp.float32)] * 2)
    border_strips(
        rows, width // 2, coupling, ends, jnp.concatenate(dense, axis=0), wind_ends, wind_dense, dense_g, strips, packed
    )


def scatter_kernel(rows, width, spread, sel, winds, factors, adjoint, low0, wind_rows, sems):
    low0[2 * rows :, :] = factors[...]
    wind_in = pltpu.make_async_copy(winds, wind_rows.at[pl.ds(1, rows)], sems.at[0])
    wind_in.start()
    wind_rows[0] = jnp.zeros_like(wind_rows[0])
    wind_rows[rows + 1] = jnp.zeros_like(wind_rows[0])
    sums = dot(spread[...], sel[:, : rows * LANES], (1, 0))
    for i in range(rows):
        lanes = slice(i * LANES, (i + 1) * LANES)
        adjoint[i] = sums[:width, lanes] + sums[width:, lanes]
        for f in range(2):
            low0[f * rows + i : f * rows + i + 1, :] = adjoint[i, f * (width // 2) : f * (width // 2) + 1, :]
    wind_in.wait()


def local(state_incr, winds, coupling, background, obs_dest, obs_col, obs_op, obs_prec):
    _, fields, levels, rows, lanes = state_incr.shape
    width = fields * levels
    groups = width // GROUP
    tiles = lax.axis_size("gx") * lax.axis_size("gy")
    count = obs_col.shape[0]
    cap = 2 * count // tiles
    halves = obs_op.shape[1] // LANES

    scale = jnp.broadcast_to(background.reshape(width, 1), (width, LANES))

    vmem = pl.BlockSpec(memory_space=pltpu.VMEM)
    anywhere = pl.BlockSpec(memory_space=pl.ANY)
    own = pltpu.VMEM((rows, width, LANES), jnp.float32)
    framed = pltpu.VMEM((rows + 2, width, LANES), jnp.float32)
    packed_shape = f32(groups // PARTS * GROUP, LANES)
    sides = pltpu.VMEM(packed_shape.shape, jnp.float32)
    strip_shapes = [f32(pair_sets(), width, LANES), packed_shape]
    long_shapes = [f32(pair_sets(), width + GROUP, LANES), f32(packed_shape.shape[0] + GROUP, LANES)]
    field_shape = f32(rows, width, LANES)
    framed_shape = f32(rows + 2, width, LANES)
    low_shape = f32(fields * rows, LANES)
    cols_shape = ((2 * width, rows * LANES), jnp.bfloat16)

    def sems(*shape):
        return pltpu.SemaphoreType.DMA(shape)

    def run(body, out_shape, scratch, args, far=(), out_far=(), **kw):
        args = [pltpu.with_memory_space_constraint(x, pltpu.HBM) if k in far else x for k, x in enumerate(args)]
        specs = [anywhere if k in far else vmem for k in range(len(args))]
        outs = [anywhere if k in out_far else vmem for k in range(len(out_shape))]
        out_shape = [pltpu.HBM(x.shape, x.dtype) if k in out_far else x for k, x in enumerate(out_shape)]
        return call(body, out_shape, scratch, in_specs=specs, out_specs=outs, **kw)(*args)

    def on_rows(body):
        return functools.partial(body, rows, levels)

    def swap_floor(floor):
        return lax.ppermute(floor, "comp", [(0, 1), (1, 0)])

    state = state_incr.reshape(width, rows, lanes)
    wind = winds.reshape(width, rows, lanes)
    floor_winds = winds[0, :, 0]
    slots = tiles * cap
    thin_shape = f32(GROUP, LANES)

    strips, packed, low0, low1 = run(
        on_rows(edges_kernel),
        strip_shapes + [low_shape] * 2,
        [pltpu.VMEM((width * rows, LANES), jnp.float32), sems(groups // PARTS)],
        (state_incr.reshape(width * rows, lanes),),
        far=(0,),
    )
    halos = exchange(strips, packed)

    send = call(functools.partial(route_kernel, tiles, cap), f32(tiles, halves * cap + GROUP, LANES))(
        obs_dest.reshape(1, count), obs_col.reshape(1, count), obs_prec.reshape(1, count), obs_op
    )
    send, halos[0], halos[2], state_far, wind_far = lax.optimization_barrier((send, halos[0], halos[2], state, wind))
    records = lax.all_to_all(send, ("gx", "gy"), split_axis=0, concat_axis=0, tiled=True)

    state_rows, wind_rows, state_later, wind_later = run(
        functools.partial(load_kernel, rows),
        [field_shape] * 4,
        [sems(4, rows)],
        (state_far, wind_far),
        far=(0, 1),
        out_far=(2, 3),
        traffic=10 * MIB,
    )
    halos[1], state_rows, wind_rows = lax.optimization_barrier((halos[1], state_rows, wind_rows))
    (floor,) = run(on_rows(forward_floor_kernel), [low_shape], [], (low0, low1, floor_winds, *halos))
    field, strips, packed, low0, low1, wind_ends, wind_dense, dense_g = run(
        on_rows(forward_kernel),
        [framed_shape]
        + long_shapes
        + [low_shape] * 2
        + [f32(2, levels, LANES), f32(groups // PARTS * GROUP // 2, LANES), thin_shape],
        [framed, sides],
        (coupling, swap_floor(floor), state_rows, wind_rows, *halos),
    )
    halos = exchange(strips, packed)
    (cols,) = run(
        on_rows(forward_again_kernel),
        [jax.ShapeDtypeStruct(*cols_shape)],
        [pltpu.VMEM(*cols_shape), sems(rows)],
        (field, wind_rows),
        out_far=(0,),
        traffic=20 * MIB,
    )
    cols, halos = lax.optimization_barrier((cols, halos))
    (floor,) = run(on_rows(forward_floor_kernel), [low_shape], [], (low0, low1, floor_winds, *halos))
    extra, bottom, factors = run(
        on_rows(outside_kernel),
        [jax.ShapeDtypeStruct((2 * width, 3 * LANES), jnp.bfloat16), low_shape, thin_shape],
        [sides],
        (coupling, floor, swap_floor(floor), wind_ends, wind_dense, *halos),
    )

    spread_shape = ((2 * width, slots), jnp.bfloat16)
    sel_shape = ((slots, (rows + 1) * LANES), jnp.bfloat16)
    spread, sel, strips, packed = run(
        functools.partial(innovate_kernel, rows, width, tiles, cap),
        [jax.ShapeDtypeStruct(*spread_shape), jax.ShapeDtypeStruct(*sel_shape)] + long_shapes,
        [
            pltpu.VMEM((2 * width, (rows + 1) * LANES), jnp.bfloat16),
            pltpu.VMEM((slots, LANES), jnp.float32),
            pltpu.VMEM((slots, 2 * width), jnp.float32),
            sems(8),
        ],
        (records, cols, extra, bottom, coupling, wind_ends, wind_dense, dense_g),
        far=(1,),
        limit=OBSERVE_VMEM,
    )
    halos = exchange(strips, packed)
    adjoint, low0, wind_rows = run(
        functools.partial(scatter_kernel, rows, width),
        [field_shape, f32(fields * rows + GROUP, LANES), framed_shape],
        [sems(1)],
        (spread, sel, wind_later, factors),
        far=(2,),
        limit=OBSERVE_VMEM,
        traffic=8 * MIB,
    )
    partner = swap_floor(low0)
    adjoint, ends, columns, low0, state_rows = run(
        on_rows(first_adjoint_kernel),
        [field_shape, f32(2, width, LANES), packed_shape, low_shape, field_shape],
        [framed, sems(1)],
        (coupling, adjoint, wind_rows, state_later),
        far=(3,),
        traffic=16 * MIB,
    )
    low0, partner, halos = lax.optimization_barrier((low0, partner, halos))
    floor, missing = run(
        on_rows(floor_kernel),
        [f32(fields * rows + GROUP, LANES), low_shape],
        [],
        (coupling, partner, low0, floor_winds, *halos),
    )
    floor, other = run(
        on_rows(level0_kernel),
        [low_shape, low_shape],
        [],
        (floor, swap_floor(floor), factors, partner),
    )
    strips, packed = run(
        on_rows(border_again_kernel),
        strip_shapes,
        [sides],
        (coupling, floor, other, missing, ends, columns, wind_ends, wind_dense, dense_g, *halos),
    )
    last_halos = exchange(strips, packed)
    (adjoint,) = run(
        on_rows(second_adjoint_kernel),
        [field_shape],
        [framed, sides],
        (coupling, floor, other, missing, adjoint, wind_rows, scale, state_rows, *halos),
        traffic=20 * MIB,
    )
    (result,) = run(
        on_rows(final_kernel),
        [f32(width, rows, LANES)],
        [own, sides, sems(rows)],
        (adjoint, *last_halos),
        out_far=(0,),
    )
    return result.reshape(state_incr.shape)


def solution(mesh):
    placed = (
        P("comp", None, None, "gx", "gy"),
        P("comp", None, None, "gx", "gy"),
        P("gx", "gy"),
        P("comp", None, None),
        P(("comp", "gx", "gy"), None),
        P(("comp", "gx", "gy")),
        P(("comp", "gx", "gy"), None),
        P(("comp", "gx", "gy")),
    )
    return jax.shard_map(
        local,
        mesh=mesh,
        in_specs=placed,
        out_specs=P("comp", None, None, "gx", "gy"),
        check_vma=False,
    )
```

```python
import functools

import jax
import jax.numpy as jnp
from jax import lax
from jax.experimental import pallas as pl
from jax.experimental.pallas import tpu as pltpu
from jax.sharding import PartitionSpec as P

HORIZ_MIX = 0.1
VERT_MIX = 0.15
LANES = 128
GROUP = 8
MIB = 1024 * 1024
SWEEP_VMEM = 16 * MIB
OBSERVE_VMEM = 22 * MIB


def call(body, out_shape, scratch=(), limit=SWEEP_VMEM, traffic=0, **kw):
    cost = pl.CostEstimate(flops=0, bytes_accessed=traffic, transcendentals=0) if traffic else None
    return pl.pallas_call(
        body,
        out_shape=out_shape,
        scratch_shapes=list(scratch),
        cost_estimate=cost,
        compiler_params=pltpu.CompilerParams(vmem_limit_bytes=limit),
        **kw,
    )


def f32(*shape):
    return jax.ShapeDtypeStruct(shape, jnp.float32)


def lane_iota(rows=GROUP):
    return lax.broadcasted_iota(jnp.int32, (rows, LANES), 1)


def sub_iota(rows=GROUP):
    return lax.broadcasted_iota(jnp.int32, (rows, LANES), 0)


def pair_swap(block, axis, start):
    count = lax.axis_size(axis)
    route = []
    for low in range(start, count - 1, 2):
        route += [(low, low + 1), (low + 1, low)]
    return lax.ppermute(block, axis, route)


def pair_sets():
    return 2 if lax.axis_size("gx") > 2 else 1


def exchange(strips, packed):
    y_even = pair_swap(packed, "gy", 0)
    y_odd = pair_swap(packed, "gy", 1)
    even, *odd = [pair_swap(strips[start], "gx", start) for start in range(pair_sets())]
    return [even, y_even, y_odd, *odd]


def is_odd(axis):
    return lax.rem(lax.axis_index(axis), 2) == 1


def read_sides(refs):
    even = refs[0]
    odd = refs[3] if len(refs) > 3 else None
    at_odd = is_odd("gx")

    def side(at, turned):
        other = jnp.zeros_like(even[at]) if odd is None else odd[at]
        return jnp.where(turned, other, even[at])

    return lambda at: side(at, jnp.logical_not(at_odd)), lambda at: side(at, at_odd)


PARTS = 4


def merged(y_even, y_odd, at):
    a, b = y_even[at, :], y_odd[at, :]
    lane = lax.broadcasted_iota(jnp.int32, a.shape, 1)
    return jnp.where((lane % 2 == 1) == jnp.logical_not(is_odd("gy")), a, b)


def merge_columns(y_even, y_odd, sides):
    sides[...] = merged(y_even, y_odd, slice(0, sides.shape[0]))


def slot_of(i, part, rows):
    return PARTS * (rows - 1 - i) + part


def side_columns(sides, i, group):
    m, part = group // PARTS, group % PARTS
    rows = LANES // (2 * PARTS)
    return pltpu.roll(sides[m * GROUP : (m + 1) * GROUP, :], LANES - 1 - 2 * slot_of(i, part, rows), 1)


def pack_into(total, value, slot):
    return jnp.where(lane_iota() // 2 == slot, pltpu.roll(value, 2 * slot + 1, 1), total)


def pack_block(packed, values, i, m):
    at = pl.ds(m * GROUP, GROUP)
    total = packed[at, :]
    for part, value in enumerate(values):
        total = pack_into(total, value, slot_of(i, part, LANES // (2 * PARTS)))
    packed[at, :] = total


CENTRE = 1.0 - 4.0 * HORIZ_MIX - 2.0 * VERT_MIX


def levels_around(cells, i, base, group, groups):
    here = cells[i + 1, pl.ds(base + group * GROUP, GROUP), :]
    if group == groups - 1:
        upper = jnp.where(sub_iota() == GROUP - 1, here, pltpu.roll(here, GROUP - 1, 0))
    else:
        upper = cells[i + 1, pl.ds(base + group * GROUP + 1, GROUP), :]
    if group == 0:
        lower = jnp.where(sub_iota() == 0, here, pltpu.roll(here, 1, 0))
    else:
        lower = cells[i + 1, pl.ds(base + group * GROUP - 1, GROUP), :]
    return here, upper, lower


def shifted(first, last, edge, rows=GROUP):
    lane = lane_iota(rows)
    right = pltpu.roll(jnp.where(lane == 0, edge, first), LANES - 1, 1)
    left = pltpu.roll(jnp.where(lane == LANES - 1, edge, last), 1, 1)
    return right, left


def forward_sum(here, vertical, after, before, right, left, u, w):
    return (
        CENTRE * here
        + VERT_MIX * vertical
        + HORIZ_MIX * ((after + before) + (right + left))
        - 0.5 * (u * (after - before) + w * (right - left))
    )


def forward_point(cells, winds, sides, i, f, group, levels):
    groups = levels // GROUP
    here, upper, lower = levels_around(cells, i, f * levels, group, groups)
    at = pl.ds(f * levels + group * GROUP, GROUP)
    right, left = shifted(here, here, 0.0 if sides is None else side_columns(sides, i, f * groups + group))
    u = winds[i, pl.ds(group * GROUP, GROUP), :]
    w = winds[i, pl.ds(levels + group * GROUP, GROUP), :]
    return forward_sum(here, upper + lower, cells[i + 2, at, :], cells[i, at, :], right, left, u, w)


def products(x, wind):
    slope = 0.5 * (wind * x)
    return HORIZ_MIX * x - slope, HORIZ_MIX * x + slope


def adjoint_point(cells, winds, i, f, group, levels):
    here, upper, lower = levels_around(cells, i, f * levels, group, levels // GROUP)
    at = pl.ds(f * levels + group * GROUP, GROUP)
    wind_at = pl.ds(group * GROUP, GROUP)
    after, before = cells[i + 2, at, :], cells[i, at, :]
    u_after, u_before = winds[i + 2, wind_at, :], winds[i, wind_at, :]
    down, up = products(here, winds[i + 1, pl.ds(levels + group * GROUP, GROUP), :])
    right, left = shifted(up, down, 0.0)
    return (
        CENTRE * here
        + VERT_MIX * (upper + lower)
        + HORIZ_MIX * (after + before)
        + 0.5 * (u_after * after - u_before * before)
        + (right + left)
    )


def shares_of(coupling):
    own = jnp.where(lax.axis_index("comp") == 0, 1.0, 0.5)
    return own * coupling, (1.5 - own) * coupling


def couple_forward(value, other, coupling):
    own, _ = shares_of(coupling)
    return value - own * (value - other)


def couple_adjoint(value, other, coupling):
    own, peer = shares_of(coupling)
    return value - own * value + peer * other


def coupled(rule, value, other, coupling, i, f, rows):
    mixed = rule(value, other[pl.ds(f * rows + i, 1), :], coupling[pl.ds(i, 1), :])
    return jnp.where(sub_iota() == 0, mixed, value)


def put_strip(strips, at, first, last):
    at_odd = is_odd("gx")
    strips[0, at, :] = jnp.where(at_odd, first, last)
    if strips.shape[0] > 1:
        strips[1, at, :] = jnp.where(at_odd, last, first)


def put_low(low, value, i, f, rows):
    for level in range(2):
        low[level][pl.ds(f * rows + i, 1), :] = value[level : level + 1]


class Rows:
    def __init__(self, source, target, sems, rows, as_it_comes, offset):
        self.source, self.target, self.sems = source, target, sems
        self.rows, self.as_it_comes, self.offset = rows, as_it_comes, offset

    def copy(self, i):
        row = self.source.at[:, i] if self.as_it_comes else self.source.at[i]
        return pltpu.make_async_copy(row, self.target.at[i + self.offset], self.sems.at[i])

    def wait(self, i):
        self.copy(i).wait()


def start_rows(rows, *groups):
    for i in range(rows):
        for group in groups:
            group.copy(i).start()


def edges_kernel(rows, levels, state, strips, packed, low0, low1, cells, sems):
    part_levels = PARTS * GROUP
    blocks = 2 * levels // part_levels

    def copy(m):
        return pltpu.make_async_copy(
            state.at[pl.ds(m * part_levels * rows, part_levels * rows)],
            cells.at[pl.ds(m * part_levels * rows, part_levels * rows)],
            sems.at[m],
        )

    for m in range(blocks):
        copy(m).start()

    def block(m, _):
        copy(m).wait()
        total = jnp.zeros((GROUP, LANES), jnp.float32)
        for part in range(PARTS):
            for i in range(rows):
                start = (m * PARTS + part) * GROUP * rows + i
                total = pack_into(total, cells[pl.ds(start, GROUP, stride=rows), :], slot_of(i, part, rows))
        packed[pl.ds(pl.multiple_of(m * GROUP, GROUP), GROUP), :] = total
        start = m * part_levels * rows
        first = cells[pl.ds(start, part_levels, stride=rows), :]
        last = cells[pl.ds(start + rows - 1, part_levels, stride=rows), :]
        put_strip(strips, pl.ds(pl.multiple_of(m * part_levels, part_levels), part_levels), first, last)
        return 0

    lax.fori_loop(0, blocks, block, 0)
    for f in range(2):
        for level, low in enumerate((low0, low1)):
            low[f * rows : (f + 1) * rows, :] = cells[pl.ds((f * levels + level) * rows, rows), :]


def floor_edge(halos, f, rows, levels):
    m = f * (levels // GROUP) // PARTS
    sides = jnp.broadcast_to(merged(halos[1], halos[2], pl.ds(m * GROUP, 1)), (rows, LANES))
    return pltpu.roll(sides, 2 * PARTS - 1, 1, stride=2 * PARTS, stride_axis=0)


def row_after(value, last, rows):
    return jnp.where(sub_iota(rows) == rows - 1, last, pltpu.roll(value, rows - 1, 0))


def row_before(value, first, rows):
    return jnp.where(sub_iota(rows) == 0, first, pltpu.roll(value, 1, 0))


def forward_floor_kernel(rows, levels, low0, low1, winds, *rest):
    *halos, floor = rest
    side_before, side_after = read_sides(halos)
    for f in range(2):
        here = pl.ds(f * rows, rows)
        at = pl.ds(f * levels, 1)
        low, up = low0[here, :], low1[here, :]
        after, before = row_after(low, side_after(at), rows), row_before(low, side_before(at), rows)
        right, left = shifted(low, low, floor_edge(halos, f, rows, levels), rows)
        floor[here, :] = forward_sum(low, up + low, after, before, right, left, winds[0], winds[1])


class Out:
    def __init__(self, source, target, sems, rows, as_it_goes):
        self.source, self.target, self.sems, self.rows, self.as_it_goes = source, target, sems, rows, as_it_goes

    def copy(self, i):
        row = self.target.at[:, i] if self.as_it_goes else self.target.at[i]
        return pltpu.make_async_copy(self.source.at[i], row, self.sems.at[i])

    def start(self, i):
        self.copy(i).start()

    def finish(self):
        for i in range(self.rows):
            self.copy(i).wait()


def dense_row(field, first, rows):
    total = jnp.zeros((1, LANES), jnp.float32)
    lane = lax.broadcasted_iota(jnp.int32, (1, LANES), 1)
    for i in range(rows):
        slot = slot_of(i, 0, rows)
        total = jnp.where(lane // 2 == slot, pltpu.roll(field[first + i : first + i + 1, :], 2 * slot + 1, 1), total)
    return total


def load_kernel(rows, state, winds, state_rows, wind_rows, state_later, wind_later, sems):
    state_in = Rows(state, state_rows, sems.at[0], rows, True, 0)
    wind_in = Rows(winds, wind_rows, sems.at[1], rows, True, 0)
    state_out = Out(state_rows, state_later, sems.at[2], rows, False)
    wind_out = Out(wind_rows, wind_later, sems.at[3], rows, False)
    start_rows(rows, state_in, wind_in)
    for i in range(rows):
        state_in.wait(i)
        wind_in.wait(i)
        state_out.start(i)
        wind_out.start(i)
    state_out.finish()
    wind_out.finish()


def forward_kernel(rows, levels, coupling, other, field, winds, *rest):
    *halos, out, strips, packed, low0, low1, wind_ends, wind_dense, dense_g, cells, sides = rest
    packed[...] = jnp.zeros_like(packed)
    wind_dense[...] = jnp.zeros_like(wind_dense)
    merge_columns(halos[1], halos[2], sides)
    before, after = read_sides(halos)
    cells[0] = before(pl.ds(0, 2 * levels))
    cells[1] = field[0]
    cells[rows + 1] = after(pl.ds(0, 2 * levels))
    out[0] = jnp.zeros_like(out[0])
    out[rows + 1] = jnp.zeros_like(out[0])
    groups = levels // GROUP

    def row(i, _):
        @pl.when(i < rows - 1)
        def _():
            cells[i + 2] = field[i + 1]

        for m in range(2 * groups // PARTS):
            f, start = m * PARTS // groups, m * PARTS % groups
            values = []
            for group in range(start, start + PARTS):
                value = forward_point(cells, winds, sides, i, f, group, levels)
                if group == 0:
                    value = coupled(couple_forward, value, other, coupling, i, f, rows)
                    put_low((low0, low1), value, i, f, rows)
                values.append(value)
            base = m * PARTS * GROUP
            for part, value in enumerate(values):
                out[i + 1, pl.ds(base + part * GROUP, GROUP), :] = value
            pack_block(packed, values, i, m)
            if f == 0:
                w = [winds[i, pl.ds(levels + base + part * GROUP, GROUP), :] for part in range(PARTS)]
                pack_block(wind_dense, w, i, m)
        return 0

    lax.fori_loop(0, rows, row, 0)
    put_strip(strips, pl.ds(0, 2 * levels), out[1], out[rows])
    wind_ends[0] = winds[0, pl.ds(0, levels), :]
    wind_ends[1] = winds[rows - 1, pl.ds(0, levels), :]
    dense_g[...] = jnp.broadcast_to(dense_row(coupling, 0, rows), dense_g.shape)
    _, peer = shares_of(coupling[...])
    first = products(peer[0:1], winds[0, 0:1, :])[1]
    last = products(peer[rows - 1 : rows], winds[rows - 1, 0:1, :])[0]
    whole = (GROUP, LANES)
    put_strip(strips, slice(2 * levels, 2 * levels + GROUP), jnp.broadcast_to(first, whole), jnp.broadcast_to(last, whole))
    _, peer = shares_of(dense_g[...])
    packed[packed.shape[0] - GROUP :, :] = first_and_last(peer, wind_dense[0:1, :])


def forward_again_kernel(rows, levels, cells, winds, cols, col_cells, col_sems):
    groups = levels // GROUP
    width = 2 * levels

    def col_copy(i):
        lanes = pl.ds(pl.multiple_of(i * LANES, LANES), LANES)
        return pltpu.make_async_copy(col_cells.at[:, lanes], cols.at[:, lanes], col_sems.at[i])

    def row(i, _):
        lanes = pl.ds(pl.multiple_of(i * LANES, LANES), LANES)
        for m in range(2 * groups // PARTS):
            f, start = m * PARTS // groups, m * PARTS % groups
            values = [forward_point(cells, winds, None, i, f, group, levels) for group in range(start, start + PARTS)]
            high, low = split(jnp.concatenate(values, axis=0), 2)
            col_cells[pl.ds(m * PARTS * GROUP, PARTS * GROUP), lanes] = high
            col_cells[pl.ds(width + m * PARTS * GROUP, PARTS * GROUP), lanes] = low
        col_copy(i).start()
        return 0

    lax.fori_loop(0, rows, row, 0)
    for i in range(rows):
        col_copy(i).wait()


def outside_kernel(rows, levels, coupling, floor, other, wind_ends, wind_dense, *rest):
    *halos, extra, bottom, factors, dense = rest
    width = 2 * levels
    tail = pl.ds(width, 1)
    factors[...] = jnp.zeros_like(factors)
    for k, side in enumerate(read_sides(halos)):
        factors[k : k + 1, :] = side(tail)
    factors[2:3, :] = merged(halos[1], halos[2], pl.ds(dense.shape[0], 1))
    for f in range(2):
        here = pl.ds(f * rows, rows)
        bottom[here, :] = couple_forward(floor[here, :], other[here, :], coupling[...])
    dense_products(dense, swap_pairs(merged(halos[1], halos[2], slice(0, dense.shape[0]))), wind_dense)
    before, after = read_sides(halos)
    sub = lax.broadcasted_iota(jnp.int32, (levels, LANES), 0)

    def put(value, f, lanes):
        high, low = split(jnp.where(sub == 0, 0.0, value), 2)
        extra[f * levels : (f + 1) * levels, lanes] = high
        extra[width + f * levels : width + (f + 1) * levels, lanes] = low

    lane = lane_iota()
    for f in range(2):
        at = pl.ds(f * levels, levels)
        put(products(before(at), wind_ends[0])[1], f, slice(0, LANES))
        put(products(after(at), wind_ends[1])[0], f, slice(LANES, 2 * LANES))
        thin = []
        for group in range(f * levels // GROUP, (f + 1) * levels // GROUP):
            m, part = group // PARTS, group % PARTS
            moved = pltpu.roll(dense[m * GROUP : (m + 1) * GROUP, :], (LANES - 2 * part) % LANES, 1)
            thin.append(jnp.where(lane % (2 * PARTS) < 2, moved, 0.0))
        put(jnp.concatenate(thin, axis=0), f, slice(2 * LANES, 3 * LANES))


def first_and_last(value, wind):
    down, up = products(value, wind)
    lane = lax.broadcasted_iota(jnp.int32, down.shape, 1)
    return jnp.where(lane % 2 == 1, up, down)


def dense_products(packed, value, wind_dense):
    half = wind_dense.shape[0]
    for f in range(2):
        at = slice(f * half, (f + 1) * half)
        packed[at, :] = first_and_last(value[at], wind_dense[...])


def level0_row(value, new, f):
    half = value.shape[0] // 2
    sub = lax.broadcasted_iota(jnp.int32, value.shape, 0)
    lane = lax.broadcasted_iota(jnp.int32, value.shape, 1)
    return jnp.where((sub == f * half) & (lane % (2 * PARTS) < 2), new, value)


def end_rows(ends, strips, wind_ends, levels):
    for f in range(2):
        at = slice(f * levels, (f + 1) * levels)
        put_strip(
            strips, at, products(ends[0][at], wind_ends[0])[1], products(ends[1][at], wind_ends[1])[0]
        )


def with_first(value, new):
    return jnp.where(lax.broadcasted_iota(jnp.int32, value.shape, 0) == 0, new, value)


def border_strips(rows, levels, coupling, ends, dense, wind_ends, wind_dense, dense_g, strips, packed):
    half = dense.shape[0] // 2
    width = 2 * levels
    own, _ = shares_of(dense_g[0:1, :])
    new = dense
    for f in range(2):
        bottom = dense[f * half : f * half + 1]
        new = level0_row(new, bottom - own * bottom, f)
        packed[2 * half + f : 2 * half + f + 1, :] = bottom
    dense_products(packed, new, wind_dense)
    full = []
    for k, i in enumerate((0, rows - 1)):
        own, _ = shares_of(coupling[i : i + 1, :])
        parts = []
        for f in range(2):
            value = ends[k][f * levels : (f + 1) * levels]
            parts.append(with_first(value, value[0:1] - own * value[0:1]))
        full.append(jnp.concatenate(parts, axis=0))
    end_rows(full, strips, wind_ends, levels)
    for f in range(2):
        at = f * levels
        put_strip(strips, slice(width + f, width + f + 1), ends[0][at : at + 1], ends[1][at : at + 1])


def to_border(low, before, after, sides, rows):
    sub, lane = sub_iota(rows), lane_iota(rows)
    low = low + jnp.where(sub == 0, before, 0.0) + jnp.where(sub == rows - 1, after, 0.0)
    edge = pltpu.roll(jnp.broadcast_to(sides, (rows, LANES)), 2 * PARTS - 1, 1, stride=2 * PARTS, stride_axis=0)
    edge = jnp.where(lane == 0, pltpu.roll(edge, 1, 1), pltpu.roll(edge, LANES - 1, 1))
    return low + jnp.where((lane == 0) | (lane == LANES - 1), edge, 0.0)


def floor_kernel(rows, levels, coupling, other, low0, winds, *rest):
    *halos, floor, missing = rest
    before, after = read_sides(halos)
    half = halos[1].shape[0] - GROUP
    for f in range(2):
        here = pl.ds(f * rows, rows)
        _, peer = shares_of(coupling[...])
        share = peer * other[here, :]
        x_down, x_up = products(share, winds[0])
        y_down, y_up = products(share, winds[1])
        right, left = shifted(y_up, y_down, 0.0, rows)
        spread = (row_after(x_up, 0.0, rows) + row_before(x_down, 0.0, rows)) + (right + left)
        spread = spread + (CENTRE + VERT_MIX) * share
        at = pl.ds(f * levels, 1)
        sides = merged(halos[1], halos[2], pl.ds(f * half // 2, 1))
        floor[here, :] = to_border(low0[here, :] + spread, before(at), after(at), sides, rows)
        missing[here, :] = VERT_MIX * share
    raw = 2 * rows
    floor[raw : raw + 2, :] = before(pl.ds(2 * levels, 2))
    floor[raw + 2 : raw + 4, :] = after(pl.ds(2 * levels, 2))
    floor[raw + 4 : raw + 6, :] = merged(halos[1], halos[2], pl.ds(half, 2))
    floor[raw + 6 : raw + GROUP, :] = jnp.zeros((2, LANES), jnp.float32)


def level0_kernel(rows, levels, floor, other, factors, partner, floor_out, other_out):
    raw = 2 * rows
    for mine, theirs, factor, at, out in ((floor, other, factors, 0, floor_out), (other, floor, partner, raw, other_out)):
        for f in range(2):
            here = pl.ds(f * rows, rows)
            parts = [factor[at + k : at + k + 1, :] * theirs[raw + 2 * k + f : raw + 2 * k + f + 1, :] for k in range(3)]
            out[here, :] = to_border(mine[here, :], *parts, rows)


def swap_pairs(value):
    lane = lax.broadcasted_iota(jnp.int32, value.shape, 1)
    return jnp.where(lane % 2 == 1, pltpu.roll(value, 1, 1), pltpu.roll(value, LANES - 1, 1))


def edge_lanes(sides, i, group):
    m, part = group // PARTS, group % PARTS
    rows = LANES // (2 * PARTS)
    moved = pltpu.roll(sides[m * GROUP : (m + 1) * GROUP, :], LANES - 1 - 2 * slot_of(i, part, rows), 1)
    lane = lane_iota()
    return jnp.where((lane == 0) | (lane == LANES - 1), moved, 0.0)


def with_level(value, level, new):
    return jnp.where(lax.broadcasted_iota(jnp.int32, value.shape, 0) == level, new, value)


def border_again_kernel(
    rows, levels, coupling, floor, other, missing, ends, columns, wind_ends, wind_dense, dense_g, *rest
):
    *halos, strips, packed, sides = rest
    before, after = read_sides(halos)
    sides[...] = swap_pairs(merged(halos[1], halos[2], slice(0, sides.shape[0])))
    half = columns.shape[0] // 2
    groups = levels // GROUP
    outer = [before(pl.ds(0, 2 * levels)), after(pl.ds(0, 2 * levels))]
    full = []
    for k, i in enumerate((0, rows - 1)):
        edges = jnp.concatenate([edge_lanes(sides, i, group) for group in range(2 * groups)], axis=0)
        value = ends[k] + outer[k] + edges
        parts = []
        for f in range(2):
            part = value[f * levels : (f + 1) * levels]
            at = slice(f * rows + i, f * rows + i + 1)
            part = part + with_level(jnp.zeros_like(part), 1, missing[at, :])
            parts.append(with_first(part, couple_adjoint(floor[at, :], other[at, :], coupling[i : i + 1, :])))
        full.append(jnp.concatenate(parts, axis=0))
    end_rows(full, strips, wind_ends, levels)
    dense = columns[...] + sides[...]
    corners = []
    for m in range(2 * groups // PARTS):
        total = jnp.zeros((GROUP, LANES), jnp.float32)
        for part in range(PARTS):
            at = slice((m * PARTS + part) * GROUP, (m * PARTS + part + 1) * GROUP)
            for k, i in enumerate((0, rows - 1)):
                total = pack_into(total, outer[k][at], slot_of(i, part, rows))
        corners.append(total)
    dense = dense + jnp.concatenate(corners, axis=0)
    for f in range(2):
        sub = lax.broadcasted_iota(jnp.int32, dense.shape, 0)
        dense = dense + jnp.where(sub == f * half + 1, dense_row(missing, f * rows, rows), 0.0)
        mine = dense_row(floor, f * rows, rows)
        mixed = couple_adjoint(mine, dense_row(other, f * rows, rows), dense_g[0:1, :])
        dense = level0_row(dense, mixed, f)
    dense_products(packed, dense, wind_dense)


def adjoint_rows(rows, levels, cells, winds, take, each, behind=None):
    groups = levels // GROUP
    cells[0] = jnp.zeros_like(cells[0])
    cells[rows + 1] = jnp.zeros_like(cells[0])
    take(0)
    take(1)

    def row(i, _):
        if behind is not None:
            behind(jnp.maximum(i - 1, 0))
        for m in range(2 * groups // PARTS):
            f, start = m * PARTS // groups, m * PARTS % groups
            each(i, m, f, start, [
                adjoint_point(cells, winds, i, f, group, levels) for group in range(start, start + PARTS)
            ])
        take(jnp.minimum(i + 2, rows - 2))
        return 0

    lax.fori_loop(0, rows, row, 0, unroll=1 if behind is None else 2)
    if behind is not None:
        behind(rows - 1)


def first_adjoint_kernel(rows, levels, coupling, field, winds, state, out, ends, columns, low0, state_rows, cells, sems):
    state_in = pltpu.make_async_copy(state, state_rows, sems.at[0])
    state_in.start()
    columns[...] = jnp.zeros_like(columns)

    def take(i):
        cells[i + 1] = field[i]
        for f in range(2):
            at = pl.ds(f * levels, GROUP)
            own, _ = shares_of(coupling[pl.ds(i, 1), :])
            value = field[i, at, :]
            cells[i + 1, at, :] = jnp.where(sub_iota() == 0, value - own * value, value)

    def each(i, m, f, start, values):
        for part, value in enumerate(values):
            out[i, pl.ds((m * PARTS + part) * GROUP, GROUP), :] = value
        if start == 0:
            low0[pl.ds(f * rows + i, 1), :] = values[0][0:1]

    def pack(i):
        for m in range(columns.shape[0] // GROUP):
            values = [out[i, pl.ds((m * PARTS + part) * GROUP, GROUP), :] for part in range(PARTS)]
            pack_block(columns, values, i, m)

    out[0] = jnp.zeros_like(out[0])
    take(rows - 1)
    adjoint_rows(rows, levels, cells, winds, take, each, pack)
    ends[0] = out[0]
    ends[1] = out[rows - 1]
    state_in.wait()


def second_adjoint_kernel(rows, levels, coupling, floor, other, missing, field, winds, scale, state, *rest):
    *halos, out, cells, sides = rest
    sides[...] = swap_pairs(merged(halos[1], halos[2], slice(0, sides.shape[0])))
    before, after = read_sides(halos)
    groups = levels // GROUP

    def take(i, outer=None):
        for group in range(2 * groups):
            at = pl.ds(group * GROUP, GROUP)
            value = field[i, at, :] + edge_lanes(sides, i, group)
            if outer is not None:
                value = value + outer(at)
            if group % groups == 0:
                here = pl.ds(group // groups * rows + i, 1)
                value = value + jnp.where(sub_iota() == 1, missing[here, :], 0.0)
                bottom = couple_adjoint(floor[here, :], other[here, :], coupling[pl.ds(i, 1), :])
                value = jnp.where(sub_iota() == 0, bottom, value)
            cells[i + 1, at, :] = value

    def take_inner(i):
        take(i, before if isinstance(i, int) and i == 0 else None)

    def each(i, m, f, start, values):
        for part, value in enumerate(values):
            at = pl.ds((m * PARTS + part) * GROUP, GROUP)
            out[i, at, :] = value + scale[at, :] * state[i, at, :]

    take(rows - 1, after)
    adjoint_rows(rows, levels, cells, winds, take_inner, each)


def final_kernel(rows, levels, field, *rest):
    *halos, out, cells, sides, sems = rest
    leaving = Out(cells, out, sems, rows, True)
    sides[...] = swap_pairs(merged(halos[1], halos[2], slice(0, sides.shape[0])))
    before, after = read_sides(halos)
    groups = levels // GROUP

    def add(i, outer):
        for group in range(2 * groups):
            at = pl.ds(group * GROUP, GROUP)
            value = field[i, at, :] + edge_lanes(sides, i, group)
            cells[i, at, :] = value if outer is None else value + outer(at)
        leaving.start(i)
        return 0

    lax.fori_loop(1, rows - 1, lambda i, _: add(i, None), 0, unroll=7)
    add(0, before)
    add(rows - 1, after)
    leaving.finish()


def split(value, terms):
    parts = []
    for _ in range(terms):
        part = value.astype(jnp.bfloat16)
        parts.append(part)
        value = value - part.astype(jnp.float32)
    return parts


def dot(a, b, contract):
    return lax.dot_general(a, b, ((contract[:1], contract[1:]), ((), ())), preferred_element_type=jnp.float32)


def route_kernel(tiles, cap, dest, col, prec, op, out):
    count = op.shape[0]
    width = op.shape[1]
    halves = width // LANES
    owner = lax.broadcasted_iota(jnp.int32, (tiles, count), 0)
    hits = owner == dest[...]
    ones = jnp.where(hits, 1.0, 0.0)
    earlier = lax.broadcasted_iota(jnp.int32, (count, count), 0) <= lax.broadcasted_iota(jnp.int32, (count, count), 1)
    running = dot(ones.astype(jnp.bfloat16), jnp.where(earlier, 1.0, 0.0).astype(jnp.bfloat16), (1, 0))
    slot = jnp.sum(running * ones, axis=0, keepdims=True) - 1.0
    slot = slot.astype(jnp.int32)
    place = dest[...] * cap + slot
    at_slot = lax.broadcasted_iota(jnp.int32, (LANES, count), 0) == slot
    at_slot = jnp.where(at_slot, 1.0, 0.0).astype(jnp.bfloat16)
    column = col[...].astype(jnp.float32)
    pieces = [ones * part.astype(jnp.float32) for part in split(column, 2) + split(prec[...], 3)]
    aux = dot(jnp.concatenate(pieces, axis=0).astype(jnp.bfloat16), at_slot, (1, 1))
    columns = aux[0:tiles] + aux[tiles : 2 * tiles]
    precs = (aux[2 * tiles : 3 * tiles] + aux[3 * tiles : 4 * tiles]) + aux[4 * tiles : 5 * tiles]
    sub = sub_iota()
    for owner_at in range(tiles):
        block = jnp.where(sub == 0, columns[owner_at : owner_at + 1], 0.0)
        block = jnp.where(sub == 1, precs[owner_at : owner_at + 1], block)
        out[owner_at, pl.ds(halves * cap, GROUP), :] = block
    rows_high, rows_low = split(op[...], 2)
    chunk = 256
    for first in range(0, tiles * cap, chunk):
        picks = lax.broadcasted_iota(jnp.int32, (chunk, count), 0) + first == place
        picks = jnp.where(picks, 1.0, 0.0).astype(jnp.bfloat16)
        moved = dot(picks, rows_high, (1, 0)) + dot(picks, rows_low, (1, 0))
        for part in range(chunk // cap):
            for half in range(halves):
                out[first // cap + part, pl.ds(half * cap, cap), :] = moved[
                    part * cap : (part + 1) * cap, half * LANES : (half + 1) * LANES
                ]


def innovate_kernel(rows, width, tiles, cap, records, cols, extra, bottom, *rest):
    coupling, wind_ends, wind_dense, dense_g, spread, sel, strips, packed = rest[:8]
    col_cells, precs, both, sems = rest[8:]
    inside = rows * LANES
    chunks = 8
    copies = []
    for part in range(chunks):
        at = pl.ds(part * (2 * width // chunks), 2 * width // chunks)
        copies.append(pltpu.make_async_copy(cols.at[at], col_cells.at[at, pl.ds(0, inside)], sems.at[part]))
        copies[-1].start()
    halves = width // LANES
    count = tiles * cap
    aux = halves * cap
    own = lax.broadcasted_iota(jnp.int32, (cap, LANES), 1) == lax.broadcasted_iota(jnp.int32, (cap, LANES), 0)
    ones = jnp.ones((LANES, LANES), jnp.bfloat16)
    step = 512
    lane = lax.broadcasted_iota(jnp.int32, (step, LANES), 1)
    border = (rows - 1 - lane // (2 * PARTS)) * LANES + jnp.where(lane % 2 == 1, 0, LANES - 1)
    border = jnp.where(lane % (2 * PARTS) < 2, border, -1).astype(jnp.float32)
    lane = lane.astype(jnp.float32)

    def select(block, _):
        sources = step // cap

        def spread_out(part):
            rows_of = [
                jnp.where(own, records[block * sources + s, pl.ds(aux + part, 1), :], 0.0) for s in range(sources)
            ]
            terms = split(jnp.concatenate(rows_of, axis=0), 2 + part)
            return sum(dot(term, ones, (1, 0)) for term in terms)

        at = pl.ds(pl.multiple_of(block * step, step), step)
        place = spread_out(0)
        column = place - lane
        precs[at, :] = spread_out(1)
        for i in range(rows):
            sel[at, i * LANES : (i + 1) * LANES] = jnp.where(column == float(i * LANES), 1.0, 0.0).astype(
                jnp.bfloat16
            )
        sel[at, inside:] = jnp.where(place == border, 1.0, 0.0).astype(jnp.bfloat16)
        return 0

    lax.fori_loop(0, count // step, select, 0)
    for copy in copies:
        copy.wait()
    pair = 2 * GROUP
    first = lax.broadcasted_iota(jnp.int32, (pair, LANES), 0) == 0
    for f in range(2):
        for i in range(rows):
            lanes = slice(i * LANES, (i + 1) * LANES)
            for term, value in enumerate(split(bottom[f * rows + i : f * rows + i + 1, :], 2)):
                at = pl.ds(term * width + f * (width // 2), pair)
                old = col_cells[at, lanes].astype(jnp.float32)
                new = jnp.where(first, value.astype(jnp.float32), old)
                col_cells[at, lanes] = new.astype(jnp.bfloat16)
    for k, i in enumerate((0, rows - 1)):
        lanes = slice(i * LANES, (i + 1) * LANES)
        old = col_cells[:width, lanes].astype(jnp.float32) + col_cells[width:, lanes].astype(jnp.float32)
        more = extra[:, k * LANES : (k + 1) * LANES].astype(jnp.float32)
        high, low = split(old + (more[:width] + more[width:]), 2)
        col_cells[:width, lanes] = high
        col_cells[width:, lanes] = low
    col_cells[:, inside:] = extra[:, 2 * LANES :]
    both[...] = dot(sel[...], col_cells[...], (1, 1))

    def weigh(block, _):
        at = pl.ds(pl.multiple_of(block * LANES, LANES), LANES)
        sources = LANES // cap
        ops = [
            jnp.concatenate(
                [records[block * sources + s, half * cap : (half + 1) * cap, :] for s in range(sources)], axis=0
            )
            for half in range(halves)
        ]
        total = sum(
            (both[at, half * LANES : (half + 1) * LANES] + both[at, width + half * LANES : width + (half + 1) * LANES])
            * ops[half]
            for half in range(halves)
        )
        innovation = jnp.sum(total, axis=1, keepdims=True) * precs[at, :]
        for half in range(halves):
            high, low = split((ops[half] * innovation).T, 2)
            spread[half * LANES : (half + 1) * LANES, at] = high
            spread[width + half * LANES : width + (half + 1) * LANES, at] = low
        return 0

    lax.fori_loop(0, count // LANES, weigh, 0, unroll=4)

    border_cells = jnp.concatenate([sel[:, 0:LANES], sel[:, (rows - 1) * LANES :]], axis=1)
    terms = dot(spread[...], border_cells, (1, 0))
    border_sums = terms[:width] + terms[width:]
    thin = border_sums[:, 2 * LANES :]
    dense = []
    for m in range(width // (GROUP * PARTS)):
        total = thin[m * PARTS * GROUP : (m * PARTS + 1) * GROUP]
        for part in range(1, PARTS):
            at = (m * PARTS + part) * GROUP
            total = total + pltpu.roll(thin[at : at + GROUP], 2 * part, 1)
        dense.append(total)
    ends = (border_sums[:, 0:LANES], border_sums[:, LANES : 2 * LANES])
    packed[packed.shape[0] - GROUP :, :] = jnp.zeros((GROUP, LANES), jnp.float32)
    put_strip(strips, slice(width, width + GROUP), *[jnp.zeros((GROUP, LANES), jnp.float32)] * 2)
    border_strips(
        rows, width // 2, coupling, ends, jnp.concatenate(dense, axis=0), wind_ends, wind_dense, dense_g, strips, packed
    )


def scatter_kernel(rows, width, spread, sel, winds, factors, adjoint, low0, wind_rows, sems):
    low0[2 * rows :, :] = factors[...]
    wind_in = pltpu.make_async_copy(winds, wind_rows.at[pl.ds(1, rows)], sems.at[0])
    wind_in.start()
    wind_rows[0] = jnp.zeros_like(wind_rows[0])
    wind_rows[rows + 1] = jnp.zeros_like(wind_rows[0])
    sums = dot(spread[...], sel[:, : rows * LANES], (1, 0))
    for i in range(rows):
        lanes = slice(i * LANES, (i + 1) * LANES)
        adjoint[i] = sums[:width, lanes] + sums[width:, lanes]
        for f in range(2):
            low0[f * rows + i : f * rows + i + 1, :] = adjoint[i, f * (width // 2) : f * (width // 2) + 1, :]
    wind_in.wait()


def local(state_incr, winds, coupling, background, obs_dest, obs_col, obs_op, obs_prec):
    _, fields, levels, rows, lanes = state_incr.shape
    width = fields * levels
    groups = width // GROUP
    tiles = lax.axis_size("gx") * lax.axis_size("gy")
    count = obs_col.shape[0]
    cap = 2 * count // tiles
    halves = obs_op.shape[1] // LANES

    scale = jnp.broadcast_to(background.reshape(width, 1), (width, LANES))

    vmem = pl.BlockSpec(memory_space=pltpu.VMEM)
    anywhere = pl.BlockSpec(memory_space=pl.ANY)
    own = pltpu.VMEM((rows, width, LANES), jnp.float32)
    framed = pltpu.VMEM((rows + 2, width, LANES), jnp.float32)
    packed_shape = f32(groups // PARTS * GROUP, LANES)
    sides = pltpu.VMEM(packed_shape.shape, jnp.float32)
    strip_shapes = [f32(pair_sets(), width, LANES), packed_shape]
    long_shapes = [f32(pair_sets(), width + GROUP, LANES), f32(packed_shape.shape[0] + GROUP, LANES)]
    field_shape = f32(rows, width, LANES)
    framed_shape = f32(rows + 2, width, LANES)
    low_shape = f32(fields * rows, LANES)
    cols_shape = ((2 * width, rows * LANES), jnp.bfloat16)

    def sems(*shape):
        return pltpu.SemaphoreType.DMA(shape)

    def run(body, out_shape, scratch, args, far=(), out_far=(), **kw):
        args = [pltpu.with_memory_space_constraint(x, pltpu.HBM) if k in far else x for k, x in enumerate(args)]
        specs = [anywhere if k in far else vmem for k in range(len(args))]
        outs = [anywhere if k in out_far else vmem for k in range(len(out_shape))]
        out_shape = [pltpu.HBM(x.shape, x.dtype) if k in out_far else x for k, x in enumerate(out_shape)]
        return call(body, out_shape, scratch, in_specs=specs, out_specs=outs, **kw)(*args)

    def on_rows(body):
        return functools.partial(body, rows, levels)

    def swap_floor(floor):
        return lax.ppermute(floor, "comp", [(0, 1), (1, 0)])

    state = state_incr.reshape(width, rows, lanes)
    wind = winds.reshape(width, rows, lanes)
    floor_winds = winds[0, :, 0]
    slots = tiles * cap
    thin_shape = f32(GROUP, LANES)

    strips, packed, low0, low1 = run(
        on_rows(edges_kernel),
        strip_shapes + [low_shape] * 2,
        [pltpu.VMEM((width * rows, LANES), jnp.float32), sems(groups // PARTS)],
        (state_incr.reshape(width * rows, lanes),),
        far=(0,),
    )
    halos = exchange(strips, packed)

    send = call(functools.partial(route_kernel, tiles, cap), f32(tiles, halves * cap + GROUP, LANES))(
        obs_dest.reshape(1, count), obs_col.reshape(1, count), obs_prec.reshape(1, count), obs_op
    )
    send, halos[0], halos[2], state_far, wind_far = lax.optimization_barrier((send, halos[0], halos[2], state, wind))
    records = lax.all_to_all(send, ("gx", "gy"), split_axis=0, concat_axis=0, tiled=True)

    state_rows, wind_rows, state_later, wind_later = run(
        functools.partial(load_kernel, rows),
        [field_shape] * 4,
        [sems(4, rows)],
        (state_far, wind_far),
        far=(0, 1),
        out_far=(2, 3),
        traffic=10 * MIB,
    )
    halos[1], state_rows, wind_rows = lax.optimization_barrier((halos[1], state_rows, wind_rows))
    (floor,) = run(on_rows(forward_floor_kernel), [low_shape], [], (low0, low1, floor_winds, *halos))
    field, strips, packed, low0, low1, wind_ends, wind_dense, dense_g = run(
        on_rows(forward_kernel),
        [framed_shape]
        + long_shapes
        + [low_shape] * 2
        + [f32(2, levels, LANES), f32(groups // PARTS * GROUP // 2, LANES), thin_shape],
        [framed, sides],
        (coupling, swap_floor(floor), state_rows, wind_rows, *halos),
    )
    halos = exchange(strips, packed)
    (cols,) = run(
        on_rows(forward_again_kernel),
        [jax.ShapeDtypeStruct(*cols_shape)],
        [pltpu.VMEM(*cols_shape), sems(rows)],
        (field, wind_rows),
        out_far=(0,),
        traffic=20 * MIB,
    )
    cols, halos = lax.optimization_barrier((cols, halos))
    (floor,) = run(on_rows(forward_floor_kernel), [low_shape], [], (low0, low1, floor_winds, *halos))
    extra, bottom, factors = run(
        on_rows(outside_kernel),
        [jax.ShapeDtypeStruct((2 * width, 3 * LANES), jnp.bfloat16), low_shape, thin_shape],
        [sides],
        (coupling, floor, swap_floor(floor), wind_ends, wind_dense, *halos),
    )

    spread_shape = ((2 * width, slots), jnp.bfloat16)
    sel_shape = ((slots, (rows + 1) * LANES), jnp.bfloat16)
    spread, sel, strips, packed = run(
        functools.partial(innovate_kernel, rows, width, tiles, cap),
        [jax.ShapeDtypeStruct(*spread_shape), jax.ShapeDtypeStruct(*sel_shape)] + long_shapes,
        [
            pltpu.VMEM((2 * width, (rows + 1) * LANES), jnp.bfloat16),
            pltpu.VMEM((slots, LANES), jnp.float32),
            pltpu.VMEM((slots, 2 * width), jnp.float32),
            sems(8),
        ],
        (records, cols, extra, bottom, coupling, wind_ends, wind_dense, dense_g),
        far=(1,),
        limit=OBSERVE_VMEM,
    )
    halos = exchange(strips, packed)
    adjoint, low0, wind_rows = run(
        functools.partial(scatter_kernel, rows, width),
        [field_shape, f32(fields * rows + GROUP, LANES), framed_shape],
        [sems(1)],
        (spread, sel, wind_later, factors),
        far=(2,),
        limit=OBSERVE_VMEM,
        traffic=8 * MIB,
    )
    partner = swap_floor(low0)
    adjoint, ends, columns, low0, state_rows = run(
        on_rows(first_adjoint_kernel),
        [field_shape, f32(2, width, LANES), packed_shape, low_shape, field_shape],
        [framed, sems(1)],
        (coupling, adjoint, wind_rows, state_later),
        far=(3,),
        traffic=16 * MIB,
    )
    low0, partner, halos = lax.optimization_barrier((low0, partner, halos))
    floor, missing = run(
        on_rows(floor_kernel),
        [f32(fields * rows + GROUP, LANES), low_shape],
        [],
        (coupling, partner, low0, floor_winds, *halos),
    )
    floor, other = run(
        on_rows(level0_kernel),
        [low_shape, low_shape],
        [],
        (floor, swap_floor(floor), factors, partner),
    )
    strips, packed = run(
        on_rows(border_again_kernel),
        strip_shapes,
        [sides],
        (coupling, floor, other, missing, ends, columns, wind_ends, wind_dense, dense_g, *halos),
    )
    last_halos = exchange(strips, packed)
    (adjoint,) = run(
        on_rows(second_adjoint_kernel),
        [field_shape],
        [framed, sides],
        (coupling, floor, other, missing, adjoint, wind_rows, scale, state_rows, *halos),
        traffic=20 * MIB,
    )
    (result,) = run(
        on_rows(final_kernel),
        [f32(width, rows, LANES)],
        [own, sides, sems(rows)],
        (adjoint, *last_halos),
        out_far=(0,),
    )
    return result.reshape(state_incr.shape)


def solution(mesh):
    placed = (
        P("comp", None, None, "gx", "gy"),
        P("comp", None, None, "gx", "gy"),
        P("gx", "gy"),
        P("comp", None, None),
        P(("comp", "gx", "gy"), None),
        P(("comp", "gx", "gy")),
        P(("comp", "gx", "gy"), None),
        P(("comp", "gx", "gy")),
    )
    return jax.shard_map(
        local,
        mesh=mesh,
        in_specs=placed,
        out_specs=P("comp", None, None, "gx", "gy"),
        check_vma=False,
    )
```

```python
import functools

import jax
import jax.numpy as jnp
from jax import lax
from jax.experimental import pallas as pl
from jax.experimental.pallas import tpu as pltpu
from jax.sharding import PartitionSpec as P

HORIZ_MIX = 0.1
VERT_MIX = 0.15
LANES = 128
GROUP = 8
MIB = 1024 * 1024
SWEEP_VMEM = 16 * MIB
OBSERVE_VMEM = 22 * MIB


def call(body, out_shape, scratch=(), limit=SWEEP_VMEM, traffic=0, **kw):
    cost = pl.CostEstimate(flops=0, bytes_accessed=traffic, transcendentals=0) if traffic else None
    return pl.pallas_call(
        body,
        out_shape=out_shape,
        scratch_shapes=list(scratch),
        cost_estimate=cost,
        compiler_params=pltpu.CompilerParams(vmem_limit_bytes=limit),
        **kw,
    )


def f32(*shape):
    return jax.ShapeDtypeStruct(shape, jnp.float32)


def lane_iota(rows=GROUP):
    return lax.broadcasted_iota(jnp.int32, (rows, LANES), 1)


def sub_iota(rows=GROUP):
    return lax.broadcasted_iota(jnp.int32, (rows, LANES), 0)


def pair_swap(block, axis, start):
    count = lax.axis_size(axis)
    route = []
    for low in range(start, count - 1, 2):
        route += [(low, low + 1), (low + 1, low)]
    return lax.ppermute(block, axis, route)


def pair_sets():
    return 2 if lax.axis_size("gx") > 2 else 1


def exchange(strips, packed):
    y_even = pair_swap(packed, "gy", 0)
    y_odd = pair_swap(packed, "gy", 1)
    even, *odd = [pair_swap(strips[start], "gx", start) for start in range(pair_sets())]
    return [even, y_even, y_odd, *odd]


def is_odd(axis):
    return lax.rem(lax.axis_index(axis), 2) == 1


def read_sides(refs):
    even = refs[0]
    odd = refs[3] if len(refs) > 3 else None
    at_odd = is_odd("gx")

    def side(at, turned):
        other = jnp.zeros_like(even[at]) if odd is None else odd[at]
        return jnp.where(turned, other, even[at])

    return lambda at: side(at, jnp.logical_not(at_odd)), lambda at: side(at, at_odd)


PARTS = 4


def merged(y_even, y_odd, at):
    a, b = y_even[at, :], y_odd[at, :]
    lane = lax.broadcasted_iota(jnp.int32, a.shape, 1)
    return jnp.where((lane % 2 == 1) == jnp.logical_not(is_odd("gy")), a, b)


def merge_columns(y_even, y_odd, sides):
    sides[...] = merged(y_even, y_odd, slice(0, sides.shape[0]))


def slot_of(i, part, rows):
    return PARTS * (rows - 1 - i) + part


def side_columns(sides, i, group):
    m, part = group // PARTS, group % PARTS
    rows = LANES // (2 * PARTS)
    return pltpu.roll(sides[m * GROUP : (m + 1) * GROUP, :], LANES - 1 - 2 * slot_of(i, part, rows), 1)


def pack_into(total, value, slot):
    return jnp.where(lane_iota() // 2 == slot, pltpu.roll(value, 2 * slot + 1, 1), total)


def pack_block(packed, values, i, m):
    at = pl.ds(m * GROUP, GROUP)
    total = packed[at, :]
    for part, value in enumerate(values):
        total = pack_into(total, value, slot_of(i, part, LANES // (2 * PARTS)))
    packed[at, :] = total


CENTRE = 1.0 - 4.0 * HORIZ_MIX - 2.0 * VERT_MIX


def levels_around(cells, i, base, group, groups):
    here = cells[i + 1, pl.ds(base + group * GROUP, GROUP), :]
    if group == groups - 1:
        upper = jnp.where(sub_iota() == GROUP - 1, here, pltpu.roll(here, GROUP - 1, 0))
    else:
        upper = cells[i + 1, pl.ds(base + group * GROUP + 1, GROUP), :]
    if group == 0:
        lower = jnp.where(sub_iota() == 0, here, pltpu.roll(here, 1, 0))
    else:
        lower = cells[i + 1, pl.ds(base + group * GROUP - 1, GROUP), :]
    return here, upper, lower


def shifted(first, last, edge, rows=GROUP):
    lane = lane_iota(rows)
    right = pltpu.roll(jnp.where(lane == 0, edge, first), LANES - 1, 1)
    left = pltpu.roll(jnp.where(lane == LANES - 1, edge, last), 1, 1)
    return right, left


def forward_sum(here, vertical, after, before, right, left, u, w):
    return (
        CENTRE * here
        + VERT_MIX * vertical
        + HORIZ_MIX * ((after + before) + (right + left))
        - 0.5 * (u * (after - before) + w * (right - left))
    )


def forward_point(cells, winds, sides, i, f, group, levels):
    groups = levels // GROUP
    here, upper, lower = levels_around(cells, i, f * levels, group, groups)
    at = pl.ds(f * levels + group * GROUP, GROUP)
    right, left = shifted(here, here, 0.0 if sides is None else side_columns(sides, i, f * groups + group))
    u = winds[i, pl.ds(group * GROUP, GROUP), :]
    w = winds[i, pl.ds(levels + group * GROUP, GROUP), :]
    return forward_sum(here, upper + lower, cells[i + 2, at, :], cells[i, at, :], right, left, u, w)


def products(x, wind):
    slope = 0.5 * (wind * x)
    return HORIZ_MIX * x - slope, HORIZ_MIX * x + slope


def adjoint_point(cells, winds, i, f, group, levels):
    here, upper, lower = levels_around(cells, i, f * levels, group, levels // GROUP)
    at = pl.ds(f * levels + group * GROUP, GROUP)
    wind_at = pl.ds(group * GROUP, GROUP)
    after, before = cells[i + 2, at, :], cells[i, at, :]
    u_after, u_before = winds[i + 2, wind_at, :], winds[i, wind_at, :]
    down, up = products(here, winds[i + 1, pl.ds(levels + group * GROUP, GROUP), :])
    right, left = shifted(up, down, 0.0)
    return (
        CENTRE * here
        + VERT_MIX * (upper + lower)
        + HORIZ_MIX * (after + before)
        + 0.5 * (u_after * after - u_before * before)
        + (right + left)
    )


def shares_of(coupling):
    own = jnp.where(lax.axis_index("comp") == 0, 1.0, 0.5)
    return own * coupling, (1.5 - own) * coupling


def couple_forward(value, other, coupling):
    own, _ = shares_of(coupling)
    return value - own * (value - other)


def couple_adjoint(value, other, coupling):
    own, peer = shares_of(coupling)
    return value - own * value + peer * other


def coupled(rule, value, other, coupling, i, f, rows):
    mixed = rule(value, other[pl.ds(f * rows + i, 1), :], coupling[pl.ds(i, 1), :])
    return jnp.where(sub_iota() == 0, mixed, value)


def put_strip(strips, at, first, last):
    at_odd = is_odd("gx")
    strips[0, at, :] = jnp.where(at_odd, first, last)
    if strips.shape[0] > 1:
        strips[1, at, :] = jnp.where(at_odd, last, first)


def put_low(low, value, i, f, rows):
    for level in range(2):
        low[level][pl.ds(f * rows + i, 1), :] = value[level : level + 1]


class Rows:
    def __init__(self, source, target, sems, rows, as_it_comes, offset):
        self.source, self.target, self.sems = source, target, sems
        self.rows, self.as_it_comes, self.offset = rows, as_it_comes, offset

    def copy(self, i):
        row = self.source.at[:, i] if self.as_it_comes else self.source.at[i]
        return pltpu.make_async_copy(row, self.target.at[i + self.offset], self.sems.at[i])

    def wait(self, i):
        self.copy(i).wait()


def start_rows(rows, *groups):
    for i in range(rows):
        for group in groups:
            group.copy(i).start()


def edges_kernel(rows, levels, state, strips, packed, low0, low1, cells, sems):
    part_levels = PARTS * GROUP
    blocks = 2 * levels // part_levels

    def copy(m):
        return pltpu.make_async_copy(
            state.at[pl.ds(m * part_levels * rows, part_levels * rows)],
            cells.at[pl.ds(m * part_levels * rows, part_levels * rows)],
            sems.at[m],
        )

    for m in range(blocks):
        copy(m).start()

    def block(m, _):
        copy(m).wait()
        total = jnp.zeros((GROUP, LANES), jnp.float32)
        for part in range(PARTS):
            for i in range(rows):
                start = (m * PARTS + part) * GROUP * rows + i
                total = pack_into(total, cells[pl.ds(start, GROUP, stride=rows), :], slot_of(i, part, rows))
        packed[pl.ds(pl.multiple_of(m * GROUP, GROUP), GROUP), :] = total
        start = m * part_levels * rows
        first = cells[pl.ds(start, part_levels, stride=rows), :]
        last = cells[pl.ds(start + rows - 1, part_levels, stride=rows), :]
        put_strip(strips, pl.ds(pl.multiple_of(m * part_levels, part_levels), part_levels), first, last)
        return 0

    lax.fori_loop(0, blocks, block, 0)
    for f in range(2):
        for level, low in enumerate((low0, low1)):
            low[f * rows : (f + 1) * rows, :] = cells[pl.ds((f * levels + level) * rows, rows), :]


def floor_edge(halos, f, rows, levels):
    m = f * (levels // GROUP) // PARTS
    sides = jnp.broadcast_to(merged(halos[1], halos[2], pl.ds(m * GROUP, 1)), (rows, LANES))
    return pltpu.roll(sides, 2 * PARTS - 1, 1, stride=2 * PARTS, stride_axis=0)


def row_after(value, last, rows):
    return jnp.where(sub_iota(rows) == rows - 1, last, pltpu.roll(value, rows - 1, 0))


def row_before(value, first, rows):
    return jnp.where(sub_iota(rows) == 0, first, pltpu.roll(value, 1, 0))


def forward_floor_kernel(rows, levels, low0, low1, winds, *rest):
    *halos, floor = rest
    side_before, side_after = read_sides(halos)
    for f in range(2):
        here = pl.ds(f * rows, rows)
        at = pl.ds(f * levels, 1)
        low, up = low0[here, :], low1[here, :]
        after, before = row_after(low, side_after(at), rows), row_before(low, side_before(at), rows)
        right, left = shifted(low, low, floor_edge(halos, f, rows, levels), rows)
        floor[here, :] = forward_sum(low, up + low, after, before, right, left, winds[0], winds[1])


class Out:
    def __init__(self, source, target, sems, rows, as_it_goes):
        self.source, self.target, self.sems, self.rows, self.as_it_goes = source, target, sems, rows, as_it_goes

    def copy(self, i):
        row = self.target.at[:, i] if self.as_it_goes else self.target.at[i]
        return pltpu.make_async_copy(self.source.at[i], row, self.sems.at[i])

    def start(self, i):
        self.copy(i).start()

    def finish(self):
        for i in range(self.rows):
            self.copy(i).wait()


def dense_row(field, first, rows):
    total = jnp.zeros((1, LANES), jnp.float32)
    lane = lax.broadcasted_iota(jnp.int32, (1, LANES), 1)
    for i in range(rows):
        slot = slot_of(i, 0, rows)
        total = jnp.where(lane // 2 == slot, pltpu.roll(field[first + i : first + i + 1, :], 2 * slot + 1, 1), total)
    return total


def load_kernel(rows, state, winds, state_rows, wind_rows, state_later, wind_later, sems):
    state_in = Rows(state, state_rows, sems.at[0], rows, True, 0)
    wind_in = Rows(winds, wind_rows, sems.at[1], rows, True, 0)
    state_out = Out(state_rows, state_later, sems.at[2], rows, False)
    wind_out = Out(wind_rows, wind_later, sems.at[3], rows, False)
    start_rows(rows, state_in, wind_in)
    for i in range(rows):
        state_in.wait(i)
        wind_in.wait(i)
        state_out.start(i)
        wind_out.start(i)
    state_out.finish()
    wind_out.finish()


def forward_kernel(rows, levels, coupling, other, field, winds, *rest):
    *halos, out, strips, packed, low0, low1, wind_ends, wind_dense, dense_g, cells, sides = rest
    packed[...] = jnp.zeros_like(packed)
    wind_dense[...] = jnp.zeros_like(wind_dense)
    merge_columns(halos[1], halos[2], sides)
    before, after = read_sides(halos)
    cells[0] = before(pl.ds(0, 2 * levels))
    cells[1] = field[0]
    cells[2] = field[1]
    cells[rows + 1] = after(pl.ds(0, 2 * levels))
    out[0] = jnp.zeros_like(out[0])
    out[rows + 1] = jnp.zeros_like(out[0])
    groups = levels // GROUP

    def row(i, _):
        for m in range(2 * groups // PARTS):
            f, start = m * PARTS // groups, m * PARTS % groups
            values = []
            for group in range(start, start + PARTS):
                value = forward_point(cells, winds, sides, i, f, group, levels)
                if group == 0:
                    value = coupled(couple_forward, value, other, coupling, i, f, rows)
                    put_low((low0, low1), value, i, f, rows)
                values.append(value)
            base = m * PARTS * GROUP
            for part, value in enumerate(values):
                out[i + 1, pl.ds(base + part * GROUP, GROUP), :] = value
            pack_block(packed, values, i, m)
            if f == 0:
                w = [winds[i, pl.ds(levels + base + part * GROUP, GROUP), :] for part in range(PARTS)]
                pack_block(wind_dense, w, i, m)
        ahead = jnp.minimum(i + 2, rows - 1)
        cells[ahead + 1] = field[ahead]
        return 0

    lax.fori_loop(0, rows, row, 0)
    put_strip(strips, pl.ds(0, 2 * levels), out[1], out[rows])
    wind_ends[0] = winds[0, pl.ds(0, levels), :]
    wind_ends[1] = winds[rows - 1, pl.ds(0, levels), :]
    dense_g[...] = jnp.broadcast_to(dense_row(coupling, 0, rows), dense_g.shape)
    _, peer = shares_of(coupling[...])
    first = products(peer[0:1], winds[0, 0:1, :])[1]
    last = products(peer[rows - 1 : rows], winds[rows - 1, 0:1, :])[0]
    whole = (GROUP, LANES)
    put_strip(strips, slice(2 * levels, 2 * levels + GROUP), jnp.broadcast_to(first, whole), jnp.broadcast_to(last, whole))
    _, peer = shares_of(dense_g[...])
    packed[packed.shape[0] - GROUP :, :] = first_and_last(peer, wind_dense[0:1, :])


def forward_again_kernel(rows, levels, cells, winds, cols, col_cells, col_sems):
    groups = levels // GROUP
    width = 2 * levels

    def col_copy(i):
        lanes = pl.ds(pl.multiple_of(i * LANES, LANES), LANES)
        return pltpu.make_async_copy(col_cells.at[:, lanes], cols.at[:, lanes], col_sems.at[i])

    def row(i, _):
        lanes = pl.ds(pl.multiple_of(i * LANES, LANES), LANES)
        for m in range(2 * groups // PARTS):
            f, start = m * PARTS // groups, m * PARTS % groups
            values = [forward_point(cells, winds, None, i, f, group, levels) for group in range(start, start + PARTS)]
            high, low = split(jnp.concatenate(values, axis=0), 2)
            col_cells[pl.ds(m * PARTS * GROUP, PARTS * GROUP), lanes] = high
            col_cells[pl.ds(width + m * PARTS * GROUP, PARTS * GROUP), lanes] = low
        col_copy(i).start()
        return 0

    lax.fori_loop(0, rows, row, 0)
    for i in range(rows):
        col_copy(i).wait()


def outside_kernel(rows, levels, coupling, floor, other, wind_ends, wind_dense, *rest):
    *halos, extra, bottom, factors, dense = rest
    width = 2 * levels
    tail = pl.ds(width, 1)
    factors[...] = jnp.zeros_like(factors)
    for k, side in enumerate(read_sides(halos)):
        factors[k : k + 1, :] = side(tail)
    factors[2:3, :] = merged(halos[1], halos[2], pl.ds(dense.shape[0], 1))
    for f in range(2):
        here = pl.ds(f * rows, rows)
        bottom[here, :] = couple_forward(floor[here, :], other[here, :], coupling[...])
    dense_products(dense, swap_pairs(merged(halos[1], halos[2], slice(0, dense.shape[0]))), wind_dense)
    before, after = read_sides(halos)
    sub = lax.broadcasted_iota(jnp.int32, (levels, LANES), 0)

    def put(value, f, lanes):
        high, low = split(jnp.where(sub == 0, 0.0, value), 2)
        extra[f * levels : (f + 1) * levels, lanes] = high
        extra[width + f * levels : width + (f + 1) * levels, lanes] = low

    lane = lane_iota()
    for f in range(2):
        at = pl.ds(f * levels, levels)
        put(products(before(at), wind_ends[0])[1], f, slice(0, LANES))
        put(products(after(at), wind_ends[1])[0], f, slice(LANES, 2 * LANES))
        thin = []
        for group in range(f * levels // GROUP, (f + 1) * levels // GROUP):
            m, part = group // PARTS, group % PARTS
            moved = pltpu.roll(dense[m * GROUP : (m + 1) * GROUP, :], (LANES - 2 * part) % LANES, 1)
            thin.append(jnp.where(lane % (2 * PARTS) < 2, moved, 0.0))
        put(jnp.concatenate(thin, axis=0), f, slice(2 * LANES, 3 * LANES))


def first_and_last(value, wind):
    down, up = products(value, wind)
    lane = lax.broadcasted_iota(jnp.int32, down.shape, 1)
    return jnp.where(lane % 2 == 1, up, down)


def dense_products(packed, value, wind_dense):
    half = wind_dense.shape[0]
    for f in range(2):
        at = slice(f * half, (f + 1) * half)
        packed[at, :] = first_and_last(value[at], wind_dense[...])


def level0_row(value, new, f):
    half = value.shape[0] // 2
    sub = lax.broadcasted_iota(jnp.int32, value.shape, 0)
    lane = lax.broadcasted_iota(jnp.int32, value.shape, 1)
    return jnp.where((sub == f * half) & (lane % (2 * PARTS) < 2), new, value)


def end_rows(ends, strips, wind_ends, levels):
    for f in range(2):
        at = slice(f * levels, (f + 1) * levels)
        put_strip(
            strips, at, products(ends[0][at], wind_ends[0])[1], products(ends[1][at], wind_ends[1])[0]
        )


def with_first(value, new):
    return jnp.where(lax.broadcasted_iota(jnp.int32, value.shape, 0) == 0, new, value)


def border_strips(rows, levels, coupling, ends, dense, wind_ends, wind_dense, dense_g, strips, packed):
    half = dense.shape[0] // 2
    width = 2 * levels
    own, _ = shares_of(dense_g[0:1, :])
    new = dense
    for f in range(2):
        bottom = dense[f * half : f * half + 1]
        new = level0_row(new, bottom - own * bottom, f)
        packed[2 * half + f : 2 * half + f + 1, :] = bottom
    dense_products(packed, new, wind_dense)
    full = []
    for k, i in enumerate((0, rows - 1)):
        own, _ = shares_of(coupling[i : i + 1, :])
        parts = []
        for f in range(2):
            value = ends[k][f * levels : (f + 1) * levels]
            parts.append(with_first(value, value[0:1] - own * value[0:1]))
        full.append(jnp.concatenate(parts, axis=0))
    end_rows(full, strips, wind_ends, levels)
    for f in range(2):
        at = f * levels
        put_strip(strips, slice(width + f, width + f + 1), ends[0][at : at + 1], ends[1][at : at + 1])


def to_border(low, before, after, sides, rows):
    sub, lane = sub_iota(rows), lane_iota(rows)
    low = low + jnp.where(sub == 0, before, 0.0) + jnp.where(sub == rows - 1, after, 0.0)
    edge = pltpu.roll(jnp.broadcast_to(sides, (rows, LANES)), 2 * PARTS - 1, 1, stride=2 * PARTS, stride_axis=0)
    edge = jnp.where(lane == 0, pltpu.roll(edge, 1, 1), pltpu.roll(edge, LANES - 1, 1))
    return low + jnp.where((lane == 0) | (lane == LANES - 1), edge, 0.0)


def floor_kernel(rows, levels, coupling, other, low0, winds, *rest):
    *halos, floor, missing = rest
    before, after = read_sides(halos)
    half = halos[1].shape[0] - GROUP
    for f in range(2):
        here = pl.ds(f * rows, rows)
        _, peer = shares_of(coupling[...])
        share = peer * other[here, :]
        x_down, x_up = products(share, winds[0])
        y_down, y_up = products(share, winds[1])
        right, left = shifted(y_up, y_down, 0.0, rows)
        spread = (row_after(x_up, 0.0, rows) + row_before(x_down, 0.0, rows)) + (right + left)
        spread = spread + (CENTRE + VERT_MIX) * share
        at = pl.ds(f * levels, 1)
        sides = merged(halos[1], halos[2], pl.ds(f * half // 2, 1))
        floor[here, :] = to_border(low0[here, :] + spread, before(at), after(at), sides, rows)
        missing[here, :] = VERT_MIX * share
    raw = 2 * rows
    floor[raw : raw + 2, :] = before(pl.ds(2 * levels, 2))
    floor[raw + 2 : raw + 4, :] = after(pl.ds(2 * levels, 2))
    floor[raw + 4 : raw + 6, :] = merged(halos[1], halos[2], pl.ds(half, 2))
    floor[raw + 6 : raw + GROUP, :] = jnp.zeros((2, LANES), jnp.float32)


def level0_kernel(rows, levels, floor, other, factors, partner, floor_out, other_out):
    raw = 2 * rows
    for mine, theirs, factor, at, out in ((floor, other, factors, 0, floor_out), (other, floor, partner, raw, other_out)):
        for f in range(2):
            here = pl.ds(f * rows, rows)
            parts = [factor[at + k : at + k + 1, :] * theirs[raw + 2 * k + f : raw + 2 * k + f + 1, :] for k in range(3)]
            out[here, :] = to_border(mine[here, :], *parts, rows)


def swap_pairs(value):
    lane = lax.broadcasted_iota(jnp.int32, value.shape, 1)
    return jnp.where(lane % 2 == 1, pltpu.roll(value, 1, 1), pltpu.roll(value, LANES - 1, 1))


def edge_lanes(sides, i, group):
    m, part = group // PARTS, group % PARTS
    rows = LANES // (2 * PARTS)
    moved = pltpu.roll(sides[m * GROUP : (m + 1) * GROUP, :], LANES - 1 - 2 * slot_of(i, part, rows), 1)
    lane = lane_iota()
    return jnp.where((lane == 0) | (lane == LANES - 1), moved, 0.0)


def with_level(value, level, new):
    return jnp.where(lax.broadcasted_iota(jnp.int32, value.shape, 0) == level, new, value)


def border_again_kernel(
    rows, levels, coupling, floor, other, missing, ends, columns, wind_ends, wind_dense, dense_g, *rest
):
    *halos, strips, packed, sides = rest
    before, after = read_sides(halos)
    sides[...] = swap_pairs(merged(halos[1], halos[2], slice(0, sides.shape[0])))
    half = columns.shape[0] // 2
    groups = levels // GROUP
    outer = [before(pl.ds(0, 2 * levels)), after(pl.ds(0, 2 * levels))]
    full = []
    for k, i in enumerate((0, rows - 1)):
        edges = jnp.concatenate([edge_lanes(sides, i, group) for group in range(2 * groups)], axis=0)
        value = ends[k] + outer[k] + edges
        parts = []
        for f in range(2):
            part = value[f * levels : (f + 1) * levels]
            at = slice(f * rows + i, f * rows + i + 1)
            part = part + with_level(jnp.zeros_like(part), 1, missing[at, :])
            parts.append(with_first(part, couple_adjoint(floor[at, :], other[at, :], coupling[i : i + 1, :])))
        full.append(jnp.concatenate(parts, axis=0))
    end_rows(full, strips, wind_ends, levels)
    dense = columns[...] + sides[...]
    corners = []
    for m in range(2 * groups // PARTS):
        total = jnp.zeros((GROUP, LANES), jnp.float32)
        for part in range(PARTS):
            at = slice((m * PARTS + part) * GROUP, (m * PARTS + part + 1) * GROUP)
            for k, i in enumerate((0, rows - 1)):
                total = pack_into(total, outer[k][at], slot_of(i, part, rows))
        corners.append(total)
    dense = dense + jnp.concatenate(corners, axis=0)
    for f in range(2):
        sub = lax.broadcasted_iota(jnp.int32, dense.shape, 0)
        dense = dense + jnp.where(sub == f * half + 1, dense_row(missing, f * rows, rows), 0.0)
        mine = dense_row(floor, f * rows, rows)
        mixed = couple_adjoint(mine, dense_row(other, f * rows, rows), dense_g[0:1, :])
        dense = level0_row(dense, mixed, f)
    dense_products(packed, dense, wind_dense)


def adjoint_rows(rows, levels, cells, winds, take, each, behind=None):
    groups = levels // GROUP
    cells[0] = jnp.zeros_like(cells[0])
    cells[rows + 1] = jnp.zeros_like(cells[0])
    take(0)
    take(1)

    def row(i, _):
        if behind is not None:
            behind(jnp.maximum(i - 1, 0))
        for m in range(2 * groups // PARTS):
            f, start = m * PARTS // groups, m * PARTS % groups
            each(i, m, f, start, [
                adjoint_point(cells, winds, i, f, group, levels) for group in range(start, start + PARTS)
            ])
        take(jnp.minimum(i + 2, rows - 2))
        return 0

    lax.fori_loop(0, rows, row, 0, unroll=1 if behind is None else 2)
    if behind is not None:
        behind(rows - 1)


def first_adjoint_kernel(rows, levels, coupling, field, winds, state, out, ends, columns, low0, state_rows, cells, sems):
    state_in = pltpu.make_async_copy(state, state_rows, sems.at[0])
    state_in.start()
    columns[...] = jnp.zeros_like(columns)

    def take(i):
        cells[i + 1] = field[i]
        for f in range(2):
            at = pl.ds(f * levels, GROUP)
            own, _ = shares_of(coupling[pl.ds(i, 1), :])
            value = field[i, at, :]
            cells[i + 1, at, :] = jnp.where(sub_iota() == 0, value - own * value, value)

    def each(i, m, f, start, values):
        for part, value in enumerate(values):
            out[i, pl.ds((m * PARTS + part) * GROUP, GROUP), :] = value
        if start == 0:
            low0[pl.ds(f * rows + i, 1), :] = values[0][0:1]

    def pack(i):
        for m in range(columns.shape[0] // GROUP):
            values = [out[i, pl.ds((m * PARTS + part) * GROUP, GROUP), :] for part in range(PARTS)]
            pack_block(columns, values, i, m)

    out[0] = jnp.zeros_like(out[0])
    take(rows - 1)
    adjoint_rows(rows, levels, cells, winds, take, each, pack)
    ends[0] = out[0]
    ends[1] = out[rows - 1]
    state_in.wait()


def second_adjoint_kernel(rows, levels, coupling, floor, other, missing, field, winds, scale, state, *rest):
    *halos, out, cells, sides = rest
    sides[...] = swap_pairs(merged(halos[1], halos[2], slice(0, sides.shape[0])))
    before, after = read_sides(halos)
    groups = levels // GROUP

    def take(i, outer=None):
        for group in range(2 * groups):
            at = pl.ds(group * GROUP, GROUP)
            value = field[i, at, :] + edge_lanes(sides, i, group)
            if outer is not None:
                value = value + outer(at)
            if group % groups == 0:
                here = pl.ds(group // groups * rows + i, 1)
                value = value + jnp.where(sub_iota() == 1, missing[here, :], 0.0)
                bottom = couple_adjoint(floor[here, :], other[here, :], coupling[pl.ds(i, 1), :])
                value = jnp.where(sub_iota() == 0, bottom, value)
            cells[i + 1, at, :] = value

    def take_inner(i):
        take(i, before if isinstance(i, int) and i == 0 else None)

    def each(i, m, f, start, values):
        for part, value in enumerate(values):
            at = pl.ds((m * PARTS + part) * GROUP, GROUP)
            out[i, at, :] = value + scale[at, :] * state[i, at, :]

    take(rows - 1, after)
    adjoint_rows(rows, levels, cells, winds, take_inner, each)


def final_kernel(rows, levels, field, *rest):
    *halos, out, cells, sides, sems = rest
    leaving = Out(cells, out, sems, rows, True)
    sides[...] = swap_pairs(merged(halos[1], halos[2], slice(0, sides.shape[0])))
    before, after = read_sides(halos)
    groups = levels // GROUP

    def add(i, outer):
        for group in range(2 * groups):
            at = pl.ds(group * GROUP, GROUP)
            value = field[i, at, :] + edge_lanes(sides, i, group)
            cells[i, at, :] = value if outer is None else value + outer(at)
        leaving.start(i)
        return 0

    lax.fori_loop(1, rows - 1, lambda i, _: add(i, None), 0, unroll=7)
    add(0, before)
    add(rows - 1, after)
    leaving.finish()


def split(value, terms):
    parts = []
    for _ in range(terms):
        part = value.astype(jnp.bfloat16)
        parts.append(part)
        value = value - part.astype(jnp.float32)
    return parts


def dot(a, b, contract):
    return lax.dot_general(a, b, ((contract[:1], contract[1:]), ((), ())), preferred_element_type=jnp.float32)


def route_kernel(tiles, cap, dest, col, prec, op, out):
    count = op.shape[0]
    width = op.shape[1]
    halves = width // LANES
    owner = lax.broadcasted_iota(jnp.int32, (tiles, count), 0)
    hits = owner == dest[...]
    ones = jnp.where(hits, 1.0, 0.0)
    earlier = lax.broadcasted_iota(jnp.int32, (count, count), 0) <= lax.broadcasted_iota(jnp.int32, (count, count), 1)
    running = dot(ones.astype(jnp.bfloat16), jnp.where(earlier, 1.0, 0.0).astype(jnp.bfloat16), (1, 0))
    slot = jnp.sum(running * ones, axis=0, keepdims=True) - 1.0
    slot = slot.astype(jnp.int32)
    place = dest[...] * cap + slot
    at_slot = lax.broadcasted_iota(jnp.int32, (LANES, count), 0) == slot
    at_slot = jnp.where(at_slot, 1.0, 0.0).astype(jnp.bfloat16)
    column = col[...].astype(jnp.float32)
    pieces = [ones * part.astype(jnp.float32) for part in split(column, 2) + split(prec[...], 3)]
    aux = dot(jnp.concatenate(pieces, axis=0).astype(jnp.bfloat16), at_slot, (1, 1))
    columns = aux[0:tiles] + aux[tiles : 2 * tiles]
    precs = (aux[2 * tiles : 3 * tiles] + aux[3 * tiles : 4 * tiles]) + aux[4 * tiles : 5 * tiles]
    sub = sub_iota()
    for owner_at in range(tiles):
        block = jnp.where(sub == 0, columns[owner_at : owner_at + 1], 0.0)
        block = jnp.where(sub == 1, precs[owner_at : owner_at + 1], block)
        out[owner_at, pl.ds(halves * cap, GROUP), :] = block
    rows_high, rows_low = split(op[...], 2)
    chunk = 256
    for first in range(0, tiles * cap, chunk):
        picks = lax.broadcasted_iota(jnp.int32, (chunk, count), 0) + first == place
        picks = jnp.where(picks, 1.0, 0.0).astype(jnp.bfloat16)
        moved = dot(picks, rows_high, (1, 0)) + dot(picks, rows_low, (1, 0))
        for part in range(chunk // cap):
            for half in range(halves):
                out[first // cap + part, pl.ds(half * cap, cap), :] = moved[
                    part * cap : (part + 1) * cap, half * LANES : (half + 1) * LANES
                ]


def innovate_kernel(rows, width, tiles, cap, records, cols, extra, bottom, *rest):
    coupling, wind_ends, wind_dense, dense_g, spread, sel, strips, packed = rest[:8]
    col_cells, precs, both, sems = rest[8:]
    inside = rows * LANES
    chunks = 8
    copies = []
    for part in range(chunks):
        at = pl.ds(part * (2 * width // chunks), 2 * width // chunks)
        copies.append(pltpu.make_async_copy(cols.at[at], col_cells.at[at, pl.ds(0, inside)], sems.at[part]))
        copies[-1].start()
    halves = width // LANES
    count = tiles * cap
    aux = halves * cap
    own = lax.broadcasted_iota(jnp.int32, (cap, LANES), 1) == lax.broadcasted_iota(jnp.int32, (cap, LANES), 0)
    ones = jnp.ones((LANES, LANES), jnp.bfloat16)
    step = 512
    lane = lax.broadcasted_iota(jnp.int32, (step, LANES), 1)
    border = (rows - 1 - lane // (2 * PARTS)) * LANES + jnp.where(lane % 2 == 1, 0, LANES - 1)
    border = jnp.where(lane % (2 * PARTS) < 2, border, -1).astype(jnp.float32)
    lane = lane.astype(jnp.float32)

    def select(block, _):
        sources = step // cap

        def spread_out(part):
            rows_of = [
                jnp.where(own, records[block * sources + s, pl.ds(aux + part, 1), :], 0.0) for s in range(sources)
            ]
            terms = split(jnp.concatenate(rows_of, axis=0), 2 + part)
            return sum(dot(term, ones, (1, 0)) for term in terms)

        at = pl.ds(pl.multiple_of(block * step, step), step)
        place = spread_out(0)
        column = place - lane
        precs[at, :] = spread_out(1)
        for i in range(rows):
            sel[at, i * LANES : (i + 1) * LANES] = jnp.where(column == float(i * LANES), 1.0, 0.0).astype(
                jnp.bfloat16
            )
        sel[at, inside:] = jnp.where(place == border, 1.0, 0.0).astype(jnp.bfloat16)
        return 0

    lax.fori_loop(0, count // step, select, 0)
    for copy in copies:
        copy.wait()
    pair = 2 * GROUP
    first = lax.broadcasted_iota(jnp.int32, (pair, LANES), 0) == 0
    for f in range(2):
        for i in range(rows):
            lanes = slice(i * LANES, (i + 1) * LANES)
            for term, value in enumerate(split(bottom[f * rows + i : f * rows + i + 1, :], 2)):
                at = pl.ds(term * width + f * (width // 2), pair)
                old = col_cells[at, lanes].astype(jnp.float32)
                new = jnp.where(first, value.astype(jnp.float32), old)
                col_cells[at, lanes] = new.astype(jnp.bfloat16)
    for k, i in enumerate((0, rows - 1)):
        lanes = slice(i * LANES, (i + 1) * LANES)
        old = col_cells[:width, lanes].astype(jnp.float32) + col_cells[width:, lanes].astype(jnp.float32)
        more = extra[:, k * LANES : (k + 1) * LANES].astype(jnp.float32)
        high, low = split(old + (more[:width] + more[width:]), 2)
        col_cells[:width, lanes] = high
        col_cells[width:, lanes] = low
    col_cells[:, inside:] = extra[:, 2 * LANES :]
    both[...] = dot(sel[...], col_cells[...], (1, 1))

    def weigh(block, _):
        at = pl.ds(pl.multiple_of(block * LANES, LANES), LANES)
        sources = LANES // cap
        ops = [
            jnp.concatenate(
                [records[block * sources + s, half * cap : (half + 1) * cap, :] for s in range(sources)], axis=0
            )
            for half in range(halves)
        ]
        total = sum(
            (both[at, half * LANES : (half + 1) * LANES] + both[at, width + half * LANES : width + (half + 1) * LANES])
            * ops[half]
            for half in range(halves)
        )
        innovation = jnp.sum(total, axis=1, keepdims=True) * precs[at, :]
        for half in range(halves):
            high, low = split((ops[half] * innovation).T, 2)
            spread[half * LANES : (half + 1) * LANES, at] = high
            spread[width + half * LANES : width + (half + 1) * LANES, at] = low
        return 0

    lax.fori_loop(0, count // LANES, weigh, 0, unroll=4)

    border_cells = jnp.concatenate([sel[:, 0:LANES], sel[:, (rows - 1) * LANES :]], axis=1)
    terms = dot(spread[...], border_cells, (1, 0))
    border_sums = terms[:width] + terms[width:]
    thin = border_sums[:, 2 * LANES :]
    dense = []
    for m in range(width // (GROUP * PARTS)):
        total = thin[m * PARTS * GROUP : (m * PARTS + 1) * GROUP]
        for part in range(1, PARTS):
            at = (m * PARTS + part) * GROUP
            total = total + pltpu.roll(thin[at : at + GROUP], 2 * part, 1)
        dense.append(total)
    ends = (border_sums[:, 0:LANES], border_sums[:, LANES : 2 * LANES])
    packed[packed.shape[0] - GROUP :, :] = jnp.zeros((GROUP, LANES), jnp.float32)
    put_strip(strips, slice(width, width + GROUP), *[jnp.zeros((GROUP, LANES), jnp.float32)] * 2)
    border_strips(
        rows, width // 2, coupling, ends, jnp.concatenate(dense, axis=0), wind_ends, wind_dense, dense_g, strips, packed
    )


def scatter_kernel(rows, width, spread, sel, winds, factors, adjoint, low0, wind_rows, sems):
    low0[2 * rows :, :] = factors[...]
    wind_in = pltpu.make_async_copy(winds, wind_rows.at[pl.ds(1, rows)], sems.at[0])
    wind_in.start()
    wind_rows[0] = jnp.zeros_like(wind_rows[0])
    wind_rows[rows + 1] = jnp.zeros_like(wind_rows[0])
    sums = dot(spread[...], sel[:, : rows * LANES], (1, 0))
    for i in range(rows):
        lanes = slice(i * LANES, (i + 1) * LANES)
        adjoint[i] = sums[:width, lanes] + sums[width:, lanes]
        for f in range(2):
            low0[f * rows + i : f * rows + i + 1, :] = adjoint[i, f * (width // 2) : f * (width // 2) + 1, :]
    wind_in.wait()


def local(state_incr, winds, coupling, background, obs_dest, obs_col, obs_op, obs_prec):
    _, fields, levels, rows, lanes = state_incr.shape
    width = fields * levels
    groups = width // GROUP
    tiles = lax.axis_size("gx") * lax.axis_size("gy")
    count = obs_col.shape[0]
    cap = 2 * count // tiles
    halves = obs_op.shape[1] // LANES

    scale = jnp.broadcast_to(background.reshape(width, 1), (width, LANES))

    vmem = pl.BlockSpec(memory_space=pltpu.VMEM)
    anywhere = pl.BlockSpec(memory_space=pl.ANY)
    own = pltpu.VMEM((rows, width, LANES), jnp.float32)
    framed = pltpu.VMEM((rows + 2, width, LANES), jnp.float32)
    packed_shape = f32(groups // PARTS * GROUP, LANES)
    sides = pltpu.VMEM(packed_shape.shape, jnp.float32)
    strip_shapes = [f32(pair_sets(), width, LANES), packed_shape]
    long_shapes = [f32(pair_sets(), width + GROUP, LANES), f32(packed_shape.shape[0] + GROUP, LANES)]
    field_shape = f32(rows, width, LANES)
    framed_shape = f32(rows + 2, width, LANES)
    low_shape = f32(fields * rows, LANES)
    cols_shape = ((2 * width, rows * LANES), jnp.bfloat16)

    def sems(*shape):
        return pltpu.SemaphoreType.DMA(shape)

    def run(body, out_shape, scratch, args, far=(), out_far=(), **kw):
        args = [pltpu.with_memory_space_constraint(x, pltpu.HBM) if k in far else x for k, x in enumerate(args)]
        specs = [anywhere if k in far else vmem for k in range(len(args))]
        outs = [anywhere if k in out_far else vmem for k in range(len(out_shape))]
        out_shape = [pltpu.HBM(x.shape, x.dtype) if k in out_far else x for k, x in enumerate(out_shape)]
        return call(body, out_shape, scratch, in_specs=specs, out_specs=outs, **kw)(*args)

    def on_rows(body):
        return functools.partial(body, rows, levels)

    def swap_floor(floor):
        return lax.ppermute(floor, "comp", [(0, 1), (1, 0)])

    state = state_incr.reshape(width, rows, lanes)
    wind = winds.reshape(width, rows, lanes)
    floor_winds = winds[0, :, 0]
    slots = tiles * cap
    thin_shape = f32(GROUP, LANES)

    strips, packed, low0, low1 = run(
        on_rows(edges_kernel),
        strip_shapes + [low_shape] * 2,
        [pltpu.VMEM((width * rows, LANES), jnp.float32), sems(groups // PARTS)],
        (state_incr.reshape(width * rows, lanes),),
        far=(0,),
    )
    halos = exchange(strips, packed)

    send = call(functools.partial(route_kernel, tiles, cap), f32(tiles, halves * cap + GROUP, LANES))(
        obs_dest.reshape(1, count), obs_col.reshape(1, count), obs_prec.reshape(1, count), obs_op
    )
    send, halos[0], halos[2], state_far, wind_far = lax.optimization_barrier((send, halos[0], halos[2], state, wind))
    records = lax.all_to_all(send, ("gx", "gy"), split_axis=0, concat_axis=0, tiled=True)

    state_rows, wind_rows, state_later, wind_later = run(
        functools.partial(load_kernel, rows),
        [field_shape] * 4,
        [sems(4, rows)],
        (state_far, wind_far),
        far=(0, 1),
        out_far=(2, 3),
        traffic=10 * MIB,
    )
    halos[1], state_rows, wind_rows = lax.optimization_barrier((halos[1], state_rows, wind_rows))
    (floor,) = run(on_rows(forward_floor_kernel), [low_shape], [], (low0, low1, floor_winds, *halos))
    field, strips, packed, low0, low1, wind_ends, wind_dense, dense_g = run(
        on_rows(forward_kernel),
        [framed_shape]
        + long_shapes
        + [low_shape] * 2
        + [f32(2, levels, LANES), f32(groups // PARTS * GROUP // 2, LANES), thin_shape],
        [framed, sides],
        (coupling, swap_floor(floor), state_rows, wind_rows, *halos),
    )
    halos = exchange(strips, packed)
    (cols,) = run(
        on_rows(forward_again_kernel),
        [jax.ShapeDtypeStruct(*cols_shape)],
        [pltpu.VMEM(*cols_shape), sems(rows)],
        (field, wind_rows),
        out_far=(0,),
        traffic=20 * MIB,
    )
    cols, halos = lax.optimization_barrier((cols, halos))
    (floor,) = run(on_rows(forward_floor_kernel), [low_shape], [], (low0, low1, floor_winds, *halos))
    extra, bottom, factors = run(
        on_rows(outside_kernel),
        [jax.ShapeDtypeStruct((2 * width, 3 * LANES), jnp.bfloat16), low_shape, thin_shape],
        [sides],
        (coupling, floor, swap_floor(floor), wind_ends, wind_dense, *halos),
    )

    spread_shape = ((2 * width, slots), jnp.bfloat16)
    sel_shape = ((slots, (rows + 1) * LANES), jnp.bfloat16)
    spread, sel, strips, packed = run(
        functools.partial(innovate_kernel, rows, width, tiles, cap),
        [jax.ShapeDtypeStruct(*spread_shape), jax.ShapeDtypeStruct(*sel_shape)] + long_shapes,
        [
            pltpu.VMEM((2 * width, (rows + 1) * LANES), jnp.bfloat16),
            pltpu.VMEM((slots, LANES), jnp.float32),
            pltpu.VMEM((slots, 2 * width), jnp.float32),
            sems(8),
        ],
        (records, cols, extra, bottom, coupling, wind_ends, wind_dense, dense_g),
        far=(1,),
        limit=OBSERVE_VMEM,
    )
    halos = exchange(strips, packed)
    adjoint, low0, wind_rows = run(
        functools.partial(scatter_kernel, rows, width),
        [field_shape, f32(fields * rows + GROUP, LANES), framed_shape],
        [sems(1)],
        (spread, sel, wind_later, factors),
        far=(2,),
        limit=OBSERVE_VMEM,
        traffic=8 * MIB,
    )
    partner = swap_floor(low0)
    adjoint, ends, columns, low0, state_rows = run(
        on_rows(first_adjoint_kernel),
        [field_shape, f32(2, width, LANES), packed_shape, low_shape, field_shape],
        [framed, sems(1)],
        (coupling, adjoint, wind_rows, state_later),
        far=(3,),
        traffic=16 * MIB,
    )
    low0, partner, halos = lax.optimization_barrier((low0, partner, halos))
    floor, missing = run(
        on_rows(floor_kernel),
        [f32(fields * rows + GROUP, LANES), low_shape],
        [],
        (coupling, partner, low0, floor_winds, *halos),
    )
    floor, other = run(
        on_rows(level0_kernel),
        [low_shape, low_shape],
        [],
        (floor, swap_floor(floor), factors, partner),
    )
    strips, packed = run(
        on_rows(border_again_kernel),
        strip_shapes,
        [sides],
        (coupling, floor, other, missing, ends, columns, wind_ends, wind_dense, dense_g, *halos),
    )
    last_halos = exchange(strips, packed)
    (adjoint,) = run(
        on_rows(second_adjoint_kernel),
        [field_shape],
        [framed, sides],
        (coupling, floor, other, missing, adjoint, wind_rows, scale, state_rows, *halos),
        traffic=20 * MIB,
    )
    (result,) = run(
        on_rows(final_kernel),
        [f32(width, rows, LANES)],
        [own, sides, sems(rows)],
        (adjoint, *last_halos),
        out_far=(0,),
    )
    return result.reshape(state_incr.shape)


def solution(mesh):
    placed = (
        P("comp", None, None, "gx", "gy"),
        P("comp", None, None, "gx", "gy"),
        P("gx", "gy"),
        P("comp", None, None),
        P(("comp", "gx", "gy"), None),
        P(("comp", "gx", "gy")),
        P(("comp", "gx", "gy"), None),
        P(("comp", "gx", "gy")),
    )
    return jax.shard_map(
        local,
        mesh=mesh,
        in_specs=placed,
        out_specs=P("comp", None, None, "gx", "gy"),
        check_vma=False,
    )
```

```python
import functools

import jax
import jax.numpy as jnp
from jax import lax
from jax.experimental import pallas as pl
from jax.experimental.pallas import tpu as pltpu
from jax.sharding import PartitionSpec as P

HORIZ_MIX = 0.1
VERT_MIX = 0.15
LANES = 128
GROUP = 8
MIB = 1024 * 1024
SWEEP_VMEM = 16 * MIB
OBSERVE_VMEM = 22 * MIB


def call(body, out_shape, scratch=(), limit=SWEEP_VMEM, traffic=0, **kw):
    cost = pl.CostEstimate(flops=0, bytes_accessed=traffic, transcendentals=0) if traffic else None
    return pl.pallas_call(
        body,
        out_shape=out_shape,
        scratch_shapes=list(scratch),
        cost_estimate=cost,
        compiler_params=pltpu.CompilerParams(vmem_limit_bytes=limit),
        **kw,
    )


def f32(*shape):
    return jax.ShapeDtypeStruct(shape, jnp.float32)


def lane_iota(rows=GROUP):
    return lax.broadcasted_iota(jnp.int32, (rows, LANES), 1)


def sub_iota(rows=GROUP):
    return lax.broadcasted_iota(jnp.int32, (rows, LANES), 0)


def pair_swap(block, axis, start):
    count = lax.axis_size(axis)
    route = []
    for low in range(start, count - 1, 2):
        route += [(low, low + 1), (low + 1, low)]
    return lax.ppermute(block, axis, route)


def pair_sets():
    return 2 if lax.axis_size("gx") > 2 else 1


def exchange(strips, packed):
    y_even = pair_swap(packed, "gy", 0)
    y_odd = pair_swap(packed, "gy", 1)
    even, *odd = [pair_swap(strips[start], "gx", start) for start in range(pair_sets())]
    return [even, y_even, y_odd, *odd]


def is_odd(axis):
    return lax.rem(lax.axis_index(axis), 2) == 1


def read_sides(refs):
    even = refs[0]
    odd = refs[3] if len(refs) > 3 else None
    at_odd = is_odd("gx")

    def side(at, turned):
        other = jnp.zeros_like(even[at]) if odd is None else odd[at]
        return jnp.where(turned, other, even[at])

    return lambda at: side(at, jnp.logical_not(at_odd)), lambda at: side(at, at_odd)


PARTS = 4


def merged(y_even, y_odd, at):
    a, b = y_even[at, :], y_odd[at, :]
    lane = lax.broadcasted_iota(jnp.int32, a.shape, 1)
    return jnp.where((lane % 2 == 1) == jnp.logical_not(is_odd("gy")), a, b)


def merge_columns(y_even, y_odd, sides):
    sides[...] = merged(y_even, y_odd, slice(0, sides.shape[0]))


def slot_of(i, part, rows):
    return PARTS * (rows - 1 - i) + part


def side_columns(sides, i, group):
    m, part = group // PARTS, group % PARTS
    rows = LANES // (2 * PARTS)
    return pltpu.roll(sides[m * GROUP : (m + 1) * GROUP, :], LANES - 1 - 2 * slot_of(i, part, rows), 1)


def pack_into(total, value, slot):
    return jnp.where(lane_iota() // 2 == slot, pltpu.roll(value, 2 * slot + 1, 1), total)


def pack_block(packed, values, i, m):
    at = pl.ds(m * GROUP, GROUP)
    total = packed[at, :]
    for part, value in enumerate(values):
        total = pack_into(total, value, slot_of(i, part, LANES // (2 * PARTS)))
    packed[at, :] = total


CENTRE = 1.0 - 4.0 * HORIZ_MIX - 2.0 * VERT_MIX


def levels_around(cells, i, base, group, groups):
    here = cells[i + 1, pl.ds(base + group * GROUP, GROUP), :]
    if group == groups - 1:
        upper = jnp.where(sub_iota() == GROUP - 1, here, pltpu.roll(here, GROUP - 1, 0))
    else:
        upper = cells[i + 1, pl.ds(base + group * GROUP + 1, GROUP), :]
    if group == 0:
        lower = jnp.where(sub_iota() == 0, here, pltpu.roll(here, 1, 0))
    else:
        lower = cells[i + 1, pl.ds(base + group * GROUP - 1, GROUP), :]
    return here, upper, lower


def shifted(first, last, edge, rows=GROUP):
    lane = lane_iota(rows)
    right = pltpu.roll(jnp.where(lane == 0, edge, first), LANES - 1, 1)
    left = pltpu.roll(jnp.where(lane == LANES - 1, edge, last), 1, 1)
    return right, left


def forward_sum(here, vertical, after, before, right, left, u, w):
    return (
        CENTRE * here
        + VERT_MIX * vertical
        + HORIZ_MIX * ((after + before) + (right + left))
        - 0.5 * (u * (after - before) + w * (right - left))
    )


def forward_point(cells, winds, sides, i, f, group, levels):
    groups = levels // GROUP
    here, upper, lower = levels_around(cells, i, f * levels, group, groups)
    at = pl.ds(f * levels + group * GROUP, GROUP)
    right, left = shifted(here, here, 0.0 if sides is None else side_columns(sides, i, f * groups + group))
    u = winds[i, pl.ds(group * GROUP, GROUP), :]
    w = winds[i, pl.ds(levels + group * GROUP, GROUP), :]
    return forward_sum(here, upper + lower, cells[i + 2, at, :], cells[i, at, :], right, left, u, w)


def products(x, wind):
    slope = 0.5 * (wind * x)
    return HORIZ_MIX * x - slope, HORIZ_MIX * x + slope


def adjoint_point(cells, winds, i, f, group, levels):
    here, upper, lower = levels_around(cells, i, f * levels, group, levels // GROUP)
    at = pl.ds(f * levels + group * GROUP, GROUP)
    wind_at = pl.ds(group * GROUP, GROUP)
    after, before = cells[i + 2, at, :], cells[i, at, :]
    u_after, u_before = winds[i + 2, wind_at, :], winds[i, wind_at, :]
    down, up = products(here, winds[i + 1, pl.ds(levels + group * GROUP, GROUP), :])
    right, left = shifted(up, down, 0.0)
    return (
        CENTRE * here
        + VERT_MIX * (upper + lower)
        + HORIZ_MIX * (after + before)
        + 0.5 * (u_after * after - u_before * before)
        + (right + left)
    )


def shares_of(coupling):
    own = jnp.where(lax.axis_index("comp") == 0, 1.0, 0.5)
    return own * coupling, (1.5 - own) * coupling


def couple_forward(value, other, coupling):
    own, _ = shares_of(coupling)
    return value - own * (value - other)


def couple_adjoint(value, other, coupling):
    own, peer = shares_of(coupling)
    return value - own * value + peer * other


def coupled(rule, value, other, coupling, i, f, rows):
    mixed = rule(value, other[pl.ds(f * rows + i, 1), :], coupling[pl.ds(i, 1), :])
    return jnp.where(sub_iota() == 0, mixed, value)


def put_strip(strips, at, first, last):
    at_odd = is_odd("gx")
    strips[0, at, :] = jnp.where(at_odd, first, last)
    if strips.shape[0] > 1:
        strips[1, at, :] = jnp.where(at_odd, last, first)


def put_low(low, value, i, f, rows):
    for level in range(2):
        low[level][pl.ds(f * rows + i, 1), :] = value[level : level + 1]


class Rows:
    def __init__(self, source, target, sems, rows, as_it_comes, offset):
        self.source, self.target, self.sems = source, target, sems
        self.rows, self.as_it_comes, self.offset = rows, as_it_comes, offset

    def copy(self, i):
        row = self.source.at[:, i] if self.as_it_comes else self.source.at[i]
        return pltpu.make_async_copy(row, self.target.at[i + self.offset], self.sems.at[i])

    def wait(self, i):
        self.copy(i).wait()


def start_rows(rows, *groups):
    for i in range(rows):
        for group in groups:
            group.copy(i).start()


def edges_kernel(rows, levels, state, strips, packed, low0, low1, cells, sems):
    part_levels = PARTS * GROUP
    blocks = 2 * levels // part_levels

    def copy(m):
        return pltpu.make_async_copy(
            state.at[pl.ds(m * part_levels * rows, part_levels * rows)],
            cells.at[pl.ds(m * part_levels * rows, part_levels * rows)],
            sems.at[m],
        )

    for m in range(blocks):
        copy(m).start()

    def block(m, _):
        copy(m).wait()
        total = jnp.zeros((GROUP, LANES), jnp.float32)
        for part in range(PARTS):
            for i in range(rows):
                start = (m * PARTS + part) * GROUP * rows + i
                total = pack_into(total, cells[pl.ds(start, GROUP, stride=rows), :], slot_of(i, part, rows))
        packed[pl.ds(pl.multiple_of(m * GROUP, GROUP), GROUP), :] = total
        start = m * part_levels * rows
        first = cells[pl.ds(start, part_levels, stride=rows), :]
        last = cells[pl.ds(start + rows - 1, part_levels, stride=rows), :]
        put_strip(strips, pl.ds(pl.multiple_of(m * part_levels, part_levels), part_levels), first, last)
        return 0

    lax.fori_loop(0, blocks, block, 0)
    for f in range(2):
        for level, low in enumerate((low0, low1)):
            low[f * rows : (f + 1) * rows, :] = cells[pl.ds((f * levels + level) * rows, rows), :]


def floor_edge(halos, f, rows, levels):
    m = f * (levels // GROUP) // PARTS
    sides = jnp.broadcast_to(merged(halos[1], halos[2], pl.ds(m * GROUP, 1)), (rows, LANES))
    return pltpu.roll(sides, 2 * PARTS - 1, 1, stride=2 * PARTS, stride_axis=0)


def row_after(value, last, rows):
    return jnp.where(sub_iota(rows) == rows - 1, last, pltpu.roll(value, rows - 1, 0))


def row_before(value, first, rows):
    return jnp.where(sub_iota(rows) == 0, first, pltpu.roll(value, 1, 0))


def forward_floor_kernel(rows, levels, low0, low1, winds, *rest):
    *halos, floor = rest
    side_before, side_after = read_sides(halos)
    for f in range(2):
        here = pl.ds(f * rows, rows)
        at = pl.ds(f * levels, 1)
        low, up = low0[here, :], low1[here, :]
        after, before = row_after(low, side_after(at), rows), row_before(low, side_before(at), rows)
        right, left = shifted(low, low, floor_edge(halos, f, rows, levels), rows)
        floor[here, :] = forward_sum(low, up + low, after, before, right, left, winds[0], winds[1])


class Out:
    def __init__(self, source, target, sems, rows, as_it_goes):
        self.source, self.target, self.sems, self.rows, self.as_it_goes = source, target, sems, rows, as_it_goes

    def copy(self, i):
        row = self.target.at[:, i] if self.as_it_goes else self.target.at[i]
        return pltpu.make_async_copy(self.source.at[i], row, self.sems.at[i])

    def start(self, i):
        self.copy(i).start()

    def finish(self):
        for i in range(self.rows):
            self.copy(i).wait()


def dense_row(field, first, rows):
    total = jnp.zeros((1, LANES), jnp.float32)
    lane = lax.broadcasted_iota(jnp.int32, (1, LANES), 1)
    for i in range(rows):
        slot = slot_of(i, 0, rows)
        total = jnp.where(lane // 2 == slot, pltpu.roll(field[first + i : first + i + 1, :], 2 * slot + 1, 1), total)
    return total


def load_kernel(rows, state, winds, state_rows, wind_rows, state_later, wind_later, sems):
    state_in = Rows(state, state_rows, sems.at[0], rows, True, 0)
    wind_in = Rows(winds, wind_rows, sems.at[1], rows, True, 0)
    state_out = Out(state_rows, state_later, sems.at[2], rows, False)
    wind_out = Out(wind_rows, wind_later, sems.at[3], rows, False)
    start_rows(rows, state_in, wind_in)
    for i in range(rows):
        state_in.wait(i)
        wind_in.wait(i)
        state_out.start(i)
        wind_out.start(i)
    state_out.finish()
    wind_out.finish()


def forward_kernel(rows, levels, coupling, other, field, winds, *rest):
    *halos, out, strips, packed, low0, low1, wind_ends, wind_dense, dense_g, cells, sides = rest
    packed[...] = jnp.zeros_like(packed)
    wind_dense[...] = jnp.zeros_like(wind_dense)
    merge_columns(halos[1], halos[2], sides)
    before, after = read_sides(halos)
    cells[0] = before(pl.ds(0, 2 * levels))
    cells[1] = field[0]
    cells[rows + 1] = after(pl.ds(0, 2 * levels))
    out[0] = jnp.zeros_like(out[0])
    out[rows + 1] = jnp.zeros_like(out[0])
    groups = levels // GROUP

    def row(i, _):
        @pl.when(i < rows - 1)
        def _():
            cells[i + 2] = field[i + 1]

        for m in range(2 * groups // PARTS):
            f, start = m * PARTS // groups, m * PARTS % groups
            values = []
            for group in range(start, start + PARTS):
                value = forward_point(cells, winds, sides, i, f, group, levels)
                if group == 0:
                    value = coupled(couple_forward, value, other, coupling, i, f, rows)
                    put_low((low0, low1), value, i, f, rows)
                values.append(value)
            base = m * PARTS * GROUP
            for part, value in enumerate(values):
                out[i + 1, pl.ds(base + part * GROUP, GROUP), :] = value
            pack_block(packed, values, i, m)
            if f == 0:
                w = [winds[i, pl.ds(levels + base + part * GROUP, GROUP), :] for part in range(PARTS)]
                pack_block(wind_dense, w, i, m)
        return 0

    lax.fori_loop(0, rows, row, 0)
    put_strip(strips, pl.ds(0, 2 * levels), out[1], out[rows])
    wind_ends[0] = winds[0, pl.ds(0, levels), :]
    wind_ends[1] = winds[rows - 1, pl.ds(0, levels), :]
    dense_g[...] = jnp.broadcast_to(dense_row(coupling, 0, rows), dense_g.shape)
    _, peer = shares_of(coupling[...])
    first = products(peer[0:1], winds[0, 0:1, :])[1]
    last = products(peer[rows - 1 : rows], winds[rows - 1, 0:1, :])[0]
    whole = (GROUP, LANES)
    put_strip(strips, slice(2 * levels, 2 * levels + GROUP), jnp.broadcast_to(first, whole), jnp.broadcast_to(last, whole))
    _, peer = shares_of(dense_g[...])
    packed[packed.shape[0] - GROUP :, :] = first_and_last(peer, wind_dense[0:1, :])


def forward_again_kernel(rows, levels, cells, winds, cols, col_cells, col_sems):
    groups = levels // GROUP
    width = 2 * levels

    def col_copy(i):
        lanes = pl.ds(pl.multiple_of(i * LANES, LANES), LANES)
        return pltpu.make_async_copy(col_cells.at[:, lanes], cols.at[:, lanes], col_sems.at[i])

    def row(i, _):
        lanes = pl.ds(pl.multiple_of(i * LANES, LANES), LANES)
        for m in range(2 * groups // PARTS):
            f, start = m * PARTS // groups, m * PARTS % groups
            values = [forward_point(cells, winds, None, i, f, group, levels) for group in range(start, start + PARTS)]
            high, low = split(jnp.concatenate(values, axis=0), 2)
            col_cells[pl.ds(m * PARTS * GROUP, PARTS * GROUP), lanes] = high
            col_cells[pl.ds(width + m * PARTS * GROUP, PARTS * GROUP), lanes] = low
        col_copy(i).start()
        return 0

    lax.fori_loop(0, rows, row, 0)
    for i in range(rows):
        col_copy(i).wait()


def outside_kernel(rows, levels, coupling, floor, other, wind_ends, wind_dense, *rest):
    *halos, extra, bottom, factors, dense = rest
    width = 2 * levels
    tail = pl.ds(width, 1)
    factors[...] = jnp.zeros_like(factors)
    for k, side in enumerate(read_sides(halos)):
        factors[k : k + 1, :] = side(tail)
    factors[2:3, :] = merged(halos[1], halos[2], pl.ds(dense.shape[0], 1))
    for f in range(2):
        here = pl.ds(f * rows, rows)
        bottom[here, :] = couple_forward(floor[here, :], other[here, :], coupling[...])
    dense_products(dense, swap_pairs(merged(halos[1], halos[2], slice(0, dense.shape[0]))), wind_dense)
    before, after = read_sides(halos)
    sub = lax.broadcasted_iota(jnp.int32, (levels, LANES), 0)

    def put(value, f, lanes):
        high, low = split(jnp.where(sub == 0, 0.0, value), 2)
        extra[f * levels : (f + 1) * levels, lanes] = high
        extra[width + f * levels : width + (f + 1) * levels, lanes] = low

    lane = lane_iota()
    for f in range(2):
        at = pl.ds(f * levels, levels)
        put(products(before(at), wind_ends[0])[1], f, slice(0, LANES))
        put(products(after(at), wind_ends[1])[0], f, slice(LANES, 2 * LANES))
        thin = []
        for group in range(f * levels // GROUP, (f + 1) * levels // GROUP):
            m, part = group // PARTS, group % PARTS
            moved = pltpu.roll(dense[m * GROUP : (m + 1) * GROUP, :], (LANES - 2 * part) % LANES, 1)
            thin.append(jnp.where(lane % (2 * PARTS) < 2, moved, 0.0))
        put(jnp.concatenate(thin, axis=0), f, slice(2 * LANES, 3 * LANES))


def first_and_last(value, wind):
    down, up = products(value, wind)
    lane = lax.broadcasted_iota(jnp.int32, down.shape, 1)
    return jnp.where(lane % 2 == 1, up, down)


def dense_products(packed, value, wind_dense):
    half = wind_dense.shape[0]
    for f in range(2):
        at = slice(f * half, (f + 1) * half)
        packed[at, :] = first_and_last(value[at], wind_dense[...])


def level0_row(value, new, f):
    half = value.shape[0] // 2
    sub = lax.broadcasted_iota(jnp.int32, value.shape, 0)
    lane = lax.broadcasted_iota(jnp.int32, value.shape, 1)
    return jnp.where((sub == f * half) & (lane % (2 * PARTS) < 2), new, value)


def end_rows(ends, strips, wind_ends, levels):
    for f in range(2):
        at = slice(f * levels, (f + 1) * levels)
        put_strip(
            strips, at, products(ends[0][at], wind_ends[0])[1], products(ends[1][at], wind_ends[1])[0]
        )


def with_first(value, new):
    return jnp.where(lax.broadcasted_iota(jnp.int32, value.shape, 0) == 0, new, value)


def border_strips(rows, levels, coupling, ends, dense, wind_ends, wind_dense, dense_g, strips, packed):
    half = dense.shape[0] // 2
    width = 2 * levels
    own, _ = shares_of(dense_g[0:1, :])
    new = dense
    for f in range(2):
        bottom = dense[f * half : f * half + 1]
        new = level0_row(new, bottom - own * bottom, f)
        packed[2 * half + f : 2 * half + f + 1, :] = bottom
    dense_products(packed, new, wind_dense)
    full = []
    for k, i in enumerate((0, rows - 1)):
        own, _ = shares_of(coupling[i : i + 1, :])
        parts = []
        for f in range(2):
            value = ends[k][f * levels : (f + 1) * levels]
            parts.append(with_first(value, value[0:1] - own * value[0:1]))
        full.append(jnp.concatenate(parts, axis=0))
    end_rows(full, strips, wind_ends, levels)
    for f in range(2):
        at = f * levels
        put_strip(strips, slice(width + f, width + f + 1), ends[0][at : at + 1], ends[1][at : at + 1])


def to_border(low, before, after, sides, rows):
    sub, lane = sub_iota(rows), lane_iota(rows)
    low = low + jnp.where(sub == 0, before, 0.0) + jnp.where(sub == rows - 1, after, 0.0)
    edge = pltpu.roll(jnp.broadcast_to(sides, (rows, LANES)), 2 * PARTS - 1, 1, stride=2 * PARTS, stride_axis=0)
    edge = jnp.where(lane == 0, pltpu.roll(edge, 1, 1), pltpu.roll(edge, LANES - 1, 1))
    return low + jnp.where((lane == 0) | (lane == LANES - 1), edge, 0.0)


def floor_kernel(rows, levels, coupling, other, low0, winds, *rest):
    *halos, floor, missing = rest
    before, after = read_sides(halos)
    half = halos[1].shape[0] - GROUP
    for f in range(2):
        here = pl.ds(f * rows, rows)
        _, peer = shares_of(coupling[...])
        share = peer * other[here, :]
        x_down, x_up = products(share, winds[0])
        y_down, y_up = products(share, winds[1])
        right, left = shifted(y_up, y_down, 0.0, rows)
        spread = (row_after(x_up, 0.0, rows) + row_before(x_down, 0.0, rows)) + (right + left)
        spread = spread + (CENTRE + VERT_MIX) * share
        at = pl.ds(f * levels, 1)
        sides = merged(halos[1], halos[2], pl.ds(f * half // 2, 1))
        floor[here, :] = to_border(low0[here, :] + spread, before(at), after(at), sides, rows)
        missing[here, :] = VERT_MIX * share
    raw = 2 * rows
    floor[raw : raw + 2, :] = before(pl.ds(2 * levels, 2))
    floor[raw + 2 : raw + 4, :] = after(pl.ds(2 * levels, 2))
    floor[raw + 4 : raw + 6, :] = merged(halos[1], halos[2], pl.ds(half, 2))
    floor[raw + 6 : raw + GROUP, :] = jnp.zeros((2, LANES), jnp.float32)


def level0_kernel(rows, levels, floor, other, factors, partner, floor_out, other_out):
    raw = 2 * rows
    for mine, theirs, factor, at, out in ((floor, other, factors, 0, floor_out), (other, floor, partner, raw, other_out)):
        for f in range(2):
            here = pl.ds(f * rows, rows)
            parts = [factor[at + k : at + k + 1, :] * theirs[raw + 2 * k + f : raw + 2 * k + f + 1, :] for k in range(3)]
            out[here, :] = to_border(mine[here, :], *parts, rows)


def swap_pairs(value):
    lane = lax.broadcasted_iota(jnp.int32, value.shape, 1)
    return jnp.where(lane % 2 == 1, pltpu.roll(value, 1, 1), pltpu.roll(value, LANES - 1, 1))


def edge_lanes(sides, i, group):
    m, part = group // PARTS, group % PARTS
    rows = LANES // (2 * PARTS)
    moved = pltpu.roll(sides[m * GROUP : (m + 1) * GROUP, :], LANES - 1 - 2 * slot_of(i, part, rows), 1)
    lane = lane_iota()
    return jnp.where((lane == 0) | (lane == LANES - 1), moved, 0.0)


def with_level(value, level, new):
    return jnp.where(lax.broadcasted_iota(jnp.int32, value.shape, 0) == level, new, value)


def border_again_kernel(
    rows, levels, coupling, floor, other, missing, ends, columns, wind_ends, wind_dense, dense_g, *rest
):
    *halos, strips, packed, sides = rest
    before, after = read_sides(halos)
    sides[...] = swap_pairs(merged(halos[1], halos[2], slice(0, sides.shape[0])))
    half = columns.shape[0] // 2
    groups = levels // GROUP
    outer = [before(pl.ds(0, 2 * levels)), after(pl.ds(0, 2 * levels))]
    full = []
    for k, i in enumerate((0, rows - 1)):
        edges = jnp.concatenate([edge_lanes(sides, i, group) for group in range(2 * groups)], axis=0)
        value = ends[k] + outer[k] + edges
        parts = []
        for f in range(2):
            part = value[f * levels : (f + 1) * levels]
            at = slice(f * rows + i, f * rows + i + 1)
            part = part + with_level(jnp.zeros_like(part), 1, missing[at, :])
            parts.append(with_first(part, couple_adjoint(floor[at, :], other[at, :], coupling[i : i + 1, :])))
        full.append(jnp.concatenate(parts, axis=0))
    end_rows(full, strips, wind_ends, levels)
    dense = columns[...] + sides[...]
    corners = []
    for m in range(2 * groups // PARTS):
        total = jnp.zeros((GROUP, LANES), jnp.float32)
        for part in range(PARTS):
            at = slice((m * PARTS + part) * GROUP, (m * PARTS + part + 1) * GROUP)
            for k, i in enumerate((0, rows - 1)):
                total = pack_into(total, outer[k][at], slot_of(i, part, rows))
        corners.append(total)
    dense = dense + jnp.concatenate(corners, axis=0)
    for f in range(2):
        sub = lax.broadcasted_iota(jnp.int32, dense.shape, 0)
        dense = dense + jnp.where(sub == f * half + 1, dense_row(missing, f * rows, rows), 0.0)
        mine = dense_row(floor, f * rows, rows)
        mixed = couple_adjoint(mine, dense_row(other, f * rows, rows), dense_g[0:1, :])
        dense = level0_row(dense, mixed, f)
    dense_products(packed, dense, wind_dense)


def adjoint_rows(rows, levels, cells, winds, take, each, behind=None):
    groups = levels // GROUP
    cells[0] = jnp.zeros_like(cells[0])
    cells[rows + 1] = jnp.zeros_like(cells[0])
    take(0)
    take(1)

    def row(i, _):
        if behind is not None:
            behind(jnp.maximum(i - 1, 0))
        for m in range(2 * groups // PARTS):
            f, start = m * PARTS // groups, m * PARTS % groups
            each(i, m, f, start, [
                adjoint_point(cells, winds, i, f, group, levels) for group in range(start, start + PARTS)
            ])
        take(jnp.minimum(i + 2, rows - 2))
        return 0

    lax.fori_loop(0, rows, row, 0, unroll=1 if behind is None else 2)
    if behind is not None:
        behind(rows - 1)


def first_adjoint_kernel(rows, levels, coupling, field, winds, state, out, ends, columns, low0, state_rows, cells, sems):
    state_in = pltpu.make_async_copy(state, state_rows, sems.at[0])
    state_in.start()
    columns[...] = jnp.zeros_like(columns)

    def take(i):
        cells[i + 1] = field[i]
        for f in range(2):
            at = pl.ds(f * levels, GROUP)
            own, _ = shares_of(coupling[pl.ds(i, 1), :])
            value = field[i, at, :]
            cells[i + 1, at, :] = jnp.where(sub_iota() == 0, value - own * value, value)

    def each(i, m, f, start, values):
        for part, value in enumerate(values):
            out[i, pl.ds((m * PARTS + part) * GROUP, GROUP), :] = value
        if start == 0:
            low0[pl.ds(f * rows + i, 1), :] = values[0][0:1]

    def pack(i):
        for m in range(columns.shape[0] // GROUP):
            values = [out[i, pl.ds((m * PARTS + part) * GROUP, GROUP), :] for part in range(PARTS)]
            pack_block(columns, values, i, m)

    out[0] = jnp.zeros_like(out[0])
    take(rows - 1)
    adjoint_rows(rows, levels, cells, winds, take, each, pack)
    ends[0] = out[0]
    ends[1] = out[rows - 1]
    state_in.wait()


def second_adjoint_kernel(rows, levels, coupling, floor, other, missing, field, winds, scale, state, *rest):
    *halos, out, cells, sides = rest
    sides[...] = swap_pairs(merged(halos[1], halos[2], slice(0, sides.shape[0])))
    before, after = read_sides(halos)
    groups = levels // GROUP

    def take(i, outer=None):
        for group in range(2 * groups):
            at = pl.ds(group * GROUP, GROUP)
            value = field[i, at, :] + edge_lanes(sides, i, group)
            if outer is not None:
                value = value + outer(at)
            if group % groups == 0:
                here = pl.ds(group // groups * rows + i, 1)
                value = value + jnp.where(sub_iota() == 1, missing[here, :], 0.0)
                bottom = couple_adjoint(floor[here, :], other[here, :], coupling[pl.ds(i, 1), :])
                value = jnp.where(sub_iota() == 0, bottom, value)
            cells[i + 1, at, :] = value

    def take_inner(i):
        take(i, before if isinstance(i, int) and i == 0 else None)

    def each(i, m, f, start, values):
        for part, value in enumerate(values):
            at = pl.ds((m * PARTS + part) * GROUP, GROUP)
            out[i, at, :] = value + scale[at, :] * state[i, at, :]

    take(rows - 1, after)
    adjoint_rows(rows, levels, cells, winds, take_inner, each)


def final_kernel(rows, levels, field, *rest):
    *halos, out, cells, sides, sems = rest
    leaving = Out(cells, out, sems, rows, True)
    sides[...] = swap_pairs(merged(halos[1], halos[2], slice(0, sides.shape[0])))
    before, after = read_sides(halos)
    groups = levels // GROUP

    def add(i, outer):
        for group in range(2 * groups):
            at = pl.ds(group * GROUP, GROUP)
            value = field[i, at, :] + edge_lanes(sides, i, group)
            cells[i, at, :] = value if outer is None else value + outer(at)
        leaving.start(i)
        return 0

    lax.fori_loop(1, rows - 1, lambda i, _: add(i, None), 0, unroll=7)
    add(0, before)
    add(rows - 1, after)
    leaving.finish()


def split(value, terms):
    parts = []
    for _ in range(terms):
        part = value.astype(jnp.bfloat16)
        parts.append(part)
        value = value - part.astype(jnp.float32)
    return parts


def dot(a, b, contract):
    return lax.dot_general(a, b, ((contract[:1], contract[1:]), ((), ())), preferred_element_type=jnp.float32)


def route_kernel(tiles, cap, dest, col, prec, op, out):
    count = op.shape[0]
    width = op.shape[1]
    halves = width // LANES
    owner = lax.broadcasted_iota(jnp.int32, (tiles, count), 0)
    hits = owner == dest[...]
    ones = jnp.where(hits, 1.0, 0.0)
    earlier = lax.broadcasted_iota(jnp.int32, (count, count), 0) <= lax.broadcasted_iota(jnp.int32, (count, count), 1)
    running = dot(ones.astype(jnp.bfloat16), jnp.where(earlier, 1.0, 0.0).astype(jnp.bfloat16), (1, 0))
    slot = jnp.sum(running * ones, axis=0, keepdims=True) - 1.0
    slot = slot.astype(jnp.int32)
    place = dest[...] * cap + slot
    at_slot = lax.broadcasted_iota(jnp.int32, (LANES, count), 0) == slot
    at_slot = jnp.where(at_slot, 1.0, 0.0).astype(jnp.bfloat16)
    column = col[...].astype(jnp.float32)
    pieces = [ones * part.astype(jnp.float32) for part in split(column, 2) + split(prec[...], 3)]
    aux = dot(jnp.concatenate(pieces, axis=0).astype(jnp.bfloat16), at_slot, (1, 1))
    columns = aux[0:tiles] + aux[tiles : 2 * tiles]
    precs = (aux[2 * tiles : 3 * tiles] + aux[3 * tiles : 4 * tiles]) + aux[4 * tiles : 5 * tiles]
    sub = sub_iota()
    for owner_at in range(tiles):
        block = jnp.where(sub == 0, columns[owner_at : owner_at + 1], 0.0)
        block = jnp.where(sub == 1, precs[owner_at : owner_at + 1], block)
        out[owner_at, pl.ds(halves * cap, GROUP), :] = block
    rows_high, rows_low = split(op[...], 2)
    chunk = 256
    for first in range(0, tiles * cap, chunk):
        picks = lax.broadcasted_iota(jnp.int32, (chunk, count), 0) + first == place
        picks = jnp.where(picks, 1.0, 0.0).astype(jnp.bfloat16)
        moved = dot(picks, rows_high, (1, 0)) + dot(picks, rows_low, (1, 0))
        for part in range(chunk // cap):
            for half in range(halves):
                out[first // cap + part, pl.ds(half * cap, cap), :] = moved[
                    part * cap : (part + 1) * cap, half * LANES : (half + 1) * LANES
                ]


def innovate_kernel(rows, width, tiles, cap, records, cols, extra, bottom, *rest):
    coupling, wind_ends, wind_dense, dense_g, spread, sel, strips, packed = rest[:8]
    col_cells, precs, both, sems = rest[8:]
    inside = rows * LANES
    chunks = 4
    copies = []
    for part in range(chunks):
        at = pl.ds(part * (2 * width // chunks), 2 * width // chunks)
        copies.append(pltpu.make_async_copy(cols.at[at], col_cells.at[at, pl.ds(0, inside)], sems.at[part]))
        copies[-1].start()
    halves = width // LANES
    count = tiles * cap
    aux = halves * cap
    own = lax.broadcasted_iota(jnp.int32, (cap, LANES), 1) == lax.broadcasted_iota(jnp.int32, (cap, LANES), 0)
    ones = jnp.ones((LANES, LANES), jnp.bfloat16)
    step = 512
    lane = lax.broadcasted_iota(jnp.int32, (step, LANES), 1)
    border = (rows - 1 - lane // (2 * PARTS)) * LANES + jnp.where(lane % 2 == 1, 0, LANES - 1)
    border = jnp.where(lane % (2 * PARTS) < 2, border, -1).astype(jnp.float32)
    lane = lane.astype(jnp.float32)

    def select(block, _):
        sources = step // cap

        def spread_out(part):
            rows_of = [
                jnp.where(own, records[block * sources + s, pl.ds(aux + part, 1), :], 0.0) for s in range(sources)
            ]
            terms = split(jnp.concatenate(rows_of, axis=0), 2 + part)
            return sum(dot(term, ones, (1, 0)) for term in terms)

        at = pl.ds(pl.multiple_of(block * step, step), step)
        place = spread_out(0)
        column = place - lane
        precs[at, :] = spread_out(1)
        for i in range(rows):
            sel[at, i * LANES : (i + 1) * LANES] = jnp.where(column == float(i * LANES), 1.0, 0.0).astype(
                jnp.bfloat16
            )
        sel[at, inside:] = jnp.where(place == border, 1.0, 0.0).astype(jnp.bfloat16)
        return 0

    lax.fori_loop(0, count // step, select, 0)
    for copy in copies:
        copy.wait()
    pair = 2 * GROUP
    first = lax.broadcasted_iota(jnp.int32, (pair, LANES), 0) == 0
    for f in range(2):
        for i in range(rows):
            lanes = slice(i * LANES, (i + 1) * LANES)
            for term, value in enumerate(split(bottom[f * rows + i : f * rows + i + 1, :], 2)):
                at = pl.ds(term * width + f * (width // 2), pair)
                old = col_cells[at, lanes].astype(jnp.float32)
                new = jnp.where(first, value.astype(jnp.float32), old)
                col_cells[at, lanes] = new.astype(jnp.bfloat16)
    for k, i in enumerate((0, rows - 1)):
        lanes = slice(i * LANES, (i + 1) * LANES)
        old = col_cells[:width, lanes].astype(jnp.float32) + col_cells[width:, lanes].astype(jnp.float32)
        more = extra[:, k * LANES : (k + 1) * LANES].astype(jnp.float32)
        high, low = split(old + (more[:width] + more[width:]), 2)
        col_cells[:width, lanes] = high
        col_cells[width:, lanes] = low
    col_cells[:, inside:] = extra[:, 2 * LANES :]
    both[...] = dot(sel[...], col_cells[...], (1, 1))

    def weigh(block, _):
        at = pl.ds(pl.multiple_of(block * LANES, LANES), LANES)
        sources = LANES // cap
        ops = [
            jnp.concatenate(
                [records[block * sources + s, half * cap : (half + 1) * cap, :] for s in range(sources)], axis=0
            )
            for half in range(halves)
        ]
        total = sum(
            (both[at, half * LANES : (half + 1) * LANES] + both[at, width + half * LANES : width + (half + 1) * LANES])
            * ops[half]
            for half in range(halves)
        )
        innovation = jnp.sum(total, axis=1, keepdims=True) * precs[at, :]
        for half in range(halves):
            high, low = split((ops[half] * innovation).T, 2)
            spread[half * LANES : (half + 1) * LANES, at] = high
            spread[width + half * LANES : width + (half + 1) * LANES, at] = low
        return 0

    lax.fori_loop(0, count // LANES, weigh, 0, unroll=4)

    border_cells = jnp.concatenate([sel[:, 0:LANES], sel[:, (rows - 1) * LANES :]], axis=1)
    terms = dot(spread[...], border_cells, (1, 0))
    border_sums = terms[:width] + terms[width:]
    thin = border_sums[:, 2 * LANES :]
    dense = []
    for m in range(width // (GROUP * PARTS)):
        total = thin[m * PARTS * GROUP : (m * PARTS + 1) * GROUP]
        for part in range(1, PARTS):
            at = (m * PARTS + part) * GROUP
            total = total + pltpu.roll(thin[at : at + GROUP], 2 * part, 1)
        dense.append(total)
    ends = (border_sums[:, 0:LANES], border_sums[:, LANES : 2 * LANES])
    packed[packed.shape[0] - GROUP :, :] = jnp.zeros((GROUP, LANES), jnp.float32)
    put_strip(strips, slice(width, width + GROUP), *[jnp.zeros((GROUP, LANES), jnp.float32)] * 2)
    border_strips(
        rows, width // 2, coupling, ends, jnp.concatenate(dense, axis=0), wind_ends, wind_dense, dense_g, strips, packed
    )


def scatter_kernel(rows, width, spread, sel, winds, factors, adjoint, low0, wind_rows, sems):
    low0[2 * rows :, :] = factors[...]
    wind_in = pltpu.make_async_copy(winds, wind_rows.at[pl.ds(1, rows)], sems.at[0])
    wind_in.start()
    wind_rows[0] = jnp.zeros_like(wind_rows[0])
    wind_rows[rows + 1] = jnp.zeros_like(wind_rows[0])
    sums = dot(spread[...], sel[:, : rows * LANES], (1, 0))
    for i in range(rows):
        lanes = slice(i * LANES, (i + 1) * LANES)
        adjoint[i] = sums[:width, lanes] + sums[width:, lanes]
        for f in range(2):
            low0[f * rows + i : f * rows + i + 1, :] = adjoint[i, f * (width // 2) : f * (width // 2) + 1, :]
    wind_in.wait()


def local(state_incr, winds, coupling, background, obs_dest, obs_col, obs_op, obs_prec):
    _, fields, levels, rows, lanes = state_incr.shape
    width = fields * levels
    groups = width // GROUP
    tiles = lax.axis_size("gx") * lax.axis_size("gy")
    count = obs_col.shape[0]
    cap = 2 * count // tiles
    halves = obs_op.shape[1] // LANES

    scale = jnp.broadcast_to(background.reshape(width, 1), (width, LANES))

    vmem = pl.BlockSpec(memory_space=pltpu.VMEM)
    anywhere = pl.BlockSpec(memory_space=pl.ANY)
    own = pltpu.VMEM((rows, width, LANES), jnp.float32)
    framed = pltpu.VMEM((rows + 2, width, LANES), jnp.float32)
    packed_shape = f32(groups // PARTS * GROUP, LANES)
    sides = pltpu.VMEM(packed_shape.shape, jnp.float32)
    strip_shapes = [f32(pair_sets(), width, LANES), packed_shape]
    long_shapes = [f32(pair_sets(), width + GROUP, LANES), f32(packed_shape.shape[0] + GROUP, LANES)]
    field_shape = f32(rows, width, LANES)
    framed_shape = f32(rows + 2, width, LANES)
    low_shape = f32(fields * rows, LANES)
    cols_shape = ((2 * width, rows * LANES), jnp.bfloat16)

    def sems(*shape):
        return pltpu.SemaphoreType.DMA(shape)

    def run(body, out_shape, scratch, args, far=(), out_far=(), **kw):
        args = [pltpu.with_memory_space_constraint(x, pltpu.HBM) if k in far else x for k, x in enumerate(args)]
        specs = [anywhere if k in far else vmem for k in range(len(args))]
        outs = [anywhere if k in out_far else vmem for k in range(len(out_shape))]
        out_shape = [pltpu.HBM(x.shape, x.dtype) if k in out_far else x for k, x in enumerate(out_shape)]
        return call(body, out_shape, scratch, in_specs=specs, out_specs=outs, **kw)(*args)

    def on_rows(body):
        return functools.partial(body, rows, levels)

    def swap_floor(floor):
        return lax.ppermute(floor, "comp", [(0, 1), (1, 0)])

    state = state_incr.reshape(width, rows, lanes)
    wind = winds.reshape(width, rows, lanes)
    floor_winds = winds[0, :, 0]
    slots = tiles * cap
    thin_shape = f32(GROUP, LANES)

    strips, packed, low0, low1 = run(
        on_rows(edges_kernel),
        strip_shapes + [low_shape] * 2,
        [pltpu.VMEM((width * rows, LANES), jnp.float32), sems(groups // PARTS)],
        (state_incr.reshape(width * rows, lanes),),
        far=(0,),
    )
    halos = exchange(strips, packed)

    send = call(functools.partial(route_kernel, tiles, cap), f32(tiles, halves * cap + GROUP, LANES))(
        obs_dest.reshape(1, count), obs_col.reshape(1, count), obs_prec.reshape(1, count), obs_op
    )
    send, halos[0], halos[2], state_far, wind_far = lax.optimization_barrier((send, halos[0], halos[2], state, wind))
    records = lax.all_to_all(send, ("gx", "gy"), split_axis=0, concat_axis=0, tiled=True)

    state_rows, wind_rows, state_later, wind_later = run(
        functools.partial(load_kernel, rows),
        [field_shape] * 4,
        [sems(4, rows)],
        (state_far, wind_far),
        far=(0, 1),
        out_far=(2, 3),
        traffic=10 * MIB,
    )
    halos[1], state_rows, wind_rows = lax.optimization_barrier((halos[1], state_rows, wind_rows))
    (floor,) = run(on_rows(forward_floor_kernel), [low_shape], [], (low0, low1, floor_winds, *halos))
    field, strips, packed, low0, low1, wind_ends, wind_dense, dense_g = run(
        on_rows(forward_kernel),
        [framed_shape]
        + long_shapes
        + [low_shape] * 2
        + [f32(2, levels, LANES), f32(groups // PARTS * GROUP // 2, LANES), thin_shape],
        [framed, sides],
        (coupling, swap_floor(floor), state_rows, wind_rows, *halos),
    )
    halos = exchange(strips, packed)
    (cols,) = run(
        on_rows(forward_again_kernel),
        [jax.ShapeDtypeStruct(*cols_shape)],
        [pltpu.VMEM(*cols_shape), sems(rows)],
        (field, wind_rows),
        out_far=(0,),
        traffic=20 * MIB,
    )
    cols, halos = lax.optimization_barrier((cols, halos))
    (floor,) = run(on_rows(forward_floor_kernel), [low_shape], [], (low0, low1, floor_winds, *halos))
    extra, bottom, factors = run(
        on_rows(outside_kernel),
        [jax.ShapeDtypeStruct((2 * width, 3 * LANES), jnp.bfloat16), low_shape, thin_shape],
        [sides],
        (coupling, floor, swap_floor(floor), wind_ends, wind_dense, *halos),
    )

    spread_shape = ((2 * width, slots), jnp.bfloat16)
    sel_shape = ((slots, (rows + 1) * LANES), jnp.bfloat16)
    spread, sel, strips, packed = run(
        functools.partial(innovate_kernel, rows, width, tiles, cap),
        [jax.ShapeDtypeStruct(*spread_shape), jax.ShapeDtypeStruct(*sel_shape)] + long_shapes,
        [
            pltpu.VMEM((2 * width, (rows + 1) * LANES), jnp.bfloat16),
            pltpu.VMEM((slots, LANES), jnp.float32),
            pltpu.VMEM((slots, 2 * width), jnp.float32),
            sems(4),
        ],
        (records, cols, extra, bottom, coupling, wind_ends, wind_dense, dense_g),
        far=(1,),
        limit=OBSERVE_VMEM,
    )
    halos = exchange(strips, packed)
    adjoint, low0, wind_rows = run(
        functools.partial(scatter_kernel, rows, width),
        [field_shape, f32(fields * rows + GROUP, LANES), framed_shape],
        [sems(1)],
        (spread, sel, wind_later, factors),
        far=(2,),
        limit=OBSERVE_VMEM,
        traffic=8 * MIB,
    )
    partner = swap_floor(low0)
    adjoint, ends, columns, low0, state_rows = run(
        on_rows(first_adjoint_kernel),
        [field_shape, f32(2, width, LANES), packed_shape, low_shape, field_shape],
        [framed, sems(1)],
        (coupling, adjoint, wind_rows, state_later),
        far=(3,),
        traffic=16 * MIB,
    )
    low0, partner, halos = lax.optimization_barrier((low0, partner, halos))
    floor, missing = run(
        on_rows(floor_kernel),
        [f32(fields * rows + GROUP, LANES), low_shape],
        [],
        (coupling, partner, low0, floor_winds, *halos),
    )
    floor, other = run(
        on_rows(level0_kernel),
        [low_shape, low_shape],
        [],
        (floor, swap_floor(floor), factors, partner),
    )
    strips, packed = run(
        on_rows(border_again_kernel),
        strip_shapes,
        [sides],
        (coupling, floor, other, missing, ends, columns, wind_ends, wind_dense, dense_g, *halos),
    )
    last_halos = exchange(strips, packed)
    (adjoint,) = run(
        on_rows(second_adjoint_kernel),
        [field_shape],
        [framed, sides],
        (coupling, floor, other, missing, adjoint, wind_rows, scale, state_rows, *halos),
        traffic=20 * MIB,
    )
    (result,) = run(
        on_rows(final_kernel),
        [f32(width, rows, LANES)],
        [own, sides, sems(rows)],
        (adjoint, *last_halos),
        out_far=(0,),
    )
    return result.reshape(state_incr.shape)


def solution(mesh):
    placed = (
        P("comp", None, None, "gx", "gy"),
        P("comp", None, None, "gx", "gy"),
        P("gx", "gy"),
        P("comp", None, None),
        P(("comp", "gx", "gy"), None),
        P(("comp", "gx", "gy")),
        P(("comp", "gx", "gy"), None),
        P(("comp", "gx", "gy")),
    )
    return jax.shard_map(
        local,
        mesh=mesh,
        in_specs=placed,
        out_specs=P("comp", None, None, "gx", "gy"),
        check_vma=False,
    )
```
